32 devices in a mesh: grp: 2 (over y), chan: 4 (over z), win: 2 (over x), rep: 2 (over core).
Axes of the slice: x: 2, y: 2, z: 4, core: 2. Of those that a mesh axis runs over, the one named last changes fastest.
Arguments:
- sources: bfloat16 [8, 256, 4096], P(('grp', 'chan'), None, 'win'), parts along dimension 0, may hold values from -6 to 6
- receivers: bfloat16 [32, 4096], P(('grp', 'chan'), 'win'), parts along dimension 0, may hold values from -6 to 6
- plan: int32 [2, 2], P('grp'), parts along dimension 0, may hold values from 0 to 3, as said below
- pair_index: int32 [2, 4, 4, 512], P('grp', 'chan'), parts along dimension 0, may hold values from 0 to 2047, as said below
- keep: int32 [2, 4, 4, 512], P('grp', 'chan'), parts along dimension 0, may hold values 0 or 1
Outputs:
- stacks: float32 [8, 1, 4, 512, 2048], P(('grp', 'chan'), None, None, None, ('win', 'rep')), parts along dimension 0
The draws below stay inside these ranges and needn't reach their ends.
There are 2 independent parts, one for each index of `grp`. The reference program is written for one: setup_inputs(seed, part) draws one part's arguments, and reference() takes and returns one part's arrays. A program takes and returns all parts, laid end to end along the dimension named above; each array names one. Nothing has to cross between parts.
Inputs may be any that keep to these rules, and one draw needn't show every extreme that they name: `plan`: the entries of one round name different blocks. For each round k and group c, pair_index[k, c] names every number below 2048 exactly once.
All inputs are finite; a program needn't handle non-finite values. No bound on the sum of `keep` on one device may be relied on, other than what follows from the above.
Results may differ from the reference program's by a relative error of at most 0.0003.
Values may be sent and summed in bfloat16 or wider, within the bound.
No kernel may reach another device: no remote copies, remote signals or barrier semaphores. Data moves between devices by JAX's collectives and lax.ppermute only.
A program may use at most 64 MiB of HBM per device.

```python
import math
import jax
import jax.numpy as jnp
from jax import lax

SB = 256
LAGS = 2048
ROUNDS = 1
R_DEV = 4
NBLK = 4
CHANNELS = 16
NT = 4096
CAP = 512
N_CHAN = 4


def draw_plan(key, part):
    key = jax.random.fold_in(key, 11)
    order_key, place_key = jax.random.split(key)
    order = jax.random.permutation(order_key, NBLK).astype(jnp.int32)
    last_place = jnp.argmax(order == NBLK - 1).astype(jnp.int32)
    target = jax.random.randint(place_key, (), 0, 2 * ROUNDS, dtype=jnp.int32)
    order = jnp.roll(order, target - last_place)
    return order[:2 * ROUNDS].reshape(ROUNDS, 2).astype(jnp.int32)


def draw_pair_index(key, part):
    key = jax.random.fold_in(key, 23)
    keys = jax.random.split(key, ROUNDS * N_CHAN)
    orders = jax.vmap(lambda single_key: jax.random.permutation(single_key, 2 * SB * R_DEV))(keys)
    return orders.reshape(ROUNDS, N_CHAN, N_CHAN, CAP).astype(jnp.int32)


def with_ends(entries, own_key, smallest, largest):
    index_at = [jax.random.randint(jax.random.fold_in(own_key, axis), (), 0, length) for axis, length in enumerate(entries.shape)]
    main_axis = entries.shape.index(max(entries.shape))
    beside = index_at[:main_axis] + [(index_at[main_axis] + 1) % entries.shape[main_axis]] + index_at[main_axis + 1:]
    return entries.at[tuple(index_at)].set(smallest).at[tuple(beside)].set(largest)


def shard_levels(own_key, dims, cuts, low, top_value):
    def one(dim, shards_of):
        steps = jax.random.uniform(jax.random.fold_in(jax.random.fold_in(own_key, 6), dim), (shards_of,), jnp.float32, low / len(cuts), top_value / len(cuts))
        return jnp.repeat(jnp.exp(steps), dims[dim] // shards_of).reshape((-1,) + (1,) * (len(dims) - dim - 1))

    factor_of = one(*cuts[0])
    for cut in cuts[1:]:
        factor_of = factor_of * one(*cut)
    return factor_of


def normal_values(rng, shape, width, most, shards=(), held_as=jnp.bfloat16):
    loudness = shard_levels(rng, shape, shards, -0.22, 0.18) if shards else 1.0
    values = jax.random.normal(rng, shape, jnp.float32) * width * loudness
    return jnp.minimum(jnp.maximum(values, -most), most).astype(held_as)


def setup_inputs(seed: int = 0, part: int = 0) -> dict:
    arg_keys = jax.random.split(jax.random.key(seed), 6)
    own_keys = jax.random.split(jax.random.fold_in(arg_keys[5], part), 6)
    return {
        "sources": normal_values(own_keys[0], (NBLK, SB, NT), 1.0, 6.0, ((0, 4), (2, 2))),
        "receivers": normal_values(own_keys[1], (CHANNELS, NT), 1.0, 6.0, ((0, 4), (1, 2))),
        "plan": draw_plan(jax.random.fold_in(jax.random.fold_in(arg_keys[5], part), 71), part),
        "pair_index": draw_pair_index(jax.random.fold_in(jax.random.fold_in(arg_keys[5], part), 71), part),
        "keep": with_ends((jax.random.randint(own_keys[4], (ROUNDS, N_CHAN, N_CHAN, CAP), 0, 4) < 3).astype(jnp.int32), jax.random.fold_in(own_keys[4], 1), 0, 1),
    }


def reference(sources, receivers, plan, pair_index, keep):
    extended = jnp.concatenate([receivers, jnp.zeros((CHANNELS, LAGS), receivers.dtype)], axis=1)
    norming = 1.0 / math.sqrt(NT)
    lag_width = min(256, LAGS)
    lag_count = LAGS // lag_width
    offsets = jnp.arange(NT, dtype=jnp.int32)[:, None] + jnp.arange(lag_width, dtype=jnp.int32)[None, :]
    results = []
    for k in range(ROUNDS):
        source_rows = jnp.take(sources, plan[k], axis=0).reshape(2 * SB, NT).astype(jnp.float32)

        def per_group(group):
            channel_rows = lax.dynamic_slice_in_dim(extended, (group * R_DEV).astype(jnp.int32), R_DEV, 0)

            def per_lags(number):
                toeplitz = jnp.take(channel_rows, offsets + number * lag_width, axis=1).astype(jnp.float32)
                return jnp.einsum('st,rtk->srk', source_rows, toeplitz)
            blocks = lax.map(per_lags, jnp.arange(lag_count, dtype=jnp.int32))
            corr = jnp.moveaxis(blocks, 0, 2).reshape(2 * SB * R_DEV, LAGS) * norming
            chosen = jnp.take(corr, pair_index[k][group], axis=0)
            return chosen * keep[k][group][..., None].astype(jnp.float32)
        per_source = lax.map(per_group, jnp.arange(N_CHAN, dtype=jnp.int32))
        results.append(jnp.transpose(per_source, (1, 0, 2, 3)))
    return jnp.stack(results, axis=1)
```

```python
import functools
import math

import jax
import jax.numpy as jnp
from jax import lax
from jax.experimental import pallas as pl
from jax.experimental.pallas import tpu as pltpu
from jax.sharding import PartitionSpec as P

LAGS = 2048
LANES = 128
SHIFT_ROWS = 8
STEP = 2 * LANES
HANKEL_BYTES = 24 * 2**20
VMEM_BYTES = 48 * 2**20


def moved(block, axis, distance):
    devices = range(lax.axis_size(axis))
    route = [(i, i + distance) for i in devices if i + distance in devices]
    return lax.ppermute(block, axis, route)


def turned(block, axis, distance):
    size = lax.axis_size(axis)
    return lax.ppermute(block, axis, [(i, (i + distance) % size) for i in range(size)])


def hankel_rows(base, width):
    length = base.shape[1]
    rows = []
    for first in range(0, LANES, 2 * SHIFT_ROWS):
        both = []
        for shift in (first, first + SHIFT_ROWS):
            rolled = base if shift == 0 else pltpu.roll(base, length - shift, 1)
            both.append(rolled[:, :width])
        rows.append(jnp.concatenate(both, axis=0).astype(jnp.bfloat16))
    return jnp.concatenate(rows, axis=0)


def hankel_kernel(base_ref, out_ref):
    out_ref[0, 0] = hankel_rows(base_ref[0, 0], out_ref.shape[3])


def build_hankel(bases, width):
    channels, spans, rows, length = bases.shape
    return pl.pallas_call(
        hankel_kernel,
        grid=(channels, spans),
        in_specs=[pl.BlockSpec((1, 1, rows, length), lambda i, j: (i, j, 0, 0))],
        out_specs=pl.BlockSpec((1, 1, LANES, width), lambda i, j: (i, j, 0, 0)),
        out_shape=jax.ShapeDtypeStruct((channels, spans, LANES, width), jnp.bfloat16),
        cost_estimate=pl.CostEstimate(
            flops=channels * spans * LANES * width * 2,
            bytes_accessed=channels * spans * LANES * width * 2,
            transcendentals=0,
        ),
        compiler_params=pltpu.CompilerParams(vmem_limit_bytes=VMEM_BYTES // 2),
        name="hankel",
    )(bases)


def correlate_kernel(
    spans, halves, tile, norming, prebuilt, first, passes_ref, counts_ref, *refs
):
    pieces = refs[: spans * halves]
    signal_ref, row_ref, code_ref = refs[spans * halves : spans * halves + 3]
    rest = refs[spans * halves + 3 :]
    if not first:
        before_ref, rest = rest[0], rest[1:]
    out_ref, gathered, high, low = rest[:4]
    r_dev = signal_ref.shape[0]
    samples = pieces[0].shape[1]
    lag_dev = out_ref.shape[2]
    width = samples - LANES + lag_dev
    half_rows = pieces[0].shape[0]
    group = pl.program_id(0)

    if not prebuilt:
        hankel_ref = rest[4]
        for r in range(r_dev):
            for v in range(spans):
                hankel_ref[r, v] = hankel_rows(signal_ref[r, v], width)
    else:
        hankel_ref = signal_ref

    if first:
        out_ref[0] = jnp.zeros(out_ref.shape[1:], jnp.float32)
    else:
        out_ref[0] = before_ref[0]

    def one_pass(number, carry):
        for r in range(r_dev):
            slots = slice(r * tile, (r + 1) * tile)
            needed = counts_ref[group * r_dev + r] > number * tile

            @pl.when(needed)
            def _():
                start = pl.multiple_of((number * r_dev + r) * tile, 8)
                rows = row_ref[0, pl.ds(start, tile), :]
                lanes = lax.broadcasted_iota(jnp.int32, (tile, half_rows * halves), 1)
                pick = jnp.where(rows == lanes, 1.0, 0.0).astype(jnp.bfloat16)
                total = jnp.zeros((tile, lag_dev), jnp.float32)
                for v in range(spans):
                    for t in range(0, samples, STEP):
                        block = jnp.concatenate(
                            [pieces[v * halves + u][:, t : t + STEP] for u in range(halves)], axis=0
                        )
                        chosen = jnp.dot(pick, block, preferred_element_type=jnp.float32)
                        gathered[:, v * samples + t : v * samples + t + STEP] = chosen.astype(jnp.bfloat16)
                for v in range(spans):
                    for t in range(0, samples, STEP):
                        wide = jnp.concatenate(
                            [
                                hankel_ref[r, v, :, t : t + lag_dev],
                                hankel_ref[r, v, :, t + LANES : t + LANES + lag_dev],
                            ],
                            axis=0,
                        )
                        total += jnp.dot(
                            gathered[:, v * samples + t : v * samples + t + STEP],
                            wide,
                            preferred_element_type=jnp.float32,
                        )
                total = total * norming
                upper = total.astype(jnp.bfloat16)
                high[slots, :] = upper
                low[slots, :] = (total - upper.astype(jnp.float32)).astype(jnp.bfloat16)

            @pl.when(jnp.logical_not(needed))
            def _():
                high[slots, :] = jnp.zeros((tile, lag_dev), jnp.bfloat16)
                low[slots, :] = jnp.zeros((tile, lag_dev), jnp.bfloat16)

        codes = code_ref[0]
        lanes = lax.broadcasted_iota(jnp.int32, (codes.shape[0], r_dev * tile), 1)
        place = jnp.where(codes == lanes + number * (r_dev * tile), 1.0, 0.0).astype(jnp.bfloat16)
        out_ref[0] += jnp.dot(place, high[...], preferred_element_type=jnp.float32) + jnp.dot(
            place, low[...], preferred_element_type=jnp.float32
        )
        return carry

    lax.fori_loop(0, passes_ref[group], one_pass, 0)


def correlate(pieces, signal, prebuilt, rows, codes, passes, counts, before, tile, norming, lag_dev):
    spans, halves = len(pieces), len(pieces[0])
    flat = [piece for span in pieces for piece in span]
    groups, cap = codes.shape[:2]
    r_dev = signal.shape[0] // groups
    samples = flat[0].shape[1]
    first = before is None
    whole = lambda i, *_: (0, 0)
    in_specs = [pl.BlockSpec(piece.shape, whole) for piece in flat]
    in_specs.append(pl.BlockSpec((r_dev,) + signal.shape[1:], lambda i, *_: (i, 0, 0, 0)))
    in_specs.append(pl.BlockSpec((1,) + rows.shape[1:], lambda i, *_: (i, 0, 0)))
    in_specs.append(pl.BlockSpec((1,) + codes.shape[1:], lambda i, *_: (i, 0, 0)))
    args = flat + [signal, rows, codes]
    aliases = {}
    if not first:
        in_specs.append(pl.BlockSpec((1, cap, lag_dev), lambda i, *_: (i, 0, 0)))
        args.append(before)
        aliases = {len(args) + 1: 0}
    scratch = [
        pltpu.VMEM((tile, spans * samples), jnp.bfloat16),
        pltpu.VMEM((r_dev * tile, lag_dev), jnp.bfloat16),
        pltpu.VMEM((r_dev * tile, lag_dev), jnp.bfloat16),
    ]
    if not prebuilt:
        scratch.append(pltpu.VMEM((r_dev, spans, LANES, samples - LANES + lag_dev), jnp.bfloat16))
    body = functools.partial(correlate_kernel, spans, halves, tile, norming, prebuilt, first)
    return pl.pallas_call(
        body,
        grid_spec=pltpu.PrefetchScalarGridSpec(
            num_scalar_prefetch=2,
            grid=(groups,),
            in_specs=in_specs,
            out_specs=pl.BlockSpec((1, cap, lag_dev), lambda i, *_: (i, 0, 0)),
            scratch_shapes=scratch,
        ),
        out_shape=jax.ShapeDtypeStruct((groups, cap, lag_dev), jnp.float32),
        input_output_aliases=aliases,
        cost_estimate=pl.CostEstimate(
            flops=2 * groups * r_dev * tile * spans * samples * (lag_dev + halves * flat[0].shape[0]),
            bytes_accessed=signal.size * signal.dtype.itemsize + groups * cap * lag_dev * 4,
            transcendentals=0,
        ),
        compiler_params=pltpu.CompilerParams(vmem_limit_bytes=VMEM_BYTES),
        name="correlate",
    )(passes, counts, *args)


def shards(sources, receivers, plan, pair_index, keep):
    _, block_rows, samples = sources.shape
    r_dev = receivers.shape[0]
    n_chan = lax.axis_size("chan")
    n_win = lax.axis_size("win")
    n_rep = lax.axis_size("rep")
    chan, win, rep = lax.axis_index("chan"), lax.axis_index("win"), lax.axis_index("rep")
    cap = pair_index.shape[3]
    lag_dev = LAGS // (n_win * n_rep)
    half_rows = block_rows // n_rep
    tile = max(16, cap // 8)
    norming = 1.0 / math.sqrt(samples * n_win)

    packed = pair_index[0, 0] * 2 + keep[0, 0]
    lists = lax.all_to_all(packed, "chan", split_axis=0, concat_axis=0, tiled=True)

    heard = lax.all_gather(receivers, ("chan", "win"))
    heard = heard.reshape(n_chan, n_win, r_dev, samples).transpose(0, 2, 1, 3)
    heard = heard.reshape(n_chan * r_dev, n_win * samples)
    heard = jnp.pad(heard, ((0, 0), (0, LAGS + SHIFT_ROWS)))
    lag_start = (win * n_rep + rep) * lag_dev
    bases = []
    for v in range(n_win):
        begin = (win + n_win - v) % n_win * samples + lag_start
        span = lax.dynamic_slice_in_dim(heard, begin, samples + lag_dev + SHIFT_ROWS, 1)
        shifted = [span[:, i : i + samples + lag_dev] for i in range(SHIFT_ROWS)]
        bases.append(jnp.stack(shifted, axis=1))
    bases = jnp.stack(bases, axis=1).astype(jnp.float32)
    width = samples - LANES + lag_dev
    prebuilt = n_chan * r_dev * n_win * LANES * width * 2 <= HANKEL_BYTES
    signal = build_hankel(bases, width) if prebuilt else bases

    distance = jnp.abs(plan[0] - chan)
    nearer = jnp.where(distance[0] <= distance[1], 0, 1)
    owners = [jnp.where(nearer == 0, plan[0, 0], plan[0, 1]), jnp.where(nearer == 0, plan[0, 1], plan[0, 0])]

    pairs, kept = lists // 2, lists % 2
    source_row, receiver = pairs // r_dev, pairs % r_dev
    position = source_row // block_rows
    row = (source_row % block_rows + block_rows - rep * half_rows) % block_rows
    most = min(block_rows, cap)
    n_pass = -(-most // tile)
    turn = jnp.where(position == nearer, 0, 1)
    segments = turn * r_dev + receiver
    member = (segments[:, None, :] == jnp.arange(2 * r_dev)[None, :, None]) & (kept[:, None, :] == 1)
    below = (jnp.arange(cap)[:, None] < jnp.arange(cap)[None, :]).astype(jnp.bfloat16)
    before = jnp.einsum(
        "csi,ij->csj", member.astype(jnp.bfloat16), below, preferred_element_type=jnp.float32
    ).astype(jnp.int32)
    rank = jnp.sum(jnp.where(member, before, 0), axis=1)
    slot = rank // tile * (r_dev * tile) + receiver * tile + rank % tile
    counts = jnp.sum(member.astype(jnp.int32), axis=2)

    own = lax.dynamic_slice_in_dim(sources[0], rep * half_rows, half_rows, 0)
    arrived = {0: own}
    lower = upper = own
    for step in range(1, n_chan):
        lower = moved(lower, "chan", 1)
        upper = moved(upper, "chan", -1)
        arrived[-step], arrived[step] = lower, upper

    result = None
    for q in range(2):
        where = owners[q] - chan
        chosen = own
        reach = n_chan - 1 if q else n_chan - 2
        for offset in range(-reach, reach + 1):
            if offset:
                chosen = jnp.where(where == offset, arrived[offset], chosen)
        spans = [chosen] + [turned(chosen, "win", v) for v in range(1, n_win)]
        pieces = [[piece] + [turned(piece, "rep", -u) for u in range(1, n_rep)] for piece in spans]
        mine = (turn == q) & (kept == 1)
        codes = jnp.where(mine, slot, -1)
        slots = jnp.arange(n_pass * r_dev * tile)
        rows = jnp.sum(jnp.where(codes[:, None, :] == slots[None, :, None], row[:, None, :], 0), axis=2)
        of_turn = counts[:, q * r_dev : (q + 1) * r_dev]
        passes = -(-jnp.max(of_turn, axis=1) // tile)
        result = correlate(
            pieces, signal, prebuilt, rows[..., None], codes[..., None], passes, of_turn.reshape(-1), result,
            tile, norming, lag_dev,
        )
    return result[None, None]


def solution(mesh):
    placed = (
        P(("grp", "chan"), None, "win"),
        P(("grp", "chan"), "win"),
        P("grp", None),
        P("grp", "chan", None, None),
        P("grp", "chan", None, None),
    )
    return jax.shard_map(
        shards,
        mesh=mesh,
        in_specs=placed,
        out_specs=P(("grp", "chan"), None, None, None, ("win", "rep")),
        check_vma=False,
    )
```

```python
import functools
import math

import jax
import jax.numpy as jnp
from jax import lax
from jax.experimental import pallas as pl
from jax.experimental.pallas import tpu as pltpu
from jax.sharding import PartitionSpec as P

LAGS = 2048
LANES = 128
SHIFT_ROWS = 8
STEP = 2 * LANES
CHAINS = 2
DIGIT = 64
HANKEL_BYTES = 24 * 2**20
VMEM_BYTES = 48 * 2**20


def moved(block, axis, distance):
    devices = range(lax.axis_size(axis))
    route = [(i, i + distance) for i in devices if i + distance in devices]
    return lax.ppermute(block, axis, route)


def turned(block, axis, distance):
    size = lax.axis_size(axis)
    return lax.ppermute(block, axis, [(i, (i + distance) % size) for i in range(size)])


def hankel_rows(signal, width):
    length = signal.shape[1]
    base = jnp.broadcast_to(signal, (SHIFT_ROWS, length))
    sublane = lax.broadcasted_iota(jnp.int32, base.shape, 0)
    for bit in (1, 2, 4):
        base = jnp.where(sublane & bit != 0, pltpu.roll(base, length - bit, 1), base)
    rows = []
    for first in range(0, LANES, 2 * SHIFT_ROWS):
        both = []
        for shift in (first, first + SHIFT_ROWS):
            rolled = base if shift == 0 else pltpu.roll(base, length - shift, 1)
            both.append(rolled[:, :width])
        rows.append(jnp.concatenate(both, axis=0).astype(jnp.bfloat16))
    return jnp.concatenate(rows, axis=0)


def span_of(signal_ref, number, begin, length):
    return signal_ref[number, :, pl.ds(pl.multiple_of(begin, LANES), length)]


def hankel_kernel(length, begins_ref, signal_ref, *out_refs):
    for v, out_ref in enumerate(out_refs):
        out_ref[0] = hankel_rows(span_of(signal_ref, 0, begins_ref[v], length), out_ref.shape[2])


def build_hankel(signals, begins, width):
    channels = signals.shape[0]
    spans = begins.shape[0]
    shape = (channels, LANES, width)
    return pl.pallas_call(
        functools.partial(hankel_kernel, width + LANES),
        grid_spec=pltpu.PrefetchScalarGridSpec(
            num_scalar_prefetch=1,
            grid=(channels,),
            in_specs=[pl.BlockSpec((1,) + signals.shape[1:], lambda i, *_: (i, 0, 0))],
            out_specs=[pl.BlockSpec((1, LANES, width), lambda i, *_: (i, 0, 0))] * spans,
        ),
        out_shape=[jax.ShapeDtypeStruct(shape, jnp.bfloat16)] * spans,
        cost_estimate=pl.CostEstimate(
            flops=spans * math.prod(shape), bytes_accessed=2 * spans * math.prod(shape), transcendentals=0
        ),
        compiler_params=pltpu.CompilerParams(vmem_limit_bytes=VMEM_BYTES // 2),
        name="hankel",
    )(begins, signals)


def correlate_kernel(parts, tile, norming, prebuilt, first, passes_ref, counts_ref, begin_ref, *refs):
    pieces = refs[: 2 * parts]
    signal_ref, row_ref, code_ref = refs[2 * parts : 2 * parts + 3]
    rest = refs[2 * parts + 3 :]
    if not first:
        before_ref, rest = rest[0], rest[1:]
    out_ref, gathered, high, low = rest[:4]
    r_dev = signal_ref.shape[0]
    samples = pieces[0].shape[1]
    lag_dev = out_ref.shape[2]
    group = pl.program_id(0)

    if prebuilt:
        hankel_ref = signal_ref
    else:
        hankel_ref = rest[4]
        for r in range(r_dev):
            span = span_of(signal_ref, r, begin_ref[0], samples + lag_dev)
            hankel_ref[r] = hankel_rows(span, hankel_ref.shape[2])

    if first:
        out_ref[0] = jnp.zeros(out_ref.shape[1:], jnp.float32)
    else:
        out_ref[0] = before_ref[0]

    def one_pass(number, carry):
        for q in range(2):
            start = pl.multiple_of(number * r_dev * tile, 8)
            rows = row_ref[0, q, pl.ds(start, r_dev * tile), :]
            block_rows = parts * pieces[0].shape[0]
            lanes = lax.broadcasted_iota(jnp.int32, (r_dev * tile, block_rows), 1)
            pick = jnp.where(rows == lanes, 1.0, 0.0).astype(jnp.bfloat16)
            for t in range(0, samples, STEP):
                block = jnp.concatenate(
                    [piece[:, t : t + STEP] for piece in pieces[q * parts : (q + 1) * parts]], axis=0
                )
                chosen = jnp.dot(pick, block, preferred_element_type=jnp.float32)
                gathered[q, :, t : t + STEP] = chosen.astype(jnp.bfloat16)
        for r in range(r_dev):
            slots = slice(r * 2 * tile, (r + 1) * 2 * tile)
            needed = (number == 0) | (counts_ref[group * r_dev + r] > number * tile)

            @pl.when(needed)
            def _():
                chosen = jnp.concatenate([gathered[q, r * tile : (r + 1) * tile, :] for q in range(2)], axis=0)
                for lag in range(0, lag_dev, STEP):
                    wide = jnp.concatenate(
                        [hankel_ref[r, :, t + lag : t + lag + STEP] for t in range(0, samples, LANES)], axis=0
                    )
                    total = jnp.dot(chosen, wide, preferred_element_type=jnp.float32) * norming
                    upper = total.astype(jnp.bfloat16)
                    high[slots, lag : lag + STEP] = upper
                    low[slots, lag : lag + STEP] = (total - upper.astype(jnp.float32)).astype(jnp.bfloat16)

            @pl.when(jnp.logical_not(needed))
            def _():
                high[slots, :] = jnp.zeros((2 * tile, lag_dev), jnp.bfloat16)
                low[slots, :] = jnp.zeros((2 * tile, lag_dev), jnp.bfloat16)

        codes = code_ref[0]
        lanes = lax.broadcasted_iota(jnp.int32, (codes.shape[0], r_dev * 2 * tile), 1)
        place = jnp.where(codes == lanes + number * (r_dev * 2 * tile), 1.0, 0.0).astype(jnp.bfloat16)
        out_ref[0] += jnp.dot(place, high[...], preferred_element_type=jnp.float32) + jnp.dot(
            place, low[...], preferred_element_type=jnp.float32
        )
        return carry

    lax.fori_loop(0, passes_ref[group], one_pass, 0)


def correlate(pieces, signal, prebuilt, begin, rows, codes, passes, counts, before, tile, norming, lag_dev):
    parts = len(pieces) // 2
    groups, cap = codes.shape[:2]
    r_dev = signal.shape[0] // groups
    part_rows, samples = pieces[0].shape
    first = before is None
    in_specs = [pl.BlockSpec(piece.shape, lambda i, *_: (0, 0)) for piece in pieces]
    in_specs.append(pl.BlockSpec((r_dev,) + signal.shape[1:], lambda i, *_: (i, 0, 0)))
    in_specs.append(pl.BlockSpec((1,) + rows.shape[1:], lambda i, *_: (i, 0, 0, 0)))
    in_specs.append(pl.BlockSpec((1,) + codes.shape[1:], lambda i, *_: (i, 0, 0)))
    args = pieces + [signal, rows, codes]
    aliases = {}
    if not first:
        in_specs.append(pl.BlockSpec((1, cap, lag_dev), lambda i, *_: (i, 0, 0)))
        args.append(before)
        aliases = {len(args) + 2: 0}
    scratch = [
        pltpu.VMEM((2, r_dev * tile, samples), jnp.bfloat16),
        pltpu.VMEM((r_dev * 2 * tile, lag_dev), jnp.bfloat16),
        pltpu.VMEM((r_dev * 2 * tile, lag_dev), jnp.bfloat16),
    ]
    if not prebuilt:
        scratch.append(pltpu.VMEM((r_dev, LANES, samples - LANES + lag_dev), jnp.bfloat16))
    body = functools.partial(correlate_kernel, parts, tile, norming, prebuilt, first)
    return pl.pallas_call(
        body,
        grid_spec=pltpu.PrefetchScalarGridSpec(
            num_scalar_prefetch=3,
            grid=(groups,),
            in_specs=in_specs,
            out_specs=pl.BlockSpec((1, cap, lag_dev), lambda i, *_: (i, 0, 0)),
            scratch_shapes=scratch,
        ),
        out_shape=jax.ShapeDtypeStruct((groups, cap, lag_dev), jnp.float32),
        input_output_aliases=aliases,
        cost_estimate=pl.CostEstimate(
            flops=4 * groups * r_dev * tile * samples * (lag_dev + parts * part_rows),
            bytes_accessed=signal.size * signal.dtype.itemsize + 2 * groups * cap * lag_dev * 4,
            transcendentals=0,
        ),
        compiler_params=pltpu.CompilerParams(vmem_limit_bytes=VMEM_BYTES),
        name="correlate",
    )(passes, counts, begin, *args)


def exchange_small(receivers, pair_index, keep):
    n_chan, n_win = lax.axis_size("chan"), lax.axis_size("win")
    r_dev, samples = receivers.shape
    cap = pair_index.shape[3]
    packed = pair_index[0, 0] * 2 + keep[0, 0]
    digits = jnp.concatenate([packed // DIGIT, packed % DIGIT], axis=1).astype(jnp.bfloat16)
    digits = jnp.pad(digits, ((0, 0), (0, samples - 2 * cap)))[:, None, None, :]
    digits = jnp.broadcast_to(digits, (n_chan, n_win, 1, samples))
    own = jnp.broadcast_to(receivers, (n_chan, n_win, r_dev, samples))
    parcels = jnp.concatenate([own, digits], axis=2).reshape(n_chan * n_win, r_dev + 1, samples)
    got = lax.all_to_all(parcels, ("chan", "win"), split_axis=0, concat_axis=0, tiled=True)
    got = got.reshape(n_chan, n_win, r_dev + 1, samples)
    heard = got[:, :, :r_dev].transpose(0, 2, 1, 3).reshape(n_chan * r_dev, n_win * samples)
    digits = got[:, 0, r_dev, : 2 * cap].astype(jnp.int32)
    packed = digits[:, :cap] * DIGIT + digits[:, cap:]
    return heard, packed // 2, packed % 2


def shards(sources, receivers, plan, pair_index, keep):
    _, block_rows, samples = sources.shape
    r_dev = receivers.shape[0]
    n_chan = lax.axis_size("chan")
    n_win = lax.axis_size("win")
    n_rep = lax.axis_size("rep")
    chan, win, rep = lax.axis_index("chan"), lax.axis_index("win"), lax.axis_index("rep")
    cap = pair_index.shape[3]
    lag_dev = LAGS // (n_win * n_rep)
    half_rows = block_rows // n_rep
    chain_rows = half_rows // CHAINS
    tile = max(16, cap // 8)
    norming = 1.0 / math.sqrt(samples * n_win)

    arrived = []
    for chain in range(CHAINS):
        own = lax.dynamic_slice_in_dim(sources[0], rep * half_rows + chain * chain_rows, chain_rows, 0)
        arrived.append({0: own})
    for step in range(1, n_chan):
        for there in arrived:
            there[-step] = moved(there[1 - step], "chan", 1)
            there[step] = moved(there[step - 1], "chan", -1)

    heard, pairs, kept = exchange_small(receivers, pair_index, keep)
    signals = jnp.pad(heard.astype(jnp.float32), ((0, 0), (0, LAGS)))[:, None, :]
    lag_start = (win * n_rep + rep) * lag_dev
    begins = (win + n_win - jnp.arange(n_win, dtype=jnp.int32)) % n_win * samples + lag_start
    width = samples - LANES + lag_dev
    prebuilt = n_chan * r_dev * n_win * LANES * width * 2 <= HANKEL_BYTES
    span_signals = build_hankel(signals, begins, width) if prebuilt else [signals] * n_win

    distance = jnp.abs(plan[0] - chan)
    nearer = jnp.where(distance[0] <= distance[1], 0, 1)
    owners = [jnp.where(nearer == 0, plan[0, 0], plan[0, 1]), jnp.where(nearer == 0, plan[0, 1], plan[0, 0])]

    source_row, receiver = pairs // r_dev, pairs % r_dev
    turn = jnp.where(source_row // block_rows == nearer, 0, 1)
    row = source_row % block_rows
    row = (row + block_rows - rep * half_rows) % block_rows
    n_pass = -(-min(block_rows, cap) // tile)
    segments = jnp.where(kept == 1, turn * r_dev + receiver, -1)
    member = segments[:, None, :] == jnp.arange(2 * r_dev)[None, :, None]
    below = (jnp.arange(cap)[:, None] < jnp.arange(cap)[None, :]).astype(jnp.bfloat16)
    earlier = jnp.einsum("csi,ij->csj", member.astype(jnp.bfloat16), below, preferred_element_type=jnp.float32)
    rank = jnp.sum(jnp.where(member, earlier.astype(jnp.int32), 0), axis=1)
    counts = jnp.sum(member.astype(jnp.int32), axis=2).reshape(n_chan, 2, r_dev)
    counts = jnp.max(counts, axis=1)
    passes = -(-jnp.max(counts, axis=1) // tile)
    codes = ((rank // tile * r_dev + receiver) * 2 + turn) * tile + rank % tile
    codes = jnp.where(kept == 1, codes, -1)
    number = jnp.arange(n_pass * r_dev)[:, None]
    wanted = (number * 2 * tile + jnp.arange(tile)[None, :]).reshape(-1)
    wanted = jnp.stack([wanted, wanted + tile])
    rows = jnp.sum(jnp.where(codes[:, None, None, :] == wanted[None, :, :, None], row[:, None, None, :], 0), axis=3)

    pieces = [[] for _ in range(n_win)]
    for q in range(2):
        where = owners[q] - chan
        reach = n_chan - 1 if q else n_chan - 2
        chosen = []
        for there in arrived:
            found = there[0]
            for offset in range(-reach, reach + 1):
                if offset:
                    found = jnp.where(where == offset, there[offset], found)
            chosen.append(found)
        for v in range(n_win):
            span = [turned(piece, "win", v) for piece in chosen] if v else chosen
            for u in range(n_rep):
                pieces[v] += [turned(piece, "rep", -u) for piece in span] if u else span

    result = None
    for v in range(n_win):
        result = correlate(
            pieces[v], span_signals[v], prebuilt, begins[v : v + 1], rows[..., None], codes[..., None], passes,
            counts.reshape(-1), result, tile, norming, lag_dev,
        )
    return result[None, None]


def solution(mesh):
    placed = (
        P(("grp", "chan"), None, "win"),
        P(("grp", "chan"), "win"),
        P("grp", None),
        P("grp", "chan", None, None),
        P("grp", "chan", None, None),
    )
    return jax.shard_map(
        shards,
        mesh=mesh,
        in_specs=placed,
        out_specs=P(("grp", "chan"), None, None, None, ("win", "rep")),
        check_vma=False,
    )
```

```python
import functools
import math

import jax
import jax.numpy as jnp
from jax import lax
from jax.experimental import pallas as pl
from jax.experimental.pallas import tpu as pltpu
from jax.sharding import PartitionSpec as P

LAGS = 2048
LANES = 128
SHIFT_ROWS = 8
STEP = 2 * LANES
CHAINS = 2
DIGIT = 64
HANKEL_BYTES = 24 * 2**20
VMEM_BYTES = 26 * 2**20


def swapped(block, axis, first):
    size = lax.axis_size(axis)
    route = []
    for i in range(first, size - 1, 2):
        route += [(i, i + 1), (i + 1, i)]
    return lax.ppermute(block, axis, route)


def turned(block, axis, distance):
    size = lax.axis_size(axis)
    return lax.ppermute(block, axis, [(i, (i + distance) % size) for i in range(size)])


def hankel_rows(signal, width):
    length = signal.shape[1]
    base = jnp.broadcast_to(signal, (SHIFT_ROWS, length))
    sublane = lax.broadcasted_iota(jnp.int32, base.shape, 0)
    for bit in (1, 2, 4):
        base = jnp.where(sublane & bit != 0, pltpu.roll(base, length - bit, 1), base)
    rows = []
    for first in range(0, LANES, 2 * SHIFT_ROWS):
        both = []
        for shift in (first, first + SHIFT_ROWS):
            rolled = base if shift == 0 else pltpu.roll(base, length - shift, 1)
            both.append(rolled[:, :width])
        rows.append(jnp.concatenate(both, axis=0).astype(jnp.bfloat16))
    return jnp.concatenate(rows, axis=0)


def span_of(signal_ref, number, begin, length):
    return signal_ref[number, :, pl.ds(pl.multiple_of(begin, LANES), length)]


def hankel_kernel(length, begins_ref, signal_ref, *out_refs):
    for v, out_ref in enumerate(out_refs):
        out_ref[0] = hankel_rows(span_of(signal_ref, 0, begins_ref[v], length), out_ref.shape[2])


def build_hankel(signals, begins, width):
    channels = signals.shape[0]
    spans = begins.shape[0]
    shape = (channels, LANES, width)
    return pl.pallas_call(
        functools.partial(hankel_kernel, width + LANES),
        grid_spec=pltpu.PrefetchScalarGridSpec(
            num_scalar_prefetch=1,
            grid=(channels,),
            in_specs=[pl.BlockSpec((1,) + signals.shape[1:], lambda i, *_: (i, 0, 0))],
            out_specs=[pl.BlockSpec((1, LANES, width), lambda i, *_: (i, 0, 0))] * spans,
        ),
        out_shape=[pltpu.HBM(shape, jnp.bfloat16)] * spans,
        cost_estimate=pl.CostEstimate(
            flops=spans * math.prod(shape), bytes_accessed=2 * spans * math.prod(shape), transcendentals=0
        ),
        compiler_params=pltpu.CompilerParams(vmem_limit_bytes=VMEM_BYTES),
        name="hankel",
    )(begins, signals)


def pick_rows(pieces, row_ref, number, gathered):
    parts = len(pieces) // 2
    count, samples = gathered.shape[1:]
    for q in range(2):
        block_pieces = pieces[q * parts : (q + 1) * parts]
        rows = row_ref[0, q, pl.ds(pl.multiple_of(number * count, 8), count), :]
        lanes = lax.broadcasted_iota(jnp.int32, (count, parts * pieces[0].shape[0]), 1)
        pick = jnp.where(rows == lanes, 1.0, 0.0).astype(jnp.bfloat16)
        for t in range(0, samples, STEP):
            block = jnp.concatenate([piece[:, t : t + STEP] for piece in block_pieces], axis=0)
            chosen = jnp.dot(pick, block, preferred_element_type=jnp.float32)
            gathered[q, :, t : t + STEP] = chosen.astype(jnp.bfloat16)


def multiply(gathered, hankel_ref, r, tile, lag):
    samples = gathered.shape[2]
    chosen = jnp.concatenate([gathered[q, r * tile : (r + 1) * tile, :] for q in range(2)], axis=0)
    wide = jnp.concatenate(
        [hankel_ref[r, :, t + lag : t + lag + STEP] for t in range(0, samples, LANES)], axis=0
    )
    return jnp.dot(chosen, wide, preferred_element_type=jnp.float32)


def split(total, high, low, slots, lags):
    upper = total.astype(jnp.bfloat16)
    high[slots, lags] = upper
    low[slots, lags] = (total - upper.astype(jnp.float32)).astype(jnp.bfloat16)


def placed(code_ref, number, high, low):
    codes = code_ref[0]
    lanes = lax.broadcasted_iota(jnp.int32, (codes.shape[0], high.shape[0]), 1)
    place = jnp.where(codes == lanes + number * high.shape[0], 1.0, 0.0).astype(jnp.bfloat16)
    return jnp.dot(place, high[...], preferred_element_type=jnp.float32) + jnp.dot(
        place, low[...], preferred_element_type=jnp.float32
    )


def correlate_kernel(parts, tile, norming, prebuilt, first, last, passes_ref, counts_ref, begin_ref, *refs):
    refs = list(refs)
    pieces = [refs.pop(0) for _ in range(2 * parts)]
    signal_ref, row_ref, code_ref = [refs.pop(0) for _ in range(3)]
    if not first:
        sums_ref, extra_ref = refs.pop(0), refs.pop(0)
    if last:
        out_ref = refs.pop(0)
    else:
        handed_ref, left_ref = refs.pop(0), refs.pop(0)
    gathered, high, low, extra = refs[:4]
    r_dev = signal_ref.shape[0]
    samples = pieces[0].shape[1]
    lag_dev = extra.shape[1]
    group = pl.program_id(0)

    if prebuilt:
        hankel_ref = signal_ref
    else:
        hankel_ref = refs[4]
        for r in range(r_dev):
            span = span_of(signal_ref, r, begin_ref[0], samples + lag_dev)
            hankel_ref[r] = hankel_rows(span, hankel_ref.shape[2])

    pick_rows(pieces, row_ref, 0, gathered)
    for r in range(r_dev):
        slots = slice(r * 2 * tile, (r + 1) * 2 * tile)
        for lag in range(0, lag_dev, STEP):
            lags = slice(lag, lag + STEP)
            total = multiply(gathered, hankel_ref, r, tile, lag)
            if not first:
                total += sums_ref[0, slots, lags]
            if last:
                split(total * norming, high, low, slots, lags)
            else:
                handed_ref[0, slots, lags] = total
    if last:
        out_ref[0] = placed(code_ref, 0, high, low)

    @pl.when(passes_ref[group] > 1)
    def _():
        if first:
            extra[...] = jnp.zeros(extra.shape, jnp.float32)
        else:
            pltpu.sync_copy(extra_ref.at[group], extra)

        def one_pass(number, carry):
            pick_rows(pieces, row_ref, number, gathered)
            for r in range(r_dev):
                slots = slice(r * 2 * tile, (r + 1) * 2 * tile)
                needed = counts_ref[group * r_dev + r] > number * tile

                @pl.when(needed)
                def _():
                    for lag in range(0, lag_dev, STEP):
                        total = multiply(gathered, hankel_ref, r, tile, lag)
                        split(total * norming, high, low, slots, slice(lag, lag + STEP))

                @pl.when(jnp.logical_not(needed))
                def _():
                    high[slots, :] = jnp.zeros((2 * tile, lag_dev), jnp.bfloat16)
                    low[slots, :] = jnp.zeros((2 * tile, lag_dev), jnp.bfloat16)

            extra[...] += placed(code_ref, number, high, low)
            return carry

        lax.fori_loop(1, passes_ref[group], one_pass, 0)
        if last:
            out_ref[0] += extra[...]
        else:
            pltpu.sync_copy(extra, left_ref.at[group])


def correlate(pieces, signal, prebuilt, begin, rows, codes, passes, counts, before, last, tile, norming, lag_dev):
    parts = len(pieces) // 2
    groups, cap = codes.shape[:2]
    r_dev = signal.shape[0] // groups
    part_rows, samples = pieces[0].shape
    slot_count = r_dev * 2 * tile
    sums_spec = pl.BlockSpec((1, slot_count, lag_dev), lambda i, *_: (i, 0, 0))
    out_spec = pl.BlockSpec((1, cap, lag_dev), lambda i, *_: (i, 0, 0))
    any_spec = pl.BlockSpec(memory_space=pl.ANY)
    sums_shape = jax.ShapeDtypeStruct((groups, slot_count, lag_dev), jnp.float32)
    out_shape = jax.ShapeDtypeStruct((groups, cap, lag_dev), jnp.float32)
    in_specs = [pl.BlockSpec(piece.shape, lambda i, *_: (0, 0)) for piece in pieces]
    in_specs.append(pl.BlockSpec((r_dev,) + signal.shape[1:], lambda i, *_: (i, 0, 0)))
    in_specs.append(pl.BlockSpec((1,) + rows.shape[1:], lambda i, *_: (i, 0, 0, 0)))
    in_specs.append(pl.BlockSpec((1,) + codes.shape[1:], lambda i, *_: (i, 0, 0)))
    args = pieces + [signal, rows, codes]
    if before is not None:
        in_specs += [sums_spec, any_spec]
        args += list(before)
    scratch = [
        pltpu.VMEM((2, r_dev * tile, samples), jnp.bfloat16),
        pltpu.VMEM((slot_count, lag_dev), jnp.bfloat16),
        pltpu.VMEM((slot_count, lag_dev), jnp.bfloat16),
        pltpu.VMEM((cap, lag_dev), jnp.float32),
    ]
    if not prebuilt:
        scratch.append(pltpu.VMEM((r_dev, LANES, samples - LANES + lag_dev), jnp.bfloat16))
    body = functools.partial(correlate_kernel, parts, tile, norming, prebuilt, before is None, last)
    return pl.pallas_call(
        body,
        grid_spec=pltpu.PrefetchScalarGridSpec(
            num_scalar_prefetch=3,
            grid=(groups,),
            in_specs=in_specs,
            out_specs=out_spec if last else [sums_spec, any_spec],
            scratch_shapes=scratch,
        ),
        out_shape=out_shape if last else [sums_shape, out_shape],
        cost_estimate=pl.CostEstimate(
            flops=4 * groups * r_dev * tile * samples * (lag_dev + parts * part_rows),
            bytes_accessed=signal.size * signal.dtype.itemsize + 2 * groups * cap * lag_dev * 4,
            transcendentals=0,
        ),
        compiler_params=pltpu.CompilerParams(vmem_limit_bytes=VMEM_BYTES if prebuilt else 2 * VMEM_BYTES),
        name="correlate",
    )(passes, counts, begin, *args)


def exchange_small(receivers, pair_index, keep):
    n_chan, n_win = lax.axis_size("chan"), lax.axis_size("win")
    r_dev, samples = receivers.shape
    cap = pair_index.shape[3]
    packed = pair_index[0, 0] * 2 + keep[0, 0]
    digits = jnp.concatenate([packed // DIGIT, packed % DIGIT], axis=1).astype(jnp.bfloat16)
    digits = jnp.pad(digits, ((0, 0), (0, samples - 2 * cap)))[:, None, None, :]
    digits = jnp.broadcast_to(digits, (n_chan, n_win, 1, samples))
    own = jnp.broadcast_to(receivers, (n_chan, n_win, r_dev, samples))
    parcels = jnp.concatenate([own, digits], axis=2).reshape(n_chan * n_win, r_dev + 1, samples)
    got = lax.all_to_all(parcels, ("chan", "win"), split_axis=0, concat_axis=0, tiled=True)
    got = got.reshape(n_chan, n_win, r_dev + 1, samples)
    heard = got[:, :, :r_dev].transpose(0, 2, 1, 3).reshape(n_chan * r_dev, n_win * samples)
    digits = got[:, 0, r_dev, : 2 * cap].astype(jnp.int32)
    packed = digits[:, :cap] * DIGIT + digits[:, cap:]
    return heard, packed // 2, packed % 2


def shards(sources, receivers, plan, pair_index, keep):
    _, block_rows, samples = sources.shape
    r_dev = receivers.shape[0]
    n_chan = lax.axis_size("chan")
    n_win = lax.axis_size("win")
    n_rep = lax.axis_size("rep")
    chan, win, rep = lax.axis_index("chan"), lax.axis_index("win"), lax.axis_index("rep")
    cap = pair_index.shape[3]
    lag_dev = LAGS // (n_win * n_rep)
    half_rows = block_rows // n_rep
    chain_rows = half_rows // CHAINS
    tile = max(16, cap // 8)
    norming = 1.0 / math.sqrt(samples * n_win)

    arrived = []
    for chain in range(CHAINS):
        own = lax.dynamic_slice_in_dim(sources[0], rep * half_rows + chain * chain_rows, chain_rows, 0)
        arrived.append({0: own})
    for step in range(1, n_chan):
        for there in arrived:
            there[step] = swapped(there[1 - step], "chan", 0)
            if step < n_chan - 1:
                there[-step] = swapped(there[step - 1], "chan", 1)

    heard, pairs, kept = exchange_small(receivers, pair_index, keep)
    signals = jnp.pad(heard.astype(jnp.float32), ((0, 0), (0, LAGS)))[:, None, :]
    lag_start = (win * n_rep + rep) * lag_dev
    begins = (win + n_win - jnp.arange(n_win, dtype=jnp.int32)) % n_win * samples + lag_start
    width = samples - LANES + lag_dev
    prebuilt = n_chan * r_dev * n_win * LANES * width * 2 <= HANKEL_BYTES
    span_signals = build_hankel(signals, begins, width) if prebuilt else [signals] * n_win

    distance = jnp.abs(plan[0] - chan)
    nearer = jnp.where(distance[0] <= distance[1], 0, 1)
    owners = [jnp.where(nearer == 0, plan[0, 0], plan[0, 1]), jnp.where(nearer == 0, plan[0, 1], plan[0, 0])]

    source_row, receiver = pairs // r_dev, pairs % r_dev
    turn = jnp.where(source_row // block_rows == nearer, 0, 1)
    row = source_row % block_rows
    row = (row + block_rows - rep * half_rows) % block_rows
    n_pass = -(-min(block_rows, cap) // tile)
    segments = jnp.where(kept == 1, turn * r_dev + receiver, -1)
    member = segments[:, None, :] == jnp.arange(2 * r_dev)[None, :, None]
    below = (jnp.arange(cap)[:, None] < jnp.arange(cap)[None, :]).astype(jnp.bfloat16)
    earlier = jnp.einsum("csi,ij->csj", member.astype(jnp.bfloat16), below, preferred_element_type=jnp.float32)
    rank = jnp.sum(jnp.where(member, earlier.astype(jnp.int32), 0), axis=1)
    counts = jnp.sum(member.astype(jnp.int32), axis=2).reshape(n_chan, 2, r_dev)
    counts = jnp.max(counts, axis=1)
    passes = -(-jnp.max(counts, axis=1) // tile)
    codes = ((rank // tile * r_dev + receiver) * 2 + turn) * tile + rank % tile
    codes = jnp.where(kept == 1, codes, -1)
    number = jnp.arange(n_pass * r_dev)[:, None]
    wanted = (number * 2 * tile + jnp.arange(tile)[None, :]).reshape(-1)
    wanted = jnp.stack([wanted, wanted + tile])
    rows = jnp.sum(jnp.where(codes[:, None, None, :] == wanted[None, :, :, None], row[:, None, None, :], 0), axis=3)

    pieces = [[] for _ in range(n_win)]
    for q in range(2):
        where = jnp.where(chan % 2 == 0, owners[q] - chan, chan - owners[q])
        reach = n_chan - 1 if q else n_chan - 2
        chosen = []
        for there in arrived:
            found = there[0]
            for offset in range(-reach, reach + 1):
                if offset and offset in there:
                    found = jnp.where(where == offset, there[offset], found)
            chosen.append(found)
        if q and prebuilt:
            chosen, span_signals = lax.optimization_barrier((chosen, span_signals))
        for v in range(n_win):
            span = [turned(piece, "win", v) for piece in chosen] if v else chosen
            for u in range(n_rep):
                pieces[v] += [turned(piece, "rep", -u) for piece in span] if u else span

    result = None
    for v in range(n_win):
        result = correlate(
            pieces[v], span_signals[v], prebuilt, begins[v : v + 1], rows[..., None], codes[..., None], passes,
            counts.reshape(-1), result, v == n_win - 1, tile, norming, lag_dev,
        )
    return result[None, None]


def solution(mesh):
    placed = (
        P(("grp", "chan"), None, "win"),
        P(("grp", "chan"), "win"),
        P("grp", None),
        P("grp", "chan", None, None),
        P("grp", "chan", None, None),
    )
    return jax.shard_map(
        shards,
        mesh=mesh,
        in_specs=placed,
        out_specs=P(("grp", "chan"), None, None, None, ("win", "rep")),
        check_vma=False,
    )
```

```python
import functools
import math

import jax
import jax.numpy as jnp
from jax import lax
from jax.experimental import pallas as pl
from jax.experimental.pallas import tpu as pltpu
from jax.sharding import PartitionSpec as P

LAGS = 2048
LANES = 128
SHIFT_ROWS = 8
PARCEL_ROWS = 8
STEP = 2 * LANES
CHAINS = 2
DIGIT = 64
HANKEL_BYTES = 24 * 2**20
VMEM_BYTES = 26 * 2**20
F32 = jnp.float32
BF16 = jnp.bfloat16


def swapped(block, axis, first):
    size = lax.axis_size(axis)
    route = []
    for i in range(first, size - 1, 2):
        route += [(i, i + 1), (i + 1, i)]
    return lax.ppermute(block, axis, route)


def turned(block, axis, distance):
    size = lax.axis_size(axis)
    return lax.ppermute(block, axis, [(i, (i + distance) % size) for i in range(size)])


def in_hbm(array):
    return pltpu.with_memory_space_constraint(array, pltpu.HBM)


def params(vmem):
    return pltpu.CompilerParams(vmem_limit_bytes=vmem)


def pack_kernel(n_win, _, source_ref, receiver_ref, pair_ref, keep_ref, parcel_ref, *chain_refs):
    r_dev, samples = receiver_ref.shape
    n_chan, cap = pair_ref.shape
    packed = pair_ref[...] * 2 + keep_ref[...]
    digits = jnp.concatenate([packed // DIGIT, packed % DIGIT], axis=1).astype(F32)
    heard = receiver_ref[...].astype(F32)
    for d in range(n_chan):
        lists = jnp.concatenate([digits[d : d + 1], jnp.zeros((1, samples - 2 * cap), F32)], axis=1)
        rest = jnp.zeros((PARCEL_ROWS - 1 - r_dev, samples), F32)
        parcel = jnp.concatenate([heard, lists, rest], axis=0).astype(BF16)
        for w in range(n_win):
            parcel_ref[d * n_win + w] = parcel
    rows = chain_refs[0].shape[0]
    for chain, chain_ref in enumerate(chain_refs):
        chain_ref[...] = source_ref[chain * rows : (chain + 1) * rows, :]


def pack(sources, receivers, pair_index, keep, half_rows, n_chan, n_win, rep):
    samples = receivers.shape[1]
    chain_rows = half_rows // CHAINS
    shapes = [jax.ShapeDtypeStruct((n_chan * n_win, PARCEL_ROWS, samples), BF16)]
    shapes += [jax.ShapeDtypeStruct((chain_rows, samples), BF16)] * CHAINS
    whole = lambda shape: pl.BlockSpec(shape, lambda i, *_: (0,) * len(shape))
    return pl.pallas_call(
        functools.partial(pack_kernel, n_win),
        grid_spec=pltpu.PrefetchScalarGridSpec(
            num_scalar_prefetch=1,
            grid=(1,),
            in_specs=[pl.BlockSpec((half_rows, samples), lambda i, rep_ref: (rep_ref[0], 0))]
            + [whole(a.shape) for a in (receivers, pair_index, keep)],
            out_specs=[whole(shape.shape) for shape in shapes],
        ),
        out_shape=shapes,
        compiler_params=params(VMEM_BYTES // 2),
        name="pack",
    )(rep, in_hbm(sources), receivers, pair_index, keep)


def column(row):
    return jnp.broadcast_to(row, (SHIFT_ROWS, row.shape[1])).T[:, :1]


def ones_where(condition):
    return jnp.where(condition, 1.0, 0.0).astype(BF16)


def index_kernel(r_dev, cap, tile, block_rows, number_ref, parcel_ref, pick_ref, place_ref, pass_ref, count_ref,
                 more_pick_ref, more_place_ref, pick_scratch, place_scratch):
    group = pl.program_id(0)
    nearer, offset = number_ref[0], number_ref[1]
    slots = 2 * r_dev * tile
    digits = parcel_ref[0].astype(F32)[r_dev : r_dev + 1]
    packed = digits[:, :cap].astype(jnp.int32) * DIGIT + digits[:, cap : 2 * cap].astype(jnp.int32)
    pairs, kept = packed // 2, packed % 2 == 1
    source_row, receiver = pairs // r_dev, pairs % r_dev
    turn = jnp.where(source_row // block_rows == nearer, 0, 1)
    row = (source_row + offset) % block_rows
    segment = jnp.where(kept, turn * r_dev + receiver, -1)
    member = lax.broadcasted_iota(jnp.int32, (2 * r_dev, cap), 0) == segment
    below = lax.broadcasted_iota(jnp.int32, (cap, cap), 0) < lax.broadcasted_iota(jnp.int32, (cap, cap), 1)
    earlier = jnp.dot(ones_where(member), ones_where(below), preferred_element_type=F32)
    rank = jnp.sum(jnp.where(member, earlier, 0.0), axis=0, keepdims=True).astype(jnp.int32)
    code = (rank // tile) * slots + (turn * r_dev + receiver) * tile + rank % tile
    code = jnp.where(kept, code, -1)
    counts = jnp.sum(jnp.where(member, 1.0, 0.0), axis=1, keepdims=True)
    which = lax.broadcasted_iota(jnp.int32, counts.shape, 0) % r_dev
    for r in range(r_dev):
        count_ref[group * r_dev + r] = jnp.max(jnp.where(which == r, counts, 0.0)).astype(jnp.int32)
    passes = (jnp.max(counts).astype(jnp.int32) + tile - 1) // tile
    pass_ref[group] = passes

    code_column = column(code.astype(F32)).astype(jnp.int32)
    row_column = column(row.astype(F32)).astype(jnp.int32)
    row_ones = ones_where(row_column == lax.broadcasted_iota(jnp.int32, (cap, block_rows), 1))

    def matrices(number):
        start = number * slots
        by_slot = ones_where(lax.broadcasted_iota(jnp.int32, (slots, cap), 0) + start == code)
        pick = jnp.dot(by_slot, row_ones, preferred_element_type=F32).astype(BF16)
        place = ones_where(lax.broadcasted_iota(jnp.int32, (cap, slots), 1) + start == code_column)
        return pick, place

    pick_ref[0], place_ref[0] = matrices(0)

    @pl.when(passes > 1)
    def _():
        def one_pass(number, carry):
            pick_scratch[...], place_scratch[...] = matrices(number)
            pltpu.sync_copy(pick_scratch, more_pick_ref.at[group, number - 1])
            pltpu.sync_copy(place_scratch, more_place_ref.at[group, number - 1])
            return carry

        lax.fori_loop(1, passes, one_pass, 0)


def index(parcels, numbers, n_win, r_dev, cap, tile, block_rows):
    groups = parcels.shape[0] // n_win
    slots = 2 * r_dev * tile
    more = max(1, -(-min(block_rows, cap) // tile) - 1)
    return pl.pallas_call(
        functools.partial(index_kernel, r_dev, cap, tile, block_rows),
        grid_spec=pltpu.PrefetchScalarGridSpec(
            num_scalar_prefetch=1,
            grid=(groups,),
            in_specs=[pl.BlockSpec((1,) + parcels.shape[1:], lambda i, *_: (i * n_win, 0, 0))],
            out_specs=[
                pl.BlockSpec((1, slots, block_rows), lambda i, *_: (i, 0, 0)),
                pl.BlockSpec((1, cap, slots), lambda i, *_: (i, 0, 0)),
                pl.BlockSpec(memory_space=pltpu.SMEM),
                pl.BlockSpec(memory_space=pltpu.SMEM),
                pl.BlockSpec(memory_space=pl.ANY),
                pl.BlockSpec(memory_space=pl.ANY),
            ],
            scratch_shapes=[pltpu.VMEM((slots, block_rows), BF16), pltpu.VMEM((cap, slots), BF16)],
        ),
        out_shape=[
            jax.ShapeDtypeStruct((groups, slots, block_rows), BF16),
            jax.ShapeDtypeStruct((groups, cap, slots), BF16),
            jax.ShapeDtypeStruct((groups,), jnp.int32),
            jax.ShapeDtypeStruct((groups * r_dev,), jnp.int32),
            pltpu.HBM((groups, more, slots, block_rows), BF16),
            pltpu.HBM((groups, more, cap, slots), BF16),
        ],
        compiler_params=params(VMEM_BYTES // 2),
        name="index",
    )(numbers, parcels)


def lay_out(parcel_ref, signal_ref):
    n_win, _, samples = parcel_ref.shape
    for w in range(n_win):
        signal_ref[:, w * samples : (w + 1) * samples] = parcel_ref[w].astype(F32)
    tail = signal_ref.shape[1] - n_win * samples
    signal_ref[:, n_win * samples :] = jnp.zeros((signal_ref.shape[0], tail), F32)


def hankel_rows(signal_ref, r, begin, width, out_ref):
    length = width + LANES
    signal = signal_ref[r : r + 1, pl.ds(pl.multiple_of(begin, LANES), length)]
    base = jnp.broadcast_to(signal, (SHIFT_ROWS, length))
    sublane = lax.broadcasted_iota(jnp.int32, base.shape, 0)
    for bit in (1, 2, 4):
        base = jnp.where(sublane & bit != 0, pltpu.roll(base, length - bit, 1), base)
    for first in range(0, LANES, 2 * SHIFT_ROWS):
        both = []
        for shift in (first, first + SHIFT_ROWS):
            rolled = base if shift == 0 else pltpu.roll(base, length - shift, 1)
            both.append(rolled[:, :width])
        out_ref[r, first : first + 2 * SHIFT_ROWS, :] = jnp.concatenate(both, axis=0).astype(BF16)


def hankel_kernel(begin_ref, parcel_ref, out_ref, signal_ref):
    lay_out(parcel_ref, signal_ref)
    for r in range(out_ref.shape[0]):
        hankel_rows(signal_ref, r, begin_ref[0], out_ref.shape[2], out_ref)


def build_hankel(parcels, begin, n_win, r_dev, width):
    groups, samples = parcels.shape[0] // n_win, parcels.shape[2]
    shape = (groups * r_dev, LANES, width)
    return pl.pallas_call(
        hankel_kernel,
        grid_spec=pltpu.PrefetchScalarGridSpec(
            num_scalar_prefetch=1,
            grid=(groups,),
            in_specs=[pl.BlockSpec((n_win,) + parcels.shape[1:], lambda i, *_: (i, 0, 0))],
            out_specs=pl.BlockSpec((r_dev, LANES, width), lambda i, *_: (i, 0, 0)),
            scratch_shapes=[pltpu.VMEM((PARCEL_ROWS, n_win * samples + LAGS), F32)],
        ),
        out_shape=pltpu.HBM(shape, BF16),
        cost_estimate=pl.CostEstimate(
            flops=math.prod(shape), bytes_accessed=2 * math.prod(shape), transcendentals=0
        ),
        compiler_params=params(VMEM_BYTES // 2),
        name="hankel",
    )(begin, parcels)


def pick_rows(pieces, pick, gathered):
    parts = len(pieces) // 2
    count, samples = gathered.shape[1:]
    for q in range(2):
        block_pieces = pieces[q * parts : (q + 1) * parts]
        ones = pick[q * count : (q + 1) * count, :]
        for t in range(0, samples, STEP):
            block = jnp.concatenate([piece[:, t : t + STEP] for piece in block_pieces], axis=0)
            gathered[q, :, t : t + STEP] = jnp.dot(ones, block, preferred_element_type=F32).astype(BF16)


def multiply(gathered, hankel_ref, r, tile, lag):
    samples = gathered.shape[2]
    chosen = jnp.concatenate([gathered[q, r * tile : (r + 1) * tile, :] for q in range(2)], axis=0)
    wide = jnp.concatenate(
        [hankel_ref[r, :, t + lag : t + lag + STEP] for t in range(0, samples, LANES)], axis=0
    )
    return jnp.dot(chosen, wide, preferred_element_type=F32)


def split(total, high, low, slots, lags):
    upper = total.astype(BF16)
    high[slots, lags] = upper
    low[slots, lags] = (total - upper.astype(F32)).astype(BF16)


def placed(place, high, low):
    return jnp.dot(place, high[...], preferred_element_type=F32) + jnp.dot(
        place, low[...], preferred_element_type=F32
    )


def correlate_kernel(parts, tile, norming, prebuilt, first, last, pass_ref, count_ref, begin_ref, *refs):
    refs = list(refs)
    pieces = [refs.pop(0) for _ in range(2 * parts)]
    signal_ref, pick_ref, place_ref, more_pick_ref, more_place_ref = [refs.pop(0) for _ in range(5)]
    if not first:
        sums_ref, extra_ref = refs.pop(0), refs.pop(0)
    if last:
        out_ref = refs.pop(0)
    else:
        handed_ref, left_ref = refs.pop(0), refs.pop(0)
    gathered, high, low, extra, pick_scratch, place_scratch = refs[:6]
    r_dev = gathered.shape[1] // tile
    samples = pieces[0].shape[1]
    lag_dev = extra.shape[1]
    group = pl.program_id(0)

    if prebuilt:
        hankel_ref = signal_ref
    else:
        hankel_ref, row_ref = refs[6:]
        lay_out(signal_ref, row_ref)
        for r in range(r_dev):
            hankel_rows(row_ref, r, begin_ref[0], hankel_ref.shape[2], hankel_ref)

    pick_rows(pieces, pick_ref.at[0], gathered)
    for r in range(r_dev):
        for lag in range(0, lag_dev, STEP):
            lags = slice(lag, lag + STEP)
            both = multiply(gathered, hankel_ref, r, tile, lag)
            for q in range(2):
                total = both[q * tile : (q + 1) * tile]
                slots = slice((q * r_dev + r) * tile, (q * r_dev + r + 1) * tile)
                if not first:
                    total += sums_ref[0, slots, lags]
                if last:
                    split(total * norming, high, low, slots, lags)
                else:
                    handed_ref[0, slots, lags] = total
    if last:
        out_ref[0] = placed(place_ref[0], high, low)

    @pl.when(pass_ref[group] > 1)
    def _():
        if first:
            extra[...] = jnp.zeros(extra.shape, F32)
        else:
            pltpu.sync_copy(extra_ref.at[group], extra)

        def one_pass(number, carry):
            pltpu.sync_copy(more_pick_ref.at[group, number - 1], pick_scratch)
            pltpu.sync_copy(more_place_ref.at[group, number - 1], place_scratch)
            pick_rows(pieces, pick_scratch, gathered)
            for r in range(r_dev):
                needed = count_ref[group * r_dev + r] > number * tile
                places = [slice((q * r_dev + r) * tile, (q * r_dev + r + 1) * tile) for q in range(2)]

                @pl.when(needed)
                def _():
                    for lag in range(0, lag_dev, STEP):
                        both = multiply(gathered, hankel_ref, r, tile, lag) * norming
                        for q, slots in enumerate(places):
                            split(both[q * tile : (q + 1) * tile], high, low, slots, slice(lag, lag + STEP))

                @pl.when(jnp.logical_not(needed))
                def _():
                    for slots in places:
                        high[slots, :] = jnp.zeros((tile, lag_dev), BF16)
                        low[slots, :] = jnp.zeros((tile, lag_dev), BF16)

            extra[...] += placed(place_scratch[...], high, low)
            return carry

        lax.fori_loop(1, pass_ref[group], one_pass, 0)
        if last:
            out_ref[0] += extra[...]
        else:
            pltpu.sync_copy(extra, left_ref.at[group])


def correlate(pieces, signal, prebuilt, begin, matrices, before, last, tile, norming, lag_dev, n_win, r_dev):
    pick, place, passes, counts, more_pick, more_place = matrices
    parts = len(pieces) // 2
    groups, cap, slots = place.shape
    part_rows, samples = pieces[0].shape
    width = samples - LANES + lag_dev
    by_group = lambda shape: pl.BlockSpec(shape, lambda i, *_: (i, 0, 0))
    any_spec = pl.BlockSpec(memory_space=pl.ANY)
    sums_spec = by_group((1, slots, lag_dev))
    sums_shape = jax.ShapeDtypeStruct((groups, slots, lag_dev), F32)
    out_shape = jax.ShapeDtypeStruct((groups, cap, lag_dev), F32)
    in_specs = [pl.BlockSpec(piece.shape, lambda i, *_: (0, 0)) for piece in pieces]
    in_specs.append(by_group((r_dev, LANES, width) if prebuilt else (n_win,) + signal.shape[1:]))
    in_specs += [by_group((1,) + pick.shape[1:]), by_group((1,) + place.shape[1:]), any_spec, any_spec]
    if prebuilt:
        signal = in_hbm(signal)
    args = pieces + [signal, pick, place, in_hbm(more_pick), in_hbm(more_place)]
    if before is not None:
        in_specs += [sums_spec, any_spec]
        args += [before[0], in_hbm(before[1])]
    scratch = [
        pltpu.VMEM((2, r_dev * tile, samples), BF16),
        pltpu.VMEM((slots, lag_dev), BF16),
        pltpu.VMEM((slots, lag_dev), BF16),
        pltpu.VMEM((cap, lag_dev), F32),
        pltpu.VMEM(pick.shape[1:], BF16),
        pltpu.VMEM(place.shape[1:], BF16),
    ]
    if not prebuilt:
        scratch.append(pltpu.VMEM((r_dev, LANES, width), BF16))
        scratch.append(pltpu.VMEM((PARCEL_ROWS, n_win * samples + LAGS), F32))
    body = functools.partial(correlate_kernel, parts, tile, norming, prebuilt, before is None, last)
    return pl.pallas_call(
        body,
        grid_spec=pltpu.PrefetchScalarGridSpec(
            num_scalar_prefetch=3,
            grid=(groups,),
            in_specs=in_specs,
            out_specs=by_group((1, cap, lag_dev)) if last else [sums_spec, any_spec],
            scratch_shapes=scratch,
        ),
        out_shape=out_shape if last else [sums_shape, pltpu.HBM(out_shape.shape, F32)],
        cost_estimate=pl.CostEstimate(
            flops=4 * groups * r_dev * tile * samples * (lag_dev + parts * part_rows),
            bytes_accessed=signal.size * signal.dtype.itemsize + 2 * groups * cap * lag_dev * 4,
            transcendentals=0,
        ),
        compiler_params=params(VMEM_BYTES if prebuilt else 2 * VMEM_BYTES),
        name="correlate",
    )(passes, counts, begin, *args)


def shards(sources, receivers, plan, pair_index, keep):
    _, block_rows, samples = sources.shape
    r_dev = receivers.shape[0]
    n_chan = lax.axis_size("chan")
    n_win = lax.axis_size("win")
    n_rep = lax.axis_size("rep")
    chan, win, rep = lax.axis_index("chan"), lax.axis_index("win"), lax.axis_index("rep")
    cap = pair_index.shape[3]
    lag_dev = LAGS // (n_win * n_rep)
    half_rows = block_rows // n_rep
    tile = max(16, cap // 8)
    norming = 1.0 / math.sqrt(samples * n_win)
    width = samples - LANES + lag_dev
    prebuilt = n_chan * r_dev * n_win * LANES * width * 2 <= HANKEL_BYTES

    parcels, *owns = pack(
        sources[0], receivers, pair_index[0, 0], keep[0, 0], half_rows, n_chan, n_win, rep.reshape(1)
    )
    parcels = lax.all_to_all(parcels, ("chan", "win"), split_axis=0, concat_axis=0, tiled=True)

    arrived = [{0: own} for own in owns]

    def relay(step):
        for there in arrived:
            there[step] = swapped(there[1 - step], "chan", 0)
            if step < n_chan - 1:
                there[-step] = swapped(there[step - 1], "chan", 1)

    def after_arrival(step, value):
        there = arrived[-1]
        value, there[step] = lax.optimization_barrier((value, there[step]))
        return value

    def before_start(step, value):
        for there in arrived:
            for key in (1 - step, step - 1):
                value, there[key] = lax.optimization_barrier((value, there[key]))
        return value

    distance = jnp.abs(plan[0] - chan)
    nearer = jnp.where(distance[0] <= distance[1], 0, 1)
    owners = [jnp.where(nearer == 0, plan[0, 0], plan[0, 1]), jnp.where(nearer == 0, plan[0, 1], plan[0, 0])]
    numbers = jnp.stack([nearer, block_rows - rep * half_rows])
    lag_start = (win * n_rep + rep) * lag_dev
    begins = [((win + n_win - v) % n_win * samples + lag_start).reshape(1) for v in range(n_win)]

    relay(1)
    parcels = after_arrival(1, parcels)
    relay(2)
    matrices = index(parcels, numbers, n_win, r_dev, cap, tile, block_rows)
    signals = [parcels] * n_win
    if prebuilt:
        signals[0] = build_hankel(parcels, begins[0], n_win, r_dev, width)
        signals[0] = before_start(3, signals[0])
    for step in range(3, n_chan):
        relay(step)
    if prebuilt:
        parcels = after_arrival(2, parcels)
        for v in range(1, n_win):
            signals[v] = build_hankel(parcels, begins[v], n_win, r_dev, width)

    pieces = [[] for _ in range(n_win)]
    for q in range(2):
        where = jnp.where(chan % 2 == 0, owners[q] - chan, chan - owners[q])
        reach = n_chan - 1 if q else n_chan - 2
        chosen = []
        for there in arrived:
            found = there[0]
            for offset in range(-reach, reach + 1):
                if offset and offset in there:
                    found = jnp.where(where == offset, there[offset], found)
            chosen.append(found)
        if q and prebuilt:
            chosen, signals = lax.optimization_barrier((chosen, signals))
        for v in range(n_win):
            span = [turned(piece, "win", v) for piece in chosen] if v else chosen
            for u in range(n_rep):
                pieces[v] += [turned(piece, "rep", -u) for piece in span] if u else span

    result = None
    for v in range(n_win):
        result = correlate(
            pieces[v], signals[v], prebuilt, begins[v], matrices, result, v == n_win - 1, tile, norming, lag_dev,
            n_win, r_dev,
        )
    return result[None, None]


def solution(mesh):
    placed_at = (
        P(("grp", "chan"), None, "win"),
        P(("grp", "chan"), "win"),
        P("grp", None),
        P("grp", "chan", None, None),
        P("grp", "chan", None, None),
    )
    return jax.shard_map(
        shards,
        mesh=mesh,
        in_specs=placed_at,
        out_specs=P(("grp", "chan"), None, None, None, ("win", "rep")),
        check_vma=False,
    )
```

```python
import functools
import math

import jax
import jax.numpy as jnp
from jax import lax
from jax.experimental import pallas as pl
from jax.experimental.pallas import tpu as pltpu
from jax.sharding import PartitionSpec as P

LAGS = 2048
LANES = 128
SHIFT_ROWS = 8
PARCEL_ROWS = 8
STEP = 2 * LANES
CHAINS = 2
DIGIT = 64
HANKEL_BYTES = 24 * 2**20
VMEM_BYTES = 26 * 2**20
F32 = jnp.float32
BF16 = jnp.bfloat16


def swapped(block, axis, first):
    size = lax.axis_size(axis)
    route = []
    for i in range(first, size - 1, 2):
        route += [(i, i + 1), (i + 1, i)]
    return lax.ppermute(block, axis, route)


def turned(block, axis, distance):
    size = lax.axis_size(axis)
    return lax.ppermute(block, axis, [(i, (i + distance) % size) for i in range(size)])


def in_hbm(array):
    return pltpu.with_memory_space_constraint(array, pltpu.HBM)


def params(vmem):
    return pltpu.CompilerParams(vmem_limit_bytes=vmem)


def pack_kernel(n_win, _, source_ref, receiver_ref, pair_ref, keep_ref, parcel_ref, *chain_refs):
    r_dev, samples = receiver_ref.shape
    n_chan, cap = pair_ref.shape
    packed = pair_ref[...] * 2 + keep_ref[...]
    digits = jnp.concatenate([packed // DIGIT, packed % DIGIT], axis=1).astype(F32)
    heard = receiver_ref[...].astype(F32)
    for d in range(n_chan):
        lists = jnp.concatenate([digits[d : d + 1], jnp.zeros((1, samples - 2 * cap), F32)], axis=1)
        rest = jnp.zeros((PARCEL_ROWS - 1 - r_dev, samples), F32)
        parcel = jnp.concatenate([heard, lists, rest], axis=0).astype(BF16)
        for w in range(n_win):
            parcel_ref[d * n_win + w] = parcel
    rows = chain_refs[0].shape[0]
    for chain, chain_ref in enumerate(chain_refs):
        chain_ref[...] = source_ref[chain * rows : (chain + 1) * rows, :]


def pack(sources, receivers, pair_index, keep, half_rows, n_chan, n_win, rep):
    samples = receivers.shape[1]
    chain_rows = half_rows // CHAINS
    shapes = [jax.ShapeDtypeStruct((n_chan * n_win, PARCEL_ROWS, samples), BF16)]
    shapes += [jax.ShapeDtypeStruct((chain_rows, samples), BF16)] * CHAINS
    whole = lambda shape: pl.BlockSpec(shape, lambda i, *_: (0,) * len(shape))
    return pl.pallas_call(
        functools.partial(pack_kernel, n_win),
        grid_spec=pltpu.PrefetchScalarGridSpec(
            num_scalar_prefetch=1,
            grid=(1,),
            in_specs=[pl.BlockSpec((half_rows, samples), lambda i, rep_ref: (rep_ref[0], 0))]
            + [whole(a.shape) for a in (receivers, pair_index, keep)],
            out_specs=[whole(shape.shape) for shape in shapes],
        ),
        out_shape=shapes,
        compiler_params=params(VMEM_BYTES // 2),
        name="pack",
    )(rep, *[in_hbm(a) for a in (sources, receivers, pair_index, keep)])


def column(row):
    return jnp.broadcast_to(row, (SHIFT_ROWS, row.shape[1])).T[:, :1]


def ones_where(condition):
    return jnp.where(condition, 1.0, 0.0).astype(BF16)


def index_kernel(r_dev, cap, tile, block_rows, number_ref, parcel_ref, pick_ref, place_ref, pass_ref, count_ref,
                 more_pick_ref, more_place_ref, pick_scratch, place_scratch):
    group = pl.program_id(0)
    nearer, offset = number_ref[0], number_ref[1]
    slots = 2 * r_dev * tile
    digits = parcel_ref[0].astype(F32)[r_dev : r_dev + 1]
    packed = digits[:, :cap].astype(jnp.int32) * DIGIT + digits[:, cap : 2 * cap].astype(jnp.int32)
    pairs, kept = packed // 2, packed % 2 == 1
    source_row, receiver = pairs // r_dev, pairs % r_dev
    turn = jnp.where(source_row // block_rows == nearer, 0, 1)
    row = (source_row + offset) % block_rows
    segment = jnp.where(kept, turn * r_dev + receiver, -1)
    member = lax.broadcasted_iota(jnp.int32, (2 * r_dev, cap), 0) == segment
    below = lax.broadcasted_iota(jnp.int32, (cap, cap), 0) < lax.broadcasted_iota(jnp.int32, (cap, cap), 1)
    earlier = jnp.dot(ones_where(member), ones_where(below), preferred_element_type=F32)
    rank = jnp.sum(jnp.where(member, earlier, 0.0), axis=0, keepdims=True).astype(jnp.int32)
    code = (rank // tile) * slots + (turn * r_dev + receiver) * tile + rank % tile
    code = jnp.where(kept, code, -1)
    counts = jnp.sum(jnp.where(member, 1.0, 0.0), axis=1, keepdims=True)
    which = lax.broadcasted_iota(jnp.int32, counts.shape, 0) % r_dev
    for r in range(r_dev):
        count_ref[group * r_dev + r] = jnp.max(jnp.where(which == r, counts, 0.0)).astype(jnp.int32)
    passes = (jnp.max(counts).astype(jnp.int32) + tile - 1) // tile
    pass_ref[group] = passes

    code_column = column(code.astype(F32)).astype(jnp.int32)
    row_column = column(row.astype(F32)).astype(jnp.int32)
    row_ones = ones_where(row_column == lax.broadcasted_iota(jnp.int32, (cap, block_rows), 1))

    def matrices(number):
        start = number * slots
        by_slot = ones_where(lax.broadcasted_iota(jnp.int32, (slots, cap), 0) + start == code)
        pick = jnp.dot(by_slot, row_ones, preferred_element_type=F32).astype(BF16)
        place = ones_where(lax.broadcasted_iota(jnp.int32, (cap, slots), 1) + start == code_column)
        return pick, place

    pick_ref[0], place_ref[0] = matrices(0)

    @pl.when(passes > 1)
    def _():
        def one_pass(number, carry):
            pick_scratch[...], place_scratch[...] = matrices(number)
            pltpu.sync_copy(pick_scratch, more_pick_ref.at[group, number - 1])
            pltpu.sync_copy(place_scratch, more_place_ref.at[group, number - 1])
            return carry

        lax.fori_loop(1, passes, one_pass, 0)


def index(parcels, numbers, n_win, r_dev, cap, tile, block_rows):
    groups = parcels.shape[0] // n_win
    slots = 2 * r_dev * tile
    more = max(1, -(-min(block_rows, cap) // tile) - 1)
    return pl.pallas_call(
        functools.partial(index_kernel, r_dev, cap, tile, block_rows),
        grid_spec=pltpu.PrefetchScalarGridSpec(
            num_scalar_prefetch=1,
            grid=(groups,),
            in_specs=[pl.BlockSpec((1,) + parcels.shape[1:], lambda i, *_: (i * n_win, 0, 0))],
            out_specs=[
                pl.BlockSpec((1, slots, block_rows), lambda i, *_: (i, 0, 0)),
                pl.BlockSpec((1, cap, slots), lambda i, *_: (i, 0, 0)),
                pl.BlockSpec(memory_space=pltpu.SMEM),
                pl.BlockSpec(memory_space=pltpu.SMEM),
                pl.BlockSpec(memory_space=pl.ANY),
                pl.BlockSpec(memory_space=pl.ANY),
            ],
            scratch_shapes=[pltpu.VMEM((slots, block_rows), BF16), pltpu.VMEM((cap, slots), BF16)],
        ),
        out_shape=[
            jax.ShapeDtypeStruct((groups, slots, block_rows), BF16),
            jax.ShapeDtypeStruct((groups, cap, slots), BF16),
            jax.ShapeDtypeStruct((groups,), jnp.int32),
            jax.ShapeDtypeStruct((groups * r_dev,), jnp.int32),
            pltpu.HBM((groups, more, slots, block_rows), BF16),
            pltpu.HBM((groups, more, cap, slots), BF16),
        ],
        compiler_params=params(VMEM_BYTES // 2),
        name="index",
    )(numbers, parcels)


def lay_out(parcel_ref, signal_ref):
    n_win, _, samples = parcel_ref.shape
    for w in range(n_win):
        signal_ref[:, w * samples : (w + 1) * samples] = parcel_ref[w].astype(F32)
    tail = signal_ref.shape[1] - n_win * samples
    signal_ref[:, n_win * samples :] = jnp.zeros((signal_ref.shape[0], tail), F32)


def hankel_rows(signal_ref, r, begin, width, out_ref):
    length = width + LANES
    signal = signal_ref[r : r + 1, pl.ds(pl.multiple_of(begin, LANES), length)]
    base = jnp.broadcast_to(signal, (SHIFT_ROWS, length))
    sublane = lax.broadcasted_iota(jnp.int32, base.shape, 0)
    for bit in (1, 2, 4):
        base = jnp.where(sublane & bit != 0, pltpu.roll(base, length - bit, 1), base)
    for first in range(0, LANES, 2 * SHIFT_ROWS):
        both = []
        for shift in (first, first + SHIFT_ROWS):
            rolled = base if shift == 0 else pltpu.roll(base, length - shift, 1)
            both.append(rolled[:, :width])
        out_ref[r, first : first + 2 * SHIFT_ROWS, :] = jnp.concatenate(both, axis=0).astype(BF16)


def hankel_kernel(begin_ref, parcel_ref, out_ref, signal_ref):
    lay_out(parcel_ref, signal_ref)
    for r in range(out_ref.shape[0]):
        hankel_rows(signal_ref, r, begin_ref[0], out_ref.shape[2], out_ref)


def build_hankel(parcels, begin, n_win, r_dev, width):
    groups, samples = parcels.shape[0] // n_win, parcels.shape[2]
    shape = (groups * r_dev, LANES, width)
    return pl.pallas_call(
        hankel_kernel,
        grid_spec=pltpu.PrefetchScalarGridSpec(
            num_scalar_prefetch=1,
            grid=(groups,),
            in_specs=[pl.BlockSpec((n_win,) + parcels.shape[1:], lambda i, *_: (i, 0, 0))],
            out_specs=pl.BlockSpec((r_dev, LANES, width), lambda i, *_: (i, 0, 0)),
            scratch_shapes=[pltpu.VMEM((PARCEL_ROWS, n_win * samples + LAGS), F32)],
        ),
        out_shape=pltpu.HBM(shape, BF16),
        cost_estimate=pl.CostEstimate(
            flops=math.prod(shape), bytes_accessed=2 * math.prod(shape), transcendentals=0
        ),
        compiler_params=params(VMEM_BYTES // 2),
        name="hankel",
    )(begin, parcels)


def pick_rows(pieces, pick, gathered):
    parts = len(pieces) // 2
    count, samples = gathered.shape[1:]
    for q in range(2):
        block_pieces = pieces[q * parts : (q + 1) * parts]
        ones = pick[q * count : (q + 1) * count, :]
        for t in range(0, samples, STEP):
            block = jnp.concatenate([piece[:, t : t + STEP] for piece in block_pieces], axis=0)
            gathered[q, :, t : t + STEP] = jnp.dot(ones, block, preferred_element_type=F32).astype(BF16)


def multiply(gathered, hankel_ref, r, tile, lag):
    samples = gathered.shape[2]
    chosen = jnp.concatenate([gathered[q, r * tile : (r + 1) * tile, :] for q in range(2)], axis=0)
    wide = jnp.concatenate(
        [hankel_ref[r, :, t + lag : t + lag + STEP] for t in range(0, samples, LANES)], axis=0
    )
    return jnp.dot(chosen, wide, preferred_element_type=F32)


def split(total, high, low, slots, lags):
    upper = total.astype(BF16)
    high[slots, lags] = upper
    low[slots, lags] = (total - upper.astype(F32)).astype(BF16)


def placed(place, high, low):
    return jnp.dot(place, high[...], preferred_element_type=F32) + jnp.dot(
        place, low[...], preferred_element_type=F32
    )


def correlate_kernel(parts, tile, norming, prebuilt, first, last, pass_ref, count_ref, begin_ref, *refs):
    refs = list(refs)
    pieces = [refs.pop(0) for _ in range(2 * parts)]
    signal_ref, pick_ref, place_ref, more_pick_ref, more_place_ref = [refs.pop(0) for _ in range(5)]
    if not first:
        sums_ref, extra_ref = refs.pop(0), refs.pop(0)
    if last:
        out_ref = refs.pop(0)
    else:
        handed_ref, left_ref = refs.pop(0), refs.pop(0)
    gathered, high, low, extra, pick_scratch, place_scratch = refs[:6]
    r_dev = gathered.shape[1] // tile
    samples = pieces[0].shape[1]
    lag_dev = extra.shape[1]
    group = pl.program_id(0)

    if prebuilt:
        hankel_ref = signal_ref
    else:
        hankel_ref, row_ref = refs[6:]
        lay_out(signal_ref, row_ref)
        for r in range(r_dev):
            hankel_rows(row_ref, r, begin_ref[0], hankel_ref.shape[2], hankel_ref)

    pick_rows(pieces, pick_ref.at[0], gathered)
    for r in range(r_dev):
        for lag in range(0, lag_dev, STEP):
            lags = slice(lag, lag + STEP)
            both = multiply(gathered, hankel_ref, r, tile, lag)
            for q in range(2):
                total = both[q * tile : (q + 1) * tile]
                slots = slice((q * r_dev + r) * tile, (q * r_dev + r + 1) * tile)
                if not first:
                    total += sums_ref[0, slots, lags]
                if last:
                    split(total * norming, high, low, slots, lags)
                else:
                    handed_ref[0, slots, lags] = total
    if last:
        out_ref[0] = placed(place_ref[0], high, low)

    @pl.when(pass_ref[group] > 1)
    def _():
        if first:
            extra[...] = jnp.zeros(extra.shape, F32)
        else:
            pltpu.sync_copy(extra_ref.at[group], extra)

        def one_pass(number, carry):
            pltpu.sync_copy(more_pick_ref.at[group, number - 1], pick_scratch)
            pltpu.sync_copy(more_place_ref.at[group, number - 1], place_scratch)
            pick_rows(pieces, pick_scratch, gathered)
            for r in range(r_dev):
                needed = count_ref[group * r_dev + r] > number * tile
                places = [slice((q * r_dev + r) * tile, (q * r_dev + r + 1) * tile) for q in range(2)]

                @pl.when(needed)
                def _():
                    for lag in range(0, lag_dev, STEP):
                        both = multiply(gathered, hankel_ref, r, tile, lag) * norming
                        for q, slots in enumerate(places):
                            split(both[q * tile : (q + 1) * tile], high, low, slots, slice(lag, lag + STEP))

                @pl.when(jnp.logical_not(needed))
                def _():
                    for slots in places:
                        high[slots, :] = jnp.zeros((tile, lag_dev), BF16)
                        low[slots, :] = jnp.zeros((tile, lag_dev), BF16)

            extra[...] += placed(place_scratch[...], high, low)
            return carry

        lax.fori_loop(1, pass_ref[group], one_pass, 0)
        if last:
            out_ref[0] += extra[...]
        else:
            pltpu.sync_copy(extra, left_ref.at[group])


def correlate(pieces, signal, prebuilt, begin, matrices, before, last, tile, norming, lag_dev, n_win, r_dev):
    pick, place, passes, counts, more_pick, more_place = matrices
    parts = len(pieces) // 2
    groups, cap, slots = place.shape
    part_rows, samples = pieces[0].shape
    width = samples - LANES + lag_dev
    by_group = lambda shape: pl.BlockSpec(shape, lambda i, *_: (i, 0, 0))
    any_spec = pl.BlockSpec(memory_space=pl.ANY)
    sums_spec = by_group((1, slots, lag_dev))
    sums_shape = jax.ShapeDtypeStruct((groups, slots, lag_dev), F32)
    out_shape = jax.ShapeDtypeStruct((groups, cap, lag_dev), F32)
    in_specs = [pl.BlockSpec(piece.shape, lambda i, *_: (0, 0)) for piece in pieces]
    in_specs.append(by_group((r_dev, LANES, width) if prebuilt else (n_win,) + signal.shape[1:]))
    in_specs += [by_group((1,) + pick.shape[1:]), by_group((1,) + place.shape[1:]), any_spec, any_spec]
    if prebuilt:
        signal = in_hbm(signal)
    args = pieces + [signal, pick, place, in_hbm(more_pick), in_hbm(more_place)]
    if before is not None:
        in_specs += [sums_spec, any_spec]
        args += [before[0], in_hbm(before[1])]
    scratch = [
        pltpu.VMEM((2, r_dev * tile, samples), BF16),
        pltpu.VMEM((slots, lag_dev), BF16),
        pltpu.VMEM((slots, lag_dev), BF16),
        pltpu.VMEM((cap, lag_dev), F32),
        pltpu.VMEM(pick.shape[1:], BF16),
        pltpu.VMEM(place.shape[1:], BF16),
    ]
    if not prebuilt:
        scratch.append(pltpu.VMEM((r_dev, LANES, width), BF16))
        scratch.append(pltpu.VMEM((PARCEL_ROWS, n_win * samples + LAGS), F32))
    body = functools.partial(correlate_kernel, parts, tile, norming, prebuilt, before is None, last)
    return pl.pallas_call(
        body,
        grid_spec=pltpu.PrefetchScalarGridSpec(
            num_scalar_prefetch=3,
            grid=(groups,),
            in_specs=in_specs,
            out_specs=by_group((1, cap, lag_dev)) if last else [sums_spec, any_spec],
            scratch_shapes=scratch,
        ),
        out_shape=out_shape if last else [sums_shape, pltpu.HBM(out_shape.shape, F32)],
        cost_estimate=pl.CostEstimate(
            flops=4 * groups * r_dev * tile * samples * (lag_dev + parts * part_rows),
            bytes_accessed=signal.size * signal.dtype.itemsize + 2 * groups * cap * lag_dev * 4,
            transcendentals=0,
        ),
        compiler_params=params(VMEM_BYTES if prebuilt else 2 * VMEM_BYTES),
        name="correlate",
    )(passes, counts, begin, *args)


def shards(sources, receivers, plan, pair_index, keep):
    _, block_rows, samples = sources.shape
    r_dev = receivers.shape[0]
    n_chan = lax.axis_size("chan")
    n_win = lax.axis_size("win")
    n_rep = lax.axis_size("rep")
    chan, win, rep = lax.axis_index("chan"), lax.axis_index("win"), lax.axis_index("rep")
    cap = pair_index.shape[3]
    lag_dev = LAGS // (n_win * n_rep)
    half_rows = block_rows // n_rep
    tile = max(16, cap // 8)
    norming = 1.0 / math.sqrt(samples * n_win)
    width = samples - LANES + lag_dev
    prebuilt = n_chan * r_dev * n_win * LANES * width * 2 <= HANKEL_BYTES

    parcels, *owns = pack(
        sources[0], receivers, pair_index[0, 0], keep[0, 0], half_rows, n_chan, n_win, rep.reshape(1)
    )
    parcels = lax.all_to_all(parcels, ("chan", "win"), split_axis=0, concat_axis=0, tiled=True)

    arrived = [{0: own} for own in owns]

    def relay(step):
        for there in arrived:
            there[step] = swapped(there[1 - step], "chan", 0)
            if step < n_chan - 1:
                there[-step] = swapped(there[step - 1], "chan", 1)

    def after_arrival(step, value):
        there = arrived[-1]
        for key in (step, -step):
            if key in there:
                value, there[key] = lax.optimization_barrier((value, there[key]))
        return value

    def before_start(step, chain, value):
        there = arrived[chain]
        for key in (1 - step, step - 1):
            value, there[key] = lax.optimization_barrier((value, there[key]))
        return value

    distance = jnp.abs(plan[0] - chan)
    nearer = jnp.where(distance[0] <= distance[1], 0, 1)
    owners = [jnp.where(nearer == 0, plan[0, 0], plan[0, 1]), jnp.where(nearer == 0, plan[0, 1], plan[0, 0])]
    numbers = jnp.stack([nearer, block_rows - rep * half_rows])
    lag_start = (win * n_rep + rep) * lag_dev
    begins = [((win + n_win - v) % n_win * samples + lag_start).reshape(1) for v in range(n_win)]

    def planned(q):
        where = jnp.where(chan % 2 == 0, owners[q] - chan, chan - owners[q])
        reach = n_chan - 1 if q else n_chan - 2
        chosen = []
        for there in arrived:
            found = there[0]
            for offset in range(-reach, reach + 1):
                if offset and offset in there:
                    found = jnp.where(where == offset, there[offset], found)
            chosen.append(found)
        return chosen

    def halves(piece):
        return [piece] + [turned(piece, "rep", -u) for u in range(1, n_rep)]

    relay(1)
    parcels = after_arrival(1, parcels)
    relay(2)
    matrices = index(parcels, numbers, n_win, r_dev, cap, tile, block_rows)
    signals = [parcels] * n_win
    if prebuilt:
        signals[0] = build_hankel(parcels, begins[0], n_win, r_dev, width)
    near = planned(0)
    near = [before_start(3, chain, piece) for chain, piece in enumerate(near)]
    signals[0], matrices = before_start(3, CHAINS - 1, (signals[0], matrices))
    near = jnp.concatenate(near, axis=0)
    for step in range(3, n_chan):
        relay(step)
    near_spans = [near] + [turned(near, "win", v) for v in range(1, n_win)]
    if prebuilt:
        parcels, near = lax.optimization_barrier((parcels, near))
        for v in range(1, n_win):
            signals[v] = build_hankel(parcels, begins[v], n_win, r_dev, width)
    near_halves = [halves(piece) for piece in near_spans]
    far = jnp.concatenate(planned(1), axis=0)
    if prebuilt:
        far, signals = lax.optimization_barrier((far, signals))
    far_spans = [far] + [turned(far, "win", v) for v in range(1, n_win)]

    result = None
    for v in range(n_win):
        if v:
            far_spans, result = lax.optimization_barrier((far_spans, result))
        result = correlate(
            near_halves[v] + halves(far_spans[v]), signals[v], prebuilt, begins[v], matrices, result, v == n_win - 1,
            tile, norming, lag_dev, n_win, r_dev,
        )
    return result[None, None]


def solution(mesh):
    placed_at = (
        P(("grp", "chan"), None, "win"),
        P(("grp", "chan"), "win"),
        P("grp", None),
        P("grp", "chan", None, None),
        P("grp", "chan", None, None),
    )
    return jax.shard_map(
        shards,
        mesh=mesh,
        in_specs=placed_at,
        out_specs=P(("grp", "chan"), None, None, None, ("win", "rep")),
        check_vma=False,
    )
```

```python
import functools
import math

import jax
import jax.numpy as jnp
from jax import lax
from jax.experimental import pallas as pl
from jax.experimental.pallas import tpu as pltpu
from jax.sharding import PartitionSpec as P

LAGS = 2048
LANES = 128
SHIFT_ROWS = 8
STEP = 2 * LANES
CHAINS = 1
DIGIT = 64
HANKEL_BYTES = 24 * 2**20
VMEM_BYTES = 26 * 2**20
F32 = jnp.float32
BF16 = jnp.bfloat16


def swapped(block, axis, first):
    size = lax.axis_size(axis)
    route = []
    for i in range(first, size - 1, 2):
        route += [(i, i + 1), (i + 1, i)]
    return lax.ppermute(block, axis, route)


def turned(block, axis, distance):
    size = lax.axis_size(axis)
    return lax.ppermute(block, axis, [(i, (i + distance) % size) for i in range(size)])


def in_hbm(array):
    return pltpu.with_memory_space_constraint(array, pltpu.HBM)


def params(vmem):
    return pltpu.CompilerParams(vmem_limit_bytes=vmem)


def pack_kernel(halves, lags, plan_hbm, source_ref, receiver_hbm, pair_hbm, keep_hbm, parcel_ref, number_ref, *refs):
    chain_refs, small_refs, sems = refs[:-5], refs[-5:-1], refs[-1]
    plan_ref, receiver_ref, pair_ref, keep_ref = small_refs
    small = []
    for place, source in enumerate((plan_hbm, receiver_hbm, pair_hbm, keep_hbm)):
        small.append(pltpu.make_async_copy(source, small_refs[place], sems.at[CHAINS + place]))
        small[-1].start()
    r_dev, samples = receiver_ref.shape
    n_chan, cap = pair_ref.shape
    n_win = parcel_ref.shape[0] // n_chan
    chan, win, rep = lax.axis_index("chan"), lax.axis_index("win"), lax.axis_index("rep")
    block_rows = source_ref.shape[0]
    half_rows = block_rows // halves
    rows = chain_refs[0].shape[0]
    copies = []
    for chain, chain_ref in enumerate(chain_refs):
        start = pl.multiple_of(rep * half_rows + chain * rows, rows)
        copies.append(pltpu.make_async_copy(source_ref.at[pl.ds(start, rows)], chain_ref, sems.at[chain]))
        copies[-1].start()
    for copy in small:
        copy.wait()

    packed = pair_ref[...] * 2 + keep_ref[...]
    digits = jnp.concatenate([packed // DIGIT, packed % DIGIT], axis=1).astype(F32)
    heard = receiver_ref[...].astype(F32)
    part = 2 * cap // r_dev
    spare = parcel_ref.shape[2] - samples - part
    for d in range(n_chan):
        lists = [digits[d : d + 1, i * part : (i + 1) * part] for i in range(r_dev)]
        parcel = [heard, jnp.concatenate(lists, axis=0)]
        if spare:
            parcel.append(jnp.zeros((r_dev, spare), F32))
        parcel = jnp.concatenate(parcel, axis=1).astype(BF16)
        for w in range(n_win):
            parcel_ref[d * n_win + w] = parcel

    one, two = plan_ref[0, 0], plan_ref[0, 1]
    nearer = jnp.where(jnp.abs(one - chan) <= jnp.abs(two - chan), 0, 1)
    sign = jnp.where(chan % 2 == 0, 1, -1)
    number_ref[0] = nearer
    number_ref[1] = block_rows - rep * half_rows
    number_ref[2] = sign * (jnp.where(nearer == 0, one, two) - chan)
    number_ref[3] = sign * (jnp.where(nearer == 0, two, one) - chan)
    for v in range(n_win):
        number_ref[4 + v] = (win + n_win - v) % n_win * samples + (win * halves + rep) * lags
    for copy in copies:
        copy.wait()


def pack(plan, sources, receivers, pair_index, keep, halves, lags, n_chan, n_win):
    r_dev, samples = receivers.shape
    chain_rows = sources.shape[0] // halves // CHAINS
    beside = -(-2 * pair_index.shape[1] // r_dev // LANES) * LANES
    vmem, smem = pl.BlockSpec(memory_space=pltpu.VMEM), pl.BlockSpec(memory_space=pltpu.SMEM)
    shapes = [jax.ShapeDtypeStruct((n_chan * n_win, r_dev, samples + beside), BF16)]
    shapes.append(jax.ShapeDtypeStruct((4 + n_win,), jnp.int32))
    shapes += [jax.ShapeDtypeStruct((chain_rows, samples), BF16)] * CHAINS
    return pl.pallas_call(
        functools.partial(pack_kernel, halves, lags),
        in_specs=[pl.BlockSpec(memory_space=pl.ANY)] * 5,
        out_specs=[vmem, smem] + [vmem] * CHAINS,
        out_shape=shapes,
        scratch_shapes=[
            pltpu.SMEM(plan.shape, plan.dtype),
            pltpu.VMEM(receivers.shape, receivers.dtype),
            pltpu.VMEM(pair_index.shape, pair_index.dtype),
            pltpu.VMEM(keep.shape, keep.dtype),
            pltpu.SemaphoreType.DMA((CHAINS + 4,)),
        ],
        compiler_params=params(VMEM_BYTES // 2),
        name="pack",
    )(*[in_hbm(a) for a in (plan, sources, receivers, pair_index, keep)])


def choose_kernel(which, offsets, number_ref, *refs):
    out_ref, sems = refs[-2:]
    rows = out_ref.shape[0] // CHAINS
    where = number_ref[which]
    waits = []
    for chain in range(CHAINS):
        target = out_ref.at[pl.ds(chain * rows, rows)]
        for place, offset in enumerate(offsets):
            copy = pltpu.make_async_copy(refs[chain * len(offsets) + place], target, sems.at[chain])

            @pl.when(where == offset)
            def _():
                copy.start()

        waits.append(copy)
    for copy in waits:
        copy.wait()


def choose(numbers, which, arrived, offsets):
    pieces = [there[offset] for there in arrived for offset in offsets]
    rows, samples = pieces[0].shape
    any_spec = pl.BlockSpec(memory_space=pl.ANY)
    return pl.pallas_call(
        functools.partial(choose_kernel, which, offsets),
        in_specs=[pl.BlockSpec(memory_space=pltpu.SMEM)] + [any_spec] * len(pieces),
        out_specs=pl.BlockSpec(memory_space=pltpu.VMEM),
        out_shape=jax.ShapeDtypeStruct((rows * CHAINS, samples), BF16),
        scratch_shapes=[pltpu.SemaphoreType.DMA((CHAINS,))],
        compiler_params=params(VMEM_BYTES // 4),
        name="choose",
    )(numbers, *pieces)


def column(row):
    return jnp.broadcast_to(row, (SHIFT_ROWS, row.shape[1])).T[:, :1]


def ones_where(condition):
    return jnp.where(condition, 1.0, 0.0).astype(BF16)


def index_kernel(r_dev, samples, cap, tile, block_rows, number_ref, parcel_ref, pick_ref, place_ref, pass_ref, count_ref,
                 more_pick_ref, more_place_ref, pick_scratch, place_scratch, below_ref):
    group = pl.program_id(0)
    nearer, offset = number_ref[0], number_ref[1]
    slots = 2 * r_dev * tile
    part = 2 * cap // r_dev
    beside = parcel_ref.shape[2] - samples
    digits = parcel_ref[0, :, pl.ds(samples, beside)].astype(F32)
    digits = jnp.concatenate([digits[i : i + 1, :part] for i in range(r_dev)], axis=1).astype(jnp.int32)
    packed = digits[:, :cap] * DIGIT + digits[:, cap:]
    pairs, kept = packed // 2, packed % 2 == 1
    source_row, receiver = pairs // r_dev, pairs % r_dev
    turn = jnp.where(source_row // block_rows == nearer, 0, 1)
    row = (source_row + offset) % block_rows
    segment = jnp.where(kept, turn * r_dev + receiver, -1)
    member = lax.broadcasted_iota(jnp.int32, (2 * r_dev, cap), 0) == segment

    @pl.when(group == 0)
    def _():
        below = lax.broadcasted_iota(jnp.int32, (cap, cap), 0) < lax.broadcasted_iota(jnp.int32, (cap, cap), 1)
        below_ref[...] = ones_where(below)

    earlier = jnp.dot(ones_where(member), below_ref[...], preferred_element_type=F32)
    rank = jnp.sum(jnp.where(member, earlier, 0.0), axis=0, keepdims=True).astype(jnp.int32)
    code = (rank // tile) * slots + (turn * r_dev + receiver) * tile + rank % tile
    code = jnp.where(kept, code, -1)
    counts = jnp.sum(jnp.where(member, 1.0, 0.0), axis=1, keepdims=True)
    which = lax.broadcasted_iota(jnp.int32, counts.shape, 0) % r_dev
    for r in range(r_dev):
        count_ref[group * r_dev + r] = jnp.max(jnp.where(which == r, counts, 0.0)).astype(jnp.int32)
    passes = (jnp.max(counts).astype(jnp.int32) + tile - 1) // tile
    pass_ref[group] = passes

    code_column = column(code.astype(F32)).astype(jnp.int32)
    row_column = column(row.astype(F32)).astype(jnp.int32)
    row_ones = ones_where(row_column == lax.broadcasted_iota(jnp.int32, (cap, block_rows), 1))

    def matrices(number):
        start = number * slots
        by_slot = ones_where(lax.broadcasted_iota(jnp.int32, (slots, cap), 0) + start == code)
        pick = jnp.dot(by_slot, row_ones, preferred_element_type=F32).astype(BF16)
        place = ones_where(lax.broadcasted_iota(jnp.int32, (cap, slots), 1) + start == code_column)
        return pick, place

    pick_ref[0], place_ref[0] = matrices(0)

    @pl.when(passes > 1)
    def _():
        def one_pass(number, carry):
            pick_scratch[...], place_scratch[...] = matrices(number)
            pltpu.sync_copy(pick_scratch, more_pick_ref.at[group, number - 1])
            pltpu.sync_copy(place_scratch, more_place_ref.at[group, number - 1])
            return carry

        lax.fori_loop(1, passes, one_pass, 0)


def index(parcels, numbers, n_win, samples, r_dev, cap, tile, block_rows):
    groups = parcels.shape[0] // n_win
    slots = 2 * r_dev * tile
    more = max(1, -(-min(block_rows, cap) // tile) - 1)
    return pl.pallas_call(
        functools.partial(index_kernel, r_dev, samples, cap, tile, block_rows),
        grid_spec=pltpu.PrefetchScalarGridSpec(
            num_scalar_prefetch=1,
            grid=(groups,),
            in_specs=[pl.BlockSpec((1,) + parcels.shape[1:], lambda i, *_: (i * n_win, 0, 0))],
            out_specs=[
                pl.BlockSpec((1, slots, block_rows), lambda i, *_: (i, 0, 0)),
                pl.BlockSpec((1, cap, slots), lambda i, *_: (i, 0, 0)),
                pl.BlockSpec(memory_space=pltpu.SMEM),
                pl.BlockSpec(memory_space=pltpu.SMEM),
                pl.BlockSpec(memory_space=pl.ANY),
                pl.BlockSpec(memory_space=pl.ANY),
            ],
            scratch_shapes=[
                pltpu.VMEM((slots, block_rows), BF16),
                pltpu.VMEM((cap, slots), BF16),
                pltpu.VMEM((cap, cap), BF16),
            ],
        ),
        out_shape=[
            jax.ShapeDtypeStruct((groups, slots, block_rows), BF16),
            jax.ShapeDtypeStruct((groups, cap, slots), BF16),
            jax.ShapeDtypeStruct((groups,), jnp.int32),
            jax.ShapeDtypeStruct((groups * r_dev,), jnp.int32),
            pltpu.HBM((groups, more, slots, block_rows), BF16),
            pltpu.HBM((groups, more, cap, slots), BF16),
        ],
        compiler_params=params(VMEM_BYTES // 2),
        name="index",
    )(numbers, parcels)


def lay_out(parcel_ref, signal_ref, samples):
    n_win, r_dev, _ = parcel_ref.shape
    for w in range(n_win):
        signal_ref[:r_dev, w * samples : (w + 1) * samples] = parcel_ref[w, :, :samples].astype(F32)
    tail = signal_ref.shape[1] - n_win * samples
    signal_ref[:r_dev, n_win * samples :] = jnp.zeros((r_dev, tail), F32)


def hankel_rows(signal_ref, r, begin, width, out_ref):
    length = width + LANES
    signal = signal_ref[r : r + 1, pl.ds(pl.multiple_of(begin, LANES), length)]
    base = jnp.broadcast_to(signal, (SHIFT_ROWS, length))
    sublane = lax.broadcasted_iota(jnp.int32, base.shape, 0)
    for bit in (1, 2, 4):
        base = jnp.where(sublane & bit != 0, pltpu.roll(base, length - bit, 1), base)
    base = jnp.concatenate([base, pltpu.roll(base, length - SHIFT_ROWS, 1)], axis=0).astype(BF16)
    for first in range(0, LANES, 2 * SHIFT_ROWS):
        rolled = pltpu.roll(base, length - first, 1) if first else base
        out_ref[r, first : first + 2 * SHIFT_ROWS, :] = rolled[:, :width]


def hankel_kernel(v, samples, number_ref, parcel_ref, out_ref, signal_ref):
    lay_out(parcel_ref, signal_ref, samples)
    for r in range(out_ref.shape[0]):
        hankel_rows(signal_ref, r, number_ref[4 + v], out_ref.shape[2], out_ref)


def build_hankel(parcels, numbers, v, n_win, samples, width):
    groups, r_dev = parcels.shape[0] // n_win, parcels.shape[1]
    shape = (groups * r_dev, LANES, width)
    return pl.pallas_call(
        functools.partial(hankel_kernel, v, samples),
        grid_spec=pltpu.PrefetchScalarGridSpec(
            num_scalar_prefetch=1,
            grid=(groups,),
            in_specs=[pl.BlockSpec((n_win,) + parcels.shape[1:], lambda i, *_: (i, 0, 0))],
            out_specs=pl.BlockSpec((r_dev, LANES, width), lambda i, *_: (i, 0, 0)),
            scratch_shapes=[pltpu.VMEM((SHIFT_ROWS, n_win * samples + LAGS), F32)],
        ),
        out_shape=pltpu.HBM(shape, BF16),
        cost_estimate=pl.CostEstimate(
            flops=math.prod(shape), bytes_accessed=2 * math.prod(shape), transcendentals=0
        ),
        compiler_params=params(VMEM_BYTES // 2),
        name="hankel",
    )(numbers, parcels)


def pick_rows(pieces, pick, gathered):
    parts = len(pieces) // 2
    count, samples = gathered.shape[1:]
    for q in range(2):
        block_pieces = pieces[q * parts : (q + 1) * parts]
        ones = pick[q * count : (q + 1) * count, :]
        for t in range(0, samples, STEP):
            block = jnp.concatenate([piece[:, t : t + STEP] for piece in block_pieces], axis=0)
            gathered[q, :, t : t + STEP] = jnp.dot(ones, block, preferred_element_type=F32).astype(BF16)


def multiply(gathered, hankel_ref, r, tile, lag):
    samples = gathered.shape[2]
    chosen = jnp.concatenate([gathered[q, r * tile : (r + 1) * tile, :] for q in range(2)], axis=0)
    wide = jnp.concatenate(
        [hankel_ref[r, :, t + lag : t + lag + STEP] for t in range(0, samples, LANES)], axis=0
    )
    return jnp.dot(chosen, wide, preferred_element_type=F32)


def split(total, high, low, slots, lags):
    upper = total.astype(BF16)
    high[slots, lags] = upper
    low[slots, lags] = (total - upper.astype(F32)).astype(BF16)


def placed(place, high, low):
    return jnp.dot(place, high[...], preferred_element_type=F32) + jnp.dot(
        place, low[...], preferred_element_type=F32
    )


def correlate_kernel(parts, v, tile, norming, prebuilt, first, last, pass_ref, count_ref, number_ref, *refs):
    refs = list(refs)
    pieces = [refs.pop(0) for _ in range(2 * parts)]
    signal_ref, pick_ref, place_ref, more_pick_ref, more_place_ref = [refs.pop(0) for _ in range(5)]
    if not first:
        sums_ref, extra_ref = refs.pop(0), refs.pop(0)
    if last:
        out_ref = refs.pop(0)
    else:
        handed_ref, left_ref = refs.pop(0), refs.pop(0)
    gathered, high, low, extra, pick_scratch, place_scratch = refs[:6]
    r_dev = gathered.shape[1] // tile
    samples = pieces[0].shape[1]
    lag_dev = extra.shape[1]
    group = pl.program_id(0)

    if prebuilt:
        hankel_ref = signal_ref
    else:
        hankel_ref, row_ref = refs[6:]
        lay_out(signal_ref, row_ref, samples)
        for r in range(r_dev):
            hankel_rows(row_ref, r, number_ref[4 + v], hankel_ref.shape[2], hankel_ref)

    pick_rows(pieces, pick_ref.at[0], gathered)
    for r in range(r_dev):
        for lag in range(0, lag_dev, STEP):
            lags = slice(lag, lag + STEP)
            both = multiply(gathered, hankel_ref, r, tile, lag)
            for q in range(2):
                total = both[q * tile : (q + 1) * tile]
                slots = slice((q * r_dev + r) * tile, (q * r_dev + r + 1) * tile)
                if not first:
                    total += sums_ref[0, slots, lags]
                if last:
                    split(total * norming, high, low, slots, lags)
                else:
                    handed_ref[0, slots, lags] = total
    if last:
        out_ref[0] = placed(place_ref[0], high, low)

    @pl.when(pass_ref[group] > 1)
    def _():
        if first:
            extra[...] = jnp.zeros(extra.shape, F32)
        else:
            pltpu.sync_copy(extra_ref.at[group], extra)

        def one_pass(number, carry):
            pltpu.sync_copy(more_pick_ref.at[group, number - 1], pick_scratch)
            pltpu.sync_copy(more_place_ref.at[group, number - 1], place_scratch)
            pick_rows(pieces, pick_scratch, gathered)
            for r in range(r_dev):
                needed = count_ref[group * r_dev + r] > number * tile
                places = [slice((q * r_dev + r) * tile, (q * r_dev + r + 1) * tile) for q in range(2)]

                @pl.when(needed)
                def _():
                    for lag in range(0, lag_dev, STEP):
                        both = multiply(gathered, hankel_ref, r, tile, lag) * norming
                        for q, slots in enumerate(places):
                            split(both[q * tile : (q + 1) * tile], high, low, slots, slice(lag, lag + STEP))

                @pl.when(jnp.logical_not(needed))
                def _():
                    for slots in places:
                        high[slots, :] = jnp.zeros((tile, lag_dev), BF16)
                        low[slots, :] = jnp.zeros((tile, lag_dev), BF16)

            extra[...] += placed(place_scratch[...], high, low)
            return carry

        lax.fori_loop(1, pass_ref[group], one_pass, 0)
        if last:
            out_ref[0] += extra[...]
        else:
            pltpu.sync_copy(extra, left_ref.at[group])


def correlate(pieces, signal, prebuilt, numbers, v, matrices, before, last, tile, norming, lag_dev, n_win, r_dev):
    pick, place, passes, counts, more_pick, more_place = matrices
    parts = len(pieces) // 2
    groups, cap, slots = place.shape
    part_rows, samples = pieces[0].shape
    width = samples - LANES + lag_dev
    by_group = lambda shape: pl.BlockSpec(shape, lambda i, *_: (i, 0, 0))
    any_spec = pl.BlockSpec(memory_space=pl.ANY)
    sums_spec = by_group((1, slots, lag_dev))
    sums_shape = jax.ShapeDtypeStruct((groups, slots, lag_dev), F32)
    out_shape = jax.ShapeDtypeStruct((groups, cap, lag_dev), F32)
    in_specs = [pl.BlockSpec(memory_space=pltpu.VMEM) for _ in pieces]
    in_specs.append(by_group((r_dev, LANES, width) if prebuilt else (n_win,) + signal.shape[1:]))
    in_specs += [by_group((1,) + pick.shape[1:]), by_group((1,) + place.shape[1:]), any_spec, any_spec]
    if prebuilt:
        signal = in_hbm(signal)
    args = pieces + [signal, pick, place, in_hbm(more_pick), in_hbm(more_place)]
    if before is not None:
        in_specs += [sums_spec, any_spec]
        args += [before[0], in_hbm(before[1])]
    scratch = [
        pltpu.VMEM((2, r_dev * tile, samples), BF16),
        pltpu.VMEM((slots, lag_dev), BF16),
        pltpu.VMEM((slots, lag_dev), BF16),
        pltpu.VMEM((cap, lag_dev), F32),
        pltpu.VMEM(pick.shape[1:], BF16),
        pltpu.VMEM(place.shape[1:], BF16),
    ]
    if not prebuilt:
        scratch.append(pltpu.VMEM((r_dev, LANES, width), BF16))
        scratch.append(pltpu.VMEM((SHIFT_ROWS, n_win * samples + LAGS), F32))
    body = functools.partial(correlate_kernel, parts, v, tile, norming, prebuilt, before is None, last)
    return pl.pallas_call(
        body,
        grid_spec=pltpu.PrefetchScalarGridSpec(
            num_scalar_prefetch=3,
            grid=(groups,),
            in_specs=in_specs,
            out_specs=by_group((1, cap, lag_dev)) if last else [sums_spec, any_spec],
            scratch_shapes=scratch,
        ),
        out_shape=out_shape if last else [sums_shape, pltpu.HBM(out_shape.shape, F32)],
        cost_estimate=pl.CostEstimate(
            flops=4 * groups * r_dev * tile * samples * (lag_dev + parts * part_rows),
            bytes_accessed=signal.size * signal.dtype.itemsize + 2 * groups * cap * lag_dev * 4,
            transcendentals=0,
        ),
        compiler_params=params(VMEM_BYTES if prebuilt else 2 * VMEM_BYTES),
        name="correlate",
    )(passes, counts, numbers, *args)


def shards(sources, receivers, plan, pair_index, keep):
    _, block_rows, samples = sources.shape
    r_dev = receivers.shape[0]
    n_chan = lax.axis_size("chan")
    n_win = lax.axis_size("win")
    n_rep = lax.axis_size("rep")
    cap = pair_index.shape[3]
    lag_dev = LAGS // (n_win * n_rep)
    tile = max(16, cap // 8)
    norming = 1.0 / math.sqrt(samples * n_win)
    width = samples - LANES + lag_dev
    prebuilt = n_chan * r_dev * n_win * LANES * width * 2 <= HANKEL_BYTES

    parcels, numbers, *owns = pack(
        plan, sources[0], receivers, pair_index[0, 0], keep[0, 0], n_rep, lag_dev, n_chan, n_win
    )
    parcels = lax.all_to_all(parcels, ("chan", "win"), split_axis=0, concat_axis=0, tiled=True)
    parcels, owns = lax.optimization_barrier((parcels, owns))

    arrived = [{0: own} for own in owns]

    def relay(step):
        for there in arrived:
            there[step] = swapped(there[1 - step], "chan", 0)
            if step < n_chan - 1:
                there[-step] = swapped(there[step - 1], "chan", 1)

    def after_arrival(step, value):
        for there in arrived:
            for key in (step, -step):
                if key in there:
                    value, there[key] = lax.optimization_barrier((value, there[key]))
        return value

    def before_start(step, value):
        for there in arrived:
            for key in (1 - step, step - 1):
                value, there[key] = lax.optimization_barrier((value, there[key]))
        return value

    def halves(piece):
        return [piece] + [turned(piece, "rep", -u) for u in range(1, n_rep)]

    def spans(piece):
        return [piece] + [turned(piece, "win", v) for v in range(1, n_win)]

    signals = [parcels] * n_win
    relay(1)
    matrices = index(parcels, numbers, n_win, samples, r_dev, cap, tile, block_rows)
    if prebuilt:
        signals[0] = build_hankel(parcels, numbers, 0, n_win, samples, width)
    matrices, signals[0] = before_start(2, (matrices, signals[0]))
    relay(2)
    if prebuilt:
        parcels = after_arrival(1, parcels)
        for v in range(1, n_win):
            signals[v] = build_hankel(parcels, numbers, v, n_win, samples, width)
        signals = before_start(3, signals)
    reach = range(-(n_chan - 2), n_chan - 1)
    near = choose(numbers, 2, arrived, [offset for offset in reach if offset in arrived[0]])
    for step in range(3, n_chan):
        relay(step)
    near_halves = [halves(piece) for piece in spans(near)]
    far_spans = spans(choose(numbers, 3, arrived, sorted(arrived[0])))

    result = None
    for v in range(n_win):
        if v:
            far_spans, result = lax.optimization_barrier((far_spans, result))
        result = correlate(
            near_halves[v] + halves(far_spans[v]), signals[v], prebuilt, numbers, v, matrices, result, v == n_win - 1,
            tile, norming, lag_dev, n_win, r_dev,
        )
    return result[None, None]


def solution(mesh):
    placed_at = (
        P(("grp", "chan"), None, "win"),
        P(("grp", "chan"), "win"),
        P("grp", None),
        P("grp", "chan", None, None),
        P("grp", "chan", None, None),
    )
    return jax.shard_map(
        shards,
        mesh=mesh,
        in_specs=placed_at,
        out_specs=P(("grp", "chan"), None, None, None, ("win", "rep")),
        check_vma=False,
    )
```

```python
import functools
import math

import jax
import jax.numpy as jnp
from jax import lax
from jax.experimental import pallas as pl
from jax.experimental.pallas import tpu as pltpu
from jax.sharding import PartitionSpec as P

LAGS = 2048
LANES = 128
SHIFT_ROWS = 8
STEP = 2 * LANES
CHAINS = 1
DIGIT = 64
HANKEL_BYTES = 24 * 2**20
VMEM_BYTES = 26 * 2**20
F32 = jnp.float32
BF16 = jnp.bfloat16


def swapped(block, axis, first):
    size = lax.axis_size(axis)
    route = []
    for i in range(first, size - 1, 2):
        route += [(i, i + 1), (i + 1, i)]
    return lax.ppermute(block, axis, route)


def turned(block, axis, distance):
    size = lax.axis_size(axis)
    return lax.ppermute(block, axis, [(i, (i + distance) % size) for i in range(size)])


def in_hbm(array):
    return pltpu.with_memory_space_constraint(array, pltpu.HBM)


def params(vmem):
    return pltpu.CompilerParams(vmem_limit_bytes=vmem)


def pack_kernel(halves, lags, plan_hbm, source_ref, receiver_hbm, pair_hbm, keep_hbm, parcel_ref, number_ref, *refs):
    chain_refs, small_refs, sems = refs[:-5], refs[-5:-1], refs[-1]
    plan_ref, receiver_ref, pair_ref, keep_ref = small_refs
    small = []
    for place, source in enumerate((plan_hbm, receiver_hbm, pair_hbm, keep_hbm)):
        small.append(pltpu.make_async_copy(source, small_refs[place], sems.at[CHAINS + place]))
        small[-1].start()
    r_dev, samples = receiver_ref.shape
    n_chan, cap = pair_ref.shape
    n_win = parcel_ref.shape[0] // n_chan
    chan, win, rep = lax.axis_index("chan"), lax.axis_index("win"), lax.axis_index("rep")
    block_rows = source_ref.shape[0]
    half_rows = block_rows // halves
    rows = chain_refs[0].shape[0]
    copies = []
    for chain, chain_ref in enumerate(chain_refs):
        start = pl.multiple_of(rep * half_rows + chain * rows, rows)
        copies.append(pltpu.make_async_copy(source_ref.at[pl.ds(start, rows)], chain_ref, sems.at[chain]))
        copies[-1].start()
    for copy in small:
        copy.wait()

    packed = pair_ref[...] * 2 + keep_ref[...]
    digits = jnp.concatenate([packed // DIGIT, packed % DIGIT], axis=1).astype(F32)
    heard = receiver_ref[...].astype(F32)
    part = 2 * cap // r_dev
    spare = parcel_ref.shape[2] - samples - part
    for d in range(n_chan):
        lists = [digits[d : d + 1, i * part : (i + 1) * part] for i in range(r_dev)]
        parcel = [heard, jnp.concatenate(lists, axis=0)]
        if spare:
            parcel.append(jnp.zeros((r_dev, spare), F32))
        parcel = jnp.concatenate(parcel, axis=1).astype(BF16)
        for w in range(n_win):
            parcel_ref[d * n_win + w] = parcel

    one, two = plan_ref[0, 0], plan_ref[0, 1]
    nearer = jnp.where(jnp.abs(one - chan) <= jnp.abs(two - chan), 0, 1)
    sign = jnp.where(chan % 2 == 0, 1, -1)
    number_ref[0] = nearer
    number_ref[1] = block_rows - rep * half_rows
    number_ref[2] = sign * (jnp.where(nearer == 0, one, two) - chan)
    number_ref[3] = sign * (jnp.where(nearer == 0, two, one) - chan)
    for v in range(n_win):
        number_ref[4 + v] = (win + n_win - v) % n_win * samples + (win * halves + rep) * lags
    for copy in copies:
        copy.wait()


def pack(plan, sources, receivers, pair_index, keep, halves, lags, n_chan, n_win):
    r_dev, samples = receivers.shape
    chain_rows = sources.shape[0] // halves // CHAINS
    beside = -(-2 * pair_index.shape[1] // r_dev // LANES) * LANES
    vmem, smem = pl.BlockSpec(memory_space=pltpu.VMEM), pl.BlockSpec(memory_space=pltpu.SMEM)
    shapes = [jax.ShapeDtypeStruct((n_chan * n_win, r_dev, samples + beside), BF16)]
    shapes.append(jax.ShapeDtypeStruct((4 + n_win,), jnp.int32))
    shapes += [jax.ShapeDtypeStruct((chain_rows, samples), BF16)] * CHAINS
    return pl.pallas_call(
        functools.partial(pack_kernel, halves, lags),
        in_specs=[pl.BlockSpec(memory_space=pl.ANY)] * 5,
        out_specs=[vmem, smem] + [vmem] * CHAINS,
        out_shape=shapes,
        scratch_shapes=[
            pltpu.SMEM(plan.shape, plan.dtype),
            pltpu.VMEM(receivers.shape, receivers.dtype),
            pltpu.VMEM(pair_index.shape, pair_index.dtype),
            pltpu.VMEM(keep.shape, keep.dtype),
            pltpu.SemaphoreType.DMA((CHAINS + 4,)),
        ],
        compiler_params=params(VMEM_BYTES // 2),
        name="pack",
    )(*[in_hbm(a) for a in (plan, sources, receivers, pair_index, keep)])


def choose_kernel(which, offsets, number_ref, *refs):
    out_ref, sems = refs[-2:]
    rows = out_ref.shape[0] // CHAINS
    where = number_ref[which]
    waits = []
    for chain in range(CHAINS):
        target = out_ref.at[pl.ds(chain * rows, rows)]
        for place, offset in enumerate(offsets):
            copy = pltpu.make_async_copy(refs[chain * len(offsets) + place], target, sems.at[chain])

            @pl.when(where == offset)
            def _():
                copy.start()

        waits.append(copy)
    for copy in waits:
        copy.wait()


def choose(numbers, which, arrived, offsets):
    pieces = [there[offset] for there in arrived for offset in offsets]
    rows, samples = pieces[0].shape
    any_spec = pl.BlockSpec(memory_space=pl.ANY)
    return pl.pallas_call(
        functools.partial(choose_kernel, which, offsets),
        in_specs=[pl.BlockSpec(memory_space=pltpu.SMEM)] + [any_spec] * len(pieces),
        out_specs=pl.BlockSpec(memory_space=pltpu.VMEM),
        out_shape=jax.ShapeDtypeStruct((rows * CHAINS, samples), BF16),
        scratch_shapes=[pltpu.SemaphoreType.DMA((CHAINS,))],
        compiler_params=params(VMEM_BYTES // 4),
        name="choose",
    )(numbers, *pieces)


def column(row):
    return jnp.broadcast_to(row, (SHIFT_ROWS, row.shape[1])).T[:, :1]


def ones_where(condition):
    return jnp.where(condition, 1.0, 0.0).astype(BF16)


def index_kernel(r_dev, n_win, samples, cap, tile, block_rows, number_ref, parcel_ref, pick_ref, place_ref, pass_ref,
                 count_ref, more_pick_ref, more_place_ref, pick_scratch, place_scratch):
    nearer, offset = number_ref[0], number_ref[1]
    slots = 2 * r_dev * tile
    part = 2 * cap // r_dev
    beside = parcel_ref.shape[2] - samples
    below = lax.broadcasted_iota(jnp.int32, (cap, cap), 0) < lax.broadcasted_iota(jnp.int32, (cap, cap), 1)
    below = ones_where(below)
    later = []
    for place in range(pick_ref.shape[0]):
        group = pl.program_id(0) * pick_ref.shape[0] + place
        digits = parcel_ref[place * n_win, :, pl.ds(samples, beside)].astype(F32)
        digits = jnp.concatenate([digits[i : i + 1, :part] for i in range(r_dev)], axis=1).astype(jnp.int32)
        packed = digits[:, :cap] * DIGIT + digits[:, cap:]
        pairs, kept = packed // 2, packed % 2 == 1
        source_row, receiver = pairs // r_dev, pairs % r_dev
        turn = jnp.where(source_row // block_rows == nearer, 0, 1)
        row = (source_row + offset) % block_rows
        segment = jnp.where(kept, turn * r_dev + receiver, -1)
        member = lax.broadcasted_iota(jnp.int32, (2 * r_dev, cap), 0) == segment
        earlier = jnp.dot(ones_where(member), below, preferred_element_type=F32)
        rank = jnp.sum(jnp.where(member, earlier, 0.0), axis=0, keepdims=True).astype(jnp.int32)
        code = (rank // tile) * slots + (turn * r_dev + receiver) * tile + rank % tile
        code = jnp.where(kept, code, -1)
        counts = jnp.sum(jnp.where(member, 1.0, 0.0), axis=1, keepdims=True)
        which = lax.broadcasted_iota(jnp.int32, counts.shape, 0) % r_dev
        passes = 0
        for r in range(r_dev):
            count = jnp.max(jnp.where(which == r, counts, 0.0)).astype(jnp.int32)
            count_ref[group * r_dev + r] = count
            passes = jnp.maximum(passes, (count + tile - 1) // tile)
        pass_ref[group] = passes
        code_column = column(code.astype(F32)).astype(jnp.int32)
        row_column = column(row.astype(F32)).astype(jnp.int32)

        def matrices(number, code=code, code_column=code_column, row_column=row_column):
            start = number * slots
            row_ones = ones_where(row_column == lax.broadcasted_iota(jnp.int32, (cap, block_rows), 1))
            by_slot = ones_where(lax.broadcasted_iota(jnp.int32, (slots, cap), 0) + start == code)
            pick = jnp.dot(by_slot, row_ones, preferred_element_type=F32).astype(BF16)
            return pick, ones_where(lax.broadcasted_iota(jnp.int32, (cap, slots), 1) + start == code_column)

        pick_ref[place], place_ref[place] = matrices(0)
        later.append((group, passes, matrices))

    for group, passes, matrices in later:

        @pl.when(passes > 1)
        def _():
            def one_pass(number, carry):
                pick_scratch[...], place_scratch[...] = matrices(number)
                pltpu.sync_copy(pick_scratch, more_pick_ref.at[group, number - 1])
                pltpu.sync_copy(place_scratch, more_place_ref.at[group, number - 1])
                return carry

            lax.fori_loop(1, passes, one_pass, 0)


def index(parcels, numbers, n_win, samples, r_dev, cap, tile, block_rows):
    groups = parcels.shape[0] // n_win
    at_once = math.gcd(groups, 4)
    slots = 2 * r_dev * tile
    more = max(1, -(-min(block_rows, cap) // tile) - 1)
    return pl.pallas_call(
        functools.partial(index_kernel, r_dev, n_win, samples, cap, tile, block_rows),
        grid_spec=pltpu.PrefetchScalarGridSpec(
            num_scalar_prefetch=1,
            grid=(groups // at_once,),
            in_specs=[pl.BlockSpec((at_once * n_win,) + parcels.shape[1:], lambda i, *_: (i, 0, 0))],
            out_specs=[
                pl.BlockSpec((at_once, slots, block_rows), lambda i, *_: (i, 0, 0)),
                pl.BlockSpec((at_once, cap, slots), lambda i, *_: (i, 0, 0)),
                pl.BlockSpec(memory_space=pltpu.SMEM),
                pl.BlockSpec(memory_space=pltpu.SMEM),
                pl.BlockSpec(memory_space=pl.ANY),
                pl.BlockSpec(memory_space=pl.ANY),
            ],
            scratch_shapes=[pltpu.VMEM((slots, block_rows), BF16), pltpu.VMEM((cap, slots), BF16)],
        ),
        out_shape=[
            jax.ShapeDtypeStruct((groups, slots, block_rows), BF16),
            jax.ShapeDtypeStruct((groups, cap, slots), BF16),
            jax.ShapeDtypeStruct((groups,), jnp.int32),
            jax.ShapeDtypeStruct((groups * r_dev,), jnp.int32),
            pltpu.HBM((groups, more, slots, block_rows), BF16),
            pltpu.HBM((groups, more, cap, slots), BF16),
        ],
        compiler_params=params(VMEM_BYTES),
        name="index",
    )(numbers, parcels)


def lay_out(parcel_ref, signal_ref, samples):
    n_win, r_dev, _ = parcel_ref.shape
    for w in range(n_win):
        signal_ref[:r_dev, w * samples : (w + 1) * samples] = parcel_ref[w, :, :samples].astype(F32)
    tail = signal_ref.shape[1] - n_win * samples
    signal_ref[:r_dev, n_win * samples :] = jnp.zeros((r_dev, tail), F32)


def hankel_rows(signal_ref, r, begin, width, out_ref, place):
    length = width + LANES
    signal = signal_ref[r : r + 1, pl.ds(pl.multiple_of(begin, LANES), length)]
    base = jnp.broadcast_to(signal, (SHIFT_ROWS, length))
    sublane = lax.broadcasted_iota(jnp.int32, base.shape, 0)
    for bit in (1, 2, 4):
        base = jnp.where(sublane & bit != 0, pltpu.roll(base, length - bit, 1), base)
    for first in range(0, LANES, 2 * SHIFT_ROWS):
        both = []
        for shift in (first, first + SHIFT_ROWS):
            rolled = pltpu.roll(base, length - shift, 1) if shift else base
            both.append(rolled[:, :width])
        out_ref[place, first : first + 2 * SHIFT_ROWS, :] = jnp.concatenate(both, axis=0).astype(BF16)


def hankel_kernel(v, samples, number_ref, parcel_ref, out_ref, signal_ref):
    lay_out(parcel_ref, signal_ref, samples)
    r_dev = parcel_ref.shape[1]
    for r in range(r_dev):
        hankel_rows(signal_ref, r, number_ref[4 + v], out_ref.shape[2], out_ref, pl.program_id(0) * r_dev + r)


def build_hankel(parcels, numbers, v, n_win, samples, width):
    groups, r_dev = parcels.shape[0] // n_win, parcels.shape[1]
    shape = (groups * r_dev, LANES, width)
    return pl.pallas_call(
        functools.partial(hankel_kernel, v, samples),
        grid_spec=pltpu.PrefetchScalarGridSpec(
            num_scalar_prefetch=1,
            grid=(groups,),
            in_specs=[pl.BlockSpec((n_win,) + parcels.shape[1:], lambda i, *_: (i, 0, 0))],
            out_specs=pl.BlockSpec(memory_space=pltpu.VMEM),
            scratch_shapes=[pltpu.VMEM((SHIFT_ROWS, n_win * samples + LAGS), F32)],
        ),
        out_shape=jax.ShapeDtypeStruct(shape, BF16),
        cost_estimate=pl.CostEstimate(
            flops=math.prod(shape), bytes_accessed=2 * math.prod(shape), transcendentals=0
        ),
        compiler_params=params(VMEM_BYTES // 2),
        name="hankel",
    )(numbers, parcels)


def pick_rows(pieces, pick, gathered):
    parts = len(pieces) // 2
    count, samples = gathered.shape[1:]
    for q in range(2):
        block_pieces = pieces[q * parts : (q + 1) * parts]
        ones = pick[q * count : (q + 1) * count, :]
        for t in range(0, samples, STEP):
            block = jnp.concatenate([piece[:, t : t + STEP] for piece in block_pieces], axis=0)
            gathered[q, :, t : t + STEP] = jnp.dot(ones, block, preferred_element_type=F32).astype(BF16)


def multiply(gathered, hankel_ref, place, r, tile, lag):
    samples = gathered.shape[2]
    chosen = jnp.concatenate([gathered[q, r * tile : (r + 1) * tile, :] for q in range(2)], axis=0)
    wide = jnp.concatenate(
        [hankel_ref[place, :, t + lag : t + lag + STEP] for t in range(0, samples, LANES)], axis=0
    )
    return jnp.dot(chosen, wide, preferred_element_type=F32)


def split(total, high, low, slots, lags):
    upper = total.astype(BF16)
    high[slots, lags] = upper
    low[slots, lags] = (total - upper.astype(F32)).astype(BF16)


def placed(place, high, low):
    return jnp.dot(place, high[...], preferred_element_type=F32) + jnp.dot(
        place, low[...], preferred_element_type=F32
    )


def correlate_kernel(parts, v, tile, norming, prebuilt, first, last, pass_ref, count_ref, number_ref, *refs):
    refs = list(refs)
    pieces = [refs.pop(0) for _ in range(2 * parts)]
    signal_ref, pick_ref, place_ref, more_pick_ref, more_place_ref = [refs.pop(0) for _ in range(5)]
    if not first:
        sums_ref, extra_ref = refs.pop(0), refs.pop(0)
    if last:
        out_ref = refs.pop(0)
    else:
        handed_ref, left_ref = refs.pop(0), refs.pop(0)
    gathered, high, low, extra, pick_scratch, place_scratch = refs[:6]
    r_dev = gathered.shape[1] // tile
    samples = pieces[0].shape[1]
    lag_dev = extra.shape[1]
    group = pl.program_id(0)

    if prebuilt:
        hankel_ref, hankel_place = signal_ref, group * r_dev
    else:
        hankel_place = 0
        hankel_ref, row_ref = refs[6:]
        lay_out(signal_ref, row_ref, samples)
        for r in range(r_dev):
            hankel_rows(row_ref, r, number_ref[4 + v], hankel_ref.shape[2], hankel_ref, r)

    pick_rows(pieces, pick_ref.at[0], gathered)
    for r in range(r_dev):
        for lag in range(0, lag_dev, STEP):
            lags = slice(lag, lag + STEP)
            both = multiply(gathered, hankel_ref, hankel_place + r, r, tile, lag)
            for q in range(2):
                total = both[q * tile : (q + 1) * tile]
                slots = slice((q * r_dev + r) * tile, (q * r_dev + r + 1) * tile)
                if not first:
                    total += sums_ref[group, slots, lags]
                if last:
                    split(total * norming, high, low, slots, lags)
                else:
                    handed_ref[group, slots, lags] = total
    if last:
        out_ref[0] = placed(place_ref[0], high, low)

    @pl.when(pass_ref[group] > 1)
    def _():
        if first:
            extra[...] = jnp.zeros(extra.shape, F32)
        else:
            pltpu.sync_copy(extra_ref.at[group], extra)

        def one_pass(number, carry):
            pltpu.sync_copy(more_pick_ref.at[group, number - 1], pick_scratch)
            pltpu.sync_copy(more_place_ref.at[group, number - 1], place_scratch)
            pick_rows(pieces, pick_scratch, gathered)
            for r in range(r_dev):
                needed = count_ref[group * r_dev + r] > number * tile
                places = [slice((q * r_dev + r) * tile, (q * r_dev + r + 1) * tile) for q in range(2)]

                @pl.when(needed)
                def _():
                    for lag in range(0, lag_dev, STEP):
                        both = multiply(gathered, hankel_ref, hankel_place + r, r, tile, lag) * norming
                        for q, slots in enumerate(places):
                            split(both[q * tile : (q + 1) * tile], high, low, slots, slice(lag, lag + STEP))

                @pl.when(jnp.logical_not(needed))
                def _():
                    for slots in places:
                        high[slots, :] = jnp.zeros((tile, lag_dev), BF16)
                        low[slots, :] = jnp.zeros((tile, lag_dev), BF16)

            extra[...] += placed(place_scratch[...], high, low)
            return carry

        lax.fori_loop(1, pass_ref[group], one_pass, 0)
        if last:
            out_ref[0] += extra[...]
        else:
            pltpu.sync_copy(extra, left_ref.at[group])


def correlate(pieces, signal, prebuilt, numbers, v, matrices, before, last, tile, norming, lag_dev, n_win, r_dev):
    pick, place, passes, counts, more_pick, more_place = matrices
    parts = len(pieces) // 2
    groups, cap, slots = place.shape
    part_rows, samples = pieces[0].shape
    width = samples - LANES + lag_dev
    by_group = lambda shape: pl.BlockSpec(shape, lambda i, *_: (i, 0, 0))
    any_spec = pl.BlockSpec(memory_space=pl.ANY)
    whole_spec = pl.BlockSpec(memory_space=pltpu.VMEM)
    sums_shape = jax.ShapeDtypeStruct((groups, slots, lag_dev), F32)
    out_shape = jax.ShapeDtypeStruct((groups, cap, lag_dev), F32)
    in_specs = [whole_spec] * len(pieces)
    in_specs.append(whole_spec if prebuilt else by_group((n_win,) + signal.shape[1:]))
    in_specs += [by_group((1,) + pick.shape[1:]), by_group((1,) + place.shape[1:]), any_spec, any_spec]
    args = pieces + [signal, pick, place, in_hbm(more_pick), in_hbm(more_place)]
    if before is not None:
        in_specs += [whole_spec, any_spec]
        args += [before[0], in_hbm(before[1])]
    scratch = [
        pltpu.VMEM((2, r_dev * tile, samples), BF16),
        pltpu.VMEM((slots, lag_dev), BF16),
        pltpu.VMEM((slots, lag_dev), BF16),
        pltpu.VMEM((cap, lag_dev), F32),
        pltpu.VMEM(pick.shape[1:], BF16),
        pltpu.VMEM(place.shape[1:], BF16),
    ]
    if not prebuilt:
        scratch.append(pltpu.VMEM((r_dev, LANES, width), BF16))
        scratch.append(pltpu.VMEM((SHIFT_ROWS, n_win * samples + LAGS), F32))
    body = functools.partial(correlate_kernel, parts, v, tile, norming, prebuilt, before is None, last)
    return pl.pallas_call(
        body,
        grid_spec=pltpu.PrefetchScalarGridSpec(
            num_scalar_prefetch=3,
            grid=(groups,),
            in_specs=in_specs,
            out_specs=by_group((1, cap, lag_dev)) if last else [whole_spec, any_spec],
            scratch_shapes=scratch,
        ),
        out_shape=out_shape if last else [sums_shape, pltpu.HBM(out_shape.shape, F32)],
        cost_estimate=pl.CostEstimate(
            flops=4 * groups * r_dev * tile * samples * (lag_dev + parts * part_rows),
            bytes_accessed=signal.size * signal.dtype.itemsize + 2 * groups * cap * lag_dev * 4,
            transcendentals=0,
        ),
        compiler_params=params(VMEM_BYTES if prebuilt else 2 * VMEM_BYTES),
        name="correlate",
    )(passes, counts, numbers, *args)


def shards(sources, receivers, plan, pair_index, keep):
    _, block_rows, samples = sources.shape
    r_dev = receivers.shape[0]
    n_chan = lax.axis_size("chan")
    n_win = lax.axis_size("win")
    n_rep = lax.axis_size("rep")
    cap = pair_index.shape[3]
    lag_dev = LAGS // (n_win * n_rep)
    tile = max(16, cap // 8)
    norming = 1.0 / math.sqrt(samples * n_win)
    width = samples - LANES + lag_dev
    prebuilt = n_chan * r_dev * n_win * LANES * width * 2 <= HANKEL_BYTES

    parcels, numbers, *owns = pack(
        plan, sources[0], receivers, pair_index[0, 0], keep[0, 0], n_rep, lag_dev, n_chan, n_win
    )
    parcels = lax.all_to_all(parcels, ("chan", "win"), split_axis=0, concat_axis=0, tiled=True)

    arrived = [{0: own} for own in owns]

    def relay(step):
        for there in arrived:
            there[step] = swapped(there[1 - step], "chan", 0)
            if step < n_chan - 1:
                there[-step] = swapped(there[step - 1], "chan", 1)

    def after_arrival(step, value):
        for there in arrived:
            for key in (step, -step):
                if key in there:
                    value, there[key] = lax.optimization_barrier((value, there[key]))
        return value

    def before_start(step, value):
        for there in arrived:
            for key in (1 - step, step - 1):
                value, there[key] = lax.optimization_barrier((value, there[key]))
        return value

    def halves(piece):
        return [piece] + [turned(piece, "rep", -u) for u in range(1, n_rep)]

    def spans(piece):
        return [piece] + [turned(piece, "win", v) for v in range(1, n_win)]

    signals = [parcels] * n_win
    relay(1)
    parcels = after_arrival(1, parcels)
    relay(2)
    matrices = index(parcels, numbers, n_win, samples, r_dev, cap, tile, block_rows)
    if prebuilt:
        signals[0] = build_hankel(parcels, numbers, 0, n_win, samples, width)
    matrices, signals[0] = before_start(3, (matrices, signals[0]))
    reach = range(-(n_chan - 2), n_chan - 1)
    near = choose(numbers, 2, arrived, [offset for offset in reach if offset in arrived[0]])
    if prebuilt:
        parcels = after_arrival(2, parcels)
        parcels, near = lax.optimization_barrier((parcels, near))
        for v in range(1, n_win):
            signals[v] = build_hankel(parcels, numbers, v, n_win, samples, width)
    for step in range(3, n_chan):
        relay(step)
    near_halves = [halves(piece) for piece in spans(near)]
    if prebuilt:
        signals = after_arrival(n_chan - 1, signals)
    far_spans = spans(choose(numbers, 3, arrived, sorted(arrived[0])))

    result = None
    for v in range(n_win):
        if v:
            far_spans, result = lax.optimization_barrier((far_spans, result))
        result = correlate(
            near_halves[v] + halves(far_spans[v]), signals[v], prebuilt, numbers, v, matrices, result, v == n_win - 1,
            tile, norming, lag_dev, n_win, r_dev,
        )
    return result[None, None]


def solution(mesh):
    placed_at = (
        P(("grp", "chan"), None, "win"),
        P(("grp", "chan"), "win"),
        P("grp", None),
        P("grp", "chan", None, None),
        P("grp", "chan", None, None),
    )
    return jax.shard_map(
        shards,
        mesh=mesh,
        in_specs=placed_at,
        out_specs=P(("grp", "chan"), None, None, None, ("win", "rep")),
        check_vma=False,
    )
```

```python
import functools
import math

import jax
import jax.numpy as jnp
from jax import lax
from jax.experimental import pallas as pl
from jax.experimental.pallas import tpu as pltpu
from jax.sharding import PartitionSpec as P

LAGS = 2048
LANES = 128
SHIFT_ROWS = 8
STEP = 2 * LANES
CHAINS = 1
SPARE = 16
DIGIT = 64
HANKEL_BYTES = 24 * 2**20
VMEM_BYTES = 26 * 2**20
F32 = jnp.float32
BF16 = jnp.bfloat16


def swapped(block, axis, first):
    size = lax.axis_size(axis)
    route = []
    for i in range(first, size - 1, 2):
        route += [(i, i + 1), (i + 1, i)]
    return lax.ppermute(block, axis, route)


def turned(block, axis, distance):
    size = lax.axis_size(axis)
    return lax.ppermute(block, axis, [(i, (i + distance) % size) for i in range(size)])


def turned_both(block, chan_distance, win_distance):
    n_chan, n_win = lax.axis_size("chan"), lax.axis_size("win")
    route = []
    for c in range(n_chan):
        for w in range(n_win):
            there = (c + chan_distance) % n_chan * n_win + (w + win_distance) % n_win
            route.append((c * n_win + w, there))
    return lax.ppermute(block, ("chan", "win"), route)


def in_hbm(array):
    return pltpu.with_memory_space_constraint(array, pltpu.HBM)


def params(vmem):
    return pltpu.CompilerParams(vmem_limit_bytes=vmem)


def pack_kernel(halves, lags, block_rows, plan_hbm, receiver_hbm, pair_hbm, keep_hbm, *refs):
    plan_ref, receiver_ref, pair_ref, keep_ref, digit_ref, sems = refs[-6:]
    parcel_refs, number_ref = refs[:-7], refs[-7]
    small = []
    for place, (source, target) in enumerate(
        ((plan_hbm, plan_ref), (receiver_hbm, receiver_ref), (pair_hbm, pair_ref), (keep_hbm, keep_ref))
    ):
        small.append(pltpu.make_async_copy(source, target, sems.at[place]))
        small[-1].start()
    r_dev, samples = receiver_ref.shape
    n_chan, cap = pair_ref.shape
    n_win = lax.axis_size("win")
    chan, win, rep = lax.axis_index("chan"), lax.axis_index("win"), lax.axis_index("rep")
    for copy in small:
        copy.wait()

    packed = pair_ref[...] * 2 + keep_ref[...]
    digit_ref[:n_chan, :] = jnp.concatenate([packed // DIGIT, packed % DIGIT], axis=1).astype(F32)
    heard = receiver_ref[...].astype(F32)
    part = 2 * cap // r_dev
    spare = parcel_refs[0].shape[1] - samples - part
    for distance, parcel_ref in enumerate(parcel_refs):
        digits = digit_ref[pl.ds(lax.rem(chan + distance, n_chan), 1), :]
        lists = [digits[:, i * part : (i + 1) * part] for i in range(r_dev)]
        parcel = [heard, jnp.concatenate(lists, axis=0)]
        if spare:
            parcel.append(jnp.zeros((r_dev, spare), F32))
        parcel_ref[...] = jnp.concatenate(parcel, axis=1).astype(BF16)

    one, two = plan_ref[0, 0], plan_ref[0, 1]
    nearer = jnp.where(jnp.abs(one - chan) <= jnp.abs(two - chan), 0, 1)
    sign = jnp.where(chan % 2 == 0, 1, -1)
    number_ref[0] = nearer
    number_ref[1] = block_rows - rep * (block_rows // halves)
    number_ref[2] = sign * (jnp.where(nearer == 0, one, two) - chan)
    number_ref[3] = sign * (jnp.where(nearer == 0, two, one) - chan)
    number_ref[4] = chan
    number_ref[5] = (win * halves + rep) * lags
    number_ref[6] = win


def pack(plan, receivers, pair_index, keep, halves, lags, block_rows, n_chan):
    r_dev, samples = receivers.shape
    cap = pair_index.shape[1]
    beside = -(-2 * cap // r_dev // LANES) * LANES
    vmem, smem = pl.BlockSpec(memory_space=pltpu.VMEM), pl.BlockSpec(memory_space=pltpu.SMEM)
    shapes = [jax.ShapeDtypeStruct((r_dev, samples + beside), BF16)] * n_chan
    shapes.append(jax.ShapeDtypeStruct((7,), jnp.int32))
    *parcels, numbers = pl.pallas_call(
        functools.partial(pack_kernel, halves, lags, block_rows),
        in_specs=[pl.BlockSpec(memory_space=pl.ANY)] * 4,
        out_specs=[vmem] * n_chan + [smem],
        out_shape=shapes,
        scratch_shapes=[
            pltpu.SMEM(plan.shape, plan.dtype),
            pltpu.VMEM(receivers.shape, receivers.dtype),
            pltpu.VMEM(pair_index.shape, pair_index.dtype),
            pltpu.VMEM(keep.shape, keep.dtype),
            pltpu.VMEM((-(-n_chan // SHIFT_ROWS) * SHIFT_ROWS, 2 * cap), F32),
            pltpu.SemaphoreType.DMA((4,)),
        ],
        compiler_params=params(VMEM_BYTES // 2),
        name="pack",
    )(*[in_hbm(a) for a in (plan, receivers, pair_index, keep)])
    return parcels, numbers


def own_kernel(number_ref, source_ref, *refs):
    chain_refs, sems = refs[:-1], refs[-1]
    rows = chain_refs[0].shape[0]
    copies = []
    for chain, chain_ref in enumerate(chain_refs):
        start = pl.multiple_of(source_ref.shape[0] - number_ref[1] + chain * rows, rows)
        copies.append(pltpu.make_async_copy(source_ref.at[pl.ds(start, rows)], chain_ref, sems.at[chain]))
        copies[-1].start()
    for copy in copies:
        copy.wait()


def own_rows(numbers, sources, halves):
    block_rows, samples = sources.shape
    shape = jax.ShapeDtypeStruct((block_rows // halves // CHAINS, samples), BF16)
    return pl.pallas_call(
        own_kernel,
        in_specs=[pl.BlockSpec(memory_space=pltpu.SMEM), pl.BlockSpec(memory_space=pl.ANY)],
        out_specs=[pl.BlockSpec(memory_space=pltpu.VMEM)] * CHAINS,
        out_shape=[shape] * CHAINS,
        scratch_shapes=[pltpu.SemaphoreType.DMA((CHAINS,))],
        compiler_params=params(VMEM_BYTES // 4),
        name="own_rows",
    )(numbers, in_hbm(sources))


def choose_kernel(which, offsets, number_ref, *refs):
    out_ref, sems = refs[-2:]
    rows = out_ref.shape[0] // CHAINS
    where = number_ref[which]
    waits = []
    for chain in range(CHAINS):
        target = out_ref.at[pl.ds(chain * rows, rows)]
        for place, offset in enumerate(offsets):
            copy = pltpu.make_async_copy(refs[chain * len(offsets) + place], target, sems.at[chain])

            @pl.when(where == offset)
            def _():
                copy.start()

        waits.append(copy)
    for copy in waits:
        copy.wait()


def choose(numbers, which, arrived, offsets):
    pieces = [there[offset] for there in arrived for offset in offsets]
    rows, samples = pieces[0].shape
    any_spec = pl.BlockSpec(memory_space=pl.ANY)
    return pl.pallas_call(
        functools.partial(choose_kernel, which, offsets),
        in_specs=[pl.BlockSpec(memory_space=pltpu.SMEM)] + [any_spec] * len(pieces),
        out_specs=pl.BlockSpec(memory_space=pltpu.VMEM),
        out_shape=jax.ShapeDtypeStruct((rows * CHAINS, samples), BF16),
        scratch_shapes=[pltpu.SemaphoreType.DMA((CHAINS,))],
        compiler_params=params(VMEM_BYTES // 4),
        name="choose",
    )(numbers, *pieces)


def column(row):
    return jnp.broadcast_to(row, (SHIFT_ROWS, row.shape[1])).T[:, :1]


def ones_where(condition):
    return jnp.where(condition, 1.0, 0.0).astype(BF16)


def index_kernel(r_dev, samples, cap, tile, block_rows, number_ref, *refs):
    pick_ref, place_ref, pass_ref, count_ref, more_pick_ref, more_place_ref, pick_scratch, place_scratch = refs[-8:]
    parcel_refs = refs[:-8]
    nearer, offset = number_ref[0], number_ref[1]
    slots = 2 * r_dev * tile
    window = tile + SPARE
    part = 2 * cap // r_dev
    below = lax.broadcasted_iota(jnp.int32, (cap, cap), 0) < lax.broadcasted_iota(jnp.int32, (cap, cap), 1)
    below = ones_where(below)
    later = []
    for group, parcel_ref in enumerate(parcel_refs):
        digits = parcel_ref[:, samples:].astype(F32)
        digits = jnp.concatenate([digits[i : i + 1, :part] for i in range(r_dev)], axis=1).astype(jnp.int32)
        packed = digits[:, :cap] * DIGIT + digits[:, cap:]
        pairs, kept = packed // 2, packed % 2 == 1
        source_row, receiver = pairs // r_dev, pairs % r_dev
        turn = jnp.where(source_row // block_rows == nearer, 0, 1)
        row = (source_row + offset) % block_rows
        segment = jnp.where(kept, turn * r_dev + receiver, -1)
        member = lax.broadcasted_iota(jnp.int32, (2 * r_dev, cap), 0) == segment
        earlier = jnp.dot(ones_where(member), below, preferred_element_type=F32)
        of_pair = lambda values: jnp.sum(jnp.where(member, values, 0.0), axis=0, keepdims=True).astype(jnp.int32)
        counts = jnp.sum(jnp.where(member, 1.0, 0.0), axis=1, keepdims=True)
        from_top = jnp.minimum(counts[:r_dev], window)
        from_bottom = jnp.minimum(jnp.minimum(counts[r_dev:], 2.0 * tile - from_top), window)
        first_pass = jnp.concatenate([from_top, from_bottom], axis=0)
        first_slot = jnp.concatenate([jnp.zeros_like(from_top), 2.0 * tile - from_bottom], axis=0)
        rank, limit, begin = of_pair(earlier), of_pair(first_pass), of_pair(first_slot)
        rest = rank - limit
        code = jnp.where(rest < 0, begin + rank, (1 + rest // tile) * slots + turn * tile + rest % tile)
        code = jnp.where(kept, code + receiver * 2 * tile, -1)
        left = counts - first_pass
        which = lax.broadcasted_iota(jnp.int32, left.shape, 0) % r_dev
        passes = 1
        for r in range(r_dev):
            count = jnp.max(jnp.where(which == r, left, 0.0)).astype(jnp.int32)
            count_ref[group * r_dev + r] = count
            passes = jnp.maximum(passes, 1 + (count + tile - 1) // tile)
        pass_ref[group] = passes
        code_column = column(code.astype(F32)).astype(jnp.int32)
        row_column = column(row.astype(F32)).astype(jnp.int32)

        def matrices(number, code=code, turn=turn, code_column=code_column, row_column=row_column):
            start = number * slots
            row_ones = ones_where(row_column == lax.broadcasted_iota(jnp.int32, (cap, block_rows), 1))
            line = lax.broadcasted_iota(jnp.int32, (r_dev * window, 1), 0)
            slot = line // window * (2 * tile) + line % window + start
            of_block = [jnp.where(turn == q, code - q * (2 * tile - window), -1) for q in range(2)]
            by_slot = jnp.concatenate([ones_where(slot == codes) for codes in of_block], axis=0)
            pick = jnp.dot(by_slot, row_ones, preferred_element_type=F32).astype(BF16)
            return pick, ones_where(lax.broadcasted_iota(jnp.int32, (cap, slots), 1) + start == code_column)

        pick_ref[group], place_ref[group] = matrices(0)
        later.append((group, passes, matrices))

    for group, passes, matrices in later:

        @pl.when(passes > 1)
        def _():
            def one_pass(number, carry):
                pick_scratch[...], place_scratch[...] = matrices(number)
                pltpu.sync_copy(pick_scratch, more_pick_ref.at[group, number - 1])
                pltpu.sync_copy(place_scratch, more_place_ref.at[group, number - 1])
                return carry

            lax.fori_loop(1, passes, one_pass, 0)


def index(parcels, numbers, samples, r_dev, cap, tile, block_rows):
    groups = len(parcels)
    slots = 2 * r_dev * tile
    lines = 2 * r_dev * (tile + SPARE)
    more = -(-(min(block_rows, cap) - (tile - SPARE)) // tile)
    vmem, smem = pl.BlockSpec(memory_space=pltpu.VMEM), pl.BlockSpec(memory_space=pltpu.SMEM)
    any_spec = pl.BlockSpec(memory_space=pl.ANY)
    return pl.pallas_call(
        functools.partial(index_kernel, r_dev, samples, cap, tile, block_rows),
        in_specs=[smem] + [vmem] * groups,
        out_specs=[vmem, vmem, smem, smem, any_spec, any_spec],
        out_shape=[
            jax.ShapeDtypeStruct((groups, lines, block_rows), BF16),
            jax.ShapeDtypeStruct((groups, cap, slots), BF16),
            jax.ShapeDtypeStruct((groups,), jnp.int32),
            jax.ShapeDtypeStruct((groups * r_dev,), jnp.int32),
            pltpu.HBM((groups, more, lines, block_rows), BF16),
            pltpu.HBM((groups, more, cap, slots), BF16),
        ],
        scratch_shapes=[pltpu.VMEM((lines, block_rows), BF16), pltpu.VMEM((cap, slots), BF16)],
        compiler_params=params(VMEM_BYTES),
        name="index",
    )(numbers, *parcels)


def lay_out(heard, number_ref, signal_ref):
    n_win = len(heard)
    r_dev, samples = heard[0].shape
    for distance, span in enumerate(heard):
        begin = lax.rem(number_ref[6] + n_win - distance, n_win) * samples
        signal_ref[:r_dev, pl.ds(pl.multiple_of(begin, LANES), samples)] = span.astype(F32)
    tail = signal_ref.shape[1] - n_win * samples
    signal_ref[:r_dev, n_win * samples :] = jnp.zeros((r_dev, tail), F32)


def first_sample(number_ref, v, n_win, samples):
    return lax.rem(number_ref[6] + n_win - v, n_win) * samples + number_ref[5]


def hankel_rows(signal_ref, r, begin, width, out_ref, place):
    length = width + LANES
    signal = signal_ref[r : r + 1, pl.ds(pl.multiple_of(begin, LANES), length)]
    base = jnp.broadcast_to(signal, (SHIFT_ROWS, length))
    sublane = lax.broadcasted_iota(jnp.int32, base.shape, 0)
    for bit in (1, 2, 4):
        base = jnp.where(sublane & bit != 0, pltpu.roll(base, length - bit, 1), base)
    for first in range(0, LANES, 2 * SHIFT_ROWS):
        both = []
        for shift in (first, first + SHIFT_ROWS):
            rolled = pltpu.roll(base, length - shift, 1) if shift else base
            both.append(rolled[:, :width])
        out_ref[place, first : first + 2 * SHIFT_ROWS, :] = jnp.concatenate(both, axis=0).astype(BF16)


def hankel_kernel(v, n_win, samples, number_ref, *refs):
    out_ref, signal_refs = refs[-2:]
    heard_refs = refs[:-2]
    r_dev = heard_refs[0].shape[0]
    begin = first_sample(number_ref, v, n_win, samples)
    for group in range(len(heard_refs) // n_win):
        signal_ref = signal_refs.at[group % 2]
        heard = [ref[:, :samples] for ref in heard_refs[group * n_win : (group + 1) * n_win]]
        lay_out(heard, number_ref, signal_ref)
        for r in range(r_dev):
            hankel_rows(signal_ref, r, begin, out_ref.shape[2], out_ref, group * r_dev + r)


def build_hankel(heard, numbers, v, samples, width):
    groups, n_win, r_dev = len(heard), len(heard[0]), heard[0][0].shape[0]
    shape = (groups * r_dev, LANES, width)
    vmem = pl.BlockSpec(memory_space=pltpu.VMEM)
    return pl.pallas_call(
        functools.partial(hankel_kernel, v, n_win, samples),
        in_specs=[pl.BlockSpec(memory_space=pltpu.SMEM)] + [vmem] * (groups * n_win),
        out_specs=vmem,
        scratch_shapes=[pltpu.VMEM((2, SHIFT_ROWS, n_win * samples + LAGS), F32)],
        out_shape=jax.ShapeDtypeStruct(shape, BF16),
        cost_estimate=pl.CostEstimate(
            flops=math.prod(shape), bytes_accessed=2 * math.prod(shape), transcendentals=0
        ),
        compiler_params=params(VMEM_BYTES // 2),
        name="hankel",
    )(numbers, *[span for spans in heard for span in spans])


def pick_rows(pieces, pick, gathered, tile):
    parts = len(pieces) // 2
    window = tile + SPARE
    shared = tile - SPARE
    r_dev, samples = gathered.shape[0] // (2 * tile), gathered.shape[1]
    for t in range(0, samples, STEP):
        chosen = []
        for q in range(2):
            block = jnp.concatenate([piece[:, t : t + STEP] for piece in pieces[q * parts : (q + 1) * parts]], axis=0)
            ones = pick[q * r_dev * window : (q + 1) * r_dev * window, :]
            chosen.append(jnp.dot(ones, block, preferred_element_type=F32))
        for r in range(r_dev):
            top, bottom = [rows[r * window : (r + 1) * window] for rows in chosen]
            rows = [top[shared:] + bottom[: window - shared]]
            if shared:
                rows = [top[:shared]] + rows + [bottom[window - shared :]]
            for place, part in zip((0, shared, window) if shared else (0,), rows):
                start = r * 2 * tile + place
                gathered[start : start + part.shape[0], t : t + STEP] = part.astype(BF16)


def multiply(gathered, hankel_ref, place, r, tile, lag):
    samples = gathered.shape[1]
    wide = jnp.concatenate(
        [hankel_ref[place, :, t + lag : t + lag + STEP] for t in range(0, samples, LANES)], axis=0
    )
    return jnp.dot(gathered[r * 2 * tile : (r + 1) * 2 * tile, :], wide, preferred_element_type=F32)


def split(total, high, low, slots, lags):
    upper = total.astype(BF16)
    high[slots, lags] = upper
    low[slots, lags] = (total - upper.astype(F32)).astype(BF16)


def placed(place, high, low):
    return jnp.dot(place, high[...], preferred_element_type=F32) + jnp.dot(
        place, low[...], preferred_element_type=F32
    )


def correlate_kernel(parts, v, tile, norming, prebuilt, first, last, pass_ref, count_ref, number_ref, *refs):
    refs = list(refs)
    pieces = [refs.pop(0) for _ in range(2 * parts)]
    signal_ref, pick_ref, place_ref, more_pick_ref, more_place_ref = [refs.pop(0) for _ in range(5)]
    if not first:
        sums_ref, extra_ref = refs.pop(0), refs.pop(0)
    if last:
        out_ref = refs.pop(0)
    else:
        handed_ref, left_ref = refs.pop(0), refs.pop(0)
    gathered, high, low, extra, pick_scratch, place_scratch = refs[:6]
    r_dev = gathered.shape[0] // (2 * tile)
    samples = pieces[0].shape[1]
    lag_dev = extra.shape[1]
    group = pl.program_id(0)

    if prebuilt:
        hankel_ref, hankel_place = signal_ref, group * r_dev
    else:
        hankel_place = 0
        hankel_ref, row_ref = refs[6:]
        n_win = signal_ref.shape[1]
        lay_out([signal_ref[0, w] for w in range(n_win)], number_ref, row_ref)
        begin = first_sample(number_ref, v, n_win, samples)
        for r in range(r_dev):
            hankel_rows(row_ref, r, begin, hankel_ref.shape[2], hankel_ref, r)

    pick_rows(pieces, pick_ref.at[0], gathered, tile)
    for r in range(r_dev):
        slots = slice(r * 2 * tile, (r + 1) * 2 * tile)
        for lag in range(0, lag_dev, STEP):
            lags = slice(lag, lag + STEP)
            total = multiply(gathered, hankel_ref, hankel_place + r, r, tile, lag)
            if not first:
                total += sums_ref[group, slots, lags]
            if last:
                split(total * norming, high, low, slots, lags)
            else:
                handed_ref[group, slots, lags] = total
    if last:
        out_ref[0] = placed(place_ref[0], high, low)

    @pl.when(pass_ref[group] > 1)
    def _():
        if first:
            extra[...] = jnp.zeros(extra.shape, F32)
        else:
            pltpu.sync_copy(extra_ref.at[group], extra)

        def one_pass(number, carry):
            pltpu.sync_copy(more_pick_ref.at[group, number - 1], pick_scratch)
            pltpu.sync_copy(more_place_ref.at[group, number - 1], place_scratch)
            pick_rows(pieces, pick_scratch, gathered, tile)
            for r in range(r_dev):
                needed = count_ref[group * r_dev + r] > (number - 1) * tile
                slots = slice(r * 2 * tile, (r + 1) * 2 * tile)

                @pl.when(needed)
                def _():
                    for lag in range(0, lag_dev, STEP):
                        total = multiply(gathered, hankel_ref, hankel_place + r, r, tile, lag)
                        split(total * norming, high, low, slots, slice(lag, lag + STEP))

                @pl.when(jnp.logical_not(needed))
                def _():
                    high[slots, :] = jnp.zeros((2 * tile, lag_dev), BF16)
                    low[slots, :] = jnp.zeros((2 * tile, lag_dev), BF16)

            extra[...] += placed(place_scratch[...], high, low)
            return carry

        lax.fori_loop(1, pass_ref[group], one_pass, 0)
        if last:
            out_ref[0] += extra[...]
        else:
            pltpu.sync_copy(extra, left_ref.at[group])


def correlate(pieces, signal, prebuilt, numbers, v, matrices, before, last, tile, norming, lag_dev, n_win, r_dev):
    pick, place, passes, counts, more_pick, more_place = matrices
    parts = len(pieces) // 2
    groups, cap, slots = place.shape
    part_rows, samples = pieces[0].shape
    width = samples - LANES + lag_dev
    by_group = lambda shape: pl.BlockSpec(shape, lambda i, *_: (i, 0, 0))
    any_spec = pl.BlockSpec(memory_space=pl.ANY)
    whole_spec = pl.BlockSpec(memory_space=pltpu.VMEM)
    out_spec = pl.BlockSpec(
        (1, cap, lag_dev), lambda i, _, __, number_ref: (lax.rem(number_ref[4] + groups - i, groups), 0, 0)
    )
    sums_shape = jax.ShapeDtypeStruct((groups, slots, lag_dev), F32)
    out_shape = jax.ShapeDtypeStruct((groups, cap, lag_dev), F32)
    in_specs = [whole_spec] * len(pieces)
    in_specs.append(whole_spec if prebuilt else pl.BlockSpec((1,) + signal.shape[1:], lambda i, *_: (i, 0, 0, 0)))
    in_specs += [by_group((1,) + pick.shape[1:]), by_group((1,) + place.shape[1:]), any_spec, any_spec]
    args = pieces + [signal, pick, place, in_hbm(more_pick), in_hbm(more_place)]
    if before is not None:
        in_specs += [whole_spec, any_spec]
        args += [before[0], in_hbm(before[1])]
    scratch = [
        pltpu.VMEM((slots, samples), BF16),
        pltpu.VMEM((slots, lag_dev), BF16),
        pltpu.VMEM((slots, lag_dev), BF16),
        pltpu.VMEM((cap, lag_dev), F32),
        pltpu.VMEM(pick.shape[1:], BF16),
        pltpu.VMEM(place.shape[1:], BF16),
    ]
    if not prebuilt:
        scratch.append(pltpu.VMEM((r_dev, LANES, width), BF16))
        scratch.append(pltpu.VMEM((SHIFT_ROWS, n_win * samples + LAGS), F32))
    body = functools.partial(correlate_kernel, parts, v, tile, norming, prebuilt, before is None, last)
    return pl.pallas_call(
        body,
        grid_spec=pltpu.PrefetchScalarGridSpec(
            num_scalar_prefetch=3,
            grid=(groups,),
            in_specs=in_specs,
            out_specs=out_spec if last else [whole_spec, any_spec],
            scratch_shapes=scratch,
        ),
        out_shape=out_shape if last else [sums_shape, pltpu.HBM(out_shape.shape, F32)],
        cost_estimate=pl.CostEstimate(
            flops=4 * groups * r_dev * tile * samples * (lag_dev + parts * part_rows),
            bytes_accessed=signal.size * signal.dtype.itemsize + 2 * groups * cap * lag_dev * 4,
            transcendentals=0,
        ),
        compiler_params=params(VMEM_BYTES if prebuilt else 2 * VMEM_BYTES),
        name="correlate",
    )(passes, counts, numbers, *args)


def shards(sources, receivers, plan, pair_index, keep):
    _, block_rows, samples = sources.shape
    r_dev = receivers.shape[0]
    n_chan = lax.axis_size("chan")
    n_win = lax.axis_size("win")
    n_rep = lax.axis_size("rep")
    cap = pair_index.shape[3]
    lag_dev = LAGS // (n_win * n_rep)
    tile = max(16, cap // 8)
    norming = 1.0 / math.sqrt(samples * n_win)
    width = samples - LANES + lag_dev
    prebuilt = n_chan * r_dev * n_win * LANES * width * 2 <= HANKEL_BYTES

    parcels, numbers = pack(plan, receivers, pair_index[0, 0], keep[0, 0], n_rep, lag_dev, block_rows, n_chan)
    parcels = [parcels[0]] + [turned(parcels[k], "chan", k) for k in range(1, n_chan)]
    heard = [[parcel] for parcel in parcels]
    for k in range(n_chan):
        heard[k] += [turned_both(receivers, k, v) for v in range(1, n_win)]
    owns = own_rows(numbers, sources[0], n_rep)

    arrived = [{0: own} for own in owns]

    def relay(step):
        for there in arrived:
            there[step] = swapped(there[1 - step], "chan", 0)
            if step < n_chan - 1:
                there[-step] = swapped(there[step - 1], "chan", 1)

    def after_arrival(step, value):
        for there in arrived:
            for key in (step, -step):
                if key in there:
                    value, there[key] = lax.optimization_barrier((value, there[key]))
        return value

    def before_start(step, value):
        for there in arrived:
            for key in (1 - step, step - 1):
                value, there[key] = lax.optimization_barrier((value, there[key]))
        return value

    def halves(piece):
        return [piece] + [turned(piece, "rep", -u) for u in range(1, n_rep)]

    def spans(piece):
        return [piece] + [turned(piece, "win", v) for v in range(1, n_win)]

    relay(1)
    matrices = index(parcels, numbers, samples, r_dev, cap, tile, block_rows)
    if prebuilt:
        signals = [build_hankel(heard, numbers, 0, samples, width)]
        matrices, signals = before_start(2, (matrices, signals))
    else:
        signals = [jnp.stack([jnp.stack([span[:, :samples] for span in spans_of]) for spans_of in heard])] * n_win
    relay(2)
    reach = range(-(n_chan - 2), n_chan - 1)
    near = choose(numbers, 2, arrived, [offset for offset in reach if offset in arrived[0]])
    if prebuilt:
        heard = after_arrival(1, heard)
        signals += [build_hankel(heard, numbers, v, samples, width) for v in range(1, n_win)]
        signals = before_start(3, signals)
    for step in range(3, n_chan):
        relay(step)
    near_halves = [halves(piece) for piece in spans(near)]
    far_spans = spans(choose(numbers, 3, arrived, sorted(arrived[0])))

    result = None
    for v in range(n_win):
        if v:
            far_spans, result = lax.optimization_barrier((far_spans, result))
        result = correlate(
            near_halves[v] + halves(far_spans[v]), signals[v], prebuilt, numbers, v, matrices, result, v == n_win - 1,
            tile, norming, lag_dev, n_win, r_dev,
        )
    return result[None, None]


def solution(mesh):
    placed_at = (
        P(("grp", "chan"), None, "win"),
        P(("grp", "chan"), "win"),
        P("grp", None),
        P("grp", "chan", None, None),
        P("grp", "chan", None, None),
    )
    return jax.shard_map(
        shards,
        mesh=mesh,
        in_specs=placed_at,
        out_specs=P(("grp", "chan"), None, None, None, ("win", "rep")),
        check_vma=False,
    )
```

```python
import functools
import math

import jax
import jax.numpy as jnp
from jax import lax
from jax.experimental import pallas as pl
from jax.experimental.pallas import tpu as pltpu
from jax.sharding import PartitionSpec as P

LAGS = 2048
LANES = 128
SHIFT_ROWS = 8
STEP = 2 * LANES
CHAINS = 1
SPARE = 16
DIGIT = 64
HANKEL_BYTES = 24 * 2**20
VMEM_BYTES = 26 * 2**20
F32 = jnp.float32
BF16 = jnp.bfloat16


def swapped(block, axis, first):
    size = lax.axis_size(axis)
    route = []
    for i in range(first, size - 1, 2):
        route += [(i, i + 1), (i + 1, i)]
    return lax.ppermute(block, axis, route)


def turned(block, axis, distance):
    size = lax.axis_size(axis)
    return lax.ppermute(block, axis, [(i, (i + distance) % size) for i in range(size)])


def turned_both(block, chan_distance, win_distance):
    n_chan, n_win = lax.axis_size("chan"), lax.axis_size("win")
    route = []
    for c in range(n_chan):
        for w in range(n_win):
            there = (c + chan_distance) % n_chan * n_win + (w + win_distance) % n_win
            route.append((c * n_win + w, there))
    return lax.ppermute(block, ("chan", "win"), route)


def in_hbm(array):
    return pltpu.with_memory_space_constraint(array, pltpu.HBM)


def params(vmem):
    return pltpu.CompilerParams(vmem_limit_bytes=vmem)


def pack_kernel(halves, lags, block_rows, plan_hbm, receiver_hbm, pair_hbm, keep_hbm, *refs):
    plan_ref, receiver_ref, pair_ref, keep_ref, digit_ref, sems = refs[-6:]
    parcel_refs, number_ref = refs[:-7], refs[-7]
    small = []
    for place, (source, target) in enumerate(
        ((plan_hbm, plan_ref), (receiver_hbm, receiver_ref), (pair_hbm, pair_ref), (keep_hbm, keep_ref))
    ):
        small.append(pltpu.make_async_copy(source, target, sems.at[place]))
        small[-1].start()
    r_dev, samples = receiver_ref.shape
    n_chan, cap = pair_ref.shape
    n_win = lax.axis_size("win")
    chan, win, rep = lax.axis_index("chan"), lax.axis_index("win"), lax.axis_index("rep")
    for copy in small:
        copy.wait()

    packed = pair_ref[...] * 2 + keep_ref[...]
    digit_ref[:n_chan, :] = jnp.concatenate([packed // DIGIT, packed % DIGIT], axis=1).astype(F32)
    heard = receiver_ref[...].astype(F32)
    part = 2 * cap // r_dev
    spare = parcel_refs[0].shape[1] - samples - part
    for distance, parcel_ref in enumerate(parcel_refs):
        digits = digit_ref[pl.ds(lax.rem(chan + distance, n_chan), 1), :]
        lists = [digits[:, i * part : (i + 1) * part] for i in range(r_dev)]
        parcel = [heard, jnp.concatenate(lists, axis=0)]
        if spare:
            parcel.append(jnp.zeros((r_dev, spare), F32))
        parcel_ref[...] = jnp.concatenate(parcel, axis=1).astype(BF16)

    one, two = plan_ref[0, 0], plan_ref[0, 1]
    nearer = jnp.where(jnp.abs(one - chan) <= jnp.abs(two - chan), 0, 1)
    sign = jnp.where(chan % 2 == 0, 1, -1)
    number_ref[0] = nearer
    number_ref[1] = block_rows - rep * (block_rows // halves)
    number_ref[2] = sign * (jnp.where(nearer == 0, one, two) - chan)
    number_ref[3] = sign * (jnp.where(nearer == 0, two, one) - chan)
    number_ref[4] = chan
    number_ref[5] = (win * halves + rep) * lags
    number_ref[6] = win


def pack(plan, receivers, pair_index, keep, halves, lags, block_rows, n_chan):
    r_dev, samples = receivers.shape
    cap = pair_index.shape[1]
    beside = -(-2 * cap // r_dev // LANES) * LANES
    vmem, smem = pl.BlockSpec(memory_space=pltpu.VMEM), pl.BlockSpec(memory_space=pltpu.SMEM)
    shapes = [jax.ShapeDtypeStruct((r_dev, samples + beside), BF16)] * n_chan
    shapes.append(jax.ShapeDtypeStruct((7,), jnp.int32))
    *parcels, numbers = pl.pallas_call(
        functools.partial(pack_kernel, halves, lags, block_rows),
        in_specs=[pl.BlockSpec(memory_space=pl.ANY)] * 4,
        out_specs=[vmem] * n_chan + [smem],
        out_shape=shapes,
        scratch_shapes=[
            pltpu.SMEM(plan.shape, plan.dtype),
            pltpu.VMEM(receivers.shape, receivers.dtype),
            pltpu.VMEM(pair_index.shape, pair_index.dtype),
            pltpu.VMEM(keep.shape, keep.dtype),
            pltpu.VMEM((-(-n_chan // SHIFT_ROWS) * SHIFT_ROWS, 2 * cap), F32),
            pltpu.SemaphoreType.DMA((4,)),
        ],
        compiler_params=params(VMEM_BYTES // 2),
        name="pack",
    )(*[in_hbm(a) for a in (plan, receivers, pair_index, keep)])
    return parcels, numbers


def own_kernel(number_ref, source_ref, *refs):
    chain_refs, sems = refs[:-1], refs[-1]
    rows = chain_refs[0].shape[0]
    copies = []
    for chain, chain_ref in enumerate(chain_refs):
        start = pl.multiple_of(source_ref.shape[0] - number_ref[1] + chain * rows, rows)
        copies.append(pltpu.make_async_copy(source_ref.at[pl.ds(start, rows)], chain_ref, sems.at[chain]))
        copies[-1].start()
    for copy in copies:
        copy.wait()


def own_rows(numbers, sources, halves):
    block_rows, samples = sources.shape
    shape = jax.ShapeDtypeStruct((block_rows // halves // CHAINS, samples), BF16)
    return pl.pallas_call(
        own_kernel,
        in_specs=[pl.BlockSpec(memory_space=pltpu.SMEM), pl.BlockSpec(memory_space=pl.ANY)],
        out_specs=[pl.BlockSpec(memory_space=pltpu.VMEM)] * CHAINS,
        out_shape=[shape] * CHAINS,
        scratch_shapes=[pltpu.SemaphoreType.DMA((CHAINS,))],
        compiler_params=params(VMEM_BYTES // 4),
        name="own_rows",
    )(numbers, in_hbm(sources))


def choose_kernel(which, offsets, number_ref, *refs):
    out_ref, sems = refs[-2:]
    rows = out_ref.shape[0] // CHAINS
    where = number_ref[which]
    waits = []
    for chain in range(CHAINS):
        target = out_ref.at[pl.ds(chain * rows, rows)]
        for place, offset in enumerate(offsets):
            copy = pltpu.make_async_copy(refs[chain * len(offsets) + place], target, sems.at[chain])

            @pl.when(where == offset)
            def _():
                copy.start()

        waits.append(copy)
    for copy in waits:
        copy.wait()


def choose(numbers, which, arrived, offsets):
    pieces = [there[offset] for there in arrived for offset in offsets]
    rows, samples = pieces[0].shape
    any_spec = pl.BlockSpec(memory_space=pl.ANY)
    return pl.pallas_call(
        functools.partial(choose_kernel, which, offsets),
        in_specs=[pl.BlockSpec(memory_space=pltpu.SMEM)] + [any_spec] * len(pieces),
        out_specs=pl.BlockSpec(memory_space=pltpu.VMEM),
        out_shape=jax.ShapeDtypeStruct((rows * CHAINS, samples), BF16),
        scratch_shapes=[pltpu.SemaphoreType.DMA((CHAINS,))],
        compiler_params=params(VMEM_BYTES // 4),
        name="choose",
    )(numbers, *pieces)


def column(row):
    return jnp.broadcast_to(row, (SHIFT_ROWS, row.shape[1])).T[:, :1]


def ones_where(condition):
    return jnp.where(condition, 1.0, 0.0).astype(BF16)


def index_kernel(r_dev, samples, cap, tile, block_rows, number_ref, *refs):
    pick_ref, place_ref, pass_ref, count_ref, more_pick_ref, more_place_ref, pick_scratch, place_scratch = refs[-8:]
    parcel_refs = refs[:-8]
    nearer, offset = number_ref[0], number_ref[1]
    slots = 2 * r_dev * tile
    window = tile + SPARE
    part = 2 * cap // r_dev
    below = lax.broadcasted_iota(jnp.int32, (cap, cap), 0) < lax.broadcasted_iota(jnp.int32, (cap, cap), 1)
    below = ones_where(below)
    later = []
    for group, parcel_ref in enumerate(parcel_refs):
        digits = parcel_ref[:, samples:].astype(F32)
        digits = jnp.concatenate([digits[i : i + 1, :part] for i in range(r_dev)], axis=1).astype(jnp.int32)
        packed = digits[:, :cap] * DIGIT + digits[:, cap:]
        pairs, kept = packed // 2, packed % 2 == 1
        source_row, receiver = pairs // r_dev, pairs % r_dev
        turn = jnp.where(source_row // block_rows == nearer, 0, 1)
        row = (source_row + offset) % block_rows
        segment = jnp.where(kept, turn * r_dev + receiver, -1)
        member = lax.broadcasted_iota(jnp.int32, (2 * r_dev, cap), 0) == segment
        earlier = jnp.dot(ones_where(member), below, preferred_element_type=F32)
        of_pair = lambda values: jnp.sum(jnp.where(member, values, 0.0), axis=0, keepdims=True).astype(jnp.int32)
        counts = jnp.sum(jnp.where(member, 1.0, 0.0), axis=1, keepdims=True)
        from_top = jnp.minimum(counts[:r_dev], window)
        from_bottom = jnp.minimum(jnp.minimum(counts[r_dev:], 2.0 * tile - from_top), window)
        first_pass = jnp.concatenate([from_top, from_bottom], axis=0)
        first_slot = jnp.concatenate([jnp.zeros_like(from_top), 2.0 * tile - from_bottom], axis=0)
        rank, limit, begin = of_pair(earlier), of_pair(first_pass), of_pair(first_slot)
        rest = rank - limit
        code = jnp.where(rest < 0, begin + rank, (1 + rest // tile) * slots + turn * tile + rest % tile)
        code = jnp.where(kept, code + receiver * 2 * tile, -1)
        left = counts - first_pass
        which = lax.broadcasted_iota(jnp.int32, left.shape, 0) % r_dev
        passes = 1
        for r in range(r_dev):
            count = jnp.max(jnp.where(which == r, left, 0.0)).astype(jnp.int32)
            count_ref[group * r_dev + r] = count
            passes = jnp.maximum(passes, 1 + (count + tile - 1) // tile)
        pass_ref[group] = passes
        code_column = column(code.astype(F32)).astype(jnp.int32)
        row_column = column(row.astype(F32)).astype(jnp.int32)

        def matrices(number, code=code, turn=turn, code_column=code_column, row_column=row_column):
            start = number * slots
            row_ones = ones_where(row_column == lax.broadcasted_iota(jnp.int32, (cap, block_rows), 1))
            line = lax.broadcasted_iota(jnp.int32, (r_dev * window, 1), 0)
            slot = line // window * (2 * tile) + line % window + start
            of_block = [jnp.where(turn == q, code - q * (2 * tile - window), -1) for q in range(2)]
            by_slot = jnp.concatenate([ones_where(slot == codes) for codes in of_block], axis=0)
            pick = jnp.dot(by_slot, row_ones, preferred_element_type=F32).astype(BF16)
            return pick, ones_where(lax.broadcasted_iota(jnp.int32, (cap, slots), 1) + start == code_column)

        pick_ref[group], place_ref[group] = matrices(0)
        later.append((group, passes, matrices))

    for group, passes, matrices in later:

        @pl.when(passes > 1)
        def _():
            def one_pass(number, carry):
                pick_scratch[...], place_scratch[...] = matrices(number)
                pltpu.sync_copy(pick_scratch, more_pick_ref.at[group, number - 1])
                pltpu.sync_copy(place_scratch, more_place_ref.at[group, number - 1])
                return carry

            lax.fori_loop(1, passes, one_pass, 0)


def index(parcels, numbers, samples, r_dev, cap, tile, block_rows):
    groups = len(parcels)
    slots = 2 * r_dev * tile
    lines = 2 * r_dev * (tile + SPARE)
    more = -(-(min(block_rows, cap) - (tile - SPARE)) // tile)
    vmem, smem = pl.BlockSpec(memory_space=pltpu.VMEM), pl.BlockSpec(memory_space=pltpu.SMEM)
    any_spec = pl.BlockSpec(memory_space=pl.ANY)
    return pl.pallas_call(
        functools.partial(index_kernel, r_dev, samples, cap, tile, block_rows),
        in_specs=[smem] + [vmem] * groups,
        out_specs=[vmem, vmem, smem, smem, any_spec, any_spec],
        out_shape=[
            jax.ShapeDtypeStruct((groups, lines, block_rows), BF16),
            jax.ShapeDtypeStruct((groups, cap, slots), BF16),
            jax.ShapeDtypeStruct((groups,), jnp.int32),
            jax.ShapeDtypeStruct((groups * r_dev,), jnp.int32),
            pltpu.HBM((groups, more, lines, block_rows), BF16),
            pltpu.HBM((groups, more, cap, slots), BF16),
        ],
        scratch_shapes=[pltpu.VMEM((lines, block_rows), BF16), pltpu.VMEM((cap, slots), BF16)],
        compiler_params=params(VMEM_BYTES),
        name="index",
    )(numbers, *parcels)


def lay_out(heard, number_ref, signal_ref):
    n_win = len(heard)
    r_dev, samples = heard[0].shape
    for distance, span in enumerate(heard):
        begin = lax.rem(number_ref[6] + n_win - distance, n_win) * samples
        signal_ref[:r_dev, pl.ds(pl.multiple_of(begin, LANES), samples)] = span.astype(F32)
    tail = signal_ref.shape[1] - n_win * samples
    signal_ref[:r_dev, n_win * samples :] = jnp.zeros((r_dev, tail), F32)


def first_sample(number_ref, v, n_win, samples):
    return lax.rem(number_ref[6] + n_win - v, n_win) * samples + number_ref[5]


def hankel_rows(signal_ref, r, begin, width, out_ref, place):
    length = width + LANES
    signal = signal_ref[r : r + 1, pl.ds(pl.multiple_of(begin, LANES), length)]
    base = jnp.broadcast_to(signal, (SHIFT_ROWS, length))
    sublane = lax.broadcasted_iota(jnp.int32, base.shape, 0)
    for bit in (1, 2, 4):
        base = jnp.where(sublane & bit != 0, pltpu.roll(base, length - bit, 1), base)
    for first in range(0, LANES, 2 * SHIFT_ROWS):
        both = []
        for shift in (first, first + SHIFT_ROWS):
            rolled = pltpu.roll(base, length - shift, 1) if shift else base
            both.append(rolled[:, :width])
        out_ref[place, first : first + 2 * SHIFT_ROWS, :] = jnp.concatenate(both, axis=0).astype(BF16)


def hankel_kernel(v, n_win, samples, number_ref, *refs):
    out_ref, signal_refs = refs[-2:]
    heard_refs = refs[:-2]
    r_dev = heard_refs[0].shape[0]
    begin = first_sample(number_ref, v, n_win, samples)
    for group in range(len(heard_refs) // n_win):
        signal_ref = signal_refs.at[group % 2]
        heard = [ref[:, :samples] for ref in heard_refs[group * n_win : (group + 1) * n_win]]
        lay_out(heard, number_ref, signal_ref)
        for r in range(r_dev):
            hankel_rows(signal_ref, r, begin, out_ref.shape[2], out_ref, group * r_dev + r)


def build_hankel(heard, numbers, v, samples, width):
    groups, n_win, r_dev = len(heard), len(heard[0]), heard[0][0].shape[0]
    shape = (groups * r_dev, LANES, width)
    vmem = pl.BlockSpec(memory_space=pltpu.VMEM)
    return pl.pallas_call(
        functools.partial(hankel_kernel, v, n_win, samples),
        in_specs=[pl.BlockSpec(memory_space=pltpu.SMEM)] + [vmem] * (groups * n_win),
        out_specs=vmem,
        scratch_shapes=[pltpu.VMEM((2, SHIFT_ROWS, n_win * samples + LAGS), F32)],
        out_shape=jax.ShapeDtypeStruct(shape, BF16),
        cost_estimate=pl.CostEstimate(
            flops=math.prod(shape), bytes_accessed=2 * math.prod(shape), transcendentals=0
        ),
        compiler_params=params(VMEM_BYTES // 2),
        name="hankel",
    )(numbers, *[span for spans in heard for span in spans])


def pick_rows(pieces, pick, gathered, tile):
    parts = len(pieces) // 2
    window = tile + SPARE
    shared = tile - SPARE
    r_dev, samples = gathered.shape[0] // (2 * tile), gathered.shape[1]
    for t in range(0, samples, STEP):
        chosen = []
        for q in range(2):
            block = jnp.concatenate([piece[:, t : t + STEP] for piece in pieces[q * parts : (q + 1) * parts]], axis=0)
            ones = pick[q * r_dev * window : (q + 1) * r_dev * window, :]
            chosen.append(jnp.dot(ones, block, preferred_element_type=F32))
        for r in range(r_dev):
            top, bottom = [rows[r * window : (r + 1) * window] for rows in chosen]
            rows = [top[shared:] + bottom[: window - shared]]
            if shared:
                rows = [top[:shared]] + rows + [bottom[window - shared :]]
            for place, part in zip((0, shared, window) if shared else (0,), rows):
                start = r * 2 * tile + place
                gathered[start : start + part.shape[0], t : t + STEP] = part.astype(BF16)


def multiply(gathered, hankel_ref, place, r, tile, lag):
    samples = gathered.shape[1]
    wide = jnp.concatenate(
        [hankel_ref[place, :, t + lag : t + lag + STEP] for t in range(0, samples, LANES)], axis=0
    )
    return jnp.dot(gathered[r * 2 * tile : (r + 1) * 2 * tile, :], wide, preferred_element_type=F32)


def split(total, high, low, slots, lags):
    upper = total.astype(BF16)
    high[slots, lags] = upper
    low[slots, lags] = (total - upper.astype(F32)).astype(BF16)


def placed(place, high, low):
    return jnp.dot(place, high[...], preferred_element_type=F32) + jnp.dot(
        place, low[...], preferred_element_type=F32
    )


def correlate_kernel(parts, v, tile, norming, prebuilt, first, last, pass_ref, count_ref, number_ref, *refs):
    refs = list(refs)
    pieces = [refs.pop(0) for _ in range(2 * parts)]
    signal_ref, pick_ref, place_ref, more_pick_ref, more_place_ref = [refs.pop(0) for _ in range(5)]
    if not first:
        sums_ref, extra_ref = refs.pop(0), refs.pop(0)
    if last:
        out_ref = refs.pop(0)
    else:
        handed_ref, left_ref = refs.pop(0), refs.pop(0)
    gathered, high, low, extra, pick_scratch, place_scratch = refs[:6]
    r_dev = gathered.shape[0] // (2 * tile)
    samples = pieces[0].shape[1]
    lag_dev = extra.shape[1]
    group = pl.program_id(0)

    if prebuilt:
        hankel_ref, hankel_place = signal_ref, group * r_dev
    else:
        hankel_place = 0
        hankel_ref, row_ref = refs[6:]
        n_win = signal_ref.shape[1]
        lay_out([signal_ref[0, w] for w in range(n_win)], number_ref, row_ref)
        begin = first_sample(number_ref, v, n_win, samples)
        for r in range(r_dev):
            hankel_rows(row_ref, r, begin, hankel_ref.shape[2], hankel_ref, r)

    pick_rows(pieces, pick_ref.at[0], gathered, tile)
    for r in range(r_dev):
        slots = slice(r * 2 * tile, (r + 1) * 2 * tile)
        for lag in range(0, lag_dev, STEP):
            lags = slice(lag, lag + STEP)
            total = multiply(gathered, hankel_ref, hankel_place + r, r, tile, lag)
            if not first:
                total += sums_ref[group, slots, lags]
            if last:
                split(total * norming, high, low, slots, lags)
            else:
                handed_ref[group, slots, lags] = total
    if last:
        out_ref[0] = placed(place_ref[0], high, low)

    @pl.when(pass_ref[group] > 1)
    def _():
        if first:
            extra[...] = jnp.zeros(extra.shape, F32)
        else:
            pltpu.sync_copy(extra_ref.at[group], extra)

        def one_pass(number, carry):
            pltpu.sync_copy(more_pick_ref.at[group, number - 1], pick_scratch)
            pltpu.sync_copy(more_place_ref.at[group, number - 1], place_scratch)
            pick_rows(pieces, pick_scratch, gathered, tile)
            for r in range(r_dev):
                needed = count_ref[group * r_dev + r] > (number - 1) * tile
                slots = slice(r * 2 * tile, (r + 1) * 2 * tile)

                @pl.when(needed)
                def _():
                    for lag in range(0, lag_dev, STEP):
                        total = multiply(gathered, hankel_ref, hankel_place + r, r, tile, lag)
                        split(total * norming, high, low, slots, slice(lag, lag + STEP))

                @pl.when(jnp.logical_not(needed))
                def _():
                    high[slots, :] = jnp.zeros((2 * tile, lag_dev), BF16)
                    low[slots, :] = jnp.zeros((2 * tile, lag_dev), BF16)

            extra[...] += placed(place_scratch[...], high, low)
            return carry

        lax.fori_loop(1, pass_ref[group], one_pass, 0)
        if last:
            out_ref[0] += extra[...]
        else:
            pltpu.sync_copy(extra, left_ref.at[group])


def correlate(pieces, signal, prebuilt, numbers, v, matrices, before, last, tile, norming, lag_dev, n_win, r_dev):
    pick, place, passes, counts, more_pick, more_place = matrices
    parts = len(pieces) // 2
    groups, cap, slots = place.shape
    part_rows, samples = pieces[0].shape
    width = samples - LANES + lag_dev
    by_group = lambda shape: pl.BlockSpec(shape, lambda i, *_: (i, 0, 0))
    any_spec = pl.BlockSpec(memory_space=pl.ANY)
    whole_spec = pl.BlockSpec(memory_space=pltpu.VMEM)
    out_spec = pl.BlockSpec(
        (1, cap, lag_dev), lambda i, _, __, number_ref: (lax.rem(number_ref[4] + groups - i, groups), 0, 0)
    )
    sums_shape = jax.ShapeDtypeStruct((groups, slots, lag_dev), F32)
    out_shape = jax.ShapeDtypeStruct((groups, cap, lag_dev), F32)
    in_specs = [whole_spec] * len(pieces)
    in_specs.append(whole_spec if prebuilt else pl.BlockSpec((1,) + signal.shape[1:], lambda i, *_: (i, 0, 0, 0)))
    in_specs += [by_group((1,) + pick.shape[1:]), by_group((1,) + place.shape[1:]), any_spec, any_spec]
    args = pieces + [signal, pick, place, in_hbm(more_pick), in_hbm(more_place)]
    if before is not None:
        in_specs += [whole_spec, any_spec]
        args += [before[0], in_hbm(before[1])]
    scratch = [
        pltpu.VMEM((slots, samples), BF16),
        pltpu.VMEM((slots, lag_dev), BF16),
        pltpu.VMEM((slots, lag_dev), BF16),
        pltpu.VMEM((cap, lag_dev), F32),
        pltpu.VMEM(pick.shape[1:], BF16),
        pltpu.VMEM(place.shape[1:], BF16),
    ]
    if not prebuilt:
        scratch.append(pltpu.VMEM((r_dev, LANES, width), BF16))
        scratch.append(pltpu.VMEM((SHIFT_ROWS, n_win * samples + LAGS), F32))
    body = functools.partial(correlate_kernel, parts, v, tile, norming, prebuilt, before is None, last)
    return pl.pallas_call(
        body,
        grid_spec=pltpu.PrefetchScalarGridSpec(
            num_scalar_prefetch=3,
            grid=(groups,),
            in_specs=in_specs,
            out_specs=out_spec if last else [whole_spec, any_spec],
            scratch_shapes=scratch,
        ),
        out_shape=out_shape if last else [sums_shape, pltpu.HBM(out_shape.shape, F32)],
        cost_estimate=pl.CostEstimate(
            flops=4 * groups * r_dev * tile * samples * (lag_dev + parts * part_rows),
            bytes_accessed=signal.size * signal.dtype.itemsize + 2 * groups * cap * lag_dev * 4,
            transcendentals=0,
        ),
        compiler_params=params(VMEM_BYTES if prebuilt else 2 * VMEM_BYTES),
        name="correlate",
    )(passes, counts, numbers, *args)


def shards(sources, receivers, plan, pair_index, keep):
    _, block_rows, samples = sources.shape
    r_dev = receivers.shape[0]
    n_chan = lax.axis_size("chan")
    n_win = lax.axis_size("win")
    n_rep = lax.axis_size("rep")
    cap = pair_index.shape[3]
    lag_dev = LAGS // (n_win * n_rep)
    tile = max(16, cap // 8)
    norming = 1.0 / math.sqrt(samples * n_win)
    width = samples - LANES + lag_dev
    prebuilt = n_chan * r_dev * n_win * LANES * width * 2 <= HANKEL_BYTES

    parcels, numbers = pack(plan, receivers, pair_index[0, 0], keep[0, 0], n_rep, lag_dev, block_rows, n_chan)
    parcels = [parcels[0]] + [turned(parcels[k], "chan", k) for k in range(1, n_chan)]
    heard = [[parcel] for parcel in parcels]
    for k in range(n_chan):
        heard[k] += [turned_both(receivers, k, v) for v in range(1, n_win)]
    sources, parcels, heard = lax.optimization_barrier((sources, parcels, heard))
    owns = own_rows(numbers, sources[0], n_rep)

    arrived = [{0: own} for own in owns]

    def relay(step):
        for there in arrived:
            there[step] = swapped(there[1 - step], "chan", 0)
            if step < n_chan - 1:
                there[-step] = swapped(there[step - 1], "chan", 1)

    def after_arrival(step, value):
        for there in arrived:
            for key in (step, -step):
                if key in there:
                    value, there[key] = lax.optimization_barrier((value, there[key]))
        return value

    def before_start(step, value):
        for there in arrived:
            for key in (1 - step, step - 1):
                value, there[key] = lax.optimization_barrier((value, there[key]))
        return value

    def halves(piece):
        return [piece] + [turned(piece, "rep", -u) for u in range(1, n_rep)]

    def spans(piece):
        return [piece] + [turned(piece, "win", v) for v in range(1, n_win)]

    relay(1)
    matrices = index(parcels, numbers, samples, r_dev, cap, tile, block_rows)
    if prebuilt:
        signals = [build_hankel(heard, numbers, 0, samples, width)]
        matrices, signals = before_start(2, (matrices, signals))
    else:
        signals = [jnp.stack([jnp.stack([span[:, :samples] for span in spans_of]) for spans_of in heard])] * n_win
    relay(2)
    reach = range(-(n_chan - 2), n_chan - 1)
    near = choose(numbers, 2, arrived, [offset for offset in reach if offset in arrived[0]])
    if prebuilt:
        heard = after_arrival(1, heard)
        signals += [build_hankel(heard, numbers, v, samples, width) for v in range(1, n_win)]
        signals = before_start(3, signals)
    for step in range(3, n_chan):
        relay(step)
    near_halves = [halves(piece) for piece in spans(near)]
    far_spans = spans(choose(numbers, 3, arrived, sorted(arrived[0])))

    result = None
    for v in range(n_win):
        if v:
            far_spans, result = lax.optimization_barrier((far_spans, result))
        result = correlate(
            near_halves[v] + halves(far_spans[v]), signals[v], prebuilt, numbers, v, matrices, result, v == n_win - 1,
            tile, norming, lag_dev, n_win, r_dev,
        )
    return result[None, None]


def solution(mesh):
    placed_at = (
        P(("grp", "chan"), None, "win"),
        P(("grp", "chan"), "win"),
        P("grp", None),
        P("grp", "chan", None, None),
        P("grp", "chan", None, None),
    )
    return jax.shard_map(
        shards,
        mesh=mesh,
        in_specs=placed_at,
        out_specs=P(("grp", "chan"), None, None, None, ("win", "rep")),
        check_vma=False,
    )
```

```python
import functools
import math

import jax
import jax.numpy as jnp
from jax import lax
from jax.experimental import pallas as pl
from jax.experimental.pallas import tpu as pltpu
from jax.sharding import PartitionSpec as P

LAGS = 2048
LANES = 128
SHIFT_ROWS = 8
STEP = 2 * LANES
CHAINS = 1
SPARE = 16
DIGIT = 64
HANKEL_BYTES = 24 * 2**20
VMEM_BYTES = 26 * 2**20
F32 = jnp.float32
BF16 = jnp.bfloat16


def swapped(block, axis, first):
    size = lax.axis_size(axis)
    route = []
    for i in range(first, size - 1, 2):
        route += [(i, i + 1), (i + 1, i)]
    return lax.ppermute(block, axis, route)


def turned(block, axis, distance):
    size = lax.axis_size(axis)
    return lax.ppermute(block, axis, [(i, (i + distance) % size) for i in range(size)])


def in_hbm(array):
    return pltpu.with_memory_space_constraint(array, pltpu.HBM)


def params(vmem):
    return pltpu.CompilerParams(vmem_limit_bytes=vmem)


def pack_kernel(halves, lags, block_rows, n_win, plan_hbm, pair_hbm, keep_hbm, *refs):
    span_hbms, refs = refs[:n_win], refs[n_win:]
    plan_ref, pair_ref, keep_ref, span_refs, digit_ref, sems = refs[-6:]
    parcel_refs, number_ref = refs[:-7], refs[-7]
    small = []
    moves = [(plan_hbm, plan_ref), (pair_hbm, pair_ref), (keep_hbm, keep_ref)]
    moves += [(span, span_refs.at[v]) for v, span in enumerate(span_hbms)]
    for place, (source, target) in enumerate(moves):
        small.append(pltpu.make_async_copy(source, target, sems.at[place]))
        small[-1].start()
    r_dev, samples = span_refs.shape[1:]
    n_chan, cap = pair_ref.shape
    chan, win, rep = lax.axis_index("chan"), lax.axis_index("win"), lax.axis_index("rep")
    for copy in small:
        copy.wait()

    packed = pair_ref[...] * 2 + keep_ref[...]
    digit_ref[:n_chan, :] = jnp.concatenate([packed // DIGIT, packed % DIGIT], axis=1).astype(F32)
    heard = [span_refs[v].astype(F32) for v in range(n_win)]
    part = 2 * cap // r_dev
    spare = parcel_refs[0].shape[1] - n_win * samples - part
    for distance, parcel_ref in enumerate(parcel_refs):
        digits = digit_ref[pl.ds(lax.rem(chan + distance, n_chan), 1), :]
        lists = [digits[:, i * part : (i + 1) * part] for i in range(r_dev)]
        parcel = heard + [jnp.concatenate(lists, axis=0)]
        if spare:
            parcel.append(jnp.zeros((r_dev, spare), F32))
        parcel_ref[...] = jnp.concatenate(parcel, axis=1).astype(BF16)

    one, two = plan_ref[0, 0], plan_ref[0, 1]
    nearer = jnp.where(jnp.abs(one - chan) <= jnp.abs(two - chan), 0, 1)
    sign = jnp.where(chan % 2 == 0, 1, -1)
    number_ref[0] = nearer
    number_ref[1] = block_rows - rep * (block_rows // halves)
    number_ref[2] = sign * (jnp.where(nearer == 0, one, two) - chan)
    number_ref[3] = sign * (jnp.where(nearer == 0, two, one) - chan)
    number_ref[4] = chan
    number_ref[5] = (win * halves + rep) * lags
    number_ref[6] = win


def pack(plan, spans, pair_index, keep, halves, lags, block_rows, n_chan):
    n_win = len(spans)
    r_dev, samples = spans[0].shape
    cap = pair_index.shape[1]
    beside = -(-2 * cap // r_dev // LANES) * LANES
    vmem, smem = pl.BlockSpec(memory_space=pltpu.VMEM), pl.BlockSpec(memory_space=pltpu.SMEM)
    shapes = [jax.ShapeDtypeStruct((r_dev, n_win * samples + beside), BF16)] * n_chan
    shapes.append(jax.ShapeDtypeStruct((7,), jnp.int32))
    *parcels, numbers = pl.pallas_call(
        functools.partial(pack_kernel, halves, lags, block_rows, n_win),
        in_specs=[pl.BlockSpec(memory_space=pl.ANY)] * (3 + n_win),
        out_specs=[vmem] * n_chan + [smem],
        out_shape=shapes,
        scratch_shapes=[
            pltpu.SMEM(plan.shape, plan.dtype),
            pltpu.VMEM(pair_index.shape, pair_index.dtype),
            pltpu.VMEM(keep.shape, keep.dtype),
            pltpu.VMEM((n_win, r_dev, samples), BF16),
            pltpu.VMEM((-(-n_chan // SHIFT_ROWS) * SHIFT_ROWS, 2 * cap), F32),
            pltpu.SemaphoreType.DMA((3 + n_win,)),
        ],
        compiler_params=params(VMEM_BYTES // 2),
        name="pack",
    )(*[in_hbm(a) for a in (plan, pair_index, keep, spans[0])], *spans[1:])
    return parcels, numbers


def own_kernel(source_ref, *refs):
    chain_refs, sems = refs[:-1], refs[-1]
    rows = chain_refs[0].shape[0]
    copies = []
    for chain, chain_ref in enumerate(chain_refs):
        start = pl.multiple_of((lax.axis_index("rep") * CHAINS + chain) * rows, rows)
        copies.append(pltpu.make_async_copy(source_ref.at[pl.ds(start, rows)], chain_ref, sems.at[chain]))
        copies[-1].start()
    for copy in copies:
        copy.wait()


def own_rows(sources, halves):
    block_rows, samples = sources.shape
    shape = jax.ShapeDtypeStruct((block_rows // halves // CHAINS, samples), BF16)
    return pl.pallas_call(
        own_kernel,
        in_specs=[pl.BlockSpec(memory_space=pl.ANY)],
        out_specs=[pl.BlockSpec(memory_space=pltpu.VMEM)] * CHAINS,
        out_shape=[shape] * CHAINS,
        scratch_shapes=[pltpu.SemaphoreType.DMA((CHAINS,))],
        compiler_params=params(VMEM_BYTES // 4),
        name="own_rows",
    )(in_hbm(sources))


def choose_kernel(which, offsets, number_ref, *refs):
    out_ref, sems = refs[-2:]
    rows = out_ref.shape[0] // CHAINS
    where = number_ref[which]
    waits = []
    for chain in range(CHAINS):
        target = out_ref.at[pl.ds(chain * rows, rows)]
        for place, offset in enumerate(offsets):
            copy = pltpu.make_async_copy(refs[chain * len(offsets) + place], target, sems.at[chain])

            @pl.when(where == offset)
            def _():
                copy.start()

        waits.append(copy)
    for copy in waits:
        copy.wait()


def choose(numbers, which, arrived, offsets):
    pieces = [there[offset] for there in arrived for offset in offsets]
    rows, samples = pieces[0].shape
    any_spec = pl.BlockSpec(memory_space=pl.ANY)
    return pl.pallas_call(
        functools.partial(choose_kernel, which, offsets),
        in_specs=[pl.BlockSpec(memory_space=pltpu.SMEM)] + [any_spec] * len(pieces),
        out_specs=pl.BlockSpec(memory_space=pltpu.VMEM),
        out_shape=jax.ShapeDtypeStruct((rows * CHAINS, samples), BF16),
        scratch_shapes=[pltpu.SemaphoreType.DMA((CHAINS,))],
        compiler_params=params(VMEM_BYTES // 4),
        name="choose",
    )(numbers, *pieces)


def column(row):
    return jnp.broadcast_to(row, (SHIFT_ROWS, row.shape[1])).T[:, :1]


def ones_where(condition):
    return jnp.where(condition, 1.0, 0.0).astype(BF16)


def index_kernel(r_dev, lists_at, cap, tile, block_rows, number_ref, *refs):
    pick_ref, place_ref, pass_ref, count_ref, more_pick_ref, more_place_ref, pick_scratch, place_scratch = refs[-8:]
    parcel_refs = refs[:-8]
    nearer, offset = number_ref[0], number_ref[1]
    slots = 2 * r_dev * tile
    window = tile + SPARE
    part = 2 * cap // r_dev
    below = lax.broadcasted_iota(jnp.int32, (cap, cap), 0) < lax.broadcasted_iota(jnp.int32, (cap, cap), 1)
    below = ones_where(below)
    later = []
    for group, parcel_ref in enumerate(parcel_refs):
        digits = parcel_ref[:, lists_at:].astype(F32)
        digits = jnp.concatenate([digits[i : i + 1, :part] for i in range(r_dev)], axis=1).astype(jnp.int32)
        packed = digits[:, :cap] * DIGIT + digits[:, cap:]
        pairs, kept = packed // 2, packed % 2 == 1
        source_row, receiver = pairs // r_dev, pairs % r_dev
        turn = jnp.where(source_row // block_rows == nearer, 0, 1)
        row = (source_row + offset) % block_rows
        segment = jnp.where(kept, turn * r_dev + receiver, -1)
        member = lax.broadcasted_iota(jnp.int32, (2 * r_dev, cap), 0) == segment
        earlier = jnp.dot(ones_where(member), below, preferred_element_type=F32)
        of_pair = lambda values: jnp.sum(jnp.where(member, values, 0.0), axis=0, keepdims=True).astype(jnp.int32)
        counts = jnp.sum(jnp.where(member, 1.0, 0.0), axis=1, keepdims=True)
        from_top = jnp.minimum(counts[:r_dev], window)
        from_bottom = jnp.minimum(jnp.minimum(counts[r_dev:], 2.0 * tile - from_top), window)
        first_pass = jnp.concatenate([from_top, from_bottom], axis=0)
        first_slot = jnp.concatenate([jnp.zeros_like(from_top), 2.0 * tile - from_bottom], axis=0)
        rank, limit, begin = of_pair(earlier), of_pair(first_pass), of_pair(first_slot)
        rest = rank - limit
        code = jnp.where(rest < 0, begin + rank, (1 + rest // tile) * slots + turn * tile + rest % tile)
        code = jnp.where(kept, code + receiver * 2 * tile, -1)
        left = counts - first_pass
        which = lax.broadcasted_iota(jnp.int32, left.shape, 0) % r_dev
        passes = 1
        for r in range(r_dev):
            count = jnp.max(jnp.where(which == r, left, 0.0)).astype(jnp.int32)
            count_ref[group * r_dev + r] = count
            passes = jnp.maximum(passes, 1 + (count + tile - 1) // tile)
        pass_ref[group] = passes
        code_column = column(code.astype(F32)).astype(jnp.int32)
        row_column = column(row.astype(F32)).astype(jnp.int32)

        def matrices(number, code=code, turn=turn, code_column=code_column, row_column=row_column):
            start = number * slots
            row_ones = ones_where(row_column == lax.broadcasted_iota(jnp.int32, (cap, block_rows), 1))
            line = lax.broadcasted_iota(jnp.int32, (r_dev * window, 1), 0)
            slot = line // window * (2 * tile) + line % window + start
            of_block = [jnp.where(turn == q, code - q * (2 * tile - window), -1) for q in range(2)]
            by_slot = jnp.concatenate([ones_where(slot == codes) for codes in of_block], axis=0)
            pick = jnp.dot(by_slot, row_ones, preferred_element_type=F32).astype(BF16)
            return pick, ones_where(lax.broadcasted_iota(jnp.int32, (cap, slots), 1) + start == code_column)

        pick_ref[group], place_ref[group] = matrices(0)
        later.append((group, passes, matrices))

    for group, passes, matrices in later:

        @pl.when(passes > 1)
        def _():
            def one_pass(number, carry):
                pick_scratch[...], place_scratch[...] = matrices(number)
                pltpu.sync_copy(pick_scratch, more_pick_ref.at[group, number - 1])
                pltpu.sync_copy(place_scratch, more_place_ref.at[group, number - 1])
                return carry

            lax.fori_loop(1, passes, one_pass, 0)


def index(parcels, numbers, lists_at, r_dev, cap, tile, block_rows):
    groups = len(parcels)
    slots = 2 * r_dev * tile
    lines = 2 * r_dev * (tile + SPARE)
    more = -(-(min(block_rows, cap) - (tile - SPARE)) // tile)
    vmem, smem = pl.BlockSpec(memory_space=pltpu.VMEM), pl.BlockSpec(memory_space=pltpu.SMEM)
    any_spec = pl.BlockSpec(memory_space=pl.ANY)
    return pl.pallas_call(
        functools.partial(index_kernel, r_dev, lists_at, cap, tile, block_rows),
        in_specs=[smem] + [vmem] * groups,
        out_specs=[vmem, vmem, smem, smem, any_spec, any_spec],
        out_shape=[
            jax.ShapeDtypeStruct((groups, lines, block_rows), BF16),
            jax.ShapeDtypeStruct((groups, cap, slots), BF16),
            jax.ShapeDtypeStruct((groups,), jnp.int32),
            jax.ShapeDtypeStruct((groups * r_dev,), jnp.int32),
            pltpu.HBM((groups, more, lines, block_rows), BF16),
            pltpu.HBM((groups, more, cap, slots), BF16),
        ],
        scratch_shapes=[pltpu.VMEM((lines, block_rows), BF16), pltpu.VMEM((cap, slots), BF16)],
        compiler_params=params(VMEM_BYTES),
        name="index",
    )(numbers, *parcels)


def lay_out(heard, number_ref, signal_ref):
    n_win = len(heard)
    r_dev, samples = heard[0].shape
    for distance, span in enumerate(heard):
        begin = lax.rem(number_ref[6] + n_win - distance, n_win) * samples
        signal_ref[:r_dev, pl.ds(pl.multiple_of(begin, LANES), samples)] = span.astype(F32)
    tail = signal_ref.shape[1] - n_win * samples
    signal_ref[:r_dev, n_win * samples :] = jnp.zeros((r_dev, tail), F32)


def first_sample(number_ref, v, n_win, samples):
    return lax.rem(number_ref[6] + n_win - v, n_win) * samples + number_ref[5]


def hankel_rows(signal_ref, r, begin, width, out_ref, place):
    length = width + LANES
    signal = signal_ref[r : r + 1, pl.ds(pl.multiple_of(begin, LANES), length)]
    base = jnp.broadcast_to(signal, (SHIFT_ROWS, length))
    sublane = lax.broadcasted_iota(jnp.int32, base.shape, 0)
    for bit in (1, 2, 4):
        base = jnp.where(sublane & bit != 0, pltpu.roll(base, length - bit, 1), base)
    for first in range(0, LANES, 2 * SHIFT_ROWS):
        both = []
        for shift in (first, first + SHIFT_ROWS):
            rolled = pltpu.roll(base, length - shift, 1) if shift else base
            both.append(rolled[:, :width])
        out_ref[place, first : first + 2 * SHIFT_ROWS, :] = jnp.concatenate(both, axis=0).astype(BF16)


def hankel_kernel(v, n_win, samples, number_ref, *refs):
    out_ref, signal_refs = refs[-2:]
    parcel_refs = refs[:-2]
    r_dev = parcel_refs[0].shape[0]
    begin = first_sample(number_ref, v, n_win, samples)
    for group, parcel_ref in enumerate(parcel_refs):
        signal_ref = signal_refs.at[group % 2]
        heard = [parcel_ref[:, w * samples : (w + 1) * samples] for w in range(n_win)]
        lay_out(heard, number_ref, signal_ref)
        for r in range(r_dev):
            hankel_rows(signal_ref, r, begin, out_ref.shape[2], out_ref, group * r_dev + r)


def build_hankel(parcels, numbers, v, n_win, samples, width):
    groups, r_dev = len(parcels), parcels[0].shape[0]
    shape = (groups * r_dev, LANES, width)
    vmem = pl.BlockSpec(memory_space=pltpu.VMEM)
    return pl.pallas_call(
        functools.partial(hankel_kernel, v, n_win, samples),
        in_specs=[pl.BlockSpec(memory_space=pltpu.SMEM)] + [vmem] * groups,
        out_specs=vmem,
        scratch_shapes=[pltpu.VMEM((2, SHIFT_ROWS, n_win * samples + LAGS), F32)],
        out_shape=jax.ShapeDtypeStruct(shape, BF16),
        cost_estimate=pl.CostEstimate(
            flops=math.prod(shape), bytes_accessed=2 * math.prod(shape), transcendentals=0
        ),
        compiler_params=params(VMEM_BYTES // 2),
        name="hankel",
    )(numbers, *parcels)


def pick_rows(pieces, pick, gathered, tile):
    parts = len(pieces) // 2
    window = tile + SPARE
    shared = tile - SPARE
    r_dev, samples = gathered.shape[0] // (2 * tile), gathered.shape[1]
    for t in range(0, samples, STEP):
        chosen = []
        for q in range(2):
            block = jnp.concatenate([piece[:, t : t + STEP] for piece in pieces[q * parts : (q + 1) * parts]], axis=0)
            ones = pick[q * r_dev * window : (q + 1) * r_dev * window, :]
            chosen.append(jnp.dot(ones, block, preferred_element_type=F32))
        for r in range(r_dev):
            top, bottom = [rows[r * window : (r + 1) * window] for rows in chosen]
            rows = [top[shared:] + bottom[: window - shared]]
            if shared:
                rows = [top[:shared]] + rows + [bottom[window - shared :]]
            for place, part in zip((0, shared, window) if shared else (0,), rows):
                start = r * 2 * tile + place
                gathered[start : start + part.shape[0], t : t + STEP] = part.astype(BF16)


def multiply(gathered, hankel_ref, place, r, tile, lag):
    samples = gathered.shape[1]
    wide = jnp.concatenate(
        [hankel_ref[place, :, t + lag : t + lag + STEP] for t in range(0, samples, LANES)], axis=0
    )
    return jnp.dot(gathered[r * 2 * tile : (r + 1) * 2 * tile, :], wide, preferred_element_type=F32)


def split(total, high, low, slots, lags):
    upper = total.astype(BF16)
    high[slots, lags] = upper
    low[slots, lags] = (total - upper.astype(F32)).astype(BF16)


def placed(place, high, low):
    return jnp.dot(place, high[...], preferred_element_type=F32) + jnp.dot(
        place, low[...], preferred_element_type=F32
    )


def correlate_kernel(parts, v, tile, norming, prebuilt, first, last, pass_ref, count_ref, number_ref, *refs):
    refs = list(refs)
    pieces = [refs.pop(0) for _ in range(2 * parts)]
    signal_ref, pick_ref, place_ref, more_pick_ref, more_place_ref = [refs.pop(0) for _ in range(5)]
    if not first:
        sums_ref, extra_ref = refs.pop(0), refs.pop(0)
    if last:
        out_ref = refs.pop(0)
    else:
        handed_ref, left_ref = refs.pop(0), refs.pop(0)
    gathered, high, low, extra, pick_scratch, place_scratch = refs[:6]
    r_dev = gathered.shape[0] // (2 * tile)
    samples = pieces[0].shape[1]
    lag_dev = extra.shape[1]
    group = pl.program_id(0)

    if prebuilt:
        hankel_ref, hankel_place = signal_ref, group * r_dev
    else:
        hankel_place = 0
        hankel_ref, row_ref = refs[6:]
        n_win = signal_ref.shape[2] // samples
        lay_out([signal_ref[0, :, w * samples : (w + 1) * samples] for w in range(n_win)], number_ref, row_ref)
        begin = first_sample(number_ref, v, n_win, samples)
        for r in range(r_dev):
            hankel_rows(row_ref, r, begin, hankel_ref.shape[2], hankel_ref, r)

    pick_rows(pieces, pick_ref.at[0], gathered, tile)
    for r in range(r_dev):
        slots = slice(r * 2 * tile, (r + 1) * 2 * tile)
        for lag in range(0, lag_dev, STEP):
            lags = slice(lag, lag + STEP)
            total = multiply(gathered, hankel_ref, hankel_place + r, r, tile, lag)
            if not first:
                total += sums_ref[group, slots, lags]
            if last:
                split(total * norming, high, low, slots, lags)
            else:
                handed_ref[group, slots, lags] = total
    if last:
        out_ref[0] = placed(place_ref[0], high, low)

    @pl.when(pass_ref[group] > 1)
    def _():
        if first:
            extra[...] = jnp.zeros(extra.shape, F32)
        else:
            pltpu.sync_copy(extra_ref.at[group], extra)

        def one_pass(number, carry):
            pltpu.sync_copy(more_pick_ref.at[group, number - 1], pick_scratch)
            pltpu.sync_copy(more_place_ref.at[group, number - 1], place_scratch)
            pick_rows(pieces, pick_scratch, gathered, tile)
            for r in range(r_dev):
                needed = count_ref[group * r_dev + r] > (number - 1) * tile
                slots = slice(r * 2 * tile, (r + 1) * 2 * tile)

                @pl.when(needed)
                def _():
                    for lag in range(0, lag_dev, STEP):
                        total = multiply(gathered, hankel_ref, hankel_place + r, r, tile, lag)
                        split(total * norming, high, low, slots, slice(lag, lag + STEP))

                @pl.when(jnp.logical_not(needed))
                def _():
                    high[slots, :] = jnp.zeros((2 * tile, lag_dev), BF16)
                    low[slots, :] = jnp.zeros((2 * tile, lag_dev), BF16)

            extra[...] += placed(place_scratch[...], high, low)
            return carry

        lax.fori_loop(1, pass_ref[group], one_pass, 0)
        if last:
            out_ref[0] += extra[...]
        else:
            pltpu.sync_copy(extra, left_ref.at[group])


def correlate(pieces, signal, prebuilt, numbers, v, matrices, before, last, tile, norming, lag_dev, n_win, r_dev):
    pick, place, passes, counts, more_pick, more_place = matrices
    parts = len(pieces) // 2
    groups, cap, slots = place.shape
    part_rows, samples = pieces[0].shape
    width = samples - LANES + lag_dev
    by_group = lambda shape: pl.BlockSpec(shape, lambda i, *_: (i, 0, 0))
    any_spec = pl.BlockSpec(memory_space=pl.ANY)
    whole_spec = pl.BlockSpec(memory_space=pltpu.VMEM)
    out_spec = pl.BlockSpec(
        (1, cap, lag_dev), lambda i, _, __, number_ref: (lax.rem(number_ref[4] + groups - i, groups), 0, 0)
    )
    sums_shape = jax.ShapeDtypeStruct((groups, slots, lag_dev), F32)
    out_shape = jax.ShapeDtypeStruct((groups, cap, lag_dev), F32)
    in_specs = [whole_spec] * len(pieces)
    in_specs.append(whole_spec if prebuilt else by_group((1,) + signal.shape[1:]))
    in_specs += [by_group((1,) + pick.shape[1:]), by_group((1,) + place.shape[1:]), any_spec, any_spec]
    args = pieces + [signal, pick, place, in_hbm(more_pick), in_hbm(more_place)]
    if before is not None:
        in_specs += [whole_spec, any_spec]
        args += [before[0], in_hbm(before[1])]
    scratch = [
        pltpu.VMEM((slots, samples), BF16),
        pltpu.VMEM((slots, lag_dev), BF16),
        pltpu.VMEM((slots, lag_dev), BF16),
        pltpu.VMEM((cap, lag_dev), F32),
        pltpu.VMEM(pick.shape[1:], BF16),
        pltpu.VMEM(place.shape[1:], BF16),
    ]
    if not prebuilt:
        scratch.append(pltpu.VMEM((r_dev, LANES, width), BF16))
        scratch.append(pltpu.VMEM((SHIFT_ROWS, n_win * samples + LAGS), F32))
    body = functools.partial(correlate_kernel, parts, v, tile, norming, prebuilt, before is None, last)
    return pl.pallas_call(
        body,
        grid_spec=pltpu.PrefetchScalarGridSpec(
            num_scalar_prefetch=3,
            grid=(groups,),
            in_specs=in_specs,
            out_specs=out_spec if last else [whole_spec, any_spec],
            scratch_shapes=scratch,
        ),
        out_shape=out_shape if last else [sums_shape, pltpu.HBM(out_shape.shape, F32)],
        cost_estimate=pl.CostEstimate(
            flops=4 * groups * r_dev * tile * samples * (lag_dev + parts * part_rows),
            bytes_accessed=signal.size * signal.dtype.itemsize + 2 * groups * cap * lag_dev * 4,
            transcendentals=0,
        ),
        compiler_params=params(VMEM_BYTES if prebuilt else 2 * VMEM_BYTES),
        name="correlate",
    )(passes, counts, numbers, *args)


def shards(sources, receivers, plan, pair_index, keep):
    _, block_rows, samples = sources.shape
    r_dev = receivers.shape[0]
    n_chan = lax.axis_size("chan")
    n_win = lax.axis_size("win")
    n_rep = lax.axis_size("rep")
    cap = pair_index.shape[3]
    lag_dev = LAGS // (n_win * n_rep)
    tile = max(16, cap // 8)
    norming = 1.0 / math.sqrt(samples * n_win)
    width = samples - LANES + lag_dev
    prebuilt = n_chan * r_dev * n_win * LANES * width * 2 <= HANKEL_BYTES

    heard = [receivers] + [turned(receivers, "win", v) for v in range(1, n_win)]
    owns = own_rows(sources[0], n_rep)
    parcels, numbers = pack(plan, heard, pair_index[0, 0], keep[0, 0], n_rep, lag_dev, block_rows, n_chan)
    parcels = [parcels[0]] + [turned(parcels[k], "chan", k) for k in range(1, n_chan)]

    arrived = [{0: own} for own in owns]

    def relay(step):
        for there in arrived:
            there[step] = swapped(there[1 - step], "chan", 0)
            if step < n_chan - 1:
                there[-step] = swapped(there[step - 1], "chan", 1)

    def after_arrival(step, value):
        for there in arrived:
            for key in (step, -step):
                if key in there:
                    value, there[key] = lax.optimization_barrier((value, there[key]))
        return value

    def before_start(step, value):
        for there in arrived:
            for key in (1 - step, step - 1):
                value, there[key] = lax.optimization_barrier((value, there[key]))
        return value

    def halves(piece):
        return [piece] + [turned(piece, "rep", -u) for u in range(1, n_rep)]

    def spans(piece):
        return [piece] + [turned(piece, "win", v) for v in range(1, n_win)]

    relay(1)
    parcels = after_arrival(1, parcels)
    relay(2)
    matrices = index(parcels, numbers, n_win * samples, r_dev, cap, tile, block_rows)
    if prebuilt:
        signals = [build_hankel(parcels, numbers, 0, n_win, samples, width)]
        matrices, signals = before_start(3, (matrices, signals))
    else:
        signals = [jnp.stack(parcels)[:, :, : n_win * samples]] * n_win
    reach = range(-(n_chan - 2), n_chan - 1)
    near = choose(numbers, 2, arrived, [offset for offset in reach if offset in arrived[0]])
    if prebuilt:
        parcels = after_arrival(2, parcels)
        parcels, near = lax.optimization_barrier((parcels, near))
        signals += [build_hankel(parcels, numbers, v, n_win, samples, width) for v in range(1, n_win)]
    for step in range(3, n_chan):
        relay(step)
    near_spans = spans(near)
    if prebuilt:
        signals, near_spans = after_arrival(n_chan - 1, (signals, near_spans))
    far_spans = spans(choose(numbers, 3, arrived, sorted(arrived[0])))

    result = None
    for v in range(n_win):
        if v:
            near_spans, far_spans, result = lax.optimization_barrier((near_spans, far_spans, result))
        result = correlate(
            halves(near_spans[v]) + halves(far_spans[v]), signals[v], prebuilt, numbers, v, matrices, result, v == n_win - 1,
            tile, norming, lag_dev, n_win, r_dev,
        )
    return result[None, None]


def solution(mesh):
    placed_at = (
        P(("grp", "chan"), None, "win"),
        P(("grp", "chan"), "win"),
        P("grp", None),
        P("grp", "chan", None, None),
        P("grp", "chan", None, None),
    )
    return jax.shard_map(
        shards,
        mesh=mesh,
        in_specs=placed_at,
        out_specs=P(("grp", "chan"), None, None, None, ("win", "rep")),
        check_vma=False,
    )
```

```python
import functools
import math

import jax
import jax.numpy as jnp
from jax import lax
from jax.experimental import pallas as pl
from jax.experimental.pallas import tpu as pltpu
from jax.sharding import PartitionSpec as P

LAGS = 2048
LANES = 128
SHIFT_ROWS = 8
STEP = 2 * LANES
CHAINS = 1
SPARE = 16
DIGIT = 64
HANKEL_BYTES = 24 * 2**20
VMEM_BYTES = 26 * 2**20
F32 = jnp.float32
BF16 = jnp.bfloat16


def swapped(block, axis, first):
    size = lax.axis_size(axis)
    route = []
    for i in range(first, size - 1, 2):
        route += [(i, i + 1), (i + 1, i)]
    return lax.ppermute(block, axis, route)


def turned(block, axis, distance):
    size = lax.axis_size(axis)
    return lax.ppermute(block, axis, [(i, (i + distance) % size) for i in range(size)])


def in_hbm(array):
    return pltpu.with_memory_space_constraint(array, pltpu.HBM)


def params(vmem):
    return pltpu.CompilerParams(vmem_limit_bytes=vmem)


def pack_kernel(halves, lags, block_rows, n_win, plan_hbm, pair_hbm, keep_hbm, *refs):
    span_hbms, refs = refs[:n_win], refs[n_win:]
    plan_ref, pair_ref, keep_ref, span_refs, digit_ref, sems = refs[-6:]
    parcel_refs, number_ref = refs[:-7], refs[-7]
    small = []
    moves = [(plan_hbm, plan_ref), (pair_hbm, pair_ref), (keep_hbm, keep_ref)]
    moves += [(span, span_refs.at[v]) for v, span in enumerate(span_hbms)]
    for place, (source, target) in enumerate(moves):
        small.append(pltpu.make_async_copy(source, target, sems.at[place]))
        small[-1].start()
    r_dev, samples = span_refs.shape[1:]
    n_chan, cap = pair_ref.shape
    chan, win, rep = lax.axis_index("chan"), lax.axis_index("win"), lax.axis_index("rep")
    for copy in small:
        copy.wait()

    packed = pair_ref[...] * 2 + keep_ref[...]
    digit_ref[:n_chan, :] = jnp.concatenate([packed // DIGIT, packed % DIGIT], axis=1).astype(F32)
    heard = [span_refs[v].astype(F32) for v in range(n_win)]
    part = 2 * cap // r_dev
    spare = parcel_refs[0].shape[1] - n_win * samples - part
    for distance, parcel_ref in enumerate(parcel_refs):
        digits = digit_ref[pl.ds(lax.rem(chan + distance, n_chan), 1), :]
        lists = [digits[:, i * part : (i + 1) * part] for i in range(r_dev)]
        parcel = heard + [jnp.concatenate(lists, axis=0)]
        if spare:
            parcel.append(jnp.zeros((r_dev, spare), F32))
        parcel_ref[...] = jnp.concatenate(parcel, axis=1).astype(BF16)

    one, two = plan_ref[0, 0], plan_ref[0, 1]
    nearer = jnp.where(jnp.abs(one - chan) <= jnp.abs(two - chan), 0, 1)
    sign = jnp.where(chan % 2 == 0, 1, -1)
    number_ref[0] = nearer
    number_ref[1] = block_rows - rep * (block_rows // halves)
    number_ref[2] = sign * (jnp.where(nearer == 0, one, two) - chan)
    number_ref[3] = sign * (jnp.where(nearer == 0, two, one) - chan)
    number_ref[4] = chan
    number_ref[5] = (win * halves + rep) * lags
    number_ref[6] = win


def pack(plan, spans, pair_index, keep, halves, lags, block_rows, n_chan):
    n_win = len(spans)
    r_dev, samples = spans[0].shape
    cap = pair_index.shape[1]
    beside = -(-2 * cap // r_dev // LANES) * LANES
    vmem, smem = pl.BlockSpec(memory_space=pltpu.VMEM), pl.BlockSpec(memory_space=pltpu.SMEM)
    shapes = [jax.ShapeDtypeStruct((r_dev, n_win * samples + beside), BF16)] * n_chan
    shapes.append(jax.ShapeDtypeStruct((7,), jnp.int32))
    *parcels, numbers = pl.pallas_call(
        functools.partial(pack_kernel, halves, lags, block_rows, n_win),
        in_specs=[pl.BlockSpec(memory_space=pl.ANY)] * (3 + n_win),
        out_specs=[vmem] * n_chan + [smem],
        out_shape=shapes,
        scratch_shapes=[
            pltpu.SMEM(plan.shape, plan.dtype),
            pltpu.VMEM(pair_index.shape, pair_index.dtype),
            pltpu.VMEM(keep.shape, keep.dtype),
            pltpu.VMEM((n_win, r_dev, samples), BF16),
            pltpu.VMEM((-(-n_chan // SHIFT_ROWS) * SHIFT_ROWS, 2 * cap), F32),
            pltpu.SemaphoreType.DMA((3 + n_win,)),
        ],
        compiler_params=params(VMEM_BYTES // 2),
        name="pack",
    )(*[in_hbm(a) for a in (plan, pair_index, keep, spans[0])], *spans[1:])
    return parcels, numbers


def own_kernel(source_ref, *refs):
    chain_refs, sems = refs[:-1], refs[-1]
    rows = chain_refs[0].shape[0]
    copies = []
    for chain, chain_ref in enumerate(chain_refs):
        start = pl.multiple_of((lax.axis_index("rep") * CHAINS + chain) * rows, rows)
        copies.append(pltpu.make_async_copy(source_ref.at[pl.ds(start, rows)], chain_ref, sems.at[chain]))
        copies[-1].start()
    for copy in copies:
        copy.wait()


def own_rows(sources, halves):
    block_rows, samples = sources.shape
    shape = jax.ShapeDtypeStruct((block_rows // halves // CHAINS, samples), BF16)
    return pl.pallas_call(
        own_kernel,
        in_specs=[pl.BlockSpec(memory_space=pl.ANY)],
        out_specs=[pl.BlockSpec(memory_space=pltpu.VMEM)] * CHAINS,
        out_shape=[shape] * CHAINS,
        scratch_shapes=[pltpu.SemaphoreType.DMA((CHAINS,))],
        compiler_params=params(VMEM_BYTES // 4),
        name="own_rows",
    )(in_hbm(sources))


def choose_kernel(which, offsets, number_ref, *refs):
    out_ref, sems = refs[-2:]
    rows = out_ref.shape[0] // CHAINS
    where = number_ref[which]
    waits = []
    for chain in range(CHAINS):
        target = out_ref.at[pl.ds(chain * rows, rows)]
        for place, offset in enumerate(offsets):
            copy = pltpu.make_async_copy(refs[chain * len(offsets) + place], target, sems.at[chain])

            @pl.when(where == offset)
            def _():
                copy.start()

        waits.append(copy)
    for copy in waits:
        copy.wait()


def choose(numbers, which, arrived, offsets):
    pieces = [there[offset] for there in arrived for offset in offsets]
    rows, samples = pieces[0].shape
    any_spec = pl.BlockSpec(memory_space=pl.ANY)
    return pl.pallas_call(
        functools.partial(choose_kernel, which, offsets),
        in_specs=[pl.BlockSpec(memory_space=pltpu.SMEM)] + [any_spec] * len(pieces),
        out_specs=pl.BlockSpec(memory_space=pltpu.VMEM),
        out_shape=jax.ShapeDtypeStruct((rows * CHAINS, samples), BF16),
        scratch_shapes=[pltpu.SemaphoreType.DMA((CHAINS,))],
        compiler_params=params(VMEM_BYTES // 4),
        name="choose",
    )(numbers, *pieces)


def column(row):
    return jnp.broadcast_to(row, (SHIFT_ROWS, row.shape[1])).T[:, :1]


def ones_where(condition):
    return jnp.where(condition, 1.0, 0.0).astype(BF16)


def index_kernel(r_dev, lists_at, cap, tile, block_rows, done, number_ref, *refs):
    pick_ref, place_ref, pass_ref, count_ref, more_pick_ref, more_place_ref, pick_scratch, place_scratch = refs[-8:]
    parcel_refs = refs[:-8]
    if done:
        parcel_refs, (_, _, earlier_pass_ref, earlier_count_ref, _, _) = parcel_refs[:-6], parcel_refs[-6:]
        for group in range(done):
            pass_ref[group] = earlier_pass_ref[group]
            for r in range(r_dev):
                count_ref[group * r_dev + r] = earlier_count_ref[group * r_dev + r]
    nearer, offset = number_ref[0], number_ref[1]
    slots = 2 * r_dev * tile
    window = tile + SPARE
    part = 2 * cap // r_dev
    below = lax.broadcasted_iota(jnp.int32, (cap, cap), 0) < lax.broadcasted_iota(jnp.int32, (cap, cap), 1)
    below = ones_where(below)
    later = []
    for group, parcel_ref in enumerate(parcel_refs, done):
        digits = parcel_ref[:, lists_at:].astype(F32)
        digits = jnp.concatenate([digits[i : i + 1, :part] for i in range(r_dev)], axis=1).astype(jnp.int32)
        packed = digits[:, :cap] * DIGIT + digits[:, cap:]
        pairs, kept = packed // 2, packed % 2 == 1
        source_row, receiver = pairs // r_dev, pairs % r_dev
        turn = jnp.where(source_row // block_rows == nearer, 0, 1)
        row = (source_row + offset) % block_rows
        segment = jnp.where(kept, turn * r_dev + receiver, -1)
        member = lax.broadcasted_iota(jnp.int32, (2 * r_dev, cap), 0) == segment
        earlier = jnp.dot(ones_where(member), below, preferred_element_type=F32)
        of_pair = lambda values: jnp.sum(jnp.where(member, values, 0.0), axis=0, keepdims=True).astype(jnp.int32)
        counts = jnp.sum(jnp.where(member, 1.0, 0.0), axis=1, keepdims=True)
        from_top = jnp.minimum(counts[:r_dev], window)
        from_bottom = jnp.minimum(jnp.minimum(counts[r_dev:], 2.0 * tile - from_top), window)
        first_pass = jnp.concatenate([from_top, from_bottom], axis=0)
        first_slot = jnp.concatenate([jnp.zeros_like(from_top), 2.0 * tile - from_bottom], axis=0)
        rank, limit, begin = of_pair(earlier), of_pair(first_pass), of_pair(first_slot)
        rest = rank - limit
        code = jnp.where(rest < 0, begin + rank, (1 + rest // tile) * slots + turn * tile + rest % tile)
        code = jnp.where(kept, code + receiver * 2 * tile, -1)
        left = counts - first_pass
        which = lax.broadcasted_iota(jnp.int32, left.shape, 0) % r_dev
        passes = 1
        for r in range(r_dev):
            count = jnp.max(jnp.where(which == r, left, 0.0)).astype(jnp.int32)
            count_ref[group * r_dev + r] = count
            passes = jnp.maximum(passes, 1 + (count + tile - 1) // tile)
        pass_ref[group] = passes
        code_column = column(code.astype(F32)).astype(jnp.int32)
        row_column = column(row.astype(F32)).astype(jnp.int32)

        def matrices(number, code=code, turn=turn, code_column=code_column, row_column=row_column):
            start = number * slots
            row_ones = ones_where(row_column == lax.broadcasted_iota(jnp.int32, (cap, block_rows), 1))
            line = lax.broadcasted_iota(jnp.int32, (r_dev * window, 1), 0)
            slot = line // window * (2 * tile) + line % window + start
            of_block = [jnp.where(turn == q, code - q * (2 * tile - window), -1) for q in range(2)]
            by_slot = jnp.concatenate([ones_where(slot == codes) for codes in of_block], axis=0)
            pick = jnp.dot(by_slot, row_ones, preferred_element_type=F32).astype(BF16)
            return pick, ones_where(lax.broadcasted_iota(jnp.int32, (cap, slots), 1) + start == code_column)

        pick_ref[group], place_ref[group] = matrices(0)
        later.append((group, passes, matrices))

    for group, passes, matrices in later:

        @pl.when(passes > 1)
        def _():
            def one_pass(number, carry):
                pick_scratch[...], place_scratch[...] = matrices(number)
                pltpu.sync_copy(pick_scratch, more_pick_ref.at[group, number - 1])
                pltpu.sync_copy(place_scratch, more_place_ref.at[group, number - 1])
                return carry

            lax.fori_loop(1, passes, one_pass, 0)


def index(parcels, numbers, earlier, groups, lists_at, r_dev, cap, tile, block_rows):
    slots = 2 * r_dev * tile
    lines = 2 * r_dev * (tile + SPARE)
    more = -(-(min(block_rows, cap) - (tile - SPARE)) // tile)
    vmem, smem = pl.BlockSpec(memory_space=pltpu.VMEM), pl.BlockSpec(memory_space=pltpu.SMEM)
    any_spec = pl.BlockSpec(memory_space=pl.ANY)
    specs = [vmem, vmem, smem, smem, any_spec, any_spec]
    args = list(parcels)
    done, aliases = 0, {}
    if earlier is not None:
        done = groups - len(parcels)
        aliases = {1 + len(parcels) + place: place for place in (0, 1, 4, 5)}
        args += list(earlier[:4]) + [in_hbm(array) for array in earlier[4:]]
    return pl.pallas_call(
        functools.partial(index_kernel, r_dev, lists_at, cap, tile, block_rows, done),
        in_specs=[smem] + [vmem] * len(parcels) + (specs if done else []),
        out_specs=specs,
        out_shape=[
            jax.ShapeDtypeStruct((groups, lines, block_rows), BF16),
            jax.ShapeDtypeStruct((groups, cap, slots), BF16),
            jax.ShapeDtypeStruct((groups,), jnp.int32),
            jax.ShapeDtypeStruct((groups * r_dev,), jnp.int32),
            pltpu.HBM((groups, more, lines, block_rows), BF16),
            pltpu.HBM((groups, more, cap, slots), BF16),
        ],
        scratch_shapes=[pltpu.VMEM((lines, block_rows), BF16), pltpu.VMEM((cap, slots), BF16)],
        input_output_aliases=aliases,
        compiler_params=params(VMEM_BYTES),
        name="index",
    )(numbers, *args)


def lay_out(heard, number_ref, signal_ref):
    n_win = len(heard)
    r_dev, samples = heard[0].shape
    for distance, span in enumerate(heard):
        begin = lax.rem(number_ref[6] + n_win - distance, n_win) * samples
        signal_ref[:r_dev, pl.ds(pl.multiple_of(begin, LANES), samples)] = span.astype(F32)
    tail = signal_ref.shape[1] - n_win * samples
    signal_ref[:r_dev, n_win * samples :] = jnp.zeros((r_dev, tail), F32)


def first_sample(number_ref, v, n_win, samples):
    return lax.rem(number_ref[6] + n_win - v, n_win) * samples + number_ref[5]


def hankel_rows(signal_ref, r, begin, width, out_ref, place):
    length = width + LANES
    signal = signal_ref[r : r + 1, pl.ds(pl.multiple_of(begin, LANES), length)]
    base = jnp.broadcast_to(signal, (SHIFT_ROWS, length))
    sublane = lax.broadcasted_iota(jnp.int32, base.shape, 0)
    for bit in (1, 2, 4):
        base = jnp.where(sublane & bit != 0, pltpu.roll(base, length - bit, 1), base)
    for first in range(0, LANES, 2 * SHIFT_ROWS):
        both = []
        for shift in (first, first + SHIFT_ROWS):
            rolled = pltpu.roll(base, length - shift, 1) if shift else base
            both.append(rolled[:, :width])
        out_ref[place, first : first + 2 * SHIFT_ROWS, :] = jnp.concatenate(both, axis=0).astype(BF16)


def hankel_kernel(v, n_win, samples, done, number_ref, *refs):
    out_ref, signal_refs = refs[-2:]
    parcel_refs = refs[: -3 if done else -2]
    r_dev = parcel_refs[0].shape[0]
    begin = first_sample(number_ref, v, n_win, samples)
    for group, parcel_ref in enumerate(parcel_refs, done):
        signal_ref = signal_refs.at[group % 2]
        heard = [parcel_ref[:, w * samples : (w + 1) * samples] for w in range(n_win)]
        lay_out(heard, number_ref, signal_ref)
        for r in range(r_dev):
            hankel_rows(signal_ref, r, begin, out_ref.shape[2], out_ref, group * r_dev + r)


def build_hankel(parcels, numbers, earlier, groups, v, n_win, samples, width):
    r_dev = parcels[0].shape[0]
    shape = (groups * r_dev, LANES, width)
    vmem = pl.BlockSpec(memory_space=pltpu.VMEM)
    done = 0 if earlier is None else groups - len(parcels)
    copies = len(parcels) * r_dev * LANES * width
    return pl.pallas_call(
        functools.partial(hankel_kernel, v, n_win, samples, done),
        in_specs=[pl.BlockSpec(memory_space=pltpu.SMEM)] + [vmem] * (len(parcels) + (1 if done else 0)),
        out_specs=vmem,
        scratch_shapes=[pltpu.VMEM((2, SHIFT_ROWS, n_win * samples + LAGS), F32)],
        out_shape=jax.ShapeDtypeStruct(shape, BF16),
        input_output_aliases={1 + len(parcels): 0} if done else {},
        cost_estimate=pl.CostEstimate(flops=copies, bytes_accessed=2 * copies, transcendentals=0),
        compiler_params=params(VMEM_BYTES // 2),
        name="hankel",
    )(numbers, *parcels, *([earlier] if done else []))


def pick_rows(pieces, pick, gathered, tile):
    parts = len(pieces) // 2
    window = tile + SPARE
    shared = tile - SPARE
    r_dev, samples = gathered.shape[0] // (2 * tile), gathered.shape[1]
    for t in range(0, samples, STEP):
        chosen = []
        for q in range(2):
            block = jnp.concatenate([piece[:, t : t + STEP] for piece in pieces[q * parts : (q + 1) * parts]], axis=0)
            ones = pick[q * r_dev * window : (q + 1) * r_dev * window, :]
            chosen.append(jnp.dot(ones, block, preferred_element_type=F32))
        for r in range(r_dev):
            top, bottom = [rows[r * window : (r + 1) * window] for rows in chosen]
            rows = [top[shared:] + bottom[: window - shared]]
            if shared:
                rows = [top[:shared]] + rows + [bottom[window - shared :]]
            for place, part in zip((0, shared, window) if shared else (0,), rows):
                start = r * 2 * tile + place
                gathered[start : start + part.shape[0], t : t + STEP] = part.astype(BF16)


def multiply(gathered, hankel_ref, place, r, tile, lag):
    samples = gathered.shape[1]
    wide = jnp.concatenate(
        [hankel_ref[place, :, t + lag : t + lag + STEP] for t in range(0, samples, LANES)], axis=0
    )
    return jnp.dot(gathered[r * 2 * tile : (r + 1) * 2 * tile, :], wide, preferred_element_type=F32)


def split(total, high, low, slots, lags):
    upper = total.astype(BF16)
    high[slots, lags] = upper
    low[slots, lags] = (total - upper.astype(F32)).astype(BF16)


def placed(place, high, low):
    return jnp.dot(place, high[...], preferred_element_type=F32) + jnp.dot(
        place, low[...], preferred_element_type=F32
    )


def correlate_kernel(parts, v, tile, norming, prebuilt, first, last, pass_ref, count_ref, number_ref, *refs):
    refs = list(refs)
    pieces = [refs.pop(0) for _ in range(2 * parts)]
    signal_ref, pick_ref, place_ref, more_pick_ref, more_place_ref = [refs.pop(0) for _ in range(5)]
    if not first:
        sums_ref, extra_ref = refs.pop(0), refs.pop(0)
    if last:
        out_ref = refs.pop(0)
    else:
        handed_ref, left_ref = refs.pop(0), refs.pop(0)
    gathered, high, low, extra, pick_scratch, place_scratch = refs[:6]
    r_dev = gathered.shape[0] // (2 * tile)
    samples = pieces[0].shape[1]
    lag_dev = extra.shape[1]
    group = pl.program_id(0)

    if prebuilt:
        hankel_ref, hankel_place = signal_ref, group * r_dev
    else:
        hankel_place = 0
        hankel_ref, row_ref = refs[6:]
        n_win = signal_ref.shape[2] // samples
        lay_out([signal_ref[0, :, w * samples : (w + 1) * samples] for w in range(n_win)], number_ref, row_ref)
        begin = first_sample(number_ref, v, n_win, samples)
        for r in range(r_dev):
            hankel_rows(row_ref, r, begin, hankel_ref.shape[2], hankel_ref, r)

    pick_rows(pieces, pick_ref.at[0], gathered, tile)
    for r in range(r_dev):
        slots = slice(r * 2 * tile, (r + 1) * 2 * tile)
        for lag in range(0, lag_dev, STEP):
            lags = slice(lag, lag + STEP)
            total = multiply(gathered, hankel_ref, hankel_place + r, r, tile, lag)
            if not first:
                total += sums_ref[group, slots, lags]
            if last:
                split(total * norming, high, low, slots, lags)
            else:
                handed_ref[group, slots, lags] = total
    if last:
        out_ref[0] = placed(place_ref[0], high, low)

    @pl.when(pass_ref[group] > 1)
    def _():
        if first:
            extra[...] = jnp.zeros(extra.shape, F32)
        else:
            pltpu.sync_copy(extra_ref.at[group], extra)

        def one_pass(number, carry):
            pltpu.sync_copy(more_pick_ref.at[group, number - 1], pick_scratch)
            pltpu.sync_copy(more_place_ref.at[group, number - 1], place_scratch)
            pick_rows(pieces, pick_scratch, gathered, tile)
            for r in range(r_dev):
                needed = count_ref[group * r_dev + r] > (number - 1) * tile
                slots = slice(r * 2 * tile, (r + 1) * 2 * tile)

                @pl.when(needed)
                def _():
                    for lag in range(0, lag_dev, STEP):
                        total = multiply(gathered, hankel_ref, hankel_place + r, r, tile, lag)
                        split(total * norming, high, low, slots, slice(lag, lag + STEP))

                @pl.when(jnp.logical_not(needed))
                def _():
                    high[slots, :] = jnp.zeros((2 * tile, lag_dev), BF16)
                    low[slots, :] = jnp.zeros((2 * tile, lag_dev), BF16)

            extra[...] += placed(place_scratch[...], high, low)
            return carry

        lax.fori_loop(1, pass_ref[group], one_pass, 0)
        if last:
            out_ref[0] += extra[...]
        else:
            pltpu.sync_copy(extra, left_ref.at[group])


def correlate(pieces, signal, prebuilt, numbers, v, matrices, before, last, tile, norming, lag_dev, n_win, r_dev):
    pick, place, passes, counts, more_pick, more_place = matrices
    parts = len(pieces) // 2
    groups, cap, slots = place.shape
    part_rows, samples = pieces[0].shape
    width = samples - LANES + lag_dev
    by_group = lambda shape: pl.BlockSpec(shape, lambda i, *_: (i, 0, 0))
    any_spec = pl.BlockSpec(memory_space=pl.ANY)
    whole_spec = pl.BlockSpec(memory_space=pltpu.VMEM)
    out_spec = pl.BlockSpec(
        (1, cap, lag_dev), lambda i, _, __, number_ref: (lax.rem(number_ref[4] + groups - i, groups), 0, 0)
    )
    sums_shape = jax.ShapeDtypeStruct((groups, slots, lag_dev), F32)
    out_shape = jax.ShapeDtypeStruct((groups, cap, lag_dev), F32)
    in_specs = [whole_spec] * len(pieces)
    in_specs.append(whole_spec if prebuilt else by_group((1,) + signal.shape[1:]))
    in_specs += [by_group((1,) + pick.shape[1:]), by_group((1,) + place.shape[1:]), any_spec, any_spec]
    args = pieces + [signal, pick, place, in_hbm(more_pick), in_hbm(more_place)]
    if before is not None:
        in_specs += [whole_spec, any_spec]
        args += [before[0], in_hbm(before[1])]
    scratch = [
        pltpu.VMEM((slots, samples), BF16),
        pltpu.VMEM((slots, lag_dev), BF16),
        pltpu.VMEM((slots, lag_dev), BF16),
        pltpu.VMEM((cap, lag_dev), F32),
        pltpu.VMEM(pick.shape[1:], BF16),
        pltpu.VMEM(place.shape[1:], BF16),
    ]
    if not prebuilt:
        scratch.append(pltpu.VMEM((r_dev, LANES, width), BF16))
        scratch.append(pltpu.VMEM((SHIFT_ROWS, n_win * samples + LAGS), F32))
    body = functools.partial(correlate_kernel, parts, v, tile, norming, prebuilt, before is None, last)
    return pl.pallas_call(
        body,
        grid_spec=pltpu.PrefetchScalarGridSpec(
            num_scalar_prefetch=3,
            grid=(groups,),
            in_specs=in_specs,
            out_specs=out_spec if last else [whole_spec, any_spec],
            scratch_shapes=scratch,
        ),
        out_shape=out_shape if last else [sums_shape, pltpu.HBM(out_shape.shape, F32)],
        cost_estimate=pl.CostEstimate(
            flops=4 * groups * r_dev * tile * samples * (lag_dev + parts * part_rows),
            bytes_accessed=signal.size * signal.dtype.itemsize + 2 * groups * cap * lag_dev * 4,
            transcendentals=0,
        ),
        compiler_params=params(VMEM_BYTES if prebuilt else 2 * VMEM_BYTES),
        name="correlate",
    )(passes, counts, numbers, *args)


def shards(sources, receivers, plan, pair_index, keep):
    _, block_rows, samples = sources.shape
    r_dev = receivers.shape[0]
    n_chan = lax.axis_size("chan")
    n_win = lax.axis_size("win")
    n_rep = lax.axis_size("rep")
    cap = pair_index.shape[3]
    lag_dev = LAGS // (n_win * n_rep)
    tile = max(16, cap // 8)
    norming = 1.0 / math.sqrt(samples * n_win)
    width = samples - LANES + lag_dev
    prebuilt = n_chan * r_dev * n_win * LANES * width * 2 <= HANKEL_BYTES

    heard = [receivers] + [turned(receivers, "win", v) for v in range(1, n_win)]
    owns = own_rows(sources[0], n_rep)
    parcels, numbers = pack(plan, heard, pair_index[0, 0], keep[0, 0], n_rep, lag_dev, block_rows, n_chan)
    own_parcel = parcels[0]
    parcels = [turned(parcels[k], "chan", k) for k in range(1, n_chan)]
    matrices = index([own_parcel], numbers, None, n_chan, n_win * samples, r_dev, cap, tile, block_rows)
    if prebuilt:
        signals = [build_hankel([own_parcel], numbers, None, n_chan, v, n_win, samples, width) for v in range(n_win)]

    arrived = [{0: own} for own in owns]

    def relay(step):
        for there in arrived:
            there[step] = swapped(there[1 - step], "chan", 0)
            if step < n_chan - 1:
                there[-step] = swapped(there[step - 1], "chan", 1)

    def after_arrival(step, value):
        for there in arrived:
            for key in (step, -step):
                if key in there:
                    value = lax.optimization_barrier((value, there[key]))[0]
        return value

    def before_start(step, value):
        for there in arrived:
            for key in (1 - step, step - 1):
                there[key] = lax.optimization_barrier((value, there[key]))[1]

    def halves(piece):
        return [piece] + [turned(piece, "rep", -u) for u in range(1, n_rep)]

    def spans(piece):
        return [piece] + [turned(piece, "win", v) for v in range(1, n_win)]

    relay(1)
    before_start(2, (matrices, parcels, signals) if prebuilt else (matrices, parcels))
    parcels = after_arrival(1, parcels)
    relay(2)
    matrices = index(parcels, numbers, matrices, n_chan, n_win * samples, r_dev, cap, tile, block_rows)
    if prebuilt:
        signals[0] = build_hankel(parcels, numbers, signals[0], n_chan, 0, n_win, samples, width)
        before_start(3, (matrices, signals[0]))
    else:
        signals = [jnp.stack([own_parcel] + parcels)[:, :, : n_win * samples]] * n_win
    reach = range(-(n_chan - 2), n_chan - 1)
    near = choose(numbers, 2, arrived, [offset for offset in reach if offset in arrived[0]])
    if prebuilt:
        parcels = after_arrival(2, parcels)
        parcels, near = lax.optimization_barrier((parcels, near))
        for v in range(1, n_win):
            signals[v] = build_hankel(parcels, numbers, signals[v], n_chan, v, n_win, samples, width)
    for step in range(3, n_chan):
        relay(step)
    near_spans = spans(near)
    if prebuilt:
        signals, near_spans = after_arrival(n_chan - 1, (signals, near_spans))
    far_spans = spans(choose(numbers, 3, arrived, sorted(arrived[0])))

    result = None
    for v in range(n_win):
        if v:
            near_spans, far_spans, result = lax.optimization_barrier((near_spans, far_spans, result))
        result = correlate(
            halves(near_spans[v]) + halves(far_spans[v]), signals[v], prebuilt, numbers, v, matrices, result, v == n_win - 1,
            tile, norming, lag_dev, n_win, r_dev,
        )
    return result[None, None]


def solution(mesh):
    placed_at = (
        P(("grp", "chan"), None, "win"),
        P(("grp", "chan"), "win"),
        P("grp", None),
        P("grp", "chan", None, None),
        P("grp", "chan", None, None),
    )
    return jax.shard_map(
        shards,
        mesh=mesh,
        in_specs=placed_at,
        out_specs=P(("grp", "chan"), None, None, None, ("win", "rep")),
        check_vma=False,
    )
```

```python
import functools
import math

import jax
import jax.numpy as jnp
from jax import lax
from jax.experimental import pallas as pl
from jax.experimental.pallas import tpu as pltpu
from jax.sharding import PartitionSpec as P

LAGS = 2048
LANES = 128
SHIFT_ROWS = 8
STEP = 2 * LANES
CHAINS = 1
SPARE = 16
DIGIT = 64
HANKEL_BYTES = 24 * 2**20
VMEM_BYTES = 26 * 2**20
F32 = jnp.float32
BF16 = jnp.bfloat16


def swapped(block, axis, first):
    size = lax.axis_size(axis)
    route = []
    for i in range(first, size - 1, 2):
        route += [(i, i + 1), (i + 1, i)]
    return lax.ppermute(block, axis, route)


def turned(block, axis, distance):
    size = lax.axis_size(axis)
    return lax.ppermute(block, axis, [(i, (i + distance) % size) for i in range(size)])


def in_hbm(array):
    return pltpu.with_memory_space_constraint(array, pltpu.HBM)


def params(vmem):
    return pltpu.CompilerParams(vmem_limit_bytes=vmem)


def pack_kernel(halves, lags, block_rows, n_win, plan_hbm, pair_hbm, keep_hbm, *refs):
    span_hbms, refs = refs[:n_win], refs[n_win:]
    plan_ref, pair_ref, keep_ref, span_refs, digit_ref, sems = refs[-6:]
    parcel_refs, number_ref = refs[:-7], refs[-7]
    small = []
    moves = [(plan_hbm, plan_ref), (pair_hbm, pair_ref), (keep_hbm, keep_ref)]
    moves += [(span, span_refs.at[v]) for v, span in enumerate(span_hbms)]
    for place, (source, target) in enumerate(moves):
        small.append(pltpu.make_async_copy(source, target, sems.at[place]))
        small[-1].start()
    r_dev, samples = span_refs.shape[1:]
    n_chan, cap = pair_ref.shape
    chan, win, rep = lax.axis_index("chan"), lax.axis_index("win"), lax.axis_index("rep")
    for copy in small:
        copy.wait()

    packed = pair_ref[...] * 2 + keep_ref[...]
    digit_ref[:n_chan, :] = jnp.concatenate([packed // DIGIT, packed % DIGIT], axis=1).astype(F32)
    heard = [span_refs[v].astype(F32) for v in range(n_win)]
    part = 2 * cap // r_dev
    spare = parcel_refs[0].shape[1] - n_win * samples - part
    for distance, parcel_ref in enumerate(parcel_refs):
        digits = digit_ref[pl.ds(lax.rem(chan + distance, n_chan), 1), :]
        lists = [digits[:, i * part : (i + 1) * part] for i in range(r_dev)]
        parcel = heard + [jnp.concatenate(lists, axis=0)]
        if spare:
            parcel.append(jnp.zeros((r_dev, spare), F32))
        parcel_ref[...] = jnp.concatenate(parcel, axis=1).astype(BF16)

    one, two = plan_ref[0, 0], plan_ref[0, 1]
    nearer = jnp.where(jnp.abs(one - chan) <= jnp.abs(two - chan), 0, 1)
    sign = jnp.where(chan % 2 == 0, 1, -1)
    number_ref[0] = nearer
    number_ref[1] = block_rows - rep * (block_rows // halves)
    number_ref[2] = sign * (jnp.where(nearer == 0, one, two) - chan)
    number_ref[3] = sign * (jnp.where(nearer == 0, two, one) - chan)
    number_ref[4] = chan
    number_ref[5] = (win * halves + rep) * lags
    number_ref[6] = win


def pack(plan, spans, pair_index, keep, halves, lags, block_rows, n_chan):
    n_win = len(spans)
    r_dev, samples = spans[0].shape
    cap = pair_index.shape[1]
    beside = -(-2 * cap // r_dev // LANES) * LANES
    vmem, smem = pl.BlockSpec(memory_space=pltpu.VMEM), pl.BlockSpec(memory_space=pltpu.SMEM)
    shapes = [jax.ShapeDtypeStruct((r_dev, n_win * samples + beside), BF16)] * n_chan
    shapes.append(jax.ShapeDtypeStruct((7,), jnp.int32))
    *parcels, numbers = pl.pallas_call(
        functools.partial(pack_kernel, halves, lags, block_rows, n_win),
        in_specs=[pl.BlockSpec(memory_space=pl.ANY)] * (3 + n_win),
        out_specs=[vmem] * n_chan + [smem],
        out_shape=shapes,
        scratch_shapes=[
            pltpu.SMEM(plan.shape, plan.dtype),
            pltpu.VMEM(pair_index.shape, pair_index.dtype),
            pltpu.VMEM(keep.shape, keep.dtype),
            pltpu.VMEM((n_win, r_dev, samples), BF16),
            pltpu.VMEM((-(-n_chan // SHIFT_ROWS) * SHIFT_ROWS, 2 * cap), F32),
            pltpu.SemaphoreType.DMA((3 + n_win,)),
        ],
        compiler_params=params(VMEM_BYTES // 2),
        name="pack",
    )(*[in_hbm(a) for a in (plan, pair_index, keep, spans[0])], *spans[1:])
    return parcels, numbers


def own_kernel(source_ref, *refs):
    chain_refs, sems = refs[:-1], refs[-1]
    rows = chain_refs[0].shape[0]
    copies = []
    for chain, chain_ref in enumerate(chain_refs):
        start = pl.multiple_of((lax.axis_index("rep") * CHAINS + chain) * rows, rows)
        copies.append(pltpu.make_async_copy(source_ref.at[pl.ds(start, rows)], chain_ref, sems.at[chain]))
        copies[-1].start()
    for copy in copies:
        copy.wait()


def own_rows(sources, halves):
    block_rows, samples = sources.shape
    shape = jax.ShapeDtypeStruct((block_rows // halves // CHAINS, samples), BF16)
    return pl.pallas_call(
        own_kernel,
        in_specs=[pl.BlockSpec(memory_space=pl.ANY)],
        out_specs=[pl.BlockSpec(memory_space=pltpu.VMEM)] * CHAINS,
        out_shape=[shape] * CHAINS,
        scratch_shapes=[pltpu.SemaphoreType.DMA((CHAINS,))],
        compiler_params=params(VMEM_BYTES // 4),
        name="own_rows",
    )(in_hbm(sources))


def choose_kernel(which, offsets, number_ref, *refs):
    out_ref, sems = refs[-2:]
    rows = out_ref.shape[0] // CHAINS
    where = number_ref[which]
    waits = []
    for chain in range(CHAINS):
        target = out_ref.at[pl.ds(chain * rows, rows)]
        for place, offset in enumerate(offsets):
            copy = pltpu.make_async_copy(refs[chain * len(offsets) + place], target, sems.at[chain])

            @pl.when(where == offset)
            def _():
                copy.start()

        waits.append(copy)
    for copy in waits:
        copy.wait()


def choose(numbers, which, arrived, offsets):
    pieces = [there[offset] for there in arrived for offset in offsets]
    rows, samples = pieces[0].shape
    any_spec = pl.BlockSpec(memory_space=pl.ANY)
    return pl.pallas_call(
        functools.partial(choose_kernel, which, offsets),
        in_specs=[pl.BlockSpec(memory_space=pltpu.SMEM)] + [any_spec] * len(pieces),
        out_specs=pl.BlockSpec(memory_space=pltpu.VMEM),
        out_shape=jax.ShapeDtypeStruct((rows * CHAINS, samples), BF16),
        scratch_shapes=[pltpu.SemaphoreType.DMA((CHAINS,))],
        compiler_params=params(VMEM_BYTES // 4),
        name="choose",
    )(numbers, *pieces)


def column(row):
    return jnp.broadcast_to(row, (SHIFT_ROWS, row.shape[1])).T[:, :1]


def ones_where(condition):
    return jnp.where(condition, 1.0, 0.0).astype(BF16)


def index_kernel(r_dev, lists_at, cap, tile, block_rows, done, number_ref, *refs):
    pick_ref, place_ref, pass_ref, count_ref, more_pick_ref, more_place_ref, pick_scratch, place_scratch = refs[-8:]
    parcel_refs = refs[:-8]
    if done:
        parcel_refs, (_, _, earlier_pass_ref, earlier_count_ref, _, _) = parcel_refs[:-6], parcel_refs[-6:]
        for group in range(done):
            pass_ref[group] = earlier_pass_ref[group]
            for r in range(r_dev):
                count_ref[group * r_dev + r] = earlier_count_ref[group * r_dev + r]
    nearer, offset = number_ref[0], number_ref[1]
    slots = 2 * r_dev * tile
    window = tile + SPARE
    part = 2 * cap // r_dev
    below = lax.broadcasted_iota(jnp.int32, (cap, cap), 0) < lax.broadcasted_iota(jnp.int32, (cap, cap), 1)
    below = ones_where(below)
    later = []
    for group, parcel_ref in enumerate(parcel_refs, done):
        digits = parcel_ref[:, lists_at:].astype(F32)
        digits = jnp.concatenate([digits[i : i + 1, :part] for i in range(r_dev)], axis=1).astype(jnp.int32)
        packed = digits[:, :cap] * DIGIT + digits[:, cap:]
        pairs, kept = packed // 2, packed % 2 == 1
        source_row, receiver = pairs // r_dev, pairs % r_dev
        turn = jnp.where(source_row // block_rows == nearer, 0, 1)
        row = (source_row + offset) % block_rows
        segment = jnp.where(kept, turn * r_dev + receiver, -1)
        member = lax.broadcasted_iota(jnp.int32, (2 * r_dev, cap), 0) == segment
        earlier = jnp.dot(ones_where(member), below, preferred_element_type=F32)
        of_pair = lambda values: jnp.sum(jnp.where(member, values, 0.0), axis=0, keepdims=True).astype(jnp.int32)
        counts = jnp.sum(jnp.where(member, 1.0, 0.0), axis=1, keepdims=True)
        from_top = jnp.minimum(counts[:r_dev], window)
        from_bottom = jnp.minimum(jnp.minimum(counts[r_dev:], 2.0 * tile - from_top), window)
        first_pass = jnp.concatenate([from_top, from_bottom], axis=0)
        first_slot = jnp.concatenate([jnp.zeros_like(from_top), 2.0 * tile - from_bottom], axis=0)
        rank, limit, begin = of_pair(earlier), of_pair(first_pass), of_pair(first_slot)
        rest = rank - limit
        code = jnp.where(rest < 0, begin + rank, (1 + rest // tile) * slots + turn * tile + rest % tile)
        code = jnp.where(kept, code + receiver * 2 * tile, -1)
        left = counts - first_pass
        which = lax.broadcasted_iota(jnp.int32, left.shape, 0) % r_dev
        passes = 1
        for r in range(r_dev):
            count = jnp.max(jnp.where(which == r, left, 0.0)).astype(jnp.int32)
            count_ref[group * r_dev + r] = count
            passes = jnp.maximum(passes, 1 + (count + tile - 1) // tile)
        pass_ref[group] = passes
        code_column = column(code.astype(F32)).astype(jnp.int32)
        row_column = column(row.astype(F32)).astype(jnp.int32)

        def matrices(number, code=code, turn=turn, code_column=code_column, row_column=row_column):
            start = number * slots
            row_ones = ones_where(row_column == lax.broadcasted_iota(jnp.int32, (cap, block_rows), 1))
            line = lax.broadcasted_iota(jnp.int32, (r_dev * window, 1), 0)
            slot = line // window * (2 * tile) + line % window + start
            of_block = [jnp.where(turn == q, code - q * (2 * tile - window), -1) for q in range(2)]
            by_slot = jnp.concatenate([ones_where(slot == codes) for codes in of_block], axis=0)
            pick = jnp.dot(by_slot, row_ones, preferred_element_type=F32).astype(BF16)
            return pick, ones_where(lax.broadcasted_iota(jnp.int32, (cap, slots), 1) + start == code_column)

        pick_ref[group], place_ref[group] = matrices(0)
        later.append((group, passes, matrices))

    for group, passes, matrices in later:

        @pl.when(passes > 1)
        def _():
            def one_pass(number, carry):
                pick_scratch[...], place_scratch[...] = matrices(number)
                pltpu.sync_copy(pick_scratch, more_pick_ref.at[group, number - 1])
                pltpu.sync_copy(place_scratch, more_place_ref.at[group, number - 1])
                return carry

            lax.fori_loop(1, passes, one_pass, 0)


def index(parcels, numbers, earlier, groups, lists_at, r_dev, cap, tile, block_rows):
    slots = 2 * r_dev * tile
    lines = 2 * r_dev * (tile + SPARE)
    more = -(-(min(block_rows, cap) - (tile - SPARE)) // tile)
    vmem, smem = pl.BlockSpec(memory_space=pltpu.VMEM), pl.BlockSpec(memory_space=pltpu.SMEM)
    any_spec = pl.BlockSpec(memory_space=pl.ANY)
    specs = [vmem, vmem, smem, smem, any_spec, any_spec]
    args = list(parcels)
    done, aliases = 0, {}
    if earlier is not None:
        done = groups - len(parcels)
        aliases = {1 + len(parcels) + place: place for place in (0, 1, 4, 5)}
        args += list(earlier[:4]) + [in_hbm(array) for array in earlier[4:]]
    return pl.pallas_call(
        functools.partial(index_kernel, r_dev, lists_at, cap, tile, block_rows, done),
        in_specs=[smem] + [vmem] * len(parcels) + (specs if done else []),
        out_specs=specs,
        out_shape=[
            jax.ShapeDtypeStruct((groups, lines, block_rows), BF16),
            jax.ShapeDtypeStruct((groups, cap, slots), BF16),
            jax.ShapeDtypeStruct((groups,), jnp.int32),
            jax.ShapeDtypeStruct((groups * r_dev,), jnp.int32),
            pltpu.HBM((groups, more, lines, block_rows), BF16),
            pltpu.HBM((groups, more, cap, slots), BF16),
        ],
        scratch_shapes=[pltpu.VMEM((lines, block_rows), BF16), pltpu.VMEM((cap, slots), BF16)],
        input_output_aliases=aliases,
        compiler_params=params(VMEM_BYTES),
        name="index",
    )(numbers, *args)


def lay_out(heard, number_ref, signal_ref):
    n_win = len(heard)
    r_dev, samples = heard[0].shape
    for distance, span in enumerate(heard):
        begin = lax.rem(number_ref[6] + n_win - distance, n_win) * samples
        signal_ref[:r_dev, pl.ds(pl.multiple_of(begin, LANES), samples)] = span.astype(F32)
    tail = signal_ref.shape[1] - n_win * samples
    signal_ref[:r_dev, n_win * samples :] = jnp.zeros((r_dev, tail), F32)


def first_sample(number_ref, v, n_win, samples):
    return lax.rem(number_ref[6] + n_win - v, n_win) * samples + number_ref[5]


def hankel_rows(signal_ref, r, begin, width, out_ref, place):
    length = width + LANES
    signal = signal_ref[r : r + 1, pl.ds(pl.multiple_of(begin, LANES), length)]
    base = jnp.broadcast_to(signal, (SHIFT_ROWS, length))
    sublane = lax.broadcasted_iota(jnp.int32, base.shape, 0)
    for bit in (1, 2, 4):
        base = jnp.where(sublane & bit != 0, pltpu.roll(base, length - bit, 1), base)
    for first in range(0, LANES, 2 * SHIFT_ROWS):
        both = []
        for shift in (first, first + SHIFT_ROWS):
            rolled = pltpu.roll(base, length - shift, 1) if shift else base
            both.append(rolled[:, :width])
        out_ref[place, first : first + 2 * SHIFT_ROWS, :] = jnp.concatenate(both, axis=0).astype(BF16)


def hankel_kernel(v, n_win, samples, done, number_ref, *refs):
    out_ref, signal_refs = refs[-2:]
    parcel_refs = refs[: -3 if done else -2]
    r_dev = parcel_refs[0].shape[0]
    begin = first_sample(number_ref, v, n_win, samples)
    for group, parcel_ref in enumerate(parcel_refs, done):
        signal_ref = signal_refs.at[group % 2]
        heard = [parcel_ref[:, w * samples : (w + 1) * samples] for w in range(n_win)]
        lay_out(heard, number_ref, signal_ref)
        for r in range(r_dev):
            hankel_rows(signal_ref, r, begin, out_ref.shape[2], out_ref, group * r_dev + r)


def build_hankel(parcels, numbers, earlier, groups, v, n_win, samples, width):
    r_dev = parcels[0].shape[0]
    shape = (groups * r_dev, LANES, width)
    vmem = pl.BlockSpec(memory_space=pltpu.VMEM)
    done = 0 if earlier is None else groups - len(parcels)
    copies = len(parcels) * r_dev * LANES * width
    return pl.pallas_call(
        functools.partial(hankel_kernel, v, n_win, samples, done),
        in_specs=[pl.BlockSpec(memory_space=pltpu.SMEM)] + [vmem] * (len(parcels) + (1 if done else 0)),
        out_specs=vmem,
        scratch_shapes=[pltpu.VMEM((2, SHIFT_ROWS, n_win * samples + LAGS), F32)],
        out_shape=jax.ShapeDtypeStruct(shape, BF16),
        input_output_aliases={1 + len(parcels): 0} if done else {},
        cost_estimate=pl.CostEstimate(flops=copies, bytes_accessed=2 * copies, transcendentals=0),
        compiler_params=params(VMEM_BYTES // 2),
        name="hankel",
    )(numbers, *parcels, *([earlier] if done else []))


def window_of(blocks, tile):
    if len(blocks) == 2:
        return 0, 2 * tile
    return (tile - SPARE if blocks[0] else 0), tile + SPARE


def pick_rows(blocks, pieces, pick, gathered, tile):
    parts = len(pieces) // len(blocks)
    window = tile + SPARE
    shared = tile - SPARE
    rows_of_channel = window_of(blocks, tile)[1]
    r_dev, samples = gathered.shape[0] // rows_of_channel, gathered.shape[1]
    for t in range(0, samples, STEP):
        chosen = []
        for place, q in enumerate(blocks):
            block = [piece[:, t : t + STEP] for piece in pieces[place * parts : (place + 1) * parts]]
            ones = pick[q * r_dev * window : (q + 1) * r_dev * window, :]
            chosen.append(jnp.dot(ones, jnp.concatenate(block, axis=0), preferred_element_type=F32))
        if len(blocks) == 1:
            gathered[:, t : t + STEP] = chosen[0].astype(BF16)
            continue
        for r in range(r_dev):
            top, bottom = [rows[r * window : (r + 1) * window] for rows in chosen]
            rows = [top[shared:] + bottom[: window - shared]]
            if shared:
                rows = [top[:shared]] + rows + [bottom[window - shared :]]
            for place, part in zip((0, shared, window) if shared else (0,), rows):
                start = r * 2 * tile + place
                gathered[start : start + part.shape[0], t : t + STEP] = part.astype(BF16)


def multiply(gathered, hankel_ref, place, r, rows, lag):
    samples = gathered.shape[1]
    wide = jnp.concatenate(
        [hankel_ref[place, :, t + lag : t + lag + STEP] for t in range(0, samples, LANES)], axis=0
    )
    return jnp.dot(gathered[r * rows : (r + 1) * rows, :], wide, preferred_element_type=F32)


def split(total, terms, slots, lags):
    count = terms.shape[0] // 2
    upper = total.astype(BF16)
    terms[slots, lags] = upper
    terms[slice(count + slots.start, count + slots.stop), lags] = (total - upper.astype(F32)).astype(BF16)


def placed(place, terms):
    return jnp.dot(jnp.concatenate([place, place], axis=1), terms[...], preferred_element_type=F32)


def correlate_kernel(blocks, parts, v, tile, norming, prebuilt, first, last, pass_ref, count_ref, number_ref, *refs):
    refs = list(refs)
    pieces = [refs.pop(0) for _ in range(len(blocks) * parts)]
    signal_ref, pick_ref, place_ref, more_pick_ref, more_place_ref = [refs.pop(0) for _ in range(5)]
    if not first:
        sums_ref, extra_ref = refs.pop(0), refs.pop(0)
    if last:
        out_ref = refs.pop(0)
    else:
        handed_ref, left_ref = refs.pop(0), refs.pop(0)
    gathered, terms, extra, pick_scratch, place_scratch = refs[:5]
    begin, rows = window_of(blocks, tile)
    r_dev = gathered.shape[0] // rows
    samples = pieces[0].shape[1]
    lag_dev = extra.shape[1]
    group = pl.program_id(0)

    if prebuilt:
        hankel_ref, hankel_place = signal_ref, group * r_dev
    else:
        hankel_place = 0
        hankel_ref, row_ref = refs[5:]
        n_win = signal_ref.shape[2] // samples
        lay_out([signal_ref[0, :, w * samples : (w + 1) * samples] for w in range(n_win)], number_ref, row_ref)
        start = first_sample(number_ref, v, n_win, samples)
        for r in range(r_dev):
            hankel_rows(row_ref, r, start, hankel_ref.shape[2], hankel_ref, r)

    pick_rows(blocks, pieces, pick_ref.at[0], gathered, tile)
    for r in range(r_dev):
        slots = slice(r * 2 * tile + begin, r * 2 * tile + begin + rows)
        others = [slice(r * 2 * tile, slots.start), slice(slots.stop, (r + 1) * 2 * tile)]
        for lag in range(0, lag_dev, STEP):
            lags = slice(lag, lag + STEP)
            total = multiply(gathered, hankel_ref, hankel_place + r, r, rows, lag)
            if not first:
                total += sums_ref[group, slots, lags]
            if last:
                split(total * norming, terms, slots, lags)
                for other in others:
                    if other.start < other.stop:
                        split(sums_ref[group, other, lags] * norming, terms, other, lags)
            else:
                handed_ref[group, slots, lags] = total
    if last:
        out_ref[0] = placed(place_ref[0], terms)

    @pl.when(pass_ref[group] > 1)
    def _():
        if first:
            extra[...] = jnp.zeros(extra.shape, F32)
        else:
            pltpu.sync_copy(extra_ref.at[group], extra)

        def one_pass(number, carry):
            pltpu.sync_copy(more_pick_ref.at[group, number - 1], pick_scratch)
            pltpu.sync_copy(more_place_ref.at[group, number - 1], place_scratch)
            pick_rows(blocks, pieces, pick_scratch, gathered, tile)
            terms[...] = jnp.zeros(terms.shape, BF16)
            for r in range(r_dev):
                needed = count_ref[group * r_dev + r] > (number - 1) * tile
                slots = slice(r * 2 * tile + begin, r * 2 * tile + begin + rows)

                @pl.when(needed)
                def _():
                    for lag in range(0, lag_dev, STEP):
                        total = multiply(gathered, hankel_ref, hankel_place + r, r, rows, lag)
                        split(total * norming, terms, slots, slice(lag, lag + STEP))

            extra[...] += placed(place_scratch[...], terms)
            return carry

        lax.fori_loop(1, pass_ref[group], one_pass, 0)
        if last:
            out_ref[0] += extra[...]
        else:
            pltpu.sync_copy(extra, left_ref.at[group])


def correlate(blocks, pieces, signal, prebuilt, numbers, v, matrices, before, last, tile, norming, lag_dev, n_win, r_dev):
    pick, place, passes, counts, more_pick, more_place = matrices
    parts = len(pieces) // len(blocks)
    groups, cap, slots = place.shape
    samples = pieces[0].shape[1]
    width = samples - LANES + lag_dev
    rows = window_of(blocks, tile)[1]
    by_group = lambda shape: pl.BlockSpec(shape, lambda i, *_: (i, 0, 0))
    any_spec = pl.BlockSpec(memory_space=pl.ANY)
    whole_spec = pl.BlockSpec(memory_space=pltpu.VMEM)
    out_spec = pl.BlockSpec(
        (1, cap, lag_dev), lambda i, _, __, number_ref: (lax.rem(number_ref[4] + groups - i, groups), 0, 0)
    )
    sums_shape = jax.ShapeDtypeStruct((groups, slots, lag_dev), F32)
    out_shape = jax.ShapeDtypeStruct((groups, cap, lag_dev), F32)
    in_specs = [whole_spec] * len(pieces)
    in_specs.append(whole_spec if prebuilt else by_group((1,) + signal.shape[1:]))
    in_specs += [by_group((1,) + pick.shape[1:]), by_group((1,) + place.shape[1:]), any_spec, any_spec]
    args = pieces + [signal, pick, place, in_hbm(more_pick), in_hbm(more_place)]
    aliases = {}
    if before is not None:
        in_specs += [whole_spec, any_spec]
        args += [before[0], in_hbm(before[1])]
        if not last:
            aliases = {3 + len(args) - 2: 0}
    scratch = [
        pltpu.VMEM((r_dev * rows, samples), BF16),
        pltpu.VMEM((2 * slots, lag_dev), BF16),
        pltpu.VMEM((cap, lag_dev), F32),
        pltpu.VMEM(pick.shape[1:], BF16),
        pltpu.VMEM(place.shape[1:], BF16),
    ]
    if not prebuilt:
        scratch.append(pltpu.VMEM((r_dev, LANES, width), BF16))
        scratch.append(pltpu.VMEM((SHIFT_ROWS, n_win * samples + LAGS), F32))
    body = functools.partial(
        correlate_kernel, blocks, parts, v, tile, norming, prebuilt, before is None, last
    )
    return pl.pallas_call(
        body,
        grid_spec=pltpu.PrefetchScalarGridSpec(
            num_scalar_prefetch=3,
            grid=(groups,),
            in_specs=in_specs,
            out_specs=out_spec if last else [whole_spec, any_spec],
            scratch_shapes=scratch,
        ),
        out_shape=out_shape if last else [sums_shape, pltpu.HBM(out_shape.shape, F32)],
        input_output_aliases=aliases,
        cost_estimate=pl.CostEstimate(
            flops=2 * groups * r_dev * rows * samples * (lag_dev + pick.shape[2]),
            bytes_accessed=2 * groups * slots * lag_dev * 4,
            transcendentals=0,
        ),
        compiler_params=params(VMEM_BYTES if prebuilt else 2 * VMEM_BYTES),
        name="correlate",
    )(passes, counts, numbers, *args)


def shards(sources, receivers, plan, pair_index, keep):
    _, block_rows, samples = sources.shape
    r_dev = receivers.shape[0]
    n_chan = lax.axis_size("chan")
    n_win = lax.axis_size("win")
    n_rep = lax.axis_size("rep")
    cap = pair_index.shape[3]
    lag_dev = LAGS // (n_win * n_rep)
    tile = max(16, cap // 8)
    norming = 1.0 / math.sqrt(samples * n_win)
    width = samples - LANES + lag_dev
    prebuilt = n_chan * r_dev * n_win * LANES * width * 2 <= HANKEL_BYTES

    heard = [receivers] + [turned(receivers, "win", v) for v in range(1, n_win)]
    owns = own_rows(sources[0], n_rep)
    parcels, numbers = pack(plan, heard, pair_index[0, 0], keep[0, 0], n_rep, lag_dev, block_rows, n_chan)
    own_parcel = parcels[0]
    parcels = [turned(parcels[k], "chan", k) for k in range(1, n_chan)]
    matrices = index([own_parcel], numbers, None, n_chan, n_win * samples, r_dev, cap, tile, block_rows)
    if prebuilt:
        signals = [build_hankel([own_parcel], numbers, None, n_chan, v, n_win, samples, width) for v in range(n_win)]

    arrived = [{0: own} for own in owns]

    def relay(step):
        for there in arrived:
            there[step] = swapped(there[1 - step], "chan", 0)
            if step < n_chan - 1:
                there[-step] = swapped(there[step - 1], "chan", 1)

    def after_arrival(step, value):
        for there in arrived:
            for key in (step, -step):
                if key in there:
                    value = lax.optimization_barrier((value, there[key]))[0]
        return value

    def before_start(step, value):
        for there in arrived:
            for key in (1 - step, step - 1):
                there[key] = lax.optimization_barrier((value, there[key]))[1]

    def halves(piece):
        return [piece] + [turned(piece, "rep", -u) for u in range(1, n_rep)]

    def spans(piece):
        return [piece] + [turned(piece, "win", v) for v in range(1, n_win)]

    relay(1)
    before_start(2, (matrices, parcels, signals) if prebuilt else (matrices, parcels))
    parcels = after_arrival(1, parcels)
    relay(2)
    matrices = index(parcels, numbers, matrices, n_chan, n_win * samples, r_dev, cap, tile, block_rows)
    if prebuilt:
        signals[0] = build_hankel(parcels, numbers, signals[0], n_chan, 0, n_win, samples, width)
        before_start(3, (matrices, signals[0]))
    else:
        signals = [jnp.stack([own_parcel] + parcels)[:, :, : n_win * samples]] * n_win
    reach = range(-(n_chan - 2), n_chan - 1)
    near = choose(numbers, 2, arrived, [offset for offset in reach if offset in arrived[0]])
    if prebuilt:
        parcels = after_arrival(2, parcels)
        parcels, near = lax.optimization_barrier((parcels, near))
        for v in range(1, n_win):
            signals[v] = build_hankel(parcels, numbers, signals[v], n_chan, v, n_win, samples, width)
    for step in range(3, n_chan):
        relay(step)
    near_spans = spans(near)
    if prebuilt:
        signals, near_spans = after_arrival(n_chan - 1, (signals, near_spans))
    far_spans = spans(choose(numbers, 3, arrived, sorted(arrived[0])))

    calls = [(0, (0, 1))] + [(v, (q,)) for q in range(2) for v in range(1, n_win)]
    result = None
    for v, blocks in calls:
        if blocks == (1,):
            far_spans, result = lax.optimization_barrier((far_spans, result))
        pieces = [half for q in blocks for half in halves((near_spans, far_spans)[q][v])]
        result = correlate(
            blocks, pieces, signals[v], prebuilt, numbers, v, matrices, result, (v, blocks) == calls[-1], tile, norming,
            lag_dev, n_win, r_dev,
        )
    return result[None, None]


def solution(mesh):
    placed_at = (
        P(("grp", "chan"), None, "win"),
        P(("grp", "chan"), "win"),
        P("grp", None),
        P("grp", "chan", None, None),
        P("grp", "chan", None, None),
    )
    return jax.shard_map(
        shards,
        mesh=mesh,
        in_specs=placed_at,
        out_specs=P(("grp", "chan"), None, None, None, ("win", "rep")),
        check_vma=False,
    )
```

```python
import functools
import math

import jax
import jax.numpy as jnp
from jax import lax
from jax.experimental import pallas as pl
from jax.experimental.pallas import tpu as pltpu
from jax.sharding import PartitionSpec as P

LAGS = 2048
LANES = 128
SHIFT_ROWS = 8
STEP = 2 * LANES
SPARE = 16
DIGIT = 64
HANKEL_BYTES = 24 * 2**20
VMEM_BYTES = 26 * 2**20
F32 = jnp.float32
BF16 = jnp.bfloat16


def swapped(block, axis, first):
    size = lax.axis_size(axis)
    route = []
    for i in range(first, size - 1, 2):
        route += [(i, i + 1), (i + 1, i)]
    return lax.ppermute(block, axis, route)


def turned(block, axis, distance):
    size = lax.axis_size(axis)
    return lax.ppermute(block, axis, [(i, (i + distance) % size) for i in range(size)])


def in_hbm(array):
    return pltpu.with_memory_space_constraint(array, pltpu.HBM)


def params(vmem):
    return pltpu.CompilerParams(vmem_limit_bytes=vmem)


def pack_kernel(halves, lags, block_rows, n_win, plan_hbm, pair_hbm, keep_hbm, *refs):
    span_hbms, refs = refs[:n_win], refs[n_win:]
    plan_ref, pair_ref, keep_ref, span_refs, digit_ref, sems = refs[-6:]
    parcel_refs, number_ref = refs[:-7], refs[-7]
    small = []
    moves = [(plan_hbm, plan_ref), (pair_hbm, pair_ref), (keep_hbm, keep_ref)]
    moves += [(span, span_refs.at[v]) for v, span in enumerate(span_hbms)]
    for place, (source, target) in enumerate(moves):
        small.append(pltpu.make_async_copy(source, target, sems.at[place]))
        small[-1].start()
    r_dev, samples = span_refs.shape[1:]
    n_chan, cap = pair_ref.shape
    chan, win, rep = lax.axis_index("chan"), lax.axis_index("win"), lax.axis_index("rep")
    for copy in small:
        copy.wait()

    packed = pair_ref[...] * 2 + keep_ref[...]
    digit_ref[:n_chan, :] = jnp.concatenate([packed // DIGIT, packed % DIGIT], axis=1).astype(F32)
    heard = [span_refs[v].astype(F32) for v in range(n_win)]
    part = 2 * cap // r_dev
    spare = parcel_refs[0].shape[1] - n_win * samples - part
    for distance, parcel_ref in enumerate(parcel_refs):
        digits = digit_ref[pl.ds(lax.rem(chan + distance, n_chan), 1), :]
        lists = [digits[:, i * part : (i + 1) * part] for i in range(r_dev)]
        parcel = heard + [jnp.concatenate(lists, axis=0)]
        if spare:
            parcel.append(jnp.zeros((r_dev, spare), F32))
        parcel_ref[...] = jnp.concatenate(parcel, axis=1).astype(BF16)

    one, two = plan_ref[0, 0], plan_ref[0, 1]
    nearer = jnp.where(jnp.abs(one - chan) <= jnp.abs(two - chan), 0, 1)
    sign = jnp.where(chan % 2 == 0, 1, -1)
    number_ref[0] = nearer
    number_ref[1] = block_rows - rep * (block_rows // halves)
    number_ref[2] = sign * (jnp.where(nearer == 0, one, two) - chan)
    number_ref[3] = sign * (jnp.where(nearer == 0, two, one) - chan)
    number_ref[4] = chan
    number_ref[5] = (win * halves + rep) * lags
    number_ref[6] = win


def pack(plan, spans, pair_index, keep, halves, lags, block_rows, n_chan):
    n_win = len(spans)
    r_dev, samples = spans[0].shape
    cap = pair_index.shape[1]
    beside = -(-2 * cap // r_dev // LANES) * LANES
    vmem, smem = pl.BlockSpec(memory_space=pltpu.VMEM), pl.BlockSpec(memory_space=pltpu.SMEM)
    shapes = [jax.ShapeDtypeStruct((r_dev, n_win * samples + beside), BF16)] * n_chan
    shapes.append(jax.ShapeDtypeStruct((7,), jnp.int32))
    *parcels, numbers = pl.pallas_call(
        functools.partial(pack_kernel, halves, lags, block_rows, n_win),
        in_specs=[pl.BlockSpec(memory_space=pl.ANY)] * (3 + n_win),
        out_specs=[vmem] * n_chan + [smem],
        out_shape=shapes,
        scratch_shapes=[
            pltpu.SMEM(plan.shape, plan.dtype),
            pltpu.VMEM(pair_index.shape, pair_index.dtype),
            pltpu.VMEM(keep.shape, keep.dtype),
            pltpu.VMEM((n_win, r_dev, samples), BF16),
            pltpu.VMEM((-(-n_chan // SHIFT_ROWS) * SHIFT_ROWS, 2 * cap), F32),
            pltpu.SemaphoreType.DMA((3 + n_win,)),
        ],
        compiler_params=params(VMEM_BYTES // 2),
        name="pack",
    )(*[in_hbm(a) for a in (plan, pair_index, keep, spans[0])], *spans[1:])
    return parcels, numbers


def own_kernel(source_ref, own_ref, sem):
    rows = own_ref.shape[0]
    start = pl.multiple_of(lax.axis_index("rep") * rows, rows)
    copy = pltpu.make_async_copy(source_ref.at[pl.ds(start, rows)], own_ref, sem)
    copy.start()
    copy.wait()


def own_rows(sources, halves):
    block_rows, samples = sources.shape
    return pl.pallas_call(
        own_kernel,
        in_specs=[pl.BlockSpec(memory_space=pl.ANY)],
        out_specs=pl.BlockSpec(memory_space=pltpu.VMEM),
        out_shape=jax.ShapeDtypeStruct((block_rows // halves, samples), BF16),
        scratch_shapes=[pltpu.SemaphoreType.DMA],
        compiler_params=params(VMEM_BYTES // 4),
        name="own_rows",
    )(in_hbm(sources))


def choose_kernel(which, offsets, number_ref, *refs):
    out_ref, sem = refs[-2:]
    for offset, block_ref in zip(offsets, refs):
        copy = pltpu.make_async_copy(block_ref, out_ref, sem)

        @pl.when(number_ref[which] == offset)
        def _():
            copy.start()

    copy.wait()


def choose(numbers, which, arrived, offsets):
    blocks = [arrived[offset] for offset in offsets]
    return pl.pallas_call(
        functools.partial(choose_kernel, which, offsets),
        in_specs=[pl.BlockSpec(memory_space=pltpu.SMEM)] + [pl.BlockSpec(memory_space=pl.ANY)] * len(blocks),
        out_specs=pl.BlockSpec(memory_space=pltpu.VMEM),
        out_shape=jax.ShapeDtypeStruct(blocks[0].shape, BF16),
        scratch_shapes=[pltpu.SemaphoreType.DMA],
        compiler_params=params(VMEM_BYTES // 4),
        name="choose",
    )(numbers, *blocks)


def column(row):
    return jnp.broadcast_to(row, (SHIFT_ROWS, row.shape[1])).T[:, :1]


def ones_where(condition):
    return jnp.where(condition, 1.0, 0.0).astype(BF16)


def index_kernel(r_dev, lists_at, cap, tile, block_rows, done, number_ref, *refs):
    pick_ref, place_ref, pass_ref, count_ref, more_pick_ref, more_place_ref, pick_scratch, place_scratch = refs[-8:]
    parcel_refs = refs[:-8]
    if done:
        parcel_refs, (_, _, earlier_pass_ref, earlier_count_ref, _, _) = parcel_refs[:-6], parcel_refs[-6:]
        for group in range(done):
            pass_ref[group] = earlier_pass_ref[group]
            for r in range(r_dev):
                count_ref[group * r_dev + r] = earlier_count_ref[group * r_dev + r]
    nearer, offset = number_ref[0], number_ref[1]
    slots = 2 * r_dev * tile
    window = tile + SPARE
    part = 2 * cap // r_dev
    below = lax.broadcasted_iota(jnp.int32, (cap, cap), 0) < lax.broadcasted_iota(jnp.int32, (cap, cap), 1)
    below = ones_where(below)
    later = []
    for group, parcel_ref in enumerate(parcel_refs, done):
        digits = parcel_ref[:, lists_at:].astype(F32)
        digits = jnp.concatenate([digits[i : i + 1, :part] for i in range(r_dev)], axis=1).astype(jnp.int32)
        packed = digits[:, :cap] * DIGIT + digits[:, cap:]
        pairs, kept = packed // 2, packed % 2 == 1
        source_row, receiver = pairs // r_dev, pairs % r_dev
        turn = jnp.where(source_row // block_rows == nearer, 0, 1)
        row = (source_row + offset) % block_rows
        segment = jnp.where(kept, turn * r_dev + receiver, -1)
        member = lax.broadcasted_iota(jnp.int32, (2 * r_dev, cap), 0) == segment
        earlier = jnp.dot(ones_where(member), below, preferred_element_type=F32)
        of_pair = lambda values: jnp.sum(jnp.where(member, values, 0.0), axis=0, keepdims=True).astype(jnp.int32)
        counts = jnp.sum(jnp.where(member, 1.0, 0.0), axis=1, keepdims=True)
        from_top = jnp.minimum(counts[:r_dev], window)
        from_bottom = jnp.minimum(jnp.minimum(counts[r_dev:], 2.0 * tile - from_top), window)
        first_pass = jnp.concatenate([from_top, from_bottom], axis=0)
        first_slot = jnp.concatenate([jnp.zeros_like(from_top), 2.0 * tile - from_bottom], axis=0)
        rank, limit, begin = of_pair(earlier), of_pair(first_pass), of_pair(first_slot)
        rest = rank - limit
        code = jnp.where(rest < 0, begin + rank, (1 + rest // tile) * slots + turn * tile + rest % tile)
        code = jnp.where(kept, code + receiver * 2 * tile, -1)
        left = counts - first_pass
        which = lax.broadcasted_iota(jnp.int32, left.shape, 0) % r_dev
        passes = 1
        for r in range(r_dev):
            count = jnp.max(jnp.where(which == r, left, 0.0)).astype(jnp.int32)
            count_ref[group * r_dev + r] = count
            passes = jnp.maximum(passes, 1 + (count + tile - 1) // tile)
        pass_ref[group] = passes
        code_column = column(code.astype(F32)).astype(jnp.int32)
        row_column = column(row.astype(F32)).astype(jnp.int32)

        def matrices(number, code=code, turn=turn, code_column=code_column, row_column=row_column):
            start = number * slots
            row_ones = ones_where(row_column == lax.broadcasted_iota(jnp.int32, (cap, block_rows), 1))
            line = lax.broadcasted_iota(jnp.int32, (r_dev * window, 1), 0)
            slot = line // window * (2 * tile) + line % window + start
            of_block = [jnp.where(turn == q, code - q * (2 * tile - window), -1) for q in range(2)]
            by_slot = jnp.concatenate([ones_where(slot == codes) for codes in of_block], axis=0)
            pick = jnp.dot(by_slot, row_ones, preferred_element_type=F32).astype(BF16)
            return pick, ones_where(lax.broadcasted_iota(jnp.int32, (cap, slots), 1) + start == code_column)

        pick_ref[group], place_ref[group] = matrices(0)
        later.append((group, passes, matrices))

    for group, passes, matrices in later:

        @pl.when(passes > 1)
        def _():
            def one_pass(number, carry):
                pick_scratch[...], place_scratch[...] = matrices(number)
                pltpu.sync_copy(pick_scratch, more_pick_ref.at[group, number - 1])
                pltpu.sync_copy(place_scratch, more_place_ref.at[group, number - 1])
                return carry

            lax.fori_loop(1, passes, one_pass, 0)


def index(parcels, numbers, earlier, groups, lists_at, r_dev, cap, tile, block_rows):
    slots = 2 * r_dev * tile
    lines = 2 * r_dev * (tile + SPARE)
    more = -(-(min(block_rows, cap) - (tile - SPARE)) // tile)
    vmem, smem = pl.BlockSpec(memory_space=pltpu.VMEM), pl.BlockSpec(memory_space=pltpu.SMEM)
    any_spec = pl.BlockSpec(memory_space=pl.ANY)
    specs = [vmem, vmem, smem, smem, any_spec, any_spec]
    args = list(parcels)
    done, aliases = 0, {}
    if earlier is not None:
        done = groups - len(parcels)
        aliases = {1 + len(parcels) + place: place for place in (0, 1, 4, 5)}
        args += list(earlier[:4]) + [in_hbm(array) for array in earlier[4:]]
    return pl.pallas_call(
        functools.partial(index_kernel, r_dev, lists_at, cap, tile, block_rows, done),
        in_specs=[smem] + [vmem] * len(parcels) + (specs if done else []),
        out_specs=specs,
        out_shape=[
            jax.ShapeDtypeStruct((groups, lines, block_rows), BF16),
            jax.ShapeDtypeStruct((groups, cap, slots), BF16),
            jax.ShapeDtypeStruct((groups,), jnp.int32),
            jax.ShapeDtypeStruct((groups * r_dev,), jnp.int32),
            pltpu.HBM((groups, more, lines, block_rows), BF16),
            pltpu.HBM((groups, more, cap, slots), BF16),
        ],
        scratch_shapes=[pltpu.VMEM((lines, block_rows), BF16), pltpu.VMEM((cap, slots), BF16)],
        input_output_aliases=aliases,
        compiler_params=params(VMEM_BYTES),
        name="index",
    )(numbers, *args)


def lay_out(heard, number_ref, signal_ref):
    n_win = len(heard)
    r_dev, samples = heard[0].shape
    for distance, span in enumerate(heard):
        begin = lax.rem(number_ref[6] + n_win - distance, n_win) * samples
        signal_ref[:r_dev, pl.ds(pl.multiple_of(begin, LANES), samples)] = span.astype(F32)
    tail = signal_ref.shape[1] - n_win * samples
    signal_ref[:r_dev, n_win * samples :] = jnp.zeros((r_dev, tail), F32)


def first_sample(number_ref, v, n_win, samples):
    return lax.rem(number_ref[6] + n_win - v, n_win) * samples + number_ref[5]


def hankel_rows(signal_ref, r, begin, width, out_ref, place):
    length = width + LANES
    signal = signal_ref[r : r + 1, pl.ds(pl.multiple_of(begin, LANES), length)]
    base = jnp.broadcast_to(signal, (SHIFT_ROWS, length))
    sublane = lax.broadcasted_iota(jnp.int32, base.shape, 0)
    for bit in (1, 2, 4):
        base = jnp.where(sublane & bit != 0, pltpu.roll(base, length - bit, 1), base)
    for first in range(0, LANES, 2 * SHIFT_ROWS):
        both = []
        for shift in (first, first + SHIFT_ROWS):
            rolled = pltpu.roll(base, length - shift, 1) if shift else base
            both.append(rolled[:, :width])
        out_ref[place, first : first + 2 * SHIFT_ROWS, :] = jnp.concatenate(both, axis=0).astype(BF16)


def hankel_kernel(v, n_win, samples, done, number_ref, *refs):
    out_ref, signal_refs = refs[-2:]
    parcel_refs = refs[: -3 if done else -2]
    r_dev = parcel_refs[0].shape[0]
    begin = first_sample(number_ref, v, n_win, samples)
    for group, parcel_ref in enumerate(parcel_refs, done):
        signal_ref = signal_refs.at[group % 2]
        heard = [parcel_ref[:, w * samples : (w + 1) * samples] for w in range(n_win)]
        lay_out(heard, number_ref, signal_ref)
        for r in range(r_dev):
            hankel_rows(signal_ref, r, begin, out_ref.shape[2], out_ref, group * r_dev + r)


def build_hankel(parcels, numbers, earlier, groups, v, n_win, samples, width):
    r_dev = parcels[0].shape[0]
    shape = (groups * r_dev, LANES, width)
    vmem = pl.BlockSpec(memory_space=pltpu.VMEM)
    done = 0 if earlier is None else groups - len(parcels)
    copies = len(parcels) * r_dev * LANES * width
    return pl.pallas_call(
        functools.partial(hankel_kernel, v, n_win, samples, done),
        in_specs=[pl.BlockSpec(memory_space=pltpu.SMEM)] + [vmem] * (len(parcels) + (1 if done else 0)),
        out_specs=vmem,
        scratch_shapes=[pltpu.VMEM((2, SHIFT_ROWS, n_win * samples + LAGS), F32)],
        out_shape=jax.ShapeDtypeStruct(shape, BF16),
        input_output_aliases={1 + len(parcels): 0} if done else {},
        cost_estimate=pl.CostEstimate(flops=copies, bytes_accessed=2 * copies, transcendentals=0),
        compiler_params=params(VMEM_BYTES // 2),
        name="hankel",
    )(numbers, *parcels, *([earlier] if done else []))


def pick_rows(pieces, pick, gathered, margin, tile):
    window = tile + SPARE
    shared = tile - SPARE
    r_dev, samples = gathered.shape[0] // (2 * tile), pieces[0][0].shape[1]
    for t in range(0, samples, STEP):
        chosen = []
        for q in range(2):
            block = jnp.concatenate([piece[:, t : t + STEP] for piece in pieces[q]], axis=0)
            ones = pick[q * r_dev * window : (q + 1) * r_dev * window, :]
            chosen.append(jnp.dot(ones, block, preferred_element_type=F32))
        for r in range(r_dev):
            top, bottom = [rows[r * window : (r + 1) * window] for rows in chosen]
            rows = [top[shared:] + bottom[: window - shared]]
            if shared:
                rows = [top[:shared]] + rows + [bottom[window - shared :]]
            for place, part in zip((0, shared, window) if shared else (0,), rows):
                start = r * 2 * tile + place
                gathered[start : start + part.shape[0], margin + t : margin + t + STEP] = part.astype(BF16)


def margin_of(lag_dev):
    return lag_dev - STEP


def multiply(gathered, hankel_ref, place, r, tile, lag_dev):
    margin = margin_of(lag_dev)
    length = gathered.shape[1] - margin
    rows = slice(r * 2 * tile, (r + 1) * 2 * tile)
    shifted = [gathered[rows, margin - lag : margin - lag + length] for lag in range(0, lag_dev, STEP)]
    tiles = [hankel_ref[place, :, t : t + STEP] for t in range(0, length, LANES)]
    both = jnp.dot(jnp.concatenate(shifted, axis=0), jnp.concatenate(tiles, axis=0), preferred_element_type=F32)
    return [(slice(lag, lag + STEP), both[lag // STEP * 2 * tile :][: 2 * tile]) for lag in range(0, lag_dev, STEP)]


def split(total, high, low, slots, lags):
    upper = total.astype(BF16)
    high[slots, lags] = upper
    low[slots, lags] = (total - upper.astype(F32)).astype(BF16)


def placed(place, high, low):
    return jnp.dot(place, high[...], preferred_element_type=F32) + jnp.dot(
        place, low[...], preferred_element_type=F32
    )


def correlate_kernel(counts, v, tile, norming, prebuilt, first, last, pass_ref, count_ref, number_ref, *refs):
    refs = list(refs)
    pieces = [[refs.pop(0) for _ in range(count)] for count in counts]
    signal_ref, pick_ref, place_ref, more_pick_ref, more_place_ref = [refs.pop(0) for _ in range(5)]
    if not first:
        sums_ref, extra_ref = refs.pop(0), refs.pop(0)
    if last:
        out_ref = refs.pop(0)
    else:
        handed_ref, left_ref = refs.pop(0), refs.pop(0)
    gathered, high, low, extra, pick_scratch, place_scratch = refs[:6]
    r_dev = gathered.shape[0] // (2 * tile)
    samples = pieces[0][0].shape[1]
    lag_dev = extra.shape[1]
    group = pl.program_id(0)

    if prebuilt:
        hankel_ref, hankel_place = signal_ref, group * r_dev
    else:
        hankel_place = 0
        hankel_ref, row_ref = refs[6:]
        n_win = signal_ref.shape[2] // samples
        lay_out([signal_ref[0, :, w * samples : (w + 1) * samples] for w in range(n_win)], number_ref, row_ref)
        begin = first_sample(number_ref, v, n_win, samples)
        for r in range(r_dev):
            hankel_rows(row_ref, r, begin, hankel_ref.shape[2], hankel_ref, r)

    margin = margin_of(lag_dev)
    if margin:

        @pl.when(group == 0)
        def _():
            for start in (0, margin + samples):
                gathered[:, start : start + margin] = jnp.zeros((gathered.shape[0], margin), BF16)

    pick_rows(pieces, pick_ref.at[0], gathered, margin, tile)
    for r in range(r_dev):
        slots = slice(r * 2 * tile, (r + 1) * 2 * tile)
        for lags, total in multiply(gathered, hankel_ref, hankel_place + r, r, tile, lag_dev):
            if not first:
                total += sums_ref[group, slots, lags]
            if last:
                split(total * norming, high, low, slots, lags)
            else:
                handed_ref[group, slots, lags] = total
    if last:
        out_ref[0] = placed(place_ref[0], high, low)

    @pl.when(pass_ref[group] > 1)
    def _():
        if first:
            extra[...] = jnp.zeros(extra.shape, F32)
        else:
            pltpu.sync_copy(extra_ref.at[group], extra)

        def one_pass(number, carry):
            pltpu.sync_copy(more_pick_ref.at[group, number - 1], pick_scratch)
            pltpu.sync_copy(more_place_ref.at[group, number - 1], place_scratch)
            pick_rows(pieces, pick_scratch, gathered, margin, tile)
            for r in range(r_dev):
                needed = count_ref[group * r_dev + r] > (number - 1) * tile
                slots = slice(r * 2 * tile, (r + 1) * 2 * tile)

                @pl.when(needed)
                def _():
                    for lags, total in multiply(gathered, hankel_ref, hankel_place + r, r, tile, lag_dev):
                        split(total * norming, high, low, slots, lags)

                @pl.when(jnp.logical_not(needed))
                def _():
                    high[slots, :] = jnp.zeros((2 * tile, lag_dev), BF16)
                    low[slots, :] = jnp.zeros((2 * tile, lag_dev), BF16)

            extra[...] += placed(place_scratch[...], high, low)
            return carry

        lax.fori_loop(1, pass_ref[group], one_pass, 0)
        if last:
            out_ref[0] += extra[...]
        else:
            pltpu.sync_copy(extra, left_ref.at[group])


def correlate(pieces, signal, prebuilt, numbers, v, matrices, before, last, tile, norming, lag_dev, n_win, r_dev):
    pick, place, passes, counts, more_pick, more_place = matrices
    groups, cap, slots = place.shape
    counts_of_blocks = [len(of_block) for of_block in pieces]
    pieces = [piece for of_block in pieces for piece in of_block]
    samples = pieces[0].shape[1]
    width = samples - LANES + lag_dev
    by_group = lambda shape: pl.BlockSpec(shape, lambda i, *_: (i, 0, 0))
    any_spec = pl.BlockSpec(memory_space=pl.ANY)
    whole_spec = pl.BlockSpec(memory_space=pltpu.VMEM)
    out_spec = pl.BlockSpec(
        (1, cap, lag_dev), lambda i, _, __, number_ref: (lax.rem(number_ref[4] + groups - i, groups), 0, 0)
    )
    sums_shape = jax.ShapeDtypeStruct((groups, slots, lag_dev), F32)
    out_shape = jax.ShapeDtypeStruct((groups, cap, lag_dev), F32)
    in_specs = [whole_spec] * len(pieces)
    in_specs.append(whole_spec if prebuilt else by_group((1,) + signal.shape[1:]))
    in_specs += [by_group((1,) + pick.shape[1:]), by_group((1,) + place.shape[1:]), any_spec, any_spec]
    args = pieces + [signal, pick, place, in_hbm(more_pick), in_hbm(more_place)]
    if before is not None:
        in_specs += [whole_spec, any_spec]
        args += [before[0], in_hbm(before[1])]
    scratch = [
        pltpu.VMEM((slots, samples + 2 * margin_of(lag_dev)), BF16),
        pltpu.VMEM((slots, lag_dev), BF16),
        pltpu.VMEM((slots, lag_dev), BF16),
        pltpu.VMEM((cap, lag_dev), F32),
        pltpu.VMEM(pick.shape[1:], BF16),
        pltpu.VMEM(place.shape[1:], BF16),
    ]
    if not prebuilt:
        scratch.append(pltpu.VMEM((r_dev, LANES, width), BF16))
        scratch.append(pltpu.VMEM((SHIFT_ROWS, n_win * samples + LAGS), F32))
    body = functools.partial(correlate_kernel, counts_of_blocks, v, tile, norming, prebuilt, before is None, last)
    return pl.pallas_call(
        body,
        grid_spec=pltpu.PrefetchScalarGridSpec(
            num_scalar_prefetch=3,
            grid=(groups,),
            in_specs=in_specs,
            out_specs=out_spec if last else [whole_spec, any_spec],
            scratch_shapes=scratch,
        ),
        out_shape=out_shape if last else [sums_shape, pltpu.HBM(out_shape.shape, F32)],
        cost_estimate=pl.CostEstimate(
            flops=4 * groups * r_dev * tile * samples * (lag_dev + pick.shape[2]),
            bytes_accessed=signal.size * signal.dtype.itemsize + 2 * groups * cap * lag_dev * 4,
            transcendentals=0,
        ),
        compiler_params=params(VMEM_BYTES if prebuilt else 2 * VMEM_BYTES),
        name="correlate",
    )(passes, counts, numbers, *args)


def shards(sources, receivers, plan, pair_index, keep):
    _, block_rows, samples = sources.shape
    r_dev = receivers.shape[0]
    n_chan = lax.axis_size("chan")
    n_win = lax.axis_size("win")
    n_rep = lax.axis_size("rep")
    cap = pair_index.shape[3]
    lag_dev = LAGS // (n_win * n_rep)
    tile = max(16, cap // 8)
    norming = 1.0 / math.sqrt(samples * n_win)
    width = samples - LANES + lag_dev
    prebuilt = n_chan * r_dev * n_win * LANES * width * 2 <= HANKEL_BYTES

    heard = [receivers] + [turned(receivers, "win", v) for v in range(1, n_win)]
    own = own_rows(sources[0], n_rep)
    parcels, numbers = pack(plan, heard, pair_index[0, 0], keep[0, 0], n_rep, lag_dev, block_rows, n_chan)
    own_parcel = parcels[0]
    parcels = [turned(parcels[k], "chan", k) for k in range(1, n_chan)]
    matrices = index([own_parcel], numbers, None, n_chan, n_win * samples, r_dev, cap, tile, block_rows)
    if prebuilt:
        signals = [build_hankel([own_parcel], numbers, None, n_chan, v, n_win, samples, width) for v in range(n_win)]

    arrived = {0: own}

    def relay(step):
        arrived[step] = swapped(arrived[1 - step], "chan", 0)
        if step < n_chan - 1:
            arrived[-step] = swapped(arrived[step - 1], "chan", 1)

    def after_arrival(step, value):
        keys = [key for key in (step, -step) if key in arrived]
        return lax.optimization_barrier((value, [arrived[key] for key in keys]))[0]

    def before_start(step, value):
        for key in (1 - step, step - 1):
            arrived[key] = lax.optimization_barrier((value, arrived[key]))[1]

    def halves(piece):
        return [piece] + [turned(piece, "rep", -u) for u in range(1, n_rep)]

    def spans(piece):
        return [piece] + [turned(piece, "win", v) for v in range(1, n_win)]

    relay(1)
    before_start(2, (matrices, parcels, signals) if prebuilt else (matrices, parcels))
    parcels = after_arrival(1, parcels)
    relay(2)
    matrices = index(parcels, numbers, matrices, n_chan, n_win * samples, r_dev, cap, tile, block_rows)
    if prebuilt:
        signals[0] = build_hankel(parcels, numbers, signals[0], n_chan, 0, n_win, samples, width)
        before_start(3, (matrices, signals[0]))
    else:
        signals = [jnp.stack([own_parcel] + parcels)[:, :, : n_win * samples]] * n_win
    reach = [offset for offset in range(-(n_chan - 2), n_chan - 1) if offset in arrived]
    near = choose(numbers, 2, arrived, reach)
    before_start(3, near)
    if prebuilt:
        parcels = after_arrival(2, parcels)
        parcels, near = lax.optimization_barrier((parcels, near))
        for v in range(1, n_win):
            signals[v] = build_hankel(parcels, numbers, signals[v], n_chan, v, n_win, samples, width)
    for step in range(3, n_chan):
        relay(step)
    near_spans = spans(near)
    if prebuilt:
        signals, near_spans = after_arrival(n_chan - 1, (signals, near_spans))
        arrived[n_chan - 1] = lax.optimization_barrier((near_spans, arrived[n_chan - 1]))[1]
    far_spans = spans(choose(numbers, 3, arrived, sorted(arrived)))

    result = None
    for v in range(n_win):
        if v:
            near_spans, far_spans, result = lax.optimization_barrier((near_spans, far_spans, result))
        pieces = halves(near_spans[v]), halves(far_spans[v])
        result = correlate(
            pieces, signals[v], prebuilt, numbers, v, matrices, result, v == n_win - 1, tile, norming, lag_dev, n_win,
            r_dev,
        )
    return result[None, None]


def solution(mesh):
    placed_at = (
        P(("grp", "chan"), None, "win"),
        P(("grp", "chan"), "win"),
        P("grp", None),
        P("grp", "chan", None, None),
        P("grp", "chan", None, None),
    )
    return jax.shard_map(
        shards,
        mesh=mesh,
        in_specs=placed_at,
        out_specs=P(("grp", "chan"), None, None, None, ("win", "rep")),
        check_vma=False,
    )
```

```python
import functools
import math

import jax
import jax.numpy as jnp
from jax import lax
from jax.experimental import pallas as pl
from jax.experimental.pallas import tpu as pltpu
from jax.sharding import PartitionSpec as P

LAGS = 2048
LANES = 128
SHIFT_ROWS = 8
STEP = 2 * LANES
CHAINS = 1
SPARE = 16
DIGIT = 64
HANKEL_BYTES = 24 * 2**20
VMEM_BYTES = 26 * 2**20
F32 = jnp.float32
BF16 = jnp.bfloat16


def swapped(block, axis, first):
    size = lax.axis_size(axis)
    route = []
    for i in range(first, size - 1, 2):
        route += [(i, i + 1), (i + 1, i)]
    return lax.ppermute(block, axis, route)


def ends_swapped(block, axis):
    last = lax.axis_size(axis) - 1
    return lax.ppermute(block, axis, [(0, last), (last, 0)])


def turned(block, axis, distance):
    size = lax.axis_size(axis)
    return lax.ppermute(block, axis, [(i, (i + distance) % size) for i in range(size)])


def in_hbm(array):
    return pltpu.with_memory_space_constraint(array, pltpu.HBM)


def params(vmem):
    return pltpu.CompilerParams(vmem_limit_bytes=vmem)


def pack_kernel(halves, lags, block_rows, n_win, plan_hbm, pair_hbm, keep_hbm, *refs):
    span_hbms, refs = refs[:n_win], refs[n_win:]
    plan_ref, pair_ref, keep_ref, span_refs, digit_ref, sems = refs[-6:]
    parcel_refs, number_ref = refs[:-7], refs[-7]
    small = []
    moves = [(plan_hbm, plan_ref), (pair_hbm, pair_ref), (keep_hbm, keep_ref)]
    moves += [(span, span_refs.at[v]) for v, span in enumerate(span_hbms)]
    for place, (source, target) in enumerate(moves):
        small.append(pltpu.make_async_copy(source, target, sems.at[place]))
        small[-1].start()
    r_dev, samples = span_refs.shape[1:]
    n_chan, cap = pair_ref.shape
    chan, win, rep = lax.axis_index("chan"), lax.axis_index("win"), lax.axis_index("rep")
    for copy in small:
        copy.wait()

    packed = pair_ref[...] * 2 + keep_ref[...]
    digit_ref[:n_chan, :] = jnp.concatenate([packed // DIGIT, packed % DIGIT], axis=1).astype(F32)
    heard = [span_refs[v].astype(F32) for v in range(n_win)]
    part = 2 * cap // r_dev
    spare = parcel_refs[0].shape[1] - n_win * samples - part
    for distance, parcel_ref in enumerate(parcel_refs):
        digits = digit_ref[pl.ds(lax.rem(chan + distance, n_chan), 1), :]
        lists = [digits[:, i * part : (i + 1) * part] for i in range(r_dev)]
        parcel = heard + [jnp.concatenate(lists, axis=0)]
        if spare:
            parcel.append(jnp.zeros((r_dev, spare), F32))
        parcel_ref[...] = jnp.concatenate(parcel, axis=1).astype(BF16)

    one, two = plan_ref[0, 0], plan_ref[0, 1]
    nearer = jnp.where(jnp.abs(one - chan) <= jnp.abs(two - chan), 0, 1)
    sign = jnp.where(chan % 2 == 0, 1, -1)
    number_ref[0] = nearer
    number_ref[1] = block_rows - rep * (block_rows // halves)
    number_ref[2] = sign * (jnp.where(nearer == 0, one, two) - chan)
    number_ref[3] = sign * (jnp.where(nearer == 0, two, one) - chan)
    number_ref[4] = chan
    number_ref[5] = (win * halves + rep) * lags
    number_ref[6] = win


def pack(plan, spans, pair_index, keep, halves, lags, block_rows, n_chan):
    n_win = len(spans)
    r_dev, samples = spans[0].shape
    cap = pair_index.shape[1]
    beside = -(-2 * cap // r_dev // LANES) * LANES
    vmem, smem = pl.BlockSpec(memory_space=pltpu.VMEM), pl.BlockSpec(memory_space=pltpu.SMEM)
    shapes = [jax.ShapeDtypeStruct((r_dev, n_win * samples + beside), BF16)] * n_chan
    shapes.append(jax.ShapeDtypeStruct((7,), jnp.int32))
    *parcels, numbers = pl.pallas_call(
        functools.partial(pack_kernel, halves, lags, block_rows, n_win),
        in_specs=[pl.BlockSpec(memory_space=pl.ANY)] * (3 + n_win),
        out_specs=[vmem] * n_chan + [smem],
        out_shape=shapes,
        scratch_shapes=[
            pltpu.SMEM(plan.shape, plan.dtype),
            pltpu.VMEM(pair_index.shape, pair_index.dtype),
            pltpu.VMEM(keep.shape, keep.dtype),
            pltpu.VMEM((n_win, r_dev, samples), BF16),
            pltpu.VMEM((-(-n_chan // SHIFT_ROWS) * SHIFT_ROWS, 2 * cap), F32),
            pltpu.SemaphoreType.DMA((3 + n_win,)),
        ],
        compiler_params=params(VMEM_BYTES // 2),
        name="pack",
    )(*[in_hbm(a) for a in (plan, pair_index, keep, spans[0])], *spans[1:])
    return parcels, numbers


def own_kernel(source_ref, *refs):
    chain_refs, sems = refs[:-1], refs[-1]
    rows = chain_refs[0].shape[0]
    copies = []
    for chain, chain_ref in enumerate(chain_refs):
        start = pl.multiple_of((lax.axis_index("rep") * CHAINS + chain) * rows, rows)
        copies.append(pltpu.make_async_copy(source_ref.at[pl.ds(start, rows)], chain_ref, sems.at[chain]))
        copies[-1].start()
    for copy in copies:
        copy.wait()


def own_rows(sources, halves):
    block_rows, samples = sources.shape
    shape = jax.ShapeDtypeStruct((block_rows // halves // CHAINS, samples), BF16)
    return pl.pallas_call(
        own_kernel,
        in_specs=[pl.BlockSpec(memory_space=pl.ANY)],
        out_specs=[pl.BlockSpec(memory_space=pltpu.VMEM)] * CHAINS,
        out_shape=[shape] * CHAINS,
        scratch_shapes=[pltpu.SemaphoreType.DMA((CHAINS,))],
        compiler_params=params(VMEM_BYTES // 4),
        name="own_rows",
    )(in_hbm(sources))


def choose_kernel(which, offsets, number_ref, *refs):
    out_ref, sems = refs[-2:]
    rows = out_ref.shape[0] // CHAINS
    where = number_ref[which]
    waits = []
    for chain in range(CHAINS):
        target = out_ref.at[pl.ds(chain * rows, rows)]
        for place, offset in enumerate(offsets):
            copy = pltpu.make_async_copy(refs[chain * len(offsets) + place], target, sems.at[chain])

            @pl.when(where == offset)
            def _():
                copy.start()

        waits.append(copy)
    for copy in waits:
        copy.wait()


def choose(numbers, which, arrived, offsets):
    pieces = [there[offset] for there in arrived for offset in offsets]
    rows, samples = pieces[0].shape
    any_spec = pl.BlockSpec(memory_space=pl.ANY)
    return pl.pallas_call(
        functools.partial(choose_kernel, which, offsets),
        in_specs=[pl.BlockSpec(memory_space=pltpu.SMEM)] + [any_spec] * len(pieces),
        out_specs=pl.BlockSpec(memory_space=pltpu.VMEM),
        out_shape=jax.ShapeDtypeStruct((rows * CHAINS, samples), BF16),
        scratch_shapes=[pltpu.SemaphoreType.DMA((CHAINS,))],
        compiler_params=params(VMEM_BYTES // 4),
        name="choose",
    )(numbers, *pieces)


def column(row):
    return jnp.broadcast_to(row, (SHIFT_ROWS, row.shape[1])).T[:, :1]


def ones_where(condition):
    return jnp.where(condition, 1.0, 0.0).astype(BF16)


def index_kernel(r_dev, lists_at, cap, tile, block_rows, done, number_ref, *refs):
    pick_ref, place_ref, pass_ref, count_ref, more_pick_ref, more_place_ref, pick_scratch, place_scratch = refs[-8:]
    parcel_refs = refs[:-8]
    if done:
        parcel_refs, (_, _, earlier_pass_ref, earlier_count_ref, _, _) = parcel_refs[:-6], parcel_refs[-6:]
        for group in range(done):
            pass_ref[group] = earlier_pass_ref[group]
            for r in range(r_dev):
                count_ref[group * r_dev + r] = earlier_count_ref[group * r_dev + r]
    nearer, offset = number_ref[0], number_ref[1]
    slots = 2 * r_dev * tile
    window = tile + SPARE
    part = 2 * cap // r_dev
    below = lax.broadcasted_iota(jnp.int32, (cap, cap), 0) < lax.broadcasted_iota(jnp.int32, (cap, cap), 1)
    below = ones_where(below)
    later = []
    for group, parcel_ref in enumerate(parcel_refs, done):
        digits = parcel_ref[:, lists_at:].astype(F32)
        digits = jnp.concatenate([digits[i : i + 1, :part] for i in range(r_dev)], axis=1).astype(jnp.int32)
        packed = digits[:, :cap] * DIGIT + digits[:, cap:]
        pairs, kept = packed // 2, packed % 2 == 1
        source_row, receiver = pairs // r_dev, pairs % r_dev
        turn = jnp.where(source_row // block_rows == nearer, 0, 1)
        row = (source_row + offset) % block_rows
        segment = jnp.where(kept, turn * r_dev + receiver, -1)
        member = lax.broadcasted_iota(jnp.int32, (2 * r_dev, cap), 0) == segment
        earlier = jnp.dot(ones_where(member), below, preferred_element_type=F32)
        of_pair = lambda values: jnp.sum(jnp.where(member, values, 0.0), axis=0, keepdims=True).astype(jnp.int32)
        counts = jnp.sum(jnp.where(member, 1.0, 0.0), axis=1, keepdims=True)
        from_top = jnp.minimum(counts[:r_dev], window)
        from_bottom = jnp.minimum(jnp.minimum(counts[r_dev:], 2.0 * tile - from_top), window)
        first_pass = jnp.concatenate([from_top, from_bottom], axis=0)
        first_slot = jnp.concatenate([jnp.zeros_like(from_top), 2.0 * tile - from_bottom], axis=0)
        rank, limit, begin = of_pair(earlier), of_pair(first_pass), of_pair(first_slot)
        rest = rank - limit
        code = jnp.where(rest < 0, begin + rank, (1 + rest // tile) * slots + turn * tile + rest % tile)
        code = jnp.where(kept, code + receiver * 2 * tile, -1)
        left = counts - first_pass
        which = lax.broadcasted_iota(jnp.int32, left.shape, 0) % r_dev
        passes = 1
        for r in range(r_dev):
            count = jnp.max(jnp.where(which == r, left, 0.0)).astype(jnp.int32)
            count_ref[group * r_dev + r] = count
            passes = jnp.maximum(passes, 1 + (count + tile - 1) // tile)
        pass_ref[group] = passes
        code_column = column(code.astype(F32)).astype(jnp.int32)
        row_column = column(row.astype(F32)).astype(jnp.int32)

        def matrices(number, code=code, turn=turn, code_column=code_column, row_column=row_column):
            start = number * slots
            row_ones = ones_where(row_column == lax.broadcasted_iota(jnp.int32, (cap, block_rows), 1))
            line = lax.broadcasted_iota(jnp.int32, (r_dev * window, 1), 0)
            slot = line // window * (2 * tile) + line % window + start
            of_block = [jnp.where(turn == q, code - q * (2 * tile - window), -1) for q in range(2)]
            by_slot = jnp.concatenate([ones_where(slot == codes) for codes in of_block], axis=0)
            pick = jnp.dot(by_slot, row_ones, preferred_element_type=F32).astype(BF16)
            return pick, ones_where(lax.broadcasted_iota(jnp.int32, (cap, slots), 1) + start == code_column)

        pick_ref[group], place_ref[group] = matrices(0)
        later.append((group, passes, matrices))

    for group, passes, matrices in later:

        @pl.when(passes > 1)
        def _():
            def one_pass(number, carry):
                pick_scratch[...], place_scratch[...] = matrices(number)
                pltpu.sync_copy(pick_scratch, more_pick_ref.at[group, number - 1])
                pltpu.sync_copy(place_scratch, more_place_ref.at[group, number - 1])
                return carry

            lax.fori_loop(1, passes, one_pass, 0)


def index(parcels, numbers, earlier, groups, lists_at, r_dev, cap, tile, block_rows):
    slots = 2 * r_dev * tile
    lines = 2 * r_dev * (tile + SPARE)
    more = -(-(min(block_rows, cap) - (tile - SPARE)) // tile)
    vmem, smem = pl.BlockSpec(memory_space=pltpu.VMEM), pl.BlockSpec(memory_space=pltpu.SMEM)
    any_spec = pl.BlockSpec(memory_space=pl.ANY)
    specs = [vmem, vmem, smem, smem, any_spec, any_spec]
    args = list(parcels)
    done, aliases = 0, {}
    if earlier is not None:
        done = groups - len(parcels)
        aliases = {1 + len(parcels) + place: place for place in (0, 1, 4, 5)}
        args += list(earlier[:4]) + [in_hbm(array) for array in earlier[4:]]
    return pl.pallas_call(
        functools.partial(index_kernel, r_dev, lists_at, cap, tile, block_rows, done),
        in_specs=[smem] + [vmem] * len(parcels) + (specs if done else []),
        out_specs=specs,
        out_shape=[
            jax.ShapeDtypeStruct((groups, lines, block_rows), BF16),
            jax.ShapeDtypeStruct((groups, cap, slots), BF16),
            jax.ShapeDtypeStruct((groups,), jnp.int32),
            jax.ShapeDtypeStruct((groups * r_dev,), jnp.int32),
            pltpu.HBM((groups, more, lines, block_rows), BF16),
            pltpu.HBM((groups, more, cap, slots), BF16),
        ],
        scratch_shapes=[pltpu.VMEM((lines, block_rows), BF16), pltpu.VMEM((cap, slots), BF16)],
        input_output_aliases=aliases,
        compiler_params=params(VMEM_BYTES),
        name="index",
    )(numbers, *args)


def lay_out(heard, number_ref, signal_ref):
    n_win = len(heard)
    r_dev, samples = heard[0].shape
    for distance, span in enumerate(heard):
        begin = lax.rem(number_ref[6] + n_win - distance, n_win) * samples
        signal_ref[:r_dev, pl.ds(pl.multiple_of(begin, LANES), samples)] = span.astype(F32)
    tail = signal_ref.shape[1] - n_win * samples
    signal_ref[:r_dev, n_win * samples :] = jnp.zeros((r_dev, tail), F32)


def first_sample(number_ref, v, n_win, samples):
    return lax.rem(number_ref[6] + n_win - v, n_win) * samples + number_ref[5]


def hankel_rows(signal_ref, r, begin, width, out_ref, place):
    length = width + LANES
    signal = signal_ref[r : r + 1, pl.ds(pl.multiple_of(begin, LANES), length)]
    base = jnp.broadcast_to(signal, (SHIFT_ROWS, length))
    sublane = lax.broadcasted_iota(jnp.int32, base.shape, 0)
    for bit in (1, 2, 4):
        base = jnp.where(sublane & bit != 0, pltpu.roll(base, length - bit, 1), base)
    for first in range(0, LANES, 2 * SHIFT_ROWS):
        both = []
        for shift in (first, first + SHIFT_ROWS):
            rolled = pltpu.roll(base, length - shift, 1) if shift else base
            both.append(rolled[:, :width])
        out_ref[place, first : first + 2 * SHIFT_ROWS, :] = jnp.concatenate(both, axis=0).astype(BF16)


def hankel_kernel(v, n_win, samples, done, number_ref, *refs):
    out_ref, signal_refs = refs[-2:]
    parcel_refs = refs[: -3 if done else -2]
    r_dev = parcel_refs[0].shape[0]
    begin = first_sample(number_ref, v, n_win, samples)
    for group, parcel_ref in enumerate(parcel_refs, done):
        signal_ref = signal_refs.at[group % 2]
        heard = [parcel_ref[:, w * samples : (w + 1) * samples] for w in range(n_win)]
        lay_out(heard, number_ref, signal_ref)
        for r in range(r_dev):
            hankel_rows(signal_ref, r, begin, out_ref.shape[2], out_ref, group * r_dev + r)


def build_hankel(parcels, numbers, earlier, groups, v, n_win, samples, width):
    r_dev = parcels[0].shape[0]
    shape = (groups * r_dev, LANES, width)
    vmem = pl.BlockSpec(memory_space=pltpu.VMEM)
    done = 0 if earlier is None else groups - len(parcels)
    copies = len(parcels) * r_dev * LANES * width
    return pl.pallas_call(
        functools.partial(hankel_kernel, v, n_win, samples, done),
        in_specs=[pl.BlockSpec(memory_space=pltpu.SMEM)] + [vmem] * (len(parcels) + (1 if done else 0)),
        out_specs=vmem,
        scratch_shapes=[pltpu.VMEM((2, SHIFT_ROWS, n_win * samples + LAGS), F32)],
        out_shape=jax.ShapeDtypeStruct(shape, BF16),
        input_output_aliases={1 + len(parcels): 0} if done else {},
        cost_estimate=pl.CostEstimate(flops=copies, bytes_accessed=2 * copies, transcendentals=0),
        compiler_params=params(VMEM_BYTES // 2),
        name="hankel",
    )(numbers, *parcels, *([earlier] if done else []))


def pick_rows(pieces, pick, gathered, tile):
    parts = len(pieces) // 2
    window = tile + SPARE
    shared = tile - SPARE
    r_dev, samples = gathered.shape[0] // (2 * tile), gathered.shape[1]
    for t in range(0, samples, STEP):
        chosen = []
        for q in range(2):
            block = jnp.concatenate([piece[:, t : t + STEP] for piece in pieces[q * parts : (q + 1) * parts]], axis=0)
            ones = pick[q * r_dev * window : (q + 1) * r_dev * window, :]
            chosen.append(jnp.dot(ones, block, preferred_element_type=F32))
        for r in range(r_dev):
            top, bottom = [rows[r * window : (r + 1) * window] for rows in chosen]
            rows = [top[shared:] + bottom[: window - shared]]
            if shared:
                rows = [top[:shared]] + rows + [bottom[window - shared :]]
            for place, part in zip((0, shared, window) if shared else (0,), rows):
                start = r * 2 * tile + place
                gathered[start : start + part.shape[0], t : t + STEP] = part.astype(BF16)


def multiply(gathered, hankel_ref, place, r, tile, lag):
    samples = gathered.shape[1]
    wide = jnp.concatenate(
        [hankel_ref[place, :, t + lag : t + lag + STEP] for t in range(0, samples, LANES)], axis=0
    )
    return jnp.dot(gathered[r * 2 * tile : (r + 1) * 2 * tile, :], wide, preferred_element_type=F32)


def split(total, high, low, slots, lags):
    upper = total.astype(BF16)
    high[slots, lags] = upper
    low[slots, lags] = (total - upper.astype(F32)).astype(BF16)


def placed(place, high, low):
    return jnp.dot(place, high[...], preferred_element_type=F32) + jnp.dot(
        place, low[...], preferred_element_type=F32
    )


def correlate_kernel(parts, v, tile, norming, prebuilt, first, last, pass_ref, count_ref, number_ref, *refs):
    refs = list(refs)
    pieces = [refs.pop(0) for _ in range(2 * parts)]
    signal_ref, pick_ref, place_ref, more_pick_ref, more_place_ref = [refs.pop(0) for _ in range(5)]
    if not first:
        sums_ref, extra_ref = refs.pop(0), refs.pop(0)
    if last:
        out_ref = refs.pop(0)
    else:
        handed_ref, left_ref = refs.pop(0), refs.pop(0)
    gathered, high, low, extra, pick_scratch, place_scratch = refs[:6]
    r_dev = gathered.shape[0] // (2 * tile)
    samples = pieces[0].shape[1]
    lag_dev = extra.shape[1]
    group = pl.program_id(0)

    if prebuilt:
        hankel_ref, hankel_place = signal_ref, group * r_dev
    else:
        hankel_place = 0
        hankel_ref, row_ref = refs[6:]
        n_win = signal_ref.shape[2] // samples
        lay_out([signal_ref[0, :, w * samples : (w + 1) * samples] for w in range(n_win)], number_ref, row_ref)
        begin = first_sample(number_ref, v, n_win, samples)
        for r in range(r_dev):
            hankel_rows(row_ref, r, begin, hankel_ref.shape[2], hankel_ref, r)

    pick_rows(pieces, pick_ref.at[0], gathered, tile)
    for r in range(r_dev):
        slots = slice(r * 2 * tile, (r + 1) * 2 * tile)
        for lag in range(0, lag_dev, STEP):
            lags = slice(lag, lag + STEP)
            total = multiply(gathered, hankel_ref, hankel_place + r, r, tile, lag)
            if not first:
                total += sums_ref[group, slots, lags]
            if last:
                split(total * norming, high, low, slots, lags)
            else:
                handed_ref[group, slots, lags] = total
    if last:
        out_ref[0] = placed(place_ref[0], high, low)

    @pl.when(pass_ref[group] > 1)
    def _():
        if first:
            extra[...] = jnp.zeros(extra.shape, F32)
        else:
            pltpu.sync_copy(extra_ref.at[group], extra)

        def one_pass(number, carry):
            pltpu.sync_copy(more_pick_ref.at[group, number - 1], pick_scratch)
            pltpu.sync_copy(more_place_ref.at[group, number - 1], place_scratch)
            pick_rows(pieces, pick_scratch, gathered, tile)
            for r in range(r_dev):
                needed = count_ref[group * r_dev + r] > (number - 1) * tile
                slots = slice(r * 2 * tile, (r + 1) * 2 * tile)

                @pl.when(needed)
                def _():
                    for lag in range(0, lag_dev, STEP):
                        total = multiply(gathered, hankel_ref, hankel_place + r, r, tile, lag)
                        split(total * norming, high, low, slots, slice(lag, lag + STEP))

                @pl.when(jnp.logical_not(needed))
                def _():
                    high[slots, :] = jnp.zeros((2 * tile, lag_dev), BF16)
                    low[slots, :] = jnp.zeros((2 * tile, lag_dev), BF16)

            extra[...] += placed(place_scratch[...], high, low)
            return carry

        lax.fori_loop(1, pass_ref[group], one_pass, 0)
        if last:
            out_ref[0] += extra[...]
        else:
            pltpu.sync_copy(extra, left_ref.at[group])


def correlate(pieces, signal, prebuilt, numbers, v, matrices, before, last, tile, norming, lag_dev, n_win, r_dev):
    pick, place, passes, counts, more_pick, more_place = matrices
    parts = len(pieces) // 2
    groups, cap, slots = place.shape
    part_rows, samples = pieces[0].shape
    width = samples - LANES + lag_dev
    by_group = lambda shape: pl.BlockSpec(shape, lambda i, *_: (i, 0, 0))
    any_spec = pl.BlockSpec(memory_space=pl.ANY)
    whole_spec = pl.BlockSpec(memory_space=pltpu.VMEM)
    out_spec = pl.BlockSpec(
        (1, cap, lag_dev), lambda i, _, __, number_ref: (lax.rem(number_ref[4] + groups - i, groups), 0, 0)
    )
    sums_shape = jax.ShapeDtypeStruct((groups, slots, lag_dev), F32)
    out_shape = jax.ShapeDtypeStruct((groups, cap, lag_dev), F32)
    in_specs = [whole_spec] * len(pieces)
    in_specs.append(whole_spec if prebuilt else by_group((1,) + signal.shape[1:]))
    in_specs += [by_group((1,) + pick.shape[1:]), by_group((1,) + place.shape[1:]), any_spec, any_spec]
    args = pieces + [signal, pick, place, in_hbm(more_pick), in_hbm(more_place)]
    if before is not None:
        in_specs += [whole_spec, any_spec]
        args += [before[0], in_hbm(before[1])]
    scratch = [
        pltpu.VMEM((slots, samples), BF16),
        pltpu.VMEM((slots, lag_dev), BF16),
        pltpu.VMEM((slots, lag_dev), BF16),
        pltpu.VMEM((cap, lag_dev), F32),
        pltpu.VMEM(pick.shape[1:], BF16),
        pltpu.VMEM(place.shape[1:], BF16),
    ]
    if not prebuilt:
        scratch.append(pltpu.VMEM((r_dev, LANES, width), BF16))
        scratch.append(pltpu.VMEM((SHIFT_ROWS, n_win * samples + LAGS), F32))
    body = functools.partial(correlate_kernel, parts, v, tile, norming, prebuilt, before is None, last)
    return pl.pallas_call(
        body,
        grid_spec=pltpu.PrefetchScalarGridSpec(
            num_scalar_prefetch=3,
            grid=(groups,),
            in_specs=in_specs,
            out_specs=out_spec if last else [whole_spec, any_spec],
            scratch_shapes=scratch,
        ),
        out_shape=out_shape if last else [sums_shape, pltpu.HBM(out_shape.shape, F32)],
        cost_estimate=pl.CostEstimate(
            flops=4 * groups * r_dev * tile * samples * (lag_dev + parts * part_rows),
            bytes_accessed=signal.size * signal.dtype.itemsize + 2 * groups * cap * lag_dev * 4,
            transcendentals=0,
        ),
        compiler_params=params(VMEM_BYTES if prebuilt else 2 * VMEM_BYTES),
        name="correlate",
    )(passes, counts, numbers, *args)


def shards(sources, receivers, plan, pair_index, keep):
    _, block_rows, samples = sources.shape
    r_dev = receivers.shape[0]
    n_chan = lax.axis_size("chan")
    n_win = lax.axis_size("win")
    n_rep = lax.axis_size("rep")
    cap = pair_index.shape[3]
    lag_dev = LAGS // (n_win * n_rep)
    tile = max(16, cap // 8)
    norming = 1.0 / math.sqrt(samples * n_win)
    width = samples - LANES + lag_dev
    prebuilt = n_chan * r_dev * n_win * LANES * width * 2 <= HANKEL_BYTES

    heard = [receivers] + [turned(receivers, "win", v) for v in range(1, n_win)]
    owns = own_rows(sources[0], n_rep)
    parcels, numbers = pack(plan, heard, pair_index[0, 0], keep[0, 0], n_rep, lag_dev, block_rows, n_chan)
    own_parcel = parcels[0]
    parcels = [turned(parcels[k], "chan", k) for k in range(1, n_chan)]
    matrices = index([own_parcel], numbers, None, n_chan, n_win * samples, r_dev, cap, tile, block_rows)
    if prebuilt:
        signals = [build_hankel([own_parcel], numbers, None, n_chan, v, n_win, samples, width) for v in range(n_win)]

    arrived = [{0: own} for own in owns]

    def relay(step):
        for there in arrived:
            there[step] = swapped(there[1 - step], "chan", 0)
            there[-step] = swapped(there[step - 1], "chan", 1)

    def after_arrival(step, value):
        for there in arrived:
            for key in (step, -step):
                if key in there:
                    value = lax.optimization_barrier((value, there[key]))[0]
        return value

    def before_start(step, value):
        for there in arrived:
            for key in (1 - step, step - 1):
                there[key] = lax.optimization_barrier((value, there[key]))[1]

    def halves(piece):
        return [piece] + [turned(piece, "rep", -u) for u in range(1, n_rep)]

    def spans(piece):
        return [piece] + [turned(piece, "win", v) for v in range(1, n_win)]

    relay(1)
    before_start(2, (matrices, parcels, signals) if prebuilt else (matrices, parcels))
    parcels = after_arrival(1, parcels)
    relay(2)
    matrices = index(parcels, numbers, matrices, n_chan, n_win * samples, r_dev, cap, tile, block_rows)
    if prebuilt:
        signals[0] = build_hankel(parcels, numbers, signals[0], n_chan, 0, n_win, samples, width)
        before_start(3, (matrices, signals[0]))
    else:
        signals = [jnp.stack([own_parcel] + parcels)[:, :, : n_win * samples]] * n_win
    own_late = [lax.optimization_barrier((matrices, own))[1] for own in owns]
    reach = range(-(n_chan - 2), n_chan - 1)
    near = choose(numbers, 2, arrived, [offset for offset in reach if offset in arrived[0]])
    if prebuilt:
        parcels = after_arrival(2, parcels)
        parcels, near = lax.optimization_barrier((parcels, near))
        for v in range(1, n_win):
            signals[v] = build_hankel(parcels, numbers, signals[v], n_chan, v, n_win, samples, width)
    for step in range(3, n_chan - 1):
        relay(step)
    for there, own in zip(arrived, own_late):
        there[n_chan - 1] = ends_swapped(own, "chan")
    near_spans = spans(near)
    if prebuilt:
        near_spans = after_arrival(n_chan - 1, near_spans)
        for there in arrived:
            there[n_chan - 1] = lax.optimization_barrier((signals, there[n_chan - 1]))[1]
    far_spans = spans(choose(numbers, 3, arrived, sorted(arrived[0])))

    result = None
    for v in range(n_win):
        if v:
            near_spans, far_spans, result = lax.optimization_barrier((near_spans, far_spans, result))
        result = correlate(
            halves(near_spans[v]) + halves(far_spans[v]), signals[v], prebuilt, numbers, v, matrices, result, v == n_win - 1,
            tile, norming, lag_dev, n_win, r_dev,
        )
    return result[None, None]


def solution(mesh):
    placed_at = (
        P(("grp", "chan"), None, "win"),
        P(("grp", "chan"), "win"),
        P("grp", None),
        P("grp", "chan", None, None),
        P("grp", "chan", None, None),
    )
    return jax.shard_map(
        shards,
        mesh=mesh,
        in_specs=placed_at,
        out_specs=P(("grp", "chan"), None, None, None, ("win", "rep")),
        check_vma=False,
    )
```

```python
import functools
import math

import jax
import jax.numpy as jnp
from jax import lax
from jax.experimental import pallas as pl
from jax.experimental.pallas import tpu as pltpu
from jax.sharding import PartitionSpec as P

LAGS = 2048
LANES = 128
SHIFT_ROWS = 8
STEP = 2 * LANES
CHAINS = 1
SPARE = 16
DIGIT = 64
HANKEL_BYTES = 24 * 2**20
VMEM_BYTES = 26 * 2**20
F32 = jnp.float32
BF16 = jnp.bfloat16


def swapped(block, axis, first):
    size = lax.axis_size(axis)
    route = []
    for i in range(first, size - 1, 2):
        route += [(i, i + 1), (i + 1, i)]
    return lax.ppermute(block, axis, route)


def turned(block, axis, distance):
    size = lax.axis_size(axis)
    return lax.ppermute(block, axis, [(i, (i + distance) % size) for i in range(size)])


def in_hbm(array):
    return pltpu.with_memory_space_constraint(array, pltpu.HBM)


def params(vmem):
    return pltpu.CompilerParams(vmem_limit_bytes=vmem)


def pack_kernel(halves, lags, block_rows, n_win, plan_hbm, pair_hbm, keep_hbm, *refs):
    span_hbms, refs = refs[:n_win], refs[n_win:]
    plan_ref, pair_ref, keep_ref, span_refs, digit_ref, sems = refs[-6:]
    parcel_refs, number_ref = refs[:-7], refs[-7]
    small = []
    moves = [(plan_hbm, plan_ref), (pair_hbm, pair_ref), (keep_hbm, keep_ref)]
    moves += [(span, span_refs.at[v]) for v, span in enumerate(span_hbms)]
    for place, (source, target) in enumerate(moves):
        small.append(pltpu.make_async_copy(source, target, sems.at[place]))
        small[-1].start()
    r_dev, samples = span_refs.shape[1:]
    n_chan, cap = pair_ref.shape
    chan, win, rep = lax.axis_index("chan"), lax.axis_index("win"), lax.axis_index("rep")
    for copy in small:
        copy.wait()

    packed = pair_ref[...] * 2 + keep_ref[...]
    digit_ref[:n_chan, :] = jnp.concatenate([packed // DIGIT, packed % DIGIT], axis=1).astype(F32)
    heard = [span_refs[v].astype(F32) for v in range(n_win)]
    part = 2 * cap // r_dev
    spare = parcel_refs[0].shape[1] - n_win * samples - part
    for distance, parcel_ref in enumerate(parcel_refs):
        digits = digit_ref[pl.ds(lax.rem(chan + distance, n_chan), 1), :]
        lists = [digits[:, i * part : (i + 1) * part] for i in range(r_dev)]
        parcel = heard + [jnp.concatenate(lists, axis=0)]
        if spare:
            parcel.append(jnp.zeros((r_dev, spare), F32))
        parcel_ref[...] = jnp.concatenate(parcel, axis=1).astype(BF16)

    one, two = plan_ref[0, 0], plan_ref[0, 1]
    nearer = jnp.where(jnp.abs(one - chan) <= jnp.abs(two - chan), 0, 1)
    sign = jnp.where(chan % 2 == 0, 1, -1)
    number_ref[0] = nearer
    number_ref[1] = block_rows - rep * (block_rows // halves)
    number_ref[2] = sign * (jnp.where(nearer == 0, one, two) - chan)
    number_ref[3] = sign * (jnp.where(nearer == 0, two, one) - chan)
    number_ref[4] = chan
    number_ref[5] = (win * halves + rep) * lags
    number_ref[6] = win


def pack(plan, spans, pair_index, keep, halves, lags, block_rows, n_chan):
    n_win = len(spans)
    r_dev, samples = spans[0].shape
    cap = pair_index.shape[1]
    beside = -(-2 * cap // r_dev // LANES) * LANES
    vmem, smem = pl.BlockSpec(memory_space=pltpu.VMEM), pl.BlockSpec(memory_space=pltpu.SMEM)
    shapes = [jax.ShapeDtypeStruct((r_dev, n_win * samples + beside), BF16)] * n_chan
    shapes.append(jax.ShapeDtypeStruct((7,), jnp.int32))
    *parcels, numbers = pl.pallas_call(
        functools.partial(pack_kernel, halves, lags, block_rows, n_win),
        in_specs=[pl.BlockSpec(memory_space=pl.ANY)] * (3 + n_win),
        out_specs=[vmem] * n_chan + [smem],
        out_shape=shapes,
        scratch_shapes=[
            pltpu.SMEM(plan.shape, plan.dtype),
            pltpu.VMEM(pair_index.shape, pair_index.dtype),
            pltpu.VMEM(keep.shape, keep.dtype),
            pltpu.VMEM((n_win, r_dev, samples), BF16),
            pltpu.VMEM((-(-n_chan // SHIFT_ROWS) * SHIFT_ROWS, 2 * cap), F32),
            pltpu.SemaphoreType.DMA((3 + n_win,)),
        ],
        compiler_params=params(VMEM_BYTES // 2),
        name="pack",
    )(*[in_hbm(a) for a in (plan, pair_index, keep, spans[0])], *spans[1:])
    return parcels, numbers


def own_kernel(source_ref, *refs):
    chain_refs, sems = refs[:-1], refs[-1]
    rows = chain_refs[0].shape[0]
    copies = []
    for chain, chain_ref in enumerate(chain_refs):
        start = pl.multiple_of((lax.axis_index("rep") * CHAINS + chain) * rows, rows)
        copies.append(pltpu.make_async_copy(source_ref.at[pl.ds(start, rows)], chain_ref, sems.at[chain]))
        copies[-1].start()
    for copy in copies:
        copy.wait()


def own_rows(sources, halves):
    block_rows, samples = sources.shape
    shape = jax.ShapeDtypeStruct((block_rows // halves // CHAINS, samples), BF16)
    return pl.pallas_call(
        own_kernel,
        in_specs=[pl.BlockSpec(memory_space=pl.ANY)],
        out_specs=[pl.BlockSpec(memory_space=pltpu.VMEM)] * CHAINS,
        out_shape=[shape] * CHAINS,
        scratch_shapes=[pltpu.SemaphoreType.DMA((CHAINS,))],
        compiler_params=params(VMEM_BYTES // 4),
        name="own_rows",
    )(in_hbm(sources))


def choose_kernel(which, offsets, number_ref, *refs):
    out_ref, sems = refs[-2:]
    rows = out_ref.shape[0] // CHAINS
    where = number_ref[which]
    waits = []
    for chain in range(CHAINS):
        target = out_ref.at[pl.ds(chain * rows, rows)]
        for place, offset in enumerate(offsets):
            copy = pltpu.make_async_copy(refs[chain * len(offsets) + place], target, sems.at[chain])

            @pl.when(where == offset)
            def _():
                copy.start()

        waits.append(copy)
    for copy in waits:
        copy.wait()


def choose(numbers, which, arrived, offsets):
    pieces = [there[offset] for there in arrived for offset in offsets]
    rows, samples = pieces[0].shape
    any_spec = pl.BlockSpec(memory_space=pl.ANY)
    return pl.pallas_call(
        functools.partial(choose_kernel, which, offsets),
        in_specs=[pl.BlockSpec(memory_space=pltpu.SMEM)] + [any_spec] * len(pieces),
        out_specs=pl.BlockSpec(memory_space=pltpu.VMEM),
        out_shape=jax.ShapeDtypeStruct((rows * CHAINS, samples), BF16),
        scratch_shapes=[pltpu.SemaphoreType.DMA((CHAINS,))],
        compiler_params=params(VMEM_BYTES // 4),
        name="choose",
    )(numbers, *pieces)


def column(row):
    return jnp.broadcast_to(row, (SHIFT_ROWS, row.shape[1])).T[:, :1]


def ones_where(condition):
    return jnp.where(condition, 1.0, 0.0).astype(BF16)


def index_kernel(r_dev, lists_at, cap, tile, block_rows, done, number_ref, *refs):
    pick_ref, place_ref, pass_ref, count_ref, more_pick_ref, more_place_ref, pick_scratch, place_scratch = refs[-8:]
    parcel_refs = refs[:-8]
    if done:
        parcel_refs, (_, _, earlier_pass_ref, earlier_count_ref, _, _) = parcel_refs[:-6], parcel_refs[-6:]
        for group in range(done):
            pass_ref[group] = earlier_pass_ref[group]
            for r in range(r_dev):
                count_ref[group * r_dev + r] = earlier_count_ref[group * r_dev + r]
    nearer, offset = number_ref[0], number_ref[1]
    slots = 2 * r_dev * tile
    window = tile + SPARE
    part = 2 * cap // r_dev
    below = lax.broadcasted_iota(jnp.int32, (cap, cap), 0) < lax.broadcasted_iota(jnp.int32, (cap, cap), 1)
    below = ones_where(below)
    later = []
    for group, parcel_ref in enumerate(parcel_refs, done):
        digits = parcel_ref[:, lists_at:].astype(F32)
        digits = jnp.concatenate([digits[i : i + 1, :part] for i in range(r_dev)], axis=1).astype(jnp.int32)
        packed = digits[:, :cap] * DIGIT + digits[:, cap:]
        pairs, kept = packed // 2, packed % 2 == 1
        source_row, receiver = pairs // r_dev, pairs % r_dev
        turn = jnp.where(source_row // block_rows == nearer, 0, 1)
        row = (source_row + offset) % block_rows
        segment = jnp.where(kept, turn * r_dev + receiver, -1)
        member = lax.broadcasted_iota(jnp.int32, (2 * r_dev, cap), 0) == segment
        earlier = jnp.dot(ones_where(member), below, preferred_element_type=F32)
        of_pair = lambda values: jnp.sum(jnp.where(member, values, 0.0), axis=0, keepdims=True).astype(jnp.int32)
        counts = jnp.sum(jnp.where(member, 1.0, 0.0), axis=1, keepdims=True)
        from_top = jnp.minimum(counts[:r_dev], window)
        from_bottom = jnp.minimum(jnp.minimum(counts[r_dev:], 2.0 * tile - from_top), window)
        first_pass = jnp.concatenate([from_top, from_bottom], axis=0)
        first_slot = jnp.concatenate([jnp.zeros_like(from_top), 2.0 * tile - from_bottom], axis=0)
        rank, limit, begin = of_pair(earlier), of_pair(first_pass), of_pair(first_slot)
        rest = rank - limit
        code = jnp.where(rest < 0, begin + rank, (1 + rest // tile) * slots + turn * tile + rest % tile)
        code = jnp.where(kept, code + receiver * 2 * tile, -1)
        left = counts - first_pass
        which = lax.broadcasted_iota(jnp.int32, left.shape, 0) % r_dev
        passes = 1
        for r in range(r_dev):
            count = jnp.max(jnp.where(which == r, left, 0.0)).astype(jnp.int32)
            count_ref[group * r_dev + r] = count
            passes = jnp.maximum(passes, 1 + (count + tile - 1) // tile)
        pass_ref[group] = passes
        code_column = column(code.astype(F32)).astype(jnp.int32)
        row_column = column(row.astype(F32)).astype(jnp.int32)

        def matrices(number, code=code, turn=turn, code_column=code_column, row_column=row_column):
            start = number * slots
            row_ones = ones_where(row_column == lax.broadcasted_iota(jnp.int32, (cap, block_rows), 1))
            line = lax.broadcasted_iota(jnp.int32, (r_dev * window, 1), 0)
            slot = line // window * (2 * tile) + line % window + start
            of_block = [jnp.where(turn == q, code - q * (2 * tile - window), -1) for q in range(2)]
            by_slot = jnp.concatenate([ones_where(slot == codes) for codes in of_block], axis=0)
            pick = jnp.dot(by_slot, row_ones, preferred_element_type=F32).astype(BF16)
            return pick, ones_where(lax.broadcasted_iota(jnp.int32, (cap, slots), 1) + start == code_column)

        pick_ref[group], place_ref[group] = matrices(0)
        later.append((group, passes, matrices))

    for group, passes, matrices in later:

        @pl.when(passes > 1)
        def _():
            def one_pass(number, carry):
                pick_scratch[...], place_scratch[...] = matrices(number)
                pltpu.sync_copy(pick_scratch, more_pick_ref.at[group, number - 1])
                pltpu.sync_copy(place_scratch, more_place_ref.at[group, number - 1])
                return carry

            lax.fori_loop(1, passes, one_pass, 0)


def index(parcels, numbers, earlier, groups, lists_at, r_dev, cap, tile, block_rows):
    slots = 2 * r_dev * tile
    lines = 2 * r_dev * (tile + SPARE)
    more = -(-(min(block_rows, cap) - (tile - SPARE)) // tile)
    vmem, smem = pl.BlockSpec(memory_space=pltpu.VMEM), pl.BlockSpec(memory_space=pltpu.SMEM)
    any_spec = pl.BlockSpec(memory_space=pl.ANY)
    specs = [vmem, vmem, smem, smem, any_spec, any_spec]
    args = list(parcels)
    done, aliases = 0, {}
    if earlier is not None:
        done = groups - len(parcels)
        aliases = {1 + len(parcels) + place: place for place in (0, 1, 4, 5)}
        args += list(earlier[:4]) + [in_hbm(array) for array in earlier[4:]]
    return pl.pallas_call(
        functools.partial(index_kernel, r_dev, lists_at, cap, tile, block_rows, done),
        in_specs=[smem] + [vmem] * len(parcels) + (specs if done else []),
        out_specs=specs,
        out_shape=[
            jax.ShapeDtypeStruct((groups, lines, block_rows), BF16),
            jax.ShapeDtypeStruct((groups, cap, slots), BF16),
            jax.ShapeDtypeStruct((groups,), jnp.int32),
            jax.ShapeDtypeStruct((groups * r_dev,), jnp.int32),
            pltpu.HBM((groups, more, lines, block_rows), BF16),
            pltpu.HBM((groups, more, cap, slots), BF16),
        ],
        scratch_shapes=[pltpu.VMEM((lines, block_rows), BF16), pltpu.VMEM((cap, slots), BF16)],
        input_output_aliases=aliases,
        compiler_params=params(VMEM_BYTES),
        name="index",
    )(numbers, *args)


def lay_out(heard, number_ref, signal_ref):
    n_win = len(heard)
    r_dev, samples = heard[0].shape
    for distance, span in enumerate(heard):
        begin = lax.rem(number_ref[6] + n_win - distance, n_win) * samples
        signal_ref[:r_dev, pl.ds(pl.multiple_of(begin, LANES), samples)] = span.astype(F32)
    tail = signal_ref.shape[1] - n_win * samples
    signal_ref[:r_dev, n_win * samples :] = jnp.zeros((r_dev, tail), F32)


def first_sample(number_ref, v, n_win, samples):
    return lax.rem(number_ref[6] + n_win - v, n_win) * samples + number_ref[5]


def hankel_rows(signal_ref, r, begin, width, out_ref, place):
    length = width + LANES
    signal = signal_ref[r : r + 1, pl.ds(pl.multiple_of(begin, LANES), length)]
    base = jnp.broadcast_to(signal, (SHIFT_ROWS, length))
    sublane = lax.broadcasted_iota(jnp.int32, base.shape, 0)
    for bit in (1, 2, 4):
        base = jnp.where(sublane & bit != 0, pltpu.roll(base, length - bit, 1), base)
    for first in range(0, LANES, 2 * SHIFT_ROWS):
        both = []
        for shift in (first, first + SHIFT_ROWS):
            rolled = pltpu.roll(base, length - shift, 1) if shift else base
            both.append(rolled[:, :width])
        out_ref[place, first : first + 2 * SHIFT_ROWS, :] = jnp.concatenate(both, axis=0).astype(BF16)


def hankel_kernel(v, n_win, samples, done, number_ref, *refs):
    out_ref, signal_refs = refs[-2:]
    parcel_refs = refs[: -3 if done else -2]
    r_dev = parcel_refs[0].shape[0]
    begin = first_sample(number_ref, v, n_win, samples)
    for group, parcel_ref in enumerate(parcel_refs, done):
        signal_ref = signal_refs.at[group % 2]
        heard = [parcel_ref[:, w * samples : (w + 1) * samples] for w in range(n_win)]
        lay_out(heard, number_ref, signal_ref)
        for r in range(r_dev):
            hankel_rows(signal_ref, r, begin, out_ref.shape[2], out_ref, group * r_dev + r)


def build_hankel(parcels, numbers, earlier, groups, v, n_win, samples, width):
    r_dev = parcels[0].shape[0]
    shape = (groups * r_dev, LANES, width)
    vmem = pl.BlockSpec(memory_space=pltpu.VMEM)
    done = 0 if earlier is None else groups - len(parcels)
    copies = len(parcels) * r_dev * LANES * width
    return pl.pallas_call(
        functools.partial(hankel_kernel, v, n_win, samples, done),
        in_specs=[pl.BlockSpec(memory_space=pltpu.SMEM)] + [vmem] * (len(parcels) + (1 if done else 0)),
        out_specs=vmem,
        scratch_shapes=[pltpu.VMEM((2, SHIFT_ROWS, n_win * samples + LAGS), F32)],
        out_shape=jax.ShapeDtypeStruct(shape, BF16),
        input_output_aliases={1 + len(parcels): 0} if done else {},
        cost_estimate=pl.CostEstimate(flops=copies, bytes_accessed=2 * copies, transcendentals=0),
        compiler_params=params(VMEM_BYTES // 2),
        name="hankel",
    )(numbers, *parcels, *([earlier] if done else []))


def window_of(block, tile):
    return (tile - SPARE if block else 0), tile + SPARE


def pick_rows(block, pieces, pick, gathered, margin):
    count, samples = gathered.shape[0], pieces[0].shape[1]
    ones = pick[block * count : (block + 1) * count, :]
    for t in range(0, samples, STEP):
        rows = jnp.concatenate([piece[:, t : t + STEP] for piece in pieces], axis=0)
        chosen = jnp.dot(ones, rows, preferred_element_type=F32)
        gathered[:, margin + t : margin + t + STEP] = chosen.astype(BF16)


def margin_of(lag_dev):
    return lag_dev - STEP


def multiply(gathered, hankel_ref, place, r, rows, lag_dev):
    margin = margin_of(lag_dev)
    length = gathered.shape[1] - margin
    of_channel = slice(r * rows, (r + 1) * rows)
    shifted = [gathered[of_channel, margin - lag : margin - lag + length] for lag in range(0, lag_dev, STEP)]
    tiles = [hankel_ref[place, :, t : t + STEP] for t in range(0, length, LANES)]
    both = jnp.dot(jnp.concatenate(shifted, axis=0), jnp.concatenate(tiles, axis=0), preferred_element_type=F32)
    return [(slice(lag, lag + STEP), both[lag // STEP * rows :][:rows]) for lag in range(0, lag_dev, STEP)]


def split(total, terms, slots, lags):
    count = terms.shape[0] // 2
    upper = total.astype(BF16)
    terms[slots, lags] = upper
    terms[slice(count + slots.start, count + slots.stop), lags] = (total - upper.astype(F32)).astype(BF16)


def placed(place, terms):
    return jnp.dot(jnp.concatenate([place, place], axis=1), terms[...], preferred_element_type=F32)


def correlate_kernel(block, parts, v, tile, norming, prebuilt, first, last, pass_ref, count_ref, number_ref, *refs):
    refs = list(refs)
    pieces = [refs.pop(0) for _ in range(parts)]
    signal_ref, pick_ref, place_ref, more_pick_ref, more_place_ref = [refs.pop(0) for _ in range(5)]
    if not first:
        sums_ref, extra_ref = refs.pop(0), refs.pop(0)
    if last:
        out_ref = refs.pop(0)
    else:
        handed_ref, left_ref = refs.pop(0), refs.pop(0)
    gathered, terms, extra, pick_scratch, place_scratch = refs[:5]
    begin, rows = window_of(block, tile)
    r_dev = gathered.shape[0] // rows
    samples = pieces[0].shape[1]
    lag_dev = extra.shape[1]
    group = pl.program_id(0)

    if prebuilt:
        hankel_ref, hankel_place = signal_ref, group * r_dev
    else:
        hankel_place = 0
        hankel_ref, row_ref = refs[5:]
        n_win = signal_ref.shape[2] // samples
        lay_out([signal_ref[0, :, w * samples : (w + 1) * samples] for w in range(n_win)], number_ref, row_ref)
        start = first_sample(number_ref, v, n_win, samples)
        for r in range(r_dev):
            hankel_rows(row_ref, r, start, hankel_ref.shape[2], hankel_ref, r)

    margin = margin_of(lag_dev)
    if margin:

        @pl.when(group == 0)
        def _():
            for start in (0, margin + samples):
                gathered[:, start : start + margin] = jnp.zeros((gathered.shape[0], margin), BF16)

    pick_rows(block, pieces, pick_ref.at[0], gathered, margin)
    for r in range(r_dev):
        slots = slice(r * 2 * tile + begin, r * 2 * tile + begin + rows)
        others = [slice(r * 2 * tile, slots.start), slice(slots.stop, (r + 1) * 2 * tile)]
        others = [other for other in others if other.start < other.stop]
        for lags, total in multiply(gathered, hankel_ref, hankel_place + r, r, rows, lag_dev):
            if not first:
                total += sums_ref[group, slots, lags]
            if last:
                split(total * norming, terms, slots, lags)
                for other in others:
                    split(sums_ref[group, other, lags] * norming, terms, other, lags)
            else:
                handed_ref[group, slots, lags] = total
                for other in others if first else []:
                    handed_ref[group, other, lags] = jnp.zeros((other.stop - other.start, STEP), F32)
    if last:
        out_ref[0] = placed(place_ref[0], terms)

    @pl.when(pass_ref[group] > 1)
    def _():
        if first:
            extra[...] = jnp.zeros(extra.shape, F32)
        else:
            pltpu.sync_copy(extra_ref.at[group], extra)

        def one_pass(number, carry):
            pltpu.sync_copy(more_pick_ref.at[group, number - 1], pick_scratch)
            pltpu.sync_copy(more_place_ref.at[group, number - 1], place_scratch)
            pick_rows(block, pieces, pick_scratch, gathered, margin)
            terms[...] = jnp.zeros(terms.shape, BF16)
            for r in range(r_dev):
                needed = count_ref[group * r_dev + r] > (number - 1) * tile
                slots = slice(r * 2 * tile + begin, r * 2 * tile + begin + rows)

                @pl.when(needed)
                def _():
                    for lags, total in multiply(gathered, hankel_ref, hankel_place + r, r, rows, lag_dev):
                        split(total * norming, terms, slots, lags)

            extra[...] += placed(place_scratch[...], terms)
            return carry

        lax.fori_loop(1, pass_ref[group], one_pass, 0)
        if last:
            out_ref[0] += extra[...]
        else:
            pltpu.sync_copy(extra, left_ref.at[group])


def correlate(block, pieces, signal, prebuilt, numbers, v, matrices, before, last, tile, norming, lag_dev, n_win, r_dev):
    pick, place, passes, counts, more_pick, more_place = matrices
    groups, cap, slots = place.shape
    samples = pieces[0].shape[1]
    width = samples - LANES + lag_dev
    rows = window_of(block, tile)[1]
    by_group = lambda shape: pl.BlockSpec(shape, lambda i, *_: (i, 0, 0))
    any_spec = pl.BlockSpec(memory_space=pl.ANY)
    whole_spec = pl.BlockSpec(memory_space=pltpu.VMEM)
    out_spec = pl.BlockSpec(
        (1, cap, lag_dev), lambda i, _, __, number_ref: (lax.rem(number_ref[4] + groups - i, groups), 0, 0)
    )
    sums_shape = jax.ShapeDtypeStruct((groups, slots, lag_dev), F32)
    out_shape = jax.ShapeDtypeStruct((groups, cap, lag_dev), F32)
    in_specs = [whole_spec] * len(pieces)
    in_specs.append(whole_spec if prebuilt else by_group((1,) + signal.shape[1:]))
    in_specs += [by_group((1,) + pick.shape[1:]), by_group((1,) + place.shape[1:]), any_spec, any_spec]
    args = pieces + [signal, pick, place, in_hbm(more_pick), in_hbm(more_place)]
    aliases = {}
    if before is not None:
        in_specs += [whole_spec, any_spec]
        args += [before[0], in_hbm(before[1])]
        if not last:
            aliases = {3 + len(args) - 2: 0}
    scratch = [
        pltpu.VMEM((r_dev * rows, samples + 2 * margin_of(lag_dev)), BF16),
        pltpu.VMEM((2 * slots, lag_dev), BF16),
        pltpu.VMEM((cap, lag_dev), F32),
        pltpu.VMEM(pick.shape[1:], BF16),
        pltpu.VMEM(place.shape[1:], BF16),
    ]
    if not prebuilt:
        scratch.append(pltpu.VMEM((r_dev, LANES, width), BF16))
        scratch.append(pltpu.VMEM((SHIFT_ROWS, n_win * samples + LAGS), F32))
    body = functools.partial(
        correlate_kernel, block, len(pieces), v, tile, norming, prebuilt, before is None, last
    )
    return pl.pallas_call(
        body,
        grid_spec=pltpu.PrefetchScalarGridSpec(
            num_scalar_prefetch=3,
            grid=(groups,),
            in_specs=in_specs,
            out_specs=out_spec if last else [whole_spec, any_spec],
            scratch_shapes=scratch,
        ),
        out_shape=out_shape if last else [sums_shape, pltpu.HBM(out_shape.shape, F32)],
        input_output_aliases=aliases,
        cost_estimate=pl.CostEstimate(
            flops=2 * groups * r_dev * rows * samples * (lag_dev + pick.shape[2]),
            bytes_accessed=2 * groups * slots * lag_dev * 4,
            transcendentals=0,
        ),
        compiler_params=params(VMEM_BYTES if prebuilt else 2 * VMEM_BYTES),
        name="correlate",
    )(passes, counts, numbers, *args)


def shards(sources, receivers, plan, pair_index, keep):
    _, block_rows, samples = sources.shape
    r_dev = receivers.shape[0]
    n_chan = lax.axis_size("chan")
    n_win = lax.axis_size("win")
    n_rep = lax.axis_size("rep")
    cap = pair_index.shape[3]
    lag_dev = LAGS // (n_win * n_rep)
    tile = max(16, cap // 8)
    norming = 1.0 / math.sqrt(samples * n_win)
    width = samples - LANES + lag_dev
    prebuilt = n_chan * r_dev * n_win * LANES * width * 2 <= HANKEL_BYTES

    heard = [receivers] + [turned(receivers, "win", v) for v in range(1, n_win)]
    owns = own_rows(sources[0], n_rep)
    parcels, numbers = pack(plan, heard, pair_index[0, 0], keep[0, 0], n_rep, lag_dev, block_rows, n_chan)
    own_parcel = parcels[0]
    parcels = [turned(parcels[k], "chan", k) for k in range(1, n_chan)]
    matrices = index([own_parcel], numbers, None, n_chan, n_win * samples, r_dev, cap, tile, block_rows)
    if prebuilt:
        signals = [build_hankel([own_parcel], numbers, None, n_chan, v, n_win, samples, width) for v in range(n_win)]

    arrived = [{0: own} for own in owns]

    def relay(step):
        for there in arrived:
            there[step] = swapped(there[1 - step], "chan", 0)
            if step < n_chan - 1:
                there[-step] = swapped(there[step - 1], "chan", 1)

    def after_arrival(step, value):
        for there in arrived:
            for key in (step, -step):
                if key in there:
                    value = lax.optimization_barrier((value, there[key]))[0]
        return value

    def before_start(step, value):
        for there in arrived:
            for key in (1 - step, step - 1):
                there[key] = lax.optimization_barrier((value, there[key]))[1]

    def halves(piece):
        return [piece] + [turned(piece, "rep", -u) for u in range(1, n_rep)]

    def spans(piece):
        return [piece] + [turned(piece, "win", v) for v in range(1, n_win)]

    relay(1)
    before_start(2, (matrices, parcels, signals) if prebuilt else (matrices, parcels))
    parcels = after_arrival(1, parcels)
    relay(2)
    matrices = index(parcels, numbers, matrices, n_chan, n_win * samples, r_dev, cap, tile, block_rows)
    if prebuilt:
        signals[0] = build_hankel(parcels, numbers, signals[0], n_chan, 0, n_win, samples, width)
        before_start(3, (matrices, signals[0]))
    else:
        signals = [jnp.stack([own_parcel] + parcels)[:, :, : n_win * samples]] * n_win
    reach = range(-(n_chan - 2), n_chan - 1)
    near = choose(numbers, 2, arrived, [offset for offset in reach if offset in arrived[0]])
    if prebuilt:
        parcels = after_arrival(2, parcels)
        parcels, near = lax.optimization_barrier((parcels, near))
        for v in range(1, n_win):
            signals[v] = build_hankel(parcels, numbers, signals[v], n_chan, v, n_win, samples, width)
    for step in range(3, n_chan):
        relay(step)
    near_spans = spans(near)
    calls = [(v, q) for v in range(n_win) for q in range(2)]
    calls = calls[:2] + [(v, q) for q in range(2) for v in range(1, n_win)]

    def add(call, span, result):
        v, q = call
        return correlate(
            q, halves(span), signals[v], prebuilt, numbers, v, matrices, result, call == calls[-1], tile, norming, lag_dev,
            n_win, r_dev,
        )

    result = add(calls[0], near, None)
    near_spans = after_arrival(n_chan - 1, near_spans)
    for there in arrived:
        there[n_chan - 1] = lax.optimization_barrier((result, signals, there[n_chan - 1]))[2]
    far_spans = spans(choose(numbers, 3, arrived, sorted(arrived[0])))
    result = add(calls[1], far_spans[0], result)
    for call in calls[2:]:
        if call == (1, 1):
            far_spans, result = lax.optimization_barrier((far_spans, result))
        result = add(call, (near_spans, far_spans)[call[1]][call[0]], result)
    return result[None, None]


def solution(mesh):
    placed_at = (
        P(("grp", "chan"), None, "win"),
        P(("grp", "chan"), "win"),
        P("grp", None),
        P("grp", "chan", None, None),
        P("grp", "chan", None, None),
    )
    return jax.shard_map(
        shards,
        mesh=mesh,
        in_specs=placed_at,
        out_specs=P(("grp", "chan"), None, None, None, ("win", "rep")),
        check_vma=False,
    )
```

```python
import functools
import math

import jax
import jax.numpy as jnp
from jax import lax
from jax.experimental import pallas as pl
from jax.experimental.pallas import tpu as pltpu
from jax.sharding import PartitionSpec as P

LAGS = 2048
LANES = 128
SHIFT_ROWS = 8
STEP = 2 * LANES
CHAINS = 1
SPARE = 16
DIGIT = 64
HANKEL_BYTES = 24 * 2**20
VMEM_BYTES = 26 * 2**20
F32 = jnp.float32
BF16 = jnp.bfloat16


def swapped(block, axis, first):
    size = lax.axis_size(axis)
    route = []
    for i in range(first, size - 1, 2):
        route += [(i, i + 1), (i + 1, i)]
    return lax.ppermute(block, axis, route)


def turned(block, axis, distance):
    size = lax.axis_size(axis)
    return lax.ppermute(block, axis, [(i, (i + distance) % size) for i in range(size)])


def in_hbm(array):
    return pltpu.with_memory_space_constraint(array, pltpu.HBM)


def params(vmem):
    return pltpu.CompilerParams(vmem_limit_bytes=vmem)


def pack_kernel(halves, lags, block_rows, plan_hbm, pair_hbm, keep_hbm, receiver_hbm, *refs):
    plan_ref, pair_ref, keep_ref, receiver_ref, digit_ref, sems = refs[-6:]
    parcel_refs, number_ref = refs[:-7], refs[-7]
    small = []
    moves = [(plan_hbm, plan_ref), (pair_hbm, pair_ref), (keep_hbm, keep_ref)]
    moves.append((receiver_hbm, receiver_ref))
    for place, (source, target) in enumerate(moves):
        small.append(pltpu.make_async_copy(source, target, sems.at[place]))
        small[-1].start()
    r_dev, samples = receiver_ref.shape
    n_chan, cap = pair_ref.shape
    chan, win, rep = lax.axis_index("chan"), lax.axis_index("win"), lax.axis_index("rep")
    for copy in small:
        copy.wait()

    packed = pair_ref[...] * 2 + keep_ref[...]
    digit_ref[:n_chan, :] = jnp.concatenate([packed // DIGIT, packed % DIGIT], axis=1).astype(F32)
    heard = receiver_ref[...].astype(F32)
    part = 2 * cap // r_dev
    spare = parcel_refs[0].shape[1] - samples - part
    for distance, parcel_ref in enumerate(parcel_refs):
        digits = digit_ref[pl.ds(lax.rem(chan + distance, n_chan), 1), :]
        lists = [digits[:, i * part : (i + 1) * part] for i in range(r_dev)]
        parcel = [heard, jnp.concatenate(lists, axis=0)]
        if spare:
            parcel.append(jnp.zeros((r_dev, spare), F32))
        parcel_ref[...] = jnp.concatenate(parcel, axis=1).astype(BF16)

    one, two = plan_ref[0, 0], plan_ref[0, 1]
    nearer = jnp.where(jnp.abs(one - chan) <= jnp.abs(two - chan), 0, 1)
    sign = jnp.where(chan % 2 == 0, 1, -1)
    number_ref[0] = nearer
    number_ref[1] = block_rows - rep * (block_rows // halves)
    number_ref[2] = sign * (jnp.where(nearer == 0, one, two) - chan)
    number_ref[3] = sign * (jnp.where(nearer == 0, two, one) - chan)
    number_ref[4] = chan
    number_ref[5] = (win * halves + rep) * lags
    number_ref[6] = win


def pack(plan, receivers, pair_index, keep, halves, lags, block_rows, n_chan):
    r_dev, samples = receivers.shape
    cap = pair_index.shape[1]
    beside = -(-2 * cap // r_dev // LANES) * LANES
    vmem, smem = pl.BlockSpec(memory_space=pltpu.VMEM), pl.BlockSpec(memory_space=pltpu.SMEM)
    shapes = [jax.ShapeDtypeStruct((r_dev, samples + beside), BF16)] * n_chan
    shapes.append(jax.ShapeDtypeStruct((7,), jnp.int32))
    *parcels, numbers = pl.pallas_call(
        functools.partial(pack_kernel, halves, lags, block_rows),
        in_specs=[pl.BlockSpec(memory_space=pl.ANY)] * 4,
        out_specs=[vmem] * n_chan + [smem],
        out_shape=shapes,
        scratch_shapes=[
            pltpu.SMEM(plan.shape, plan.dtype),
            pltpu.VMEM(pair_index.shape, pair_index.dtype),
            pltpu.VMEM(keep.shape, keep.dtype),
            pltpu.VMEM(receivers.shape, receivers.dtype),
            pltpu.VMEM((-(-n_chan // SHIFT_ROWS) * SHIFT_ROWS, 2 * cap), F32),
            pltpu.SemaphoreType.DMA((4,)),
        ],
        compiler_params=params(VMEM_BYTES // 2),
        name="pack",
    )(*[in_hbm(a) for a in (plan, pair_index, keep, receivers)])
    return parcels, numbers


def join_kernel(*refs):
    out_ref = refs[-1]
    samples = out_ref.shape[1]
    out_ref[...] = jnp.concatenate([ref[:, :samples].astype(F32) for ref in refs[:-1]], axis=0).astype(BF16)


def join(parcels, samples):
    vmem = pl.BlockSpec(memory_space=pltpu.VMEM)
    return pl.pallas_call(
        join_kernel,
        in_specs=[vmem] * len(parcels),
        out_specs=vmem,
        out_shape=jax.ShapeDtypeStruct((len(parcels) * parcels[0].shape[0], samples), BF16),
        compiler_params=params(VMEM_BYTES // 4),
        name="join",
    )(*parcels)


def own_kernel(source_ref, *refs):
    chain_refs, sems = refs[:-1], refs[-1]
    rows = chain_refs[0].shape[0]
    copies = []
    for chain, chain_ref in enumerate(chain_refs):
        start = pl.multiple_of((lax.axis_index("rep") * CHAINS + chain) * rows, rows)
        copies.append(pltpu.make_async_copy(source_ref.at[pl.ds(start, rows)], chain_ref, sems.at[chain]))
        copies[-1].start()
    for copy in copies:
        copy.wait()


def own_rows(sources, halves):
    block_rows, samples = sources.shape
    shape = jax.ShapeDtypeStruct((block_rows // halves // CHAINS, samples), BF16)
    return pl.pallas_call(
        own_kernel,
        in_specs=[pl.BlockSpec(memory_space=pl.ANY)],
        out_specs=[pl.BlockSpec(memory_space=pltpu.VMEM)] * CHAINS,
        out_shape=[shape] * CHAINS,
        scratch_shapes=[pltpu.SemaphoreType.DMA((CHAINS,))],
        compiler_params=params(VMEM_BYTES // 4),
        name="own_rows",
    )(in_hbm(sources))


def choose_kernel(which, offsets, number_ref, *refs):
    out_ref, sems = refs[-2:]
    rows = out_ref.shape[0] // CHAINS
    where = number_ref[which]
    waits = []
    for chain in range(CHAINS):
        target = out_ref.at[pl.ds(chain * rows, rows)]
        for place, offset in enumerate(offsets):
            copy = pltpu.make_async_copy(refs[chain * len(offsets) + place], target, sems.at[chain])

            @pl.when(where == offset)
            def _():
                copy.start()

        waits.append(copy)
    for copy in waits:
        copy.wait()


def choose(numbers, which, arrived, offsets):
    pieces = [there[offset] for there in arrived for offset in offsets]
    rows, samples = pieces[0].shape
    any_spec = pl.BlockSpec(memory_space=pl.ANY)
    return pl.pallas_call(
        functools.partial(choose_kernel, which, offsets),
        in_specs=[pl.BlockSpec(memory_space=pltpu.SMEM)] + [any_spec] * len(pieces),
        out_specs=pl.BlockSpec(memory_space=pltpu.VMEM),
        out_shape=jax.ShapeDtypeStruct((rows * CHAINS, samples), BF16),
        scratch_shapes=[pltpu.SemaphoreType.DMA((CHAINS,))],
        compiler_params=params(VMEM_BYTES // 4),
        name="choose",
    )(numbers, *pieces)


def column(row):
    return jnp.broadcast_to(row, (SHIFT_ROWS, row.shape[1])).T[:, :1]


def ones_where(condition):
    return jnp.where(condition, 1.0, 0.0).astype(BF16)


def index_kernel(r_dev, lists_at, cap, tile, block_rows, number_ref, *refs):
    pick_ref, place_ref, pass_ref, count_ref, more_pick_ref, more_place_ref, pick_scratch, place_scratch = refs[-8:]
    parcel_refs = refs[:-8]
    nearer, offset = number_ref[0], number_ref[1]
    slots = 2 * r_dev * tile
    window = tile + SPARE
    part = 2 * cap // r_dev
    below = lax.broadcasted_iota(jnp.int32, (cap, cap), 0) < lax.broadcasted_iota(jnp.int32, (cap, cap), 1)
    below = ones_where(below)
    later = []
    for group, parcel_ref in enumerate(parcel_refs):
        digits = parcel_ref[:, lists_at:].astype(F32)
        digits = jnp.concatenate([digits[i : i + 1, :part] for i in range(r_dev)], axis=1).astype(jnp.int32)
        packed = digits[:, :cap] * DIGIT + digits[:, cap:]
        pairs, kept = packed // 2, packed % 2 == 1
        source_row, receiver = pairs // r_dev, pairs % r_dev
        turn = jnp.where(source_row // block_rows == nearer, 0, 1)
        row = (source_row + offset) % block_rows
        segment = jnp.where(kept, turn * r_dev + receiver, -1)
        member = lax.broadcasted_iota(jnp.int32, (2 * r_dev, cap), 0) == segment
        earlier = jnp.dot(ones_where(member), below, preferred_element_type=F32)
        of_pair = lambda values: jnp.sum(jnp.where(member, values, 0.0), axis=0, keepdims=True).astype(jnp.int32)
        counts = jnp.sum(jnp.where(member, 1.0, 0.0), axis=1, keepdims=True)
        from_top = jnp.minimum(counts[:r_dev], window)
        from_bottom = jnp.minimum(jnp.minimum(counts[r_dev:], 2.0 * tile - from_top), window)
        first_pass = jnp.concatenate([from_top, from_bottom], axis=0)
        first_slot = jnp.concatenate([jnp.zeros_like(from_top), 2.0 * tile - from_bottom], axis=0)
        rank, limit, begin = of_pair(earlier), of_pair(first_pass), of_pair(first_slot)
        rest = rank - limit
        code = jnp.where(rest < 0, begin + rank, (1 + rest // tile) * slots + turn * tile + rest % tile)
        code = jnp.where(kept, code + receiver * 2 * tile, -1)
        left = counts - first_pass
        which = lax.broadcasted_iota(jnp.int32, left.shape, 0) % r_dev
        passes = 1
        for r in range(r_dev):
            count = jnp.max(jnp.where(which == r, left, 0.0)).astype(jnp.int32)
            count_ref[group * r_dev + r] = count
            passes = jnp.maximum(passes, 1 + (count + tile - 1) // tile)
        pass_ref[group] = passes
        code_column = column(code.astype(F32)).astype(jnp.int32)
        row_column = column(row.astype(F32)).astype(jnp.int32)

        def matrices(number, code=code, turn=turn, code_column=code_column, row_column=row_column):
            start = number * slots
            row_ones = ones_where(row_column == lax.broadcasted_iota(jnp.int32, (cap, block_rows), 1))
            line = lax.broadcasted_iota(jnp.int32, (r_dev * window, 1), 0)
            slot = line // window * (2 * tile) + line % window + start
            of_block = [jnp.where(turn == q, code - q * (2 * tile - window), -1) for q in range(2)]
            by_slot = jnp.concatenate([ones_where(slot == codes) for codes in of_block], axis=0)
            pick = jnp.dot(by_slot, row_ones, preferred_element_type=F32).astype(BF16)
            return pick, ones_where(lax.broadcasted_iota(jnp.int32, (cap, slots), 1) + start == code_column)

        pick_ref[group], place_ref[group] = matrices(0)
        later.append((group, passes, matrices))

    for group, passes, matrices in later:

        @pl.when(passes > 1)
        def _():
            def one_pass(number, carry):
                pick_scratch[...], place_scratch[...] = matrices(number)
                pltpu.sync_copy(pick_scratch, more_pick_ref.at[group, number - 1])
                pltpu.sync_copy(place_scratch, more_place_ref.at[group, number - 1])
                return carry

            lax.fori_loop(1, passes, one_pass, 0)


def index(parcels, numbers, lists_at, r_dev, cap, tile, block_rows):
    groups = len(parcels)
    slots = 2 * r_dev * tile
    lines = 2 * r_dev * (tile + SPARE)
    more = -(-(min(block_rows, cap) - (tile - SPARE)) // tile)
    vmem, smem = pl.BlockSpec(memory_space=pltpu.VMEM), pl.BlockSpec(memory_space=pltpu.SMEM)
    any_spec = pl.BlockSpec(memory_space=pl.ANY)
    return pl.pallas_call(
        functools.partial(index_kernel, r_dev, lists_at, cap, tile, block_rows),
        in_specs=[smem] + [vmem] * groups,
        out_specs=[vmem, vmem, smem, smem, any_spec, any_spec],
        out_shape=[
            jax.ShapeDtypeStruct((groups, lines, block_rows), BF16),
            jax.ShapeDtypeStruct((groups, cap, slots), BF16),
            jax.ShapeDtypeStruct((groups,), jnp.int32),
            jax.ShapeDtypeStruct((groups * r_dev,), jnp.int32),
            pltpu.HBM((groups, more, lines, block_rows), BF16),
            pltpu.HBM((groups, more, cap, slots), BF16),
        ],
        scratch_shapes=[pltpu.VMEM((lines, block_rows), BF16), pltpu.VMEM((cap, slots), BF16)],
        compiler_params=params(VMEM_BYTES),
        name="index",
    )(numbers, *parcels)


def lay_out(heard, number_ref, signal_ref):
    n_win = len(heard)
    r_dev, samples = heard[0].shape
    for distance, span in enumerate(heard):
        begin = lax.rem(number_ref[6] + n_win - distance, n_win) * samples
        signal_ref[:r_dev, pl.ds(pl.multiple_of(begin, LANES), samples)] = span.astype(F32)
    tail = signal_ref.shape[1] - n_win * samples
    signal_ref[:r_dev, n_win * samples :] = jnp.zeros((r_dev, tail), F32)


def first_sample(number_ref, v, n_win, samples):
    return lax.rem(number_ref[6] + n_win - v, n_win) * samples + number_ref[5]


def hankel_rows(signal_ref, r, begin, width, out_ref, place):
    length = width + LANES
    signal = signal_ref[r : r + 1, pl.ds(pl.multiple_of(begin, LANES), length)]
    base = jnp.broadcast_to(signal, (SHIFT_ROWS, length))
    sublane = lax.broadcasted_iota(jnp.int32, base.shape, 0)
    for bit in (1, 2, 4):
        base = jnp.where(sublane & bit != 0, pltpu.roll(base, length - bit, 1), base)
    for first in range(0, LANES, 2 * SHIFT_ROWS):
        both = []
        for shift in (first, first + SHIFT_ROWS):
            rolled = pltpu.roll(base, length - shift, 1) if shift else base
            both.append(rolled[:, :width])
        out_ref[place, first : first + 2 * SHIFT_ROWS, :] = jnp.concatenate(both, axis=0).astype(BF16)


def hankel_kernel(v, number_ref, *refs):
    heard_refs, (out_ref, signal_ref) = refs[:-2], refs[-2:]
    channels, samples = heard_refs[0].shape
    begin = first_sample(number_ref, v, len(heard_refs), samples)
    lay_out([ref[...] for ref in heard_refs], number_ref, signal_ref)
    for channel in range(channels):
        hankel_rows(signal_ref, channel, begin, out_ref.shape[2], out_ref, channel)


def build_hankel(heard, numbers, v, width):
    channels, samples = heard[0].shape
    shape = (channels, LANES, width)
    vmem = pl.BlockSpec(memory_space=pltpu.VMEM)
    return pl.pallas_call(
        functools.partial(hankel_kernel, v),
        in_specs=[pl.BlockSpec(memory_space=pltpu.SMEM)] + [vmem] * len(heard),
        out_specs=vmem,
        scratch_shapes=[pltpu.VMEM((channels, len(heard) * samples + LAGS), F32)],
        out_shape=jax.ShapeDtypeStruct(shape, BF16),
        cost_estimate=pl.CostEstimate(flops=math.prod(shape), bytes_accessed=2 * math.prod(shape), transcendentals=0),
        compiler_params=params(VMEM_BYTES // 2),
        name="hankel",
    )(numbers, *heard)


def window_of(block, tile):
    return (tile - SPARE if block else 0), tile + SPARE


def pick_rows(block, pieces, pick, gathered, margin):
    count, samples = gathered.shape[0], pieces[0].shape[1]
    ones = pick[block * count : (block + 1) * count, :]
    for t in range(0, samples, STEP):
        rows = jnp.concatenate([piece[:, t : t + STEP] for piece in pieces], axis=0)
        chosen = jnp.dot(ones, rows, preferred_element_type=F32)
        gathered[:, margin + t : margin + t + STEP] = chosen.astype(BF16)


def margin_of(lag_dev):
    return lag_dev - STEP


def multiply(gathered, hankel_ref, place, r, rows, lag_dev):
    margin = margin_of(lag_dev)
    length = gathered.shape[1] - margin
    of_channel = slice(r * rows, (r + 1) * rows)
    shifted = [gathered[of_channel, margin - lag : margin - lag + length] for lag in range(0, lag_dev, STEP)]
    tiles = [hankel_ref[place, :, t : t + STEP] for t in range(0, length, LANES)]
    both = jnp.dot(jnp.concatenate(shifted, axis=0), jnp.concatenate(tiles, axis=0), preferred_element_type=F32)
    return [(slice(lag, lag + STEP), both[lag // STEP * rows :][:rows]) for lag in range(0, lag_dev, STEP)]


def split(total, terms, slots, lags):
    count = terms.shape[0] // 2
    upper = total.astype(BF16)
    terms[slots, lags] = upper
    terms[slice(count + slots.start, count + slots.stop), lags] = (total - upper.astype(F32)).astype(BF16)


def placed(place, terms):
    return jnp.dot(jnp.concatenate([place, place], axis=1), terms[...], preferred_element_type=F32)


def correlate_kernel(block, parts, v, tile, norming, prebuilt, first, last, pass_ref, count_ref, number_ref, *refs):
    refs = list(refs)
    pieces = [refs.pop(0) for _ in range(parts)]
    signal_ref, pick_ref, place_ref, more_pick_ref, more_place_ref = [refs.pop(0) for _ in range(5)]
    if not first:
        sums_ref, extra_ref = refs.pop(0), refs.pop(0)
    if last:
        out_ref = refs.pop(0)
    else:
        handed_ref, left_ref = refs.pop(0), refs.pop(0)
    gathered, terms, extra, pick_scratch, place_scratch = refs[:5]
    begin, rows = window_of(block, tile)
    r_dev = gathered.shape[0] // rows
    samples = pieces[0].shape[1]
    lag_dev = extra.shape[1]
    group = pl.program_id(0)

    if prebuilt:
        hankel_ref, hankel_place = signal_ref, group * r_dev
    else:
        hankel_place = 0
        hankel_ref, row_ref = refs[5:]
        n_win = signal_ref.shape[2] // samples
        lay_out([signal_ref[0, :, w * samples : (w + 1) * samples] for w in range(n_win)], number_ref, row_ref)
        start = first_sample(number_ref, v, n_win, samples)
        for r in range(r_dev):
            hankel_rows(row_ref, r, start, hankel_ref.shape[2], hankel_ref, r)

    margin = margin_of(lag_dev)
    if margin:

        @pl.when(group == 0)
        def _():
            for start in (0, margin + samples):
                gathered[:, start : start + margin] = jnp.zeros((gathered.shape[0], margin), BF16)

    pick_rows(block, pieces, pick_ref.at[0], gathered, margin)
    for r in range(r_dev):
        slots = slice(r * 2 * tile + begin, r * 2 * tile + begin + rows)
        others = [slice(r * 2 * tile, slots.start), slice(slots.stop, (r + 1) * 2 * tile)]
        others = [other for other in others if other.start < other.stop]
        for lags, total in multiply(gathered, hankel_ref, hankel_place + r, r, rows, lag_dev):
            if not first:
                total += sums_ref[group, slots, lags]
            if last:
                split(total * norming, terms, slots, lags)
                for other in others:
                    split(sums_ref[group, other, lags] * norming, terms, other, lags)
            else:
                handed_ref[group, slots, lags] = total
                for other in others if first else []:
                    handed_ref[group, other, lags] = jnp.zeros((other.stop - other.start, STEP), F32)
    if last:
        out_ref[0] = placed(place_ref[0], terms)

    @pl.when(pass_ref[group] > 1)
    def _():
        if first:
            extra[...] = jnp.zeros(extra.shape, F32)
        else:
            pltpu.sync_copy(extra_ref.at[group], extra)

        def one_pass(number, carry):
            pltpu.sync_copy(more_pick_ref.at[group, number - 1], pick_scratch)
            pltpu.sync_copy(more_place_ref.at[group, number - 1], place_scratch)
            pick_rows(block, pieces, pick_scratch, gathered, margin)
            terms[...] = jnp.zeros(terms.shape, BF16)
            for r in range(r_dev):
                needed = count_ref[group * r_dev + r] > (number - 1) * tile
                slots = slice(r * 2 * tile + begin, r * 2 * tile + begin + rows)

                @pl.when(needed)
                def _():
                    for lags, total in multiply(gathered, hankel_ref, hankel_place + r, r, rows, lag_dev):
                        split(total * norming, terms, slots, lags)

            extra[...] += placed(place_scratch[...], terms)
            return carry

        lax.fori_loop(1, pass_ref[group], one_pass, 0)
        if last:
            out_ref[0] += extra[...]
        else:
            pltpu.sync_copy(extra, left_ref.at[group])


def correlate(block, pieces, signal, prebuilt, numbers, v, matrices, before, last, tile, norming, lag_dev, n_win, r_dev):
    pick, place, passes, counts, more_pick, more_place = matrices
    groups, cap, slots = place.shape
    samples = pieces[0].shape[1]
    width = samples - LANES + lag_dev
    rows = window_of(block, tile)[1]
    by_group = lambda shape: pl.BlockSpec(shape, lambda i, *_: (i, 0, 0))
    any_spec = pl.BlockSpec(memory_space=pl.ANY)
    whole_spec = pl.BlockSpec(memory_space=pltpu.VMEM)
    out_spec = pl.BlockSpec(
        (1, cap, lag_dev), lambda i, _, __, number_ref: (lax.rem(number_ref[4] + groups - i, groups), 0, 0)
    )
    sums_shape = jax.ShapeDtypeStruct((groups, slots, lag_dev), F32)
    out_shape = jax.ShapeDtypeStruct((groups, cap, lag_dev), F32)
    in_specs = [whole_spec] * len(pieces)
    in_specs.append(whole_spec if prebuilt else by_group((1,) + signal.shape[1:]))
    in_specs += [by_group((1,) + pick.shape[1:]), by_group((1,) + place.shape[1:]), any_spec, any_spec]
    args = pieces + [signal, pick, place, in_hbm(more_pick), in_hbm(more_place)]
    aliases = {}
    if before is not None:
        in_specs += [whole_spec, any_spec]
        args += [before[0], in_hbm(before[1])]
        if not last:
            aliases = {3 + len(args) - 2: 0}
    scratch = [
        pltpu.VMEM((r_dev * rows, samples + 2 * margin_of(lag_dev)), BF16),
        pltpu.VMEM((2 * slots, lag_dev), BF16),
        pltpu.VMEM((cap, lag_dev), F32),
        pltpu.VMEM(pick.shape[1:], BF16),
        pltpu.VMEM(place.shape[1:], BF16),
    ]
    if not prebuilt:
        scratch.append(pltpu.VMEM((r_dev, LANES, width), BF16))
        scratch.append(pltpu.VMEM((SHIFT_ROWS, n_win * samples + LAGS), F32))
    body = functools.partial(
        correlate_kernel, block, len(pieces), v, tile, norming, prebuilt, before is None, last
    )
    return pl.pallas_call(
        body,
        grid_spec=pltpu.PrefetchScalarGridSpec(
            num_scalar_prefetch=3,
            grid=(groups,),
            in_specs=in_specs,
            out_specs=out_spec if last else [whole_spec, any_spec],
            scratch_shapes=scratch,
        ),
        out_shape=out_shape if last else [sums_shape, pltpu.HBM(out_shape.shape, F32)],
        input_output_aliases=aliases,
        cost_estimate=pl.CostEstimate(
            flops=2 * groups * r_dev * rows * samples * (lag_dev + pick.shape[2]),
            bytes_accessed=2 * groups * slots * lag_dev * 4,
            transcendentals=0,
        ),
        compiler_params=params(VMEM_BYTES if prebuilt else 2 * VMEM_BYTES),
        name="correlate",
    )(passes, counts, numbers, *args)


def shards(sources, receivers, plan, pair_index, keep):
    _, block_rows, samples = sources.shape
    r_dev = receivers.shape[0]
    n_chan = lax.axis_size("chan")
    n_win = lax.axis_size("win")
    n_rep = lax.axis_size("rep")
    cap = pair_index.shape[3]
    lag_dev = LAGS // (n_win * n_rep)
    tile = max(16, cap // 8)
    norming = 1.0 / math.sqrt(samples * n_win)
    width = samples - LANES + lag_dev
    prebuilt = n_chan * r_dev * n_win * LANES * width * 2 <= HANKEL_BYTES

    parcels, numbers = pack(plan, receivers, pair_index[0, 0], keep[0, 0], n_rep, lag_dev, block_rows, n_chan)
    parcels = [parcels[0]] + [turned(parcels[k], "chan", k) for k in range(1, n_chan)]
    owns = lax.optimization_barrier((own_rows(sources[0], n_rep), parcels))[0]
    matrices = index(parcels, numbers, samples, r_dev, cap, tile, block_rows)
    heard = join(parcels, samples)
    heard = [heard] + [turned(heard, "win", v) for v in range(1, n_win)]
    if prebuilt:
        signals = [build_hankel(heard, numbers, 0, width)]
    else:
        signals = [jnp.concatenate([span.reshape(n_chan, r_dev, samples) for span in heard], axis=2)] * n_win

    arrived = [{0: own} for own in owns]

    def relay(step):
        for there in arrived:
            there[step] = swapped(there[1 - step], "chan", 0)
            if step < n_chan - 1:
                there[-step] = swapped(there[step - 1], "chan", 1)

    def after_arrival(step, value):
        for there in arrived:
            for key in (step, -step):
                if key in there:
                    value = lax.optimization_barrier((value, there[key]))[0]
        return value

    def before_start(step, value):
        for there in arrived:
            for key in (1 - step, step - 1):
                there[key] = lax.optimization_barrier((value, there[key]))[1]

    def halves(piece):
        return [piece] + [turned(piece, "rep", -u) for u in range(1, n_rep)]

    def spans(piece):
        return [piece] + [turned(piece, "win", v) for v in range(1, n_win)]

    relay(1)
    before_start(2, (matrices, signals[0]))
    relay(2)
    if prebuilt:
        heard = after_arrival(1, heard)
        signals += [build_hankel(heard, numbers, v, width) for v in range(1, n_win)]
        before_start(3, signals)
    reach = range(-(n_chan - 2), n_chan - 1)
    near = choose(numbers, 2, arrived, [offset for offset in reach if offset in arrived[0]])
    for step in range(3, n_chan):
        relay(step)
    near_spans = spans(near)
    calls = [(v, q) for v in range(n_win) for q in range(2)]
    calls = calls[:2] + [(v, q) for q in range(2) for v in range(1, n_win)]

    def add(call, span, result):
        v, q = call
        return correlate(
            q, halves(span), signals[v], prebuilt, numbers, v, matrices, result, call == calls[-1], tile, norming, lag_dev,
            n_win, r_dev,
        )

    result = add(calls[0], near, None)
    near_spans = after_arrival(n_chan - 1, near_spans)
    for there in arrived:
        there[n_chan - 1] = lax.optimization_barrier((result, signals, there[n_chan - 1]))[2]
    far_spans = spans(choose(numbers, 3, arrived, sorted(arrived[0])))
    result = add(calls[1], far_spans[0], result)
    for call in calls[2:]:
        if call == (1, 1):
            far_spans, result = lax.optimization_barrier((far_spans, result))
        result = add(call, (near_spans, far_spans)[call[1]][call[0]], result)
    return result[None, None]


def solution(mesh):
    placed_at = (
        P(("grp", "chan"), None, "win"),
        P(("grp", "chan"), "win"),
        P("grp", None),
        P("grp", "chan", None, None),
        P("grp", "chan", None, None),
    )
    return jax.shard_map(
        shards,
        mesh=mesh,
        in_specs=placed_at,
        out_specs=P(("grp", "chan"), None, None, None, ("win", "rep")),
        check_vma=False,
    )
```

```python
import functools
import math

import jax
import jax.numpy as jnp
from jax import lax
from jax.experimental import pallas as pl
from jax.experimental.pallas import tpu as pltpu
from jax.sharding import PartitionSpec as P

LAGS = 2048
LANES = 128
SHIFT_ROWS = 8
STEP = 2 * LANES
CHAINS = 1
SPARE = 16
DIGIT = 64
HANKEL_BYTES = 24 * 2**20
VMEM_BYTES = 26 * 2**20
F32 = jnp.float32
BF16 = jnp.bfloat16


def swapped(block, axis, first):
    size = lax.axis_size(axis)
    route = []
    for i in range(first, size - 1, 2):
        route += [(i, i + 1), (i + 1, i)]
    return lax.ppermute(block, axis, route)


def turned(block, axis, distance):
    size = lax.axis_size(axis)
    return lax.ppermute(block, axis, [(i, (i + distance) % size) for i in range(size)])


def in_hbm(array):
    return pltpu.with_memory_space_constraint(array, pltpu.HBM)


def params(vmem):
    return pltpu.CompilerParams(vmem_limit_bytes=vmem)


def pack_kernel(halves, lags, block_rows, n_win, plan_hbm, pair_hbm, keep_hbm, *refs):
    span_hbms, refs = refs[:n_win], refs[n_win:]
    plan_ref, pair_ref, keep_ref, span_refs, digit_ref, sems = refs[-6:]
    parcel_refs, number_ref = refs[:-7], refs[-7]
    small = []
    moves = [(plan_hbm, plan_ref), (pair_hbm, pair_ref), (keep_hbm, keep_ref)]
    moves += [(span, span_refs.at[v]) for v, span in enumerate(span_hbms)]
    for place, (source, target) in enumerate(moves):
        small.append(pltpu.make_async_copy(source, target, sems.at[place]))
        small[-1].start()
    r_dev, samples = span_refs.shape[1:]
    n_chan, cap = pair_ref.shape
    chan, win, rep = lax.axis_index("chan"), lax.axis_index("win"), lax.axis_index("rep")
    for copy in small:
        copy.wait()

    packed = pair_ref[...] * 2 + keep_ref[...]
    digit_ref[:n_chan, :] = jnp.concatenate([packed // DIGIT, packed % DIGIT], axis=1).astype(F32)
    heard = [span_refs[v].astype(F32) for v in range(n_win)]
    part = 2 * cap // r_dev
    spare = parcel_refs[0].shape[1] - n_win * samples - part
    for distance, parcel_ref in enumerate(parcel_refs):
        digits = digit_ref[pl.ds(lax.rem(chan + distance, n_chan), 1), :]
        lists = [digits[:, i * part : (i + 1) * part] for i in range(r_dev)]
        parcel = heard + [jnp.concatenate(lists, axis=0)]
        if spare:
            parcel.append(jnp.zeros((r_dev, spare), F32))
        parcel_ref[...] = jnp.concatenate(parcel, axis=1).astype(BF16)

    one, two = plan_ref[0, 0], plan_ref[0, 1]
    nearer = jnp.where(jnp.abs(one - chan) <= jnp.abs(two - chan), 0, 1)
    sign = jnp.where(chan % 2 == 0, 1, -1)
    number_ref[0] = nearer
    number_ref[1] = block_rows - rep * (block_rows // halves)
    number_ref[2] = sign * (jnp.where(nearer == 0, one, two) - chan)
    number_ref[3] = sign * (jnp.where(nearer == 0, two, one) - chan)
    number_ref[4] = chan
    number_ref[5] = (win * halves + rep) * lags
    number_ref[6] = win


def pack(plan, spans, pair_index, keep, halves, lags, block_rows, n_chan):
    n_win = len(spans)
    r_dev, samples = spans[0].shape
    cap = pair_index.shape[1]
    beside = -(-2 * cap // r_dev // LANES) * LANES
    vmem, smem = pl.BlockSpec(memory_space=pltpu.VMEM), pl.BlockSpec(memory_space=pltpu.SMEM)
    shapes = [jax.ShapeDtypeStruct((r_dev, n_win * samples + beside), BF16)] * n_chan
    shapes.append(jax.ShapeDtypeStruct((7,), jnp.int32))
    *parcels, numbers = pl.pallas_call(
        functools.partial(pack_kernel, halves, lags, block_rows, n_win),
        in_specs=[pl.BlockSpec(memory_space=pl.ANY)] * (3 + n_win),
        out_specs=[vmem] * n_chan + [smem],
        out_shape=shapes,
        scratch_shapes=[
            pltpu.SMEM(plan.shape, plan.dtype),
            pltpu.VMEM(pair_index.shape, pair_index.dtype),
            pltpu.VMEM(keep.shape, keep.dtype),
            pltpu.VMEM((n_win, r_dev, samples), BF16),
            pltpu.VMEM((-(-n_chan // SHIFT_ROWS) * SHIFT_ROWS, 2 * cap), F32),
            pltpu.SemaphoreType.DMA((3 + n_win,)),
        ],
        compiler_params=params(VMEM_BYTES // 2),
        name="pack",
    )(*[in_hbm(a) for a in (plan, pair_index, keep, spans[0])], *spans[1:])
    return parcels, numbers


def own_kernel(source_ref, *refs):
    chain_refs, sems = refs[:-1], refs[-1]
    rows = chain_refs[0].shape[0]
    copies = []
    for chain, chain_ref in enumerate(chain_refs):
        start = pl.multiple_of((lax.axis_index("rep") * CHAINS + chain) * rows, rows)
        copies.append(pltpu.make_async_copy(source_ref.at[pl.ds(start, rows)], chain_ref, sems.at[chain]))
        copies[-1].start()
    for copy in copies:
        copy.wait()


def own_rows(sources, halves):
    block_rows, samples = sources.shape
    shape = jax.ShapeDtypeStruct((block_rows // halves // CHAINS, samples), BF16)
    return pl.pallas_call(
        own_kernel,
        in_specs=[pl.BlockSpec(memory_space=pl.ANY)],
        out_specs=[pl.BlockSpec(memory_space=pltpu.VMEM)] * CHAINS,
        out_shape=[shape] * CHAINS,
        scratch_shapes=[pltpu.SemaphoreType.DMA((CHAINS,))],
        compiler_params=params(VMEM_BYTES // 4),
        name="own_rows",
    )(in_hbm(sources))


def choose_kernel(which, offsets, number_ref, *refs):
    out_ref, sems = refs[-2:]
    rows = out_ref.shape[0] // CHAINS
    where = number_ref[which]
    waits = []
    for chain in range(CHAINS):
        target = out_ref.at[pl.ds(chain * rows, rows)]
        for place, offset in enumerate(offsets):
            copy = pltpu.make_async_copy(refs[chain * len(offsets) + place], target, sems.at[chain])

            @pl.when(where == offset)
            def _():
                copy.start()

        waits.append(copy)
    for copy in waits:
        copy.wait()


def choose(numbers, which, arrived, offsets):
    pieces = [there[offset] for there in arrived for offset in offsets]
    rows, samples = pieces[0].shape
    any_spec = pl.BlockSpec(memory_space=pl.ANY)
    return pl.pallas_call(
        functools.partial(choose_kernel, which, offsets),
        in_specs=[pl.BlockSpec(memory_space=pltpu.SMEM)] + [any_spec] * len(pieces),
        out_specs=pl.BlockSpec(memory_space=pltpu.VMEM),
        out_shape=jax.ShapeDtypeStruct((rows * CHAINS, samples), BF16),
        scratch_shapes=[pltpu.SemaphoreType.DMA((CHAINS,))],
        compiler_params=params(VMEM_BYTES // 4),
        name="choose",
    )(numbers, *pieces)


def column(row):
    return jnp.broadcast_to(row, (SHIFT_ROWS, row.shape[1])).T[:, :1]


def ones_where(condition):
    return jnp.where(condition, 1.0, 0.0).astype(BF16)


def index_kernel(r_dev, lists_at, cap, tile, block_rows, done, number_ref, *refs):
    pick_ref, place_ref, pass_ref, count_ref, more_pick_ref, more_place_ref, pick_scratch, place_scratch = refs[-8:]
    parcel_refs = refs[:-8]
    if done:
        parcel_refs, (_, _, earlier_pass_ref, earlier_count_ref, _, _) = parcel_refs[:-6], parcel_refs[-6:]
        for group in range(done):
            pass_ref[group] = earlier_pass_ref[group]
            for r in range(r_dev):
                count_ref[group * r_dev + r] = earlier_count_ref[group * r_dev + r]
    nearer, offset = number_ref[0], number_ref[1]
    slots = 2 * r_dev * tile
    window = tile + SPARE
    part = 2 * cap // r_dev
    below = lax.broadcasted_iota(jnp.int32, (cap, cap), 0) < lax.broadcasted_iota(jnp.int32, (cap, cap), 1)
    below = ones_where(below)
    later = []
    for group, parcel_ref in enumerate(parcel_refs, done):
        digits = parcel_ref[:, lists_at:].astype(F32)
        digits = jnp.concatenate([digits[i : i + 1, :part] for i in range(r_dev)], axis=1).astype(jnp.int32)
        packed = digits[:, :cap] * DIGIT + digits[:, cap:]
        pairs, kept = packed // 2, packed % 2 == 1
        source_row, receiver = pairs // r_dev, pairs % r_dev
        turn = jnp.where(source_row // block_rows == nearer, 0, 1)
        row = (source_row + offset) % block_rows
        segment = jnp.where(kept, turn * r_dev + receiver, -1)
        member = lax.broadcasted_iota(jnp.int32, (2 * r_dev, cap), 0) == segment
        earlier = jnp.dot(ones_where(member), below, preferred_element_type=F32)
        of_pair = lambda values: jnp.sum(jnp.where(member, values, 0.0), axis=0, keepdims=True).astype(jnp.int32)
        counts = jnp.sum(jnp.where(member, 1.0, 0.0), axis=1, keepdims=True)
        from_top = jnp.minimum(counts[:r_dev], window)
        from_bottom = jnp.minimum(jnp.minimum(counts[r_dev:], 2.0 * tile - from_top), window)
        first_pass = jnp.concatenate([from_top, from_bottom], axis=0)
        first_slot = jnp.concatenate([jnp.zeros_like(from_top), 2.0 * tile - from_bottom], axis=0)
        rank, limit, begin = of_pair(earlier), of_pair(first_pass), of_pair(first_slot)
        rest = rank - limit
        code = jnp.where(rest < 0, begin + rank, (1 + rest // tile) * slots + turn * tile + rest % tile)
        code = jnp.where(kept, code + receiver * 2 * tile, -1)
        left = counts - first_pass
        which = lax.broadcasted_iota(jnp.int32, left.shape, 0) % r_dev
        passes = 1
        for r in range(r_dev):
            count = jnp.max(jnp.where(which == r, left, 0.0)).astype(jnp.int32)
            count_ref[group * r_dev + r] = count
            passes = jnp.maximum(passes, 1 + (count + tile - 1) // tile)
        pass_ref[group] = passes
        code_column = column(code.astype(F32)).astype(jnp.int32)
        row_column = column(row.astype(F32)).astype(jnp.int32)

        def matrices(number, code=code, turn=turn, code_column=code_column, row_column=row_column):
            start = number * slots
            row_ones = ones_where(row_column == lax.broadcasted_iota(jnp.int32, (cap, block_rows), 1))
            line = lax.broadcasted_iota(jnp.int32, (r_dev * window, 1), 0)
            slot = line // window * (2 * tile) + line % window + start
            of_block = [jnp.where(turn == q, code - q * (2 * tile - window), -1) for q in range(2)]
            by_slot = jnp.concatenate([ones_where(slot == codes) for codes in of_block], axis=0)
            pick = jnp.dot(by_slot, row_ones, preferred_element_type=F32).astype(BF16)
            return pick, ones_where(lax.broadcasted_iota(jnp.int32, (cap, slots), 1) + start == code_column)

        pick_ref[group], place_ref[group] = matrices(0)
        later.append((group, passes, matrices))

    for group, passes, matrices in later:

        @pl.when(passes > 1)
        def _():
            def one_pass(number, carry):
                pick_scratch[...], place_scratch[...] = matrices(number)
                pltpu.sync_copy(pick_scratch, more_pick_ref.at[group, number - 1])
                pltpu.sync_copy(place_scratch, more_place_ref.at[group, number - 1])
                return carry

            lax.fori_loop(1, passes, one_pass, 0)


def index(parcels, numbers, earlier, groups, lists_at, r_dev, cap, tile, block_rows):
    slots = 2 * r_dev * tile
    lines = 2 * r_dev * (tile + SPARE)
    more = -(-(min(block_rows, cap) - (tile - SPARE)) // tile)
    vmem, smem = pl.BlockSpec(memory_space=pltpu.VMEM), pl.BlockSpec(memory_space=pltpu.SMEM)
    any_spec = pl.BlockSpec(memory_space=pl.ANY)
    specs = [vmem, vmem, smem, smem, any_spec, any_spec]
    args = list(parcels)
    done, aliases = 0, {}
    if earlier is not None:
        done = groups - len(parcels)
        aliases = {1 + len(parcels) + place: place for place in (0, 1, 4, 5)}
        args += list(earlier[:4]) + [in_hbm(array) for array in earlier[4:]]
    return pl.pallas_call(
        functools.partial(index_kernel, r_dev, lists_at, cap, tile, block_rows, done),
        in_specs=[smem] + [vmem] * len(parcels) + (specs if done else []),
        out_specs=specs,
        out_shape=[
            jax.ShapeDtypeStruct((groups, lines, block_rows), BF16),
            jax.ShapeDtypeStruct((groups, cap, slots), BF16),
            jax.ShapeDtypeStruct((groups,), jnp.int32),
            jax.ShapeDtypeStruct((groups * r_dev,), jnp.int32),
            pltpu.HBM((groups, more, lines, block_rows), BF16),
            pltpu.HBM((groups, more, cap, slots), BF16),
        ],
        scratch_shapes=[pltpu.VMEM((lines, block_rows), BF16), pltpu.VMEM((cap, slots), BF16)],
        input_output_aliases=aliases,
        compiler_params=params(VMEM_BYTES),
        name="index",
    )(numbers, *args)


def lay_out(heard, number_ref, signal_ref):
    n_win = len(heard)
    r_dev, samples = heard[0].shape
    for distance, span in enumerate(heard):
        begin = lax.rem(number_ref[6] + n_win - distance, n_win) * samples
        signal_ref[:r_dev, pl.ds(pl.multiple_of(begin, LANES), samples)] = span.astype(F32)
    tail = signal_ref.shape[1] - n_win * samples
    signal_ref[:r_dev, n_win * samples :] = jnp.zeros((r_dev, tail), F32)


def first_sample(number_ref, v, n_win, samples):
    return lax.rem(number_ref[6] + n_win - v, n_win) * samples + number_ref[5]


def hankel_rows(signal_ref, r, begin, width, out_ref, place):
    length = width + LANES
    signal = signal_ref[r : r + 1, pl.ds(pl.multiple_of(begin, LANES), length)]
    base = jnp.broadcast_to(signal, (SHIFT_ROWS, length))
    sublane = lax.broadcasted_iota(jnp.int32, base.shape, 0)
    for bit in (1, 2, 4):
        base = jnp.where(sublane & bit != 0, pltpu.roll(base, length - bit, 1), base)
    for first in range(0, LANES, 2 * SHIFT_ROWS):
        both = []
        for shift in (first, first + SHIFT_ROWS):
            rolled = pltpu.roll(base, length - shift, 1) if shift else base
            both.append(rolled[:, :width])
        out_ref[place, first : first + 2 * SHIFT_ROWS, :] = jnp.concatenate(both, axis=0).astype(BF16)


def hankel_kernel(v, n_win, samples, done, number_ref, *refs):
    out_ref, signal_refs = refs[-2:]
    parcel_refs = refs[: -3 if done else -2]
    r_dev = parcel_refs[0].shape[0]
    begin = first_sample(number_ref, v, n_win, samples)
    for group, parcel_ref in enumerate(parcel_refs, done):
        signal_ref = signal_refs.at[group % 2]
        heard = [parcel_ref[:, w * samples : (w + 1) * samples] for w in range(n_win)]
        lay_out(heard, number_ref, signal_ref)
        for r in range(r_dev):
            hankel_rows(signal_ref, r, begin, out_ref.shape[2], out_ref, group * r_dev + r)


def build_hankel(parcels, numbers, earlier, groups, v, n_win, samples, width):
    r_dev = parcels[0].shape[0]
    shape = (groups * r_dev, LANES, width)
    vmem = pl.BlockSpec(memory_space=pltpu.VMEM)
    done = 0 if earlier is None else groups - len(parcels)
    copies = len(parcels) * r_dev * LANES * width
    return pl.pallas_call(
        functools.partial(hankel_kernel, v, n_win, samples, done),
        in_specs=[pl.BlockSpec(memory_space=pltpu.SMEM)] + [vmem] * (len(parcels) + (1 if done else 0)),
        out_specs=vmem,
        scratch_shapes=[pltpu.VMEM((2, SHIFT_ROWS, n_win * samples + LAGS), F32)],
        out_shape=jax.ShapeDtypeStruct(shape, BF16),
        input_output_aliases={1 + len(parcels): 0} if done else {},
        cost_estimate=pl.CostEstimate(flops=copies, bytes_accessed=2 * copies, transcendentals=0),
        compiler_params=params(VMEM_BYTES // 2),
        name="hankel",
    )(numbers, *parcels, *([earlier] if done else []))


def window_of(block, tile):
    return (tile - SPARE if block else 0), tile + SPARE


def pick_rows(block, pieces, pick, gathered, margin):
    count, samples = gathered.shape[0], pieces[0].shape[1]

    def step(t):
        ones = pick[block * count : (block + 1) * count, :]
        rows = jnp.concatenate([piece[:, t : t + STEP] for piece in pieces], axis=0)
        chosen = jnp.dot(ones, rows, preferred_element_type=F32)
        gathered[:, margin + t : margin + t + STEP] = chosen.astype(BF16)

    return [functools.partial(step, t) for t in range(0, samples, STEP)]


def margin_of(lag_dev):
    return lag_dev - STEP


def multiply(gathered, hankel_ref, place, r, rows, lag_dev):
    margin = margin_of(lag_dev)
    length = gathered.shape[1] - margin
    of_channel = slice(r * rows, (r + 1) * rows)
    shifted = [gathered[of_channel, margin - lag : margin - lag + length] for lag in range(0, lag_dev, STEP)]
    tiles = [hankel_ref[place, :, t : t + STEP] for t in range(0, length, LANES)]
    both = jnp.dot(jnp.concatenate(shifted, axis=0), jnp.concatenate(tiles, axis=0), preferred_element_type=F32)
    return [(slice(lag, lag + STEP), both[lag // STEP * rows :][:rows]) for lag in range(0, lag_dev, STEP)]


def split(total, terms, slots, lags):
    count = terms.shape[0] // 2
    upper = total.astype(BF16)
    terms[slots, lags] = upper
    terms[slice(count + slots.start, count + slots.stop), lags] = (total - upper.astype(F32)).astype(BF16)


def placed(place, terms):
    return jnp.dot(jnp.concatenate([place, place], axis=1), terms[...], preferred_element_type=F32)


def correlate_kernel(
    block, parts, v, tile, norming, prebuilt, first, last, steps, pass_ref, count_ref, number_ref, *refs
):
    refs = list(refs)
    pieces = [refs.pop(0) for _ in range(parts)]
    signal_ref, pick_ref, place_ref, more_pick_ref, more_place_ref = [refs.pop(0) for _ in range(5)]
    if not first:
        sums_ref, extra_ref = refs.pop(0), refs.pop(0)
    if last:
        out_hbm = refs.pop(0)
    else:
        handed_ref, left_ref = refs.pop(0), refs.pop(0)
    gathered, terms, extra, pick_scratch, place_scratch, out_ref, sems = refs[:7]
    begin, rows = window_of(block, tile)
    r_dev = gathered.shape[1] // rows
    samples = pieces[0].shape[1]
    at_once, lag_dev = out_ref.shape[0], out_ref.shape[2]
    base = pl.program_id(0) * at_once if steps > 1 else 0
    groups = steps * at_once
    margin = margin_of(lag_dev)

    def hankel_place(group):
        return group * r_dev if prebuilt else 0

    def target(group):
        return out_hbm.at[lax.rem(number_ref[4] + groups - group, groups)]

    if prebuilt:
        hankel_ref = signal_ref
    else:
        hankel_ref, row_ref = refs[7:]
        n_win = signal_ref.shape[2] // samples
        lay_out([signal_ref[0, :, w * samples : (w + 1) * samples] for w in range(n_win)], number_ref, row_ref)
        start = first_sample(number_ref, v, n_win, samples)
        for r in range(r_dev):
            hankel_rows(row_ref, r, start, hankel_ref.shape[2], hankel_ref, r)
    for start in (0, margin + samples) if margin else ():
        gathered[:, :, start : start + margin] = jnp.zeros(gathered.shape[:2] + (margin,), BF16)

    def channel(group, r, rows_of_pass, terms_of_pass):
        slots = slice(r * 2 * tile + begin, r * 2 * tile + begin + rows)
        others = [slice(r * 2 * tile, slots.start), slice(slots.stop, (r + 1) * 2 * tile)]
        others = [other for other in others if other.start < other.stop]
        for lags, total in multiply(rows_of_pass, hankel_ref, hankel_place(group) + r, r, rows, lag_dev):
            if not first:
                total += sums_ref[group, slots, lags]
            if last:
                split(total * norming, terms_of_pass, slots, lags)
                for other in others:
                    split(sums_ref[group, other, lags] * norming, terms_of_pass, other, lags)
            else:
                handed_ref[group, slots, lags] = total
                for other in others if first else []:
                    handed_ref[group, other, lags] = jnp.zeros((other.stop - other.start, STEP), F32)

    for step in pick_rows(block, pieces, pick_ref.at[0], gathered.at[0], margin):
        step()
    copies = []
    for place in range(at_once):
        ahead = []
        if place + 1 < at_once:
            ahead = pick_rows(block, pieces, pick_ref.at[place + 1], gathered.at[(place + 1) % 2], margin)
        share = -(-len(ahead) // r_dev)
        for r in range(r_dev):
            channel(base + place, r, gathered.at[place % 2], terms.at[place % 2])
            for step in ahead[r * share : (r + 1) * share]:
                step()
        if last:
            out_ref[place] = placed(place_ref[place], terms.at[place % 2])
            copies.append(pltpu.make_async_copy(out_ref.at[place], target(base + place), sems.at[place]))
            copies[-1].start()
    for copy in copies:
        copy.wait()

    def later_passes(place, carry):
        group = base + place

        @pl.when(pass_ref[group] > 1)
        def _():
            if first:
                extra[...] = jnp.zeros(extra.shape, F32)
            else:
                pltpu.sync_copy(extra_ref.at[group], extra)

            def one_pass(number, carry):
                pltpu.sync_copy(more_pick_ref.at[group, number - 1], pick_scratch)
                pltpu.sync_copy(more_place_ref.at[group, number - 1], place_scratch)
                for step in pick_rows(block, pieces, pick_scratch, gathered.at[0], margin):
                    step()
                terms[0] = jnp.zeros(terms.shape[1:], BF16)
                for r in range(r_dev):
                    needed = count_ref[group * r_dev + r] > (number - 1) * tile
                    slots = slice(r * 2 * tile + begin, r * 2 * tile + begin + rows)

                    @pl.when(needed)
                    def _():
                        hankel = hankel_place(group) + r
                        for lags, total in multiply(gathered.at[0], hankel_ref, hankel, r, rows, lag_dev):
                            split(total * norming, terms.at[0], slots, lags)

                extra[...] += placed(place_scratch[...], terms.at[0])
                return carry

            lax.fori_loop(1, pass_ref[group], one_pass, 0)
            if last:
                out_ref[place] += extra[...]
                pltpu.sync_copy(out_ref.at[place], target(group))
            else:
                pltpu.sync_copy(extra, left_ref.at[group])

        return carry

    lax.fori_loop(0, at_once, later_passes, 0)


def correlate(block, pieces, signal, prebuilt, numbers, v, matrices, before, last, tile, norming, lag_dev, n_win, r_dev):
    pick, place, passes, counts, more_pick, more_place = matrices
    groups, cap, slots = place.shape
    samples = pieces[0].shape[1]
    width = samples - LANES + lag_dev
    rows = window_of(block, tile)[1]
    at_once = math.gcd(groups, 4) if prebuilt else 1
    by_group = lambda shape: pl.BlockSpec(shape, lambda i, *_: (i, 0, 0))
    any_spec = pl.BlockSpec(memory_space=pl.ANY)
    whole_spec = pl.BlockSpec(memory_space=pltpu.VMEM)
    sums_shape = jax.ShapeDtypeStruct((groups, slots, lag_dev), F32)
    out_shape = jax.ShapeDtypeStruct((groups, cap, lag_dev), F32)
    in_specs = [whole_spec] * len(pieces)
    in_specs.append(whole_spec if prebuilt else by_group((1,) + signal.shape[1:]))
    in_specs += [by_group((at_once,) + pick.shape[1:]), by_group((at_once,) + place.shape[1:]), any_spec, any_spec]
    args = pieces + [signal, pick, place, in_hbm(more_pick), in_hbm(more_place)]
    aliases = {}
    if before is not None:
        in_specs += [whole_spec, any_spec]
        args += [before[0], in_hbm(before[1])]
        if not last:
            aliases = {3 + len(args) - 2: 0}
    scratch = [
        pltpu.VMEM((2, r_dev * rows, samples + 2 * margin_of(lag_dev)), BF16),
        pltpu.VMEM((2, 2 * slots, lag_dev), BF16),
        pltpu.VMEM((cap, lag_dev), F32),
        pltpu.VMEM(pick.shape[1:], BF16),
        pltpu.VMEM(place.shape[1:], BF16),
        pltpu.VMEM((at_once, cap, lag_dev), F32),
        pltpu.SemaphoreType.DMA((at_once,)),
    ]
    if not prebuilt:
        scratch.append(pltpu.VMEM((r_dev, LANES, width), BF16))
        scratch.append(pltpu.VMEM((SHIFT_ROWS, n_win * samples + LAGS), F32))
    body = functools.partial(
        correlate_kernel, block, len(pieces), v, tile, norming, prebuilt, before is None, last, groups // at_once
    )
    return pl.pallas_call(
        body,
        grid_spec=pltpu.PrefetchScalarGridSpec(
            num_scalar_prefetch=3,
            grid=(groups // at_once,),
            in_specs=in_specs,
            out_specs=any_spec if last else [whole_spec, any_spec],
            scratch_shapes=scratch,
        ),
        out_shape=pltpu.HBM(out_shape.shape, F32) if last else [sums_shape, pltpu.HBM(out_shape.shape, F32)],
        input_output_aliases=aliases,
        cost_estimate=pl.CostEstimate(
            flops=2 * groups * r_dev * rows * samples * (lag_dev + pick.shape[2]),
            bytes_accessed=2 * groups * slots * lag_dev * 4,
            transcendentals=0,
        ),
        compiler_params=params(VMEM_BYTES if prebuilt else 2 * VMEM_BYTES),
        name="correlate",
    )(passes, counts, numbers, *args)


def shards(sources, receivers, plan, pair_index, keep):
    _, block_rows, samples = sources.shape
    r_dev = receivers.shape[0]
    n_chan = lax.axis_size("chan")
    n_win = lax.axis_size("win")
    n_rep = lax.axis_size("rep")
    cap = pair_index.shape[3]
    lag_dev = LAGS // (n_win * n_rep)
    tile = max(16, cap // 8)
    norming = 1.0 / math.sqrt(samples * n_win)
    width = samples - LANES + lag_dev
    prebuilt = n_chan * r_dev * n_win * LANES * width * 2 <= HANKEL_BYTES

    heard = [receivers] + [turned(receivers, "win", v) for v in range(1, n_win)]
    owns = own_rows(sources[0], n_rep)
    parcels, numbers = pack(plan, heard, pair_index[0, 0], keep[0, 0], n_rep, lag_dev, block_rows, n_chan)
    own_parcel = parcels[0]
    parcels = [turned(parcels[k], "chan", k) for k in range(1, n_chan)]
    matrices = index([own_parcel], numbers, None, n_chan, n_win * samples, r_dev, cap, tile, block_rows)
    if prebuilt:
        signals = [build_hankel([own_parcel], numbers, None, n_chan, v, n_win, samples, width) for v in range(n_win)]

    arrived = [{0: own} for own in owns]

    def relay(step):
        for there in arrived:
            there[step] = swapped(there[1 - step], "chan", 0)
            if step < n_chan - 1:
                there[-step] = swapped(there[step - 1], "chan", 1)

    def after_arrival(step, value):
        for there in arrived:
            for key in (step, -step):
                if key in there:
                    value = lax.optimization_barrier((value, there[key]))[0]
        return value

    def before_start(step, value):
        for there in arrived:
            for key in (1 - step, step - 1):
                there[key] = lax.optimization_barrier((value, there[key]))[1]

    def halves(piece):
        return [piece] + [turned(piece, "rep", -u) for u in range(1, n_rep)]

    def spans(piece):
        return [piece] + [turned(piece, "win", v) for v in range(1, n_win)]

    relay(1)
    before_start(2, (matrices, parcels, signals) if prebuilt else (matrices, parcels))
    parcels = after_arrival(1, parcels)
    relay(2)
    matrices = index(parcels, numbers, matrices, n_chan, n_win * samples, r_dev, cap, tile, block_rows)
    if prebuilt:
        signals[0] = build_hankel(parcels, numbers, signals[0], n_chan, 0, n_win, samples, width)
        before_start(3, (matrices, signals[0]))
    else:
        signals = [jnp.stack([own_parcel] + parcels)[:, :, : n_win * samples]] * n_win
    reach = range(-(n_chan - 2), n_chan - 1)
    near = choose(numbers, 2, arrived, [offset for offset in reach if offset in arrived[0]])
    if prebuilt:
        parcels = after_arrival(2, parcels)
        parcels, near = lax.optimization_barrier((parcels, near))
        for v in range(1, n_win):
            signals[v] = build_hankel(parcels, numbers, signals[v], n_chan, v, n_win, samples, width)
    for step in range(3, n_chan):
        relay(step)
    near_spans = spans(near)
    calls = [(v, q) for v in range(n_win) for q in range(2)]
    calls = calls[:2] + [(v, q) for q in range(2) for v in range(1, n_win)]

    def add(call, span, result):
        v, q = call
        return correlate(
            q, halves(span), signals[v], prebuilt, numbers, v, matrices, result, call == calls[-1], tile, norming, lag_dev,
            n_win, r_dev,
        )

    result = add(calls[0], near, None)
    near_spans = after_arrival(n_chan - 1, near_spans)
    for there in arrived:
        there[n_chan - 1] = lax.optimization_barrier((result, signals, there[n_chan - 1]))[2]
    far_spans = spans(choose(numbers, 3, arrived, sorted(arrived[0])))
    result = add(calls[1], far_spans[0], result)
    for call in calls[2:]:
        if call == (1, 1):
            far_spans, result = lax.optimization_barrier((far_spans, result))
        result = add(call, (near_spans, far_spans)[call[1]][call[0]], result)
    return result[None, None]


def solution(mesh):
    placed_at = (
        P(("grp", "chan"), None, "win"),
        P(("grp", "chan"), "win"),
        P("grp", None),
        P("grp", "chan", None, None),
        P("grp", "chan", None, None),
    )
    return jax.shard_map(
        shards,
        mesh=mesh,
        in_specs=placed_at,
        out_specs=P(("grp", "chan"), None, None, None, ("win", "rep")),
        check_vma=False,
    )
```

```python
import functools
import math

import jax
import jax.numpy as jnp
from jax import lax
from jax.experimental import pallas as pl
from jax.experimental.pallas import tpu as pltpu
from jax.sharding import PartitionSpec as P

LAGS = 2048
LANES = 128
SHIFT_ROWS = 8
STEP = 2 * LANES
CHAINS = 1
SPARE = 16
DIGIT = 64
HANKEL_BYTES = 24 * 2**20
VMEM_BYTES = 26 * 2**20
F32 = jnp.float32
BF16 = jnp.bfloat16


def swapped(block, axis, first):
    size = lax.axis_size(axis)
    route = []
    for i in range(first, size - 1, 2):
        route += [(i, i + 1), (i + 1, i)]
    return lax.ppermute(block, axis, route)


def turned(block, axis, distance):
    size = lax.axis_size(axis)
    return lax.ppermute(block, axis, [(i, (i + distance) % size) for i in range(size)])


def in_hbm(array):
    return pltpu.with_memory_space_constraint(array, pltpu.HBM)


def params(vmem):
    return pltpu.CompilerParams(vmem_limit_bytes=vmem)


def pack_kernel(halves, lags, block_rows, n_win, plan_hbm, pair_hbm, keep_hbm, *refs):
    span_hbms, refs = refs[:n_win], refs[n_win:]
    plan_ref, pair_ref, keep_ref, span_refs, digit_ref, sems = refs[-6:]
    parcel_refs, number_ref = refs[:-7], refs[-7]
    small = []
    moves = [(plan_hbm, plan_ref), (pair_hbm, pair_ref), (keep_hbm, keep_ref)]
    moves += [(span, span_refs.at[v]) for v, span in enumerate(span_hbms)]
    for place, (source, target) in enumerate(moves):
        small.append(pltpu.make_async_copy(source, target, sems.at[place]))
        small[-1].start()
    r_dev, samples = span_refs.shape[1:]
    n_chan, cap = pair_ref.shape
    chan, win, rep = lax.axis_index("chan"), lax.axis_index("win"), lax.axis_index("rep")
    for copy in small:
        copy.wait()

    packed = pair_ref[...] * 2 + keep_ref[...]
    digit_ref[:n_chan, :] = jnp.concatenate([packed // DIGIT, packed % DIGIT], axis=1).astype(F32)
    heard = [span_refs[v].astype(F32) for v in range(n_win)]
    part = 2 * cap // r_dev
    spare = parcel_refs[0].shape[1] - n_win * samples - part
    for distance, parcel_ref in enumerate(parcel_refs):
        digits = digit_ref[pl.ds(lax.rem(chan + distance, n_chan), 1), :]
        lists = [digits[:, i * part : (i + 1) * part] for i in range(r_dev)]
        parcel = heard + [jnp.concatenate(lists, axis=0)]
        if spare:
            parcel.append(jnp.zeros((r_dev, spare), F32))
        parcel_ref[...] = jnp.concatenate(parcel, axis=1).astype(BF16)

    one, two = plan_ref[0, 0], plan_ref[0, 1]
    nearer = jnp.where(jnp.abs(one - chan) <= jnp.abs(two - chan), 0, 1)
    sign = jnp.where(chan % 2 == 0, 1, -1)
    number_ref[0] = nearer
    number_ref[1] = block_rows - rep * (block_rows // halves)
    number_ref[2] = sign * (jnp.where(nearer == 0, one, two) - chan)
    number_ref[3] = sign * (jnp.where(nearer == 0, two, one) - chan)
    number_ref[4] = chan
    number_ref[5] = (win * halves + rep) * lags
    number_ref[6] = win


def pack(plan, spans, pair_index, keep, halves, lags, block_rows, n_chan):
    n_win = len(spans)
    r_dev, samples = spans[0].shape
    cap = pair_index.shape[1]
    beside = -(-2 * cap // r_dev // LANES) * LANES
    vmem, smem = pl.BlockSpec(memory_space=pltpu.VMEM), pl.BlockSpec(memory_space=pltpu.SMEM)
    shapes = [jax.ShapeDtypeStruct((r_dev, n_win * samples + beside), BF16)] * n_chan
    shapes.append(jax.ShapeDtypeStruct((7,), jnp.int32))
    *parcels, numbers = pl.pallas_call(
        functools.partial(pack_kernel, halves, lags, block_rows, n_win),
        in_specs=[pl.BlockSpec(memory_space=pl.ANY)] * (3 + n_win),
        out_specs=[vmem] * n_chan + [smem],
        out_shape=shapes,
        scratch_shapes=[
            pltpu.SMEM(plan.shape, plan.dtype),
            pltpu.VMEM(pair_index.shape, pair_index.dtype),
            pltpu.VMEM(keep.shape, keep.dtype),
            pltpu.VMEM((n_win, r_dev, samples), BF16),
            pltpu.VMEM((-(-n_chan // SHIFT_ROWS) * SHIFT_ROWS, 2 * cap), F32),
            pltpu.SemaphoreType.DMA((3 + n_win,)),
        ],
        compiler_params=params(VMEM_BYTES // 2),
        name="pack",
    )(*[in_hbm(a) for a in (plan, pair_index, keep, spans[0])], *spans[1:])
    return parcels, numbers


def own_kernel(source_ref, *refs):
    chain_refs, sems = refs[:-1], refs[-1]
    rows = chain_refs[0].shape[0]
    copies = []
    for chain, chain_ref in enumerate(chain_refs):
        start = pl.multiple_of((lax.axis_index("rep") * CHAINS + chain) * rows, rows)
        copies.append(pltpu.make_async_copy(source_ref.at[pl.ds(start, rows)], chain_ref, sems.at[chain]))
        copies[-1].start()
    for copy in copies:
        copy.wait()


def own_rows(sources, halves):
    block_rows, samples = sources.shape
    shape = jax.ShapeDtypeStruct((block_rows // halves // CHAINS, samples), BF16)
    return pl.pallas_call(
        own_kernel,
        in_specs=[pl.BlockSpec(memory_space=pl.ANY)],
        out_specs=[pl.BlockSpec(memory_space=pltpu.VMEM)] * CHAINS,
        out_shape=[shape] * CHAINS,
        scratch_shapes=[pltpu.SemaphoreType.DMA((CHAINS,))],
        compiler_params=params(VMEM_BYTES // 4),
        name="own_rows",
    )(in_hbm(sources))


def choose_kernel(which, offsets, number_ref, *refs):
    out_ref, sems = refs[-2:]
    rows = out_ref.shape[0] // CHAINS
    where = number_ref[which]
    waits = []
    for chain in range(CHAINS):
        target = out_ref.at[pl.ds(chain * rows, rows)]
        for place, offset in enumerate(offsets):
            copy = pltpu.make_async_copy(refs[chain * len(offsets) + place], target, sems.at[chain])

            @pl.when(where == offset)
            def _():
                copy.start()

        waits.append(copy)
    for copy in waits:
        copy.wait()


def choose(numbers, which, arrived, offsets):
    pieces = [there[offset] for there in arrived for offset in offsets]
    rows, samples = pieces[0].shape
    any_spec = pl.BlockSpec(memory_space=pl.ANY)
    return pl.pallas_call(
        functools.partial(choose_kernel, which, offsets),
        in_specs=[pl.BlockSpec(memory_space=pltpu.SMEM)] + [any_spec] * len(pieces),
        out_specs=pl.BlockSpec(memory_space=pltpu.VMEM),
        out_shape=jax.ShapeDtypeStruct((rows * CHAINS, samples), BF16),
        scratch_shapes=[pltpu.SemaphoreType.DMA((CHAINS,))],
        compiler_params=params(VMEM_BYTES // 4),
        name="choose",
    )(numbers, *pieces)


def column(row):
    return jnp.broadcast_to(row, (SHIFT_ROWS, row.shape[1])).T[:, :1]


def ones_where(condition):
    return jnp.where(condition, 1.0, 0.0).astype(BF16)


def index_kernel(r_dev, lists_at, cap, tile, block_rows, done, number_ref, *refs):
    pick_ref, place_ref, pass_ref, count_ref, more_pick_ref, more_place_ref, pick_scratch, place_scratch = refs[-8:]
    parcel_refs = refs[:-8]
    if done:
        parcel_refs, (_, _, earlier_pass_ref, earlier_count_ref, _, _) = parcel_refs[:-6], parcel_refs[-6:]
        for group in range(done):
            pass_ref[group] = earlier_pass_ref[group]
            for r in range(r_dev):
                count_ref[group * r_dev + r] = earlier_count_ref[group * r_dev + r]
    nearer, offset = number_ref[0], number_ref[1]
    slots = 2 * r_dev * tile
    window = tile + SPARE
    part = 2 * cap // r_dev
    below = lax.broadcasted_iota(jnp.int32, (cap, cap), 0) < lax.broadcasted_iota(jnp.int32, (cap, cap), 1)
    below = ones_where(below)
    later = []
    for group, parcel_ref in enumerate(parcel_refs, done):
        digits = parcel_ref[:, lists_at:].astype(F32)
        digits = jnp.concatenate([digits[i : i + 1, :part] for i in range(r_dev)], axis=1).astype(jnp.int32)
        packed = digits[:, :cap] * DIGIT + digits[:, cap:]
        pairs, kept = packed // 2, packed % 2 == 1
        source_row, receiver = pairs // r_dev, pairs % r_dev
        turn = jnp.where(source_row // block_rows == nearer, 0, 1)
        row = (source_row + offset) % block_rows
        segment = jnp.where(kept, turn * r_dev + receiver, -1)
        member = lax.broadcasted_iota(jnp.int32, (2 * r_dev, cap), 0) == segment
        earlier = jnp.dot(ones_where(member), below, preferred_element_type=F32)
        of_pair = lambda values: jnp.sum(jnp.where(member, values, 0.0), axis=0, keepdims=True).astype(jnp.int32)
        counts = jnp.sum(jnp.where(member, 1.0, 0.0), axis=1, keepdims=True)
        from_top = jnp.minimum(counts[:r_dev], window)
        from_bottom = jnp.minimum(jnp.minimum(counts[r_dev:], 2.0 * tile - from_top), window)
        first_pass = jnp.concatenate([from_top, from_bottom], axis=0)
        first_slot = jnp.concatenate([jnp.zeros_like(from_top), 2.0 * tile - from_bottom], axis=0)
        rank, limit, begin = of_pair(earlier), of_pair(first_pass), of_pair(first_slot)
        rest = rank - limit
        code = jnp.where(rest < 0, begin + rank, (1 + rest // tile) * slots + turn * tile + rest % tile)
        code = jnp.where(kept, code + receiver * 2 * tile, -1)
        left = counts - first_pass
        which = lax.broadcasted_iota(jnp.int32, left.shape, 0) % r_dev
        passes = 1
        for r in range(r_dev):
            count = jnp.max(jnp.where(which == r, left, 0.0)).astype(jnp.int32)
            count_ref[group * r_dev + r] = count
            passes = jnp.maximum(passes, 1 + (count + tile - 1) // tile)
        pass_ref[group] = passes
        code_column = column(code.astype(F32)).astype(jnp.int32)
        row_column = column(row.astype(F32)).astype(jnp.int32)

        def matrices(number, code=code, turn=turn, code_column=code_column, row_column=row_column):
            start = number * slots
            row_ones = ones_where(row_column == lax.broadcasted_iota(jnp.int32, (cap, block_rows), 1))
            line = lax.broadcasted_iota(jnp.int32, (r_dev * window, 1), 0)
            slot = line // window * (2 * tile) + line % window + start
            of_block = [jnp.where(turn == q, code - q * (2 * tile - window), -1) for q in range(2)]
            by_slot = jnp.concatenate([ones_where(slot == codes) for codes in of_block], axis=0)
            pick = jnp.dot(by_slot, row_ones, preferred_element_type=F32).astype(BF16)
            return pick, ones_where(lax.broadcasted_iota(jnp.int32, (cap, slots), 1) + start == code_column)

        pick_ref[group], place_ref[group] = matrices(0)
        later.append((group, passes, matrices))

    for group, passes, matrices in later:

        @pl.when(passes > 1)
        def _():
            def one_pass(number, carry):
                pick_scratch[...], place_scratch[...] = matrices(number)
                pltpu.sync_copy(pick_scratch, more_pick_ref.at[group, number - 1])
                pltpu.sync_copy(place_scratch, more_place_ref.at[group, number - 1])
                return carry

            lax.fori_loop(1, passes, one_pass, 0)


def index(parcels, numbers, earlier, groups, lists_at, r_dev, cap, tile, block_rows):
    slots = 2 * r_dev * tile
    lines = 2 * r_dev * (tile + SPARE)
    more = -(-(min(block_rows, cap) - (tile - SPARE)) // tile)
    vmem, smem = pl.BlockSpec(memory_space=pltpu.VMEM), pl.BlockSpec(memory_space=pltpu.SMEM)
    any_spec = pl.BlockSpec(memory_space=pl.ANY)
    specs = [vmem, vmem, smem, smem, any_spec, any_spec]
    args = list(parcels)
    done, aliases = 0, {}
    if earlier is not None:
        done = groups - len(parcels)
        aliases = {1 + len(parcels) + place: place for place in (0, 1, 4, 5)}
        args += list(earlier[:4]) + [in_hbm(array) for array in earlier[4:]]
    return pl.pallas_call(
        functools.partial(index_kernel, r_dev, lists_at, cap, tile, block_rows, done),
        in_specs=[smem] + [vmem] * len(parcels) + (specs if done else []),
        out_specs=specs,
        out_shape=[
            jax.ShapeDtypeStruct((groups, lines, block_rows), BF16),
            jax.ShapeDtypeStruct((groups, cap, slots), BF16),
            jax.ShapeDtypeStruct((groups,), jnp.int32),
            jax.ShapeDtypeStruct((groups * r_dev,), jnp.int32),
            pltpu.HBM((groups, more, lines, block_rows), BF16),
            pltpu.HBM((groups, more, cap, slots), BF16),
        ],
        scratch_shapes=[pltpu.VMEM((lines, block_rows), BF16), pltpu.VMEM((cap, slots), BF16)],
        input_output_aliases=aliases,
        compiler_params=params(VMEM_BYTES),
        name="index",
    )(numbers, *args)


def lay_out(heard, number_ref, signal_ref):
    n_win = len(heard)
    r_dev, samples = heard[0].shape
    for distance, span in enumerate(heard):
        begin = lax.rem(number_ref[6] + n_win - distance, n_win) * samples
        signal_ref[:r_dev, pl.ds(pl.multiple_of(begin, LANES), samples)] = span.astype(F32)
    tail = signal_ref.shape[1] - n_win * samples
    signal_ref[:r_dev, n_win * samples :] = jnp.zeros((r_dev, tail), F32)


def first_sample(number_ref, v, n_win, samples):
    return lax.rem(number_ref[6] + n_win - v, n_win) * samples + number_ref[5]


def hankel_rows(signal_ref, r, begin, width, out_ref, place):
    length = width + LANES
    signal = signal_ref[r : r + 1, pl.ds(pl.multiple_of(begin, LANES), length)]
    base = jnp.broadcast_to(signal, (SHIFT_ROWS, length))
    sublane = lax.broadcasted_iota(jnp.int32, base.shape, 0)
    for bit in (1, 2, 4):
        base = jnp.where(sublane & bit != 0, pltpu.roll(base, length - bit, 1), base)
    for first in range(0, LANES, 2 * SHIFT_ROWS):
        both = []
        for shift in (first, first + SHIFT_ROWS):
            rolled = pltpu.roll(base, length - shift, 1) if shift else base
            both.append(rolled[:, :width])
        out_ref[place, first : first + 2 * SHIFT_ROWS, :] = jnp.concatenate(both, axis=0).astype(BF16)


def hankel_kernel(v, n_win, samples, done, number_ref, *refs):
    out_ref, signal_refs = refs[-2:]
    parcel_refs = refs[: -3 if done else -2]
    r_dev = parcel_refs[0].shape[0]
    begin = first_sample(number_ref, v, n_win, samples)
    for group, parcel_ref in enumerate(parcel_refs, done):
        signal_ref = signal_refs.at[group % 2]
        heard = [parcel_ref[:, w * samples : (w + 1) * samples] for w in range(n_win)]
        lay_out(heard, number_ref, signal_ref)
        for r in range(r_dev):
            hankel_rows(signal_ref, r, begin, out_ref.shape[2], out_ref, group * r_dev + r)


def build_hankel(parcels, numbers, earlier, groups, v, n_win, samples, width):
    r_dev = parcels[0].shape[0]
    shape = (groups * r_dev, LANES, width)
    vmem = pl.BlockSpec(memory_space=pltpu.VMEM)
    done = 0 if earlier is None else groups - len(parcels)
    copies = len(parcels) * r_dev * LANES * width
    return pl.pallas_call(
        functools.partial(hankel_kernel, v, n_win, samples, done),
        in_specs=[pl.BlockSpec(memory_space=pltpu.SMEM)] + [vmem] * (len(parcels) + (1 if done else 0)),
        out_specs=vmem,
        scratch_shapes=[pltpu.VMEM((2, SHIFT_ROWS, n_win * samples + LAGS), F32)],
        out_shape=jax.ShapeDtypeStruct(shape, BF16),
        input_output_aliases={1 + len(parcels): 0} if done else {},
        cost_estimate=pl.CostEstimate(flops=copies, bytes_accessed=2 * copies, transcendentals=0),
        compiler_params=params(VMEM_BYTES // 2),
        name="hankel",
    )(numbers, *parcels, *([earlier] if done else []))


def window_of(block, tile):
    return (tile - SPARE if block else 0), tile + SPARE


def pick_rows(block, pieces, pick, gathered, margin):
    count, samples = gathered.shape[0], pieces[0].shape[1]

    def step(t):
        ones = pick[block * count : (block + 1) * count, :]
        rows = jnp.concatenate([piece[:, t : t + STEP] for piece in pieces], axis=0)
        chosen = jnp.dot(ones, rows, preferred_element_type=F32)
        gathered[:, margin + t : margin + t + STEP] = chosen.astype(BF16)

    return [functools.partial(step, t) for t in range(0, samples, STEP)]


def margin_of(lag_dev):
    return lag_dev - STEP


def multiply(gathered, hankel_ref, place, r, rows, lag_dev):
    margin = margin_of(lag_dev)
    length = gathered.shape[1] - margin
    of_channel = slice(r * rows, (r + 1) * rows)
    shifted = [gathered[of_channel, margin - lag : margin - lag + length] for lag in range(0, lag_dev, STEP)]
    tiles = [hankel_ref[place, :, t : t + STEP] for t in range(0, length, LANES)]
    both = jnp.dot(jnp.concatenate(shifted, axis=0), jnp.concatenate(tiles, axis=0), preferred_element_type=F32)
    return [(slice(lag, lag + STEP), both[lag // STEP * rows :][:rows]) for lag in range(0, lag_dev, STEP)]


def split(total, terms, slots, lags):
    count = terms.shape[0] // 2
    upper = total.astype(BF16)
    terms[slots, lags] = upper
    terms[slice(count + slots.start, count + slots.stop), lags] = (total - upper.astype(F32)).astype(BF16)


def placed(place, terms):
    return jnp.dot(jnp.concatenate([place, place], axis=1), terms[...], preferred_element_type=F32)


def correlate_kernel(
    block, parts, v, tile, norming, prebuilt, first, last, steps, pass_ref, count_ref, number_ref, *refs
):
    refs = list(refs)
    pieces = [refs.pop(0) for _ in range(parts)]
    signal_ref, pick_ref, place_ref, more_pick_ref, more_place_ref = [refs.pop(0) for _ in range(5)]
    if not first:
        sums_ref, extra_ref = refs.pop(0), refs.pop(0)
    if last:
        out_hbm = refs.pop(0)
    else:
        handed_ref, left_ref = refs.pop(0), refs.pop(0)
    gathered, terms, extra, pick_scratch, place_scratch, out_ref, sems = refs[:7]
    begin, rows = window_of(block, tile)
    r_dev = gathered.shape[1] // rows
    samples = pieces[0].shape[1]
    at_once, lag_dev = out_ref.shape[0], out_ref.shape[2]
    base = pl.program_id(0) * at_once if steps > 1 else 0
    groups = steps * at_once
    margin = margin_of(lag_dev)

    def hankel_place(group):
        return group * r_dev if prebuilt else 0

    def target(group):
        return out_hbm.at[lax.rem(number_ref[4] + groups - group, groups)]

    if prebuilt:
        hankel_ref = signal_ref
    else:
        hankel_ref, row_ref = refs[7:]
        n_win = signal_ref.shape[2] // samples
        lay_out([signal_ref[0, :, w * samples : (w + 1) * samples] for w in range(n_win)], number_ref, row_ref)
        start = first_sample(number_ref, v, n_win, samples)
        for r in range(r_dev):
            hankel_rows(row_ref, r, start, hankel_ref.shape[2], hankel_ref, r)
    for start in (0, margin + samples) if margin else ():
        gathered[:, :, start : start + margin] = jnp.zeros(gathered.shape[:2] + (margin,), BF16)

    def channel(group, r, rows_of_pass, terms_of_pass):
        slots = slice(r * 2 * tile + begin, r * 2 * tile + begin + rows)
        others = [slice(r * 2 * tile, slots.start), slice(slots.stop, (r + 1) * 2 * tile)]
        others = [other for other in others if other.start < other.stop]
        for lags, total in multiply(rows_of_pass, hankel_ref, hankel_place(group) + r, r, rows, lag_dev):
            if not first:
                total += sums_ref[group, slots, lags]
            if last:
                split(total * norming, terms_of_pass, slots, lags)
                for other in others:
                    split(sums_ref[group, other, lags] * norming, terms_of_pass, other, lags)
            else:
                handed_ref[group, slots, lags] = total
                for other in others if first else []:
                    handed_ref[group, other, lags] = jnp.zeros((other.stop - other.start, STEP), F32)

    for step in pick_rows(block, pieces, pick_ref.at[0], gathered.at[0], margin):
        step()
    copies = []
    for place in range(at_once):
        ahead = []
        if place + 1 < at_once:
            ahead = pick_rows(block, pieces, pick_ref.at[place + 1], gathered.at[(place + 1) % 2], margin)
        share = -(-len(ahead) // r_dev)
        for r in range(r_dev):
            channel(base + place, r, gathered.at[place % 2], terms.at[place % 2])
            for step in ahead[r * share : (r + 1) * share]:
                step()
        if last:
            out_ref[place] = placed(place_ref[place], terms.at[place % 2])
            copies.append(pltpu.make_async_copy(out_ref.at[place], target(base + place), sems.at[place]))
            copies[-1].start()
    for copy in copies:
        copy.wait()

    def later_passes(place, carry):
        group = base + place

        @pl.when(pass_ref[group] > 1)
        def _():
            if first:
                extra[...] = jnp.zeros(extra.shape, F32)
            else:
                pltpu.sync_copy(extra_ref.at[group], extra)

            def one_pass(number, carry):
                pltpu.sync_copy(more_pick_ref.at[group, number - 1], pick_scratch)
                pltpu.sync_copy(more_place_ref.at[group, number - 1], place_scratch)
                for step in pick_rows(block, pieces, pick_scratch, gathered.at[0], margin):
                    step()
                terms[0] = jnp.zeros(terms.shape[1:], BF16)
                for r in range(r_dev):
                    needed = count_ref[group * r_dev + r] > (number - 1) * tile
                    slots = slice(r * 2 * tile + begin, r * 2 * tile + begin + rows)

                    @pl.when(needed)
                    def _():
                        hankel = hankel_place(group) + r
                        for lags, total in multiply(gathered.at[0], hankel_ref, hankel, r, rows, lag_dev):
                            split(total * norming, terms.at[0], slots, lags)

                extra[...] += placed(place_scratch[...], terms.at[0])
                return carry

            lax.fori_loop(1, pass_ref[group], one_pass, 0)
            if last:
                out_ref[place] += extra[...]
                pltpu.sync_copy(out_ref.at[place], target(group))
            else:
                pltpu.sync_copy(extra, left_ref.at[group])

        return carry

    lax.fori_loop(0, at_once, later_passes, 0)


def correlate(block, pieces, signal, prebuilt, numbers, v, matrices, before, last, tile, norming, lag_dev, n_win, r_dev):
    pick, place, passes, counts, more_pick, more_place = matrices
    groups, cap, slots = place.shape
    samples = pieces[0].shape[1]
    width = samples - LANES + lag_dev
    rows = window_of(block, tile)[1]
    at_once = math.gcd(groups, 4 if last else 2) if prebuilt else 1
    by_group = lambda shape: pl.BlockSpec(shape, lambda i, *_: (i, 0, 0))
    any_spec = pl.BlockSpec(memory_space=pl.ANY)
    whole_spec = pl.BlockSpec(memory_space=pltpu.VMEM)
    sums_shape = jax.ShapeDtypeStruct((groups, slots, lag_dev), F32)
    out_shape = jax.ShapeDtypeStruct((groups, cap, lag_dev), F32)
    in_specs = [whole_spec] * len(pieces)
    in_specs.append(whole_spec if prebuilt else by_group((1,) + signal.shape[1:]))
    in_specs += [by_group((at_once,) + pick.shape[1:]), by_group((at_once,) + place.shape[1:]), any_spec, any_spec]
    args = pieces + [signal, pick, place, in_hbm(more_pick), in_hbm(more_place)]
    aliases = {}
    if before is not None:
        in_specs += [whole_spec, any_spec]
        args += [before[0], in_hbm(before[1])]
        if not last:
            aliases = {3 + len(args) - 2: 0}
    scratch = [
        pltpu.VMEM((2, r_dev * rows, samples + 2 * margin_of(lag_dev)), BF16),
        pltpu.VMEM((2, 2 * slots, lag_dev), BF16),
        pltpu.VMEM((cap, lag_dev), F32),
        pltpu.VMEM(pick.shape[1:], BF16),
        pltpu.VMEM(place.shape[1:], BF16),
        pltpu.VMEM((at_once, cap, lag_dev), F32),
        pltpu.SemaphoreType.DMA((at_once,)),
    ]
    if not prebuilt:
        scratch.append(pltpu.VMEM((r_dev, LANES, width), BF16))
        scratch.append(pltpu.VMEM((SHIFT_ROWS, n_win * samples + LAGS), F32))
    body = functools.partial(
        correlate_kernel, block, len(pieces), v, tile, norming, prebuilt, before is None, last, groups // at_once
    )
    return pl.pallas_call(
        body,
        grid_spec=pltpu.PrefetchScalarGridSpec(
            num_scalar_prefetch=3,
            grid=(groups // at_once,),
            in_specs=in_specs,
            out_specs=any_spec if last else [whole_spec, any_spec],
            scratch_shapes=scratch,
        ),
        out_shape=out_shape if last else [sums_shape, pltpu.HBM(out_shape.shape, F32)],
        input_output_aliases=aliases,
        cost_estimate=pl.CostEstimate(
            flops=2 * groups * r_dev * rows * samples * (lag_dev + pick.shape[2]),
            bytes_accessed=2 * groups * slots * lag_dev * 4,
            transcendentals=0,
        ),
        compiler_params=params(VMEM_BYTES if prebuilt else 2 * VMEM_BYTES),
        name="correlate",
    )(passes, counts, numbers, *args)


def shards(sources, receivers, plan, pair_index, keep):
    _, block_rows, samples = sources.shape
    r_dev = receivers.shape[0]
    n_chan = lax.axis_size("chan")
    n_win = lax.axis_size("win")
    n_rep = lax.axis_size("rep")
    cap = pair_index.shape[3]
    lag_dev = LAGS // (n_win * n_rep)
    tile = max(16, cap // 8)
    norming = 1.0 / math.sqrt(samples * n_win)
    width = samples - LANES + lag_dev
    prebuilt = n_chan * r_dev * n_win * LANES * width * 2 <= HANKEL_BYTES

    heard = [receivers] + [turned(receivers, "win", v) for v in range(1, n_win)]
    owns = own_rows(sources[0], n_rep)
    parcels, numbers = pack(plan, heard, pair_index[0, 0], keep[0, 0], n_rep, lag_dev, block_rows, n_chan)
    own_parcel = parcels[0]
    parcels = [turned(parcels[k], "chan", k) for k in range(1, n_chan)]
    matrices = index([own_parcel], numbers, None, n_chan, n_win * samples, r_dev, cap, tile, block_rows)
    if prebuilt:
        signals = [build_hankel([own_parcel], numbers, None, n_chan, v, n_win, samples, width) for v in range(n_win)]

    arrived = [{0: own} for own in owns]

    def relay(step):
        for there in arrived:
            there[step] = swapped(there[1 - step], "chan", 0)
            if step < n_chan - 1:
                there[-step] = swapped(there[step - 1], "chan", 1)

    def after_arrival(step, value):
        for there in arrived:
            for key in (step, -step):
                if key in there:
                    value = lax.optimization_barrier((value, there[key]))[0]
        return value

    def before_start(step, value):
        for there in arrived:
            for key in (1 - step, step - 1):
                there[key] = lax.optimization_barrier((value, there[key]))[1]

    def halves(piece):
        return [piece] + [turned(piece, "rep", -u) for u in range(1, n_rep)]

    def spans(piece):
        return [piece] + [turned(piece, "win", v) for v in range(1, n_win)]

    relay(1)
    before_start(2, (matrices, parcels, signals) if prebuilt else (matrices, parcels))
    parcels = after_arrival(1, parcels)
    relay(2)
    matrices = index(parcels, numbers, matrices, n_chan, n_win * samples, r_dev, cap, tile, block_rows)
    if prebuilt:
        signals[0] = build_hankel(parcels, numbers, signals[0], n_chan, 0, n_win, samples, width)
        before_start(3, (matrices, signals[0]))
    else:
        signals = [jnp.stack([own_parcel] + parcels)[:, :, : n_win * samples]] * n_win
    reach = range(-(n_chan - 2), n_chan - 1)
    near = choose(numbers, 2, arrived, [offset for offset in reach if offset in arrived[0]])
    if prebuilt:
        parcels = after_arrival(2, parcels)
        parcels, near = lax.optimization_barrier((parcels, near))
        for v in range(1, n_win):
            signals[v] = build_hankel(parcels, numbers, signals[v], n_chan, v, n_win, samples, width)
    for step in range(3, n_chan):
        relay(step)
    near_spans = spans(near)
    calls = [(v, q) for v in range(n_win) for q in range(2)]
    calls = calls[:2] + [(v, q) for q in range(2) for v in range(1, n_win)]

    def add(call, span, result):
        v, q = call
        return correlate(
            q, halves(span), signals[v], prebuilt, numbers, v, matrices, result, call == calls[-1], tile, norming, lag_dev,
            n_win, r_dev,
        )

    result = add(calls[0], near, None)
    near_spans = after_arrival(n_chan - 1, near_spans)
    for there in arrived:
        there[n_chan - 1] = lax.optimization_barrier((result, signals, there[n_chan - 1]))[2]
    far_spans = spans(choose(numbers, 3, arrived, sorted(arrived[0])))
    result = add(calls[1], far_spans[0], result)
    for call in calls[2:]:
        if call == (1, 1):
            far_spans, result = lax.optimization_barrier((far_spans, result))
        result = add(call, (near_spans, far_spans)[call[1]][call[0]], result)
    return result[None, None]


def solution(mesh):
    placed_at = (
        P(("grp", "chan"), None, "win"),
        P(("grp", "chan"), "win"),
        P("grp", None),
        P("grp", "chan", None, None),
        P("grp", "chan", None, None),
    )
    return jax.shard_map(
        shards,
        mesh=mesh,
        in_specs=placed_at,
        out_specs=P(("grp", "chan"), None, None, None, ("win", "rep")),
        check_vma=False,
    )
```

```python
import functools
import math

import jax
import jax.numpy as jnp
from jax import lax
from jax.experimental import pallas as pl
from jax.experimental.pallas import tpu as pltpu
from jax.sharding import PartitionSpec as P

LAGS = 2048
LANES = 128
SHIFT_ROWS = 8
STEP = 2 * LANES
CHAINS = 1
COPIES = 4
SPARE = 16
DIGIT = 64
HANKEL_BYTES = 24 * 2**20
VMEM_BYTES = 26 * 2**20
F32 = jnp.float32
BF16 = jnp.bfloat16


def swapped(block, axis, first):
    size = lax.axis_size(axis)
    route = []
    for i in range(first, size - 1, 2):
        route += [(i, i + 1), (i + 1, i)]
    return lax.ppermute(block, axis, route)


def turned(block, axis, distance):
    size = lax.axis_size(axis)
    return lax.ppermute(block, axis, [(i, (i + distance) % size) for i in range(size)])


def in_hbm(array):
    return pltpu.with_memory_space_constraint(array, pltpu.HBM)


def params(vmem):
    return pltpu.CompilerParams(vmem_limit_bytes=vmem)


def pack_kernel(halves, lags, block_rows, n_win, plan_hbm, pair_hbm, keep_hbm, *refs):
    span_hbms, refs = refs[:n_win], refs[n_win:]
    plan_ref, pair_ref, keep_ref, span_refs, digit_ref, sems = refs[-6:]
    parcel_refs, number_ref = refs[:-7], refs[-7]
    small = []
    moves = [(plan_hbm, plan_ref), (pair_hbm, pair_ref), (keep_hbm, keep_ref)]
    moves += [(span, span_refs.at[v]) for v, span in enumerate(span_hbms)]
    for place, (source, target) in enumerate(moves):
        small.append(pltpu.make_async_copy(source, target, sems.at[place]))
        small[-1].start()
    r_dev, samples = span_refs.shape[1:]
    n_chan, cap = pair_ref.shape
    chan, win, rep = lax.axis_index("chan"), lax.axis_index("win"), lax.axis_index("rep")
    for copy in small:
        copy.wait()

    packed = pair_ref[...] * 2 + keep_ref[...]
    digit_ref[:n_chan, :] = jnp.concatenate([packed // DIGIT, packed % DIGIT], axis=1).astype(F32)
    heard = [span_refs[v].astype(F32) for v in range(n_win)]
    part = 2 * cap // r_dev
    spare = parcel_refs[0].shape[1] - n_win * samples - part
    for distance, parcel_ref in enumerate(parcel_refs):
        digits = digit_ref[pl.ds(lax.rem(chan + distance, n_chan), 1), :]
        lists = [digits[:, i * part : (i + 1) * part] for i in range(r_dev)]
        parcel = heard + [jnp.concatenate(lists, axis=0)]
        if spare:
            parcel.append(jnp.zeros((r_dev, spare), F32))
        parcel_ref[...] = jnp.concatenate(parcel, axis=1).astype(BF16)

    one, two = plan_ref[0, 0], plan_ref[0, 1]
    nearer = jnp.where(jnp.abs(one - chan) <= jnp.abs(two - chan), 0, 1)
    sign = jnp.where(chan % 2 == 0, 1, -1)
    number_ref[0] = nearer
    number_ref[1] = block_rows - rep * (block_rows // halves)
    number_ref[2] = sign * (jnp.where(nearer == 0, one, two) - chan)
    number_ref[3] = sign * (jnp.where(nearer == 0, two, one) - chan)
    number_ref[4] = chan
    number_ref[5] = (win * halves + rep) * lags
    number_ref[6] = win


def pack(plan, spans, pair_index, keep, halves, lags, block_rows, n_chan):
    n_win = len(spans)
    r_dev, samples = spans[0].shape
    cap = pair_index.shape[1]
    beside = -(-2 * cap // r_dev // LANES) * LANES
    vmem, smem = pl.BlockSpec(memory_space=pltpu.VMEM), pl.BlockSpec(memory_space=pltpu.SMEM)
    shapes = [jax.ShapeDtypeStruct((r_dev, n_win * samples + beside), BF16)] * n_chan
    shapes.append(jax.ShapeDtypeStruct((7,), jnp.int32))
    *parcels, numbers = pl.pallas_call(
        functools.partial(pack_kernel, halves, lags, block_rows, n_win),
        in_specs=[pl.BlockSpec(memory_space=pl.ANY)] * (3 + n_win),
        out_specs=[vmem] * n_chan + [smem],
        out_shape=shapes,
        scratch_shapes=[
            pltpu.SMEM(plan.shape, plan.dtype),
            pltpu.VMEM(pair_index.shape, pair_index.dtype),
            pltpu.VMEM(keep.shape, keep.dtype),
            pltpu.VMEM((n_win, r_dev, samples), BF16),
            pltpu.VMEM((-(-n_chan // SHIFT_ROWS) * SHIFT_ROWS, 2 * cap), F32),
            pltpu.SemaphoreType.DMA((3 + n_win,)),
        ],
        compiler_params=params(VMEM_BYTES // 2),
        name="pack",
    )(*[in_hbm(a) for a in (plan, pair_index, keep, spans[0])], *spans[1:])
    return parcels, numbers


def own_kernel(source_ref, *refs):
    chain_refs, sems = refs[:-1], refs[-1]
    rows = chain_refs[0].shape[0]
    part = rows // COPIES
    copies = []
    for chain, chain_ref in enumerate(chain_refs):
        for place in range(COPIES):
            start = pl.multiple_of((lax.axis_index("rep") * CHAINS + chain) * rows + place * part, part)
            target = chain_ref.at[pl.ds(place * part, part)]
            copies.append(
                pltpu.make_async_copy(source_ref.at[pl.ds(start, part)], target, sems.at[chain * COPIES + place])
            )
            copies[-1].start()
    for copy in copies:
        copy.wait()


def own_rows(sources, halves):
    block_rows, samples = sources.shape
    shape = jax.ShapeDtypeStruct((block_rows // halves // CHAINS, samples), BF16)
    return pl.pallas_call(
        own_kernel,
        in_specs=[pl.BlockSpec(memory_space=pl.ANY)],
        out_specs=[pl.BlockSpec(memory_space=pltpu.VMEM)] * CHAINS,
        out_shape=[shape] * CHAINS,
        scratch_shapes=[pltpu.SemaphoreType.DMA((CHAINS * COPIES,))],
        compiler_params=params(VMEM_BYTES // 4),
        name="own_rows",
    )(in_hbm(sources))


def choose_kernel(which, offsets, number_ref, *refs):
    out_ref, sems = refs[-2:]
    rows = out_ref.shape[0] // CHAINS
    part = rows // COPIES
    where = number_ref[which]
    waits = []
    for chain in range(CHAINS):
        for piece in range(COPIES):
            target = out_ref.at[pl.ds(chain * rows + piece * part, part)]
            for place, offset in enumerate(offsets):
                source = refs[chain * len(offsets) + place].at[pl.ds(piece * part, part)]
                copy = pltpu.make_async_copy(source, target, sems.at[chain * COPIES + piece])

                @pl.when(where == offset)
                def _():
                    copy.start()

            waits.append(copy)
    for copy in waits:
        copy.wait()


def choose(numbers, which, arrived, offsets):
    pieces = [there[offset] for there in arrived for offset in offsets]
    rows, samples = pieces[0].shape
    any_spec = pl.BlockSpec(memory_space=pl.ANY)
    return pl.pallas_call(
        functools.partial(choose_kernel, which, offsets),
        in_specs=[pl.BlockSpec(memory_space=pltpu.SMEM)] + [any_spec] * len(pieces),
        out_specs=pl.BlockSpec(memory_space=pltpu.VMEM),
        out_shape=jax.ShapeDtypeStruct((rows * CHAINS, samples), BF16),
        scratch_shapes=[pltpu.SemaphoreType.DMA((CHAINS * COPIES,))],
        compiler_params=params(VMEM_BYTES // 4),
        name="choose",
    )(numbers, *pieces)


def column(row):
    return jnp.broadcast_to(row, (SHIFT_ROWS, row.shape[1])).T[:, :1]


def ones_where(condition):
    return jnp.where(condition, 1.0, 0.0).astype(BF16)


def index_kernel(r_dev, lists_at, cap, tile, block_rows, done, number_ref, *refs):
    pick_ref, place_ref, pass_ref, count_ref, more_pick_ref, more_place_ref, pick_scratch, place_scratch = refs[-8:]
    parcel_refs = refs[:-8]
    if done:
        parcel_refs, (_, _, earlier_pass_ref, earlier_count_ref, _, _) = parcel_refs[:-6], parcel_refs[-6:]
        for group in range(done):
            pass_ref[group] = earlier_pass_ref[group]
            for r in range(r_dev):
                count_ref[group * r_dev + r] = earlier_count_ref[group * r_dev + r]
    nearer, offset = number_ref[0], number_ref[1]
    slots = 2 * r_dev * tile
    window = tile + SPARE
    part = 2 * cap // r_dev
    below = lax.broadcasted_iota(jnp.int32, (cap, cap), 0) < lax.broadcasted_iota(jnp.int32, (cap, cap), 1)
    below = ones_where(below)
    later = []
    for group, parcel_ref in enumerate(parcel_refs, done):
        digits = parcel_ref[:, lists_at:].astype(F32)
        digits = jnp.concatenate([digits[i : i + 1, :part] for i in range(r_dev)], axis=1).astype(jnp.int32)
        packed = digits[:, :cap] * DIGIT + digits[:, cap:]
        pairs, kept = packed // 2, packed % 2 == 1
        source_row, receiver = pairs // r_dev, pairs % r_dev
        turn = jnp.where(source_row // block_rows == nearer, 0, 1)
        row = (source_row + offset) % block_rows
        segment = jnp.where(kept, turn * r_dev + receiver, -1)
        member = lax.broadcasted_iota(jnp.int32, (2 * r_dev, cap), 0) == segment
        earlier = jnp.dot(ones_where(member), below, preferred_element_type=F32)
        of_pair = lambda values: jnp.sum(jnp.where(member, values, 0.0), axis=0, keepdims=True).astype(jnp.int32)
        counts = jnp.sum(jnp.where(member, 1.0, 0.0), axis=1, keepdims=True)
        from_top = jnp.minimum(counts[:r_dev], window)
        from_bottom = jnp.minimum(jnp.minimum(counts[r_dev:], 2.0 * tile - from_top), window)
        first_pass = jnp.concatenate([from_top, from_bottom], axis=0)
        first_slot = jnp.concatenate([jnp.zeros_like(from_top), 2.0 * tile - from_bottom], axis=0)
        rank, limit, begin = of_pair(earlier), of_pair(first_pass), of_pair(first_slot)
        rest = rank - limit
        code = jnp.where(rest < 0, begin + rank, (1 + rest // tile) * slots + turn * tile + rest % tile)
        code = jnp.where(kept, code + receiver * 2 * tile, -1)
        left = counts - first_pass
        which = lax.broadcasted_iota(jnp.int32, left.shape, 0) % r_dev
        passes = 1
        for r in range(r_dev):
            count = jnp.max(jnp.where(which == r, left, 0.0)).astype(jnp.int32)
            count_ref[group * r_dev + r] = count
            passes = jnp.maximum(passes, 1 + (count + tile - 1) // tile)
        pass_ref[group] = passes
        code_column = column(code.astype(F32)).astype(jnp.int32)
        row_column = column(row.astype(F32)).astype(jnp.int32)

        def matrices(number, code=code, turn=turn, code_column=code_column, row_column=row_column):
            start = number * slots
            row_ones = ones_where(row_column == lax.broadcasted_iota(jnp.int32, (cap, block_rows), 1))
            line = lax.broadcasted_iota(jnp.int32, (r_dev * window, 1), 0)
            slot = line // window * (2 * tile) + line % window + start
            of_block = [jnp.where(turn == q, code - q * (2 * tile - window), -1) for q in range(2)]
            by_slot = jnp.concatenate([ones_where(slot == codes) for codes in of_block], axis=0)
            pick = jnp.dot(by_slot, row_ones, preferred_element_type=F32).astype(BF16)
            return pick, ones_where(lax.broadcasted_iota(jnp.int32, (cap, slots), 1) + start == code_column)

        pick_ref[group], place_ref[group] = matrices(0)
        later.append((group, passes, matrices))

    for group, passes, matrices in later:

        @pl.when(passes > 1)
        def _():
            def one_pass(number, carry):
                pick_scratch[...], place_scratch[...] = matrices(number)
                pltpu.sync_copy(pick_scratch, more_pick_ref.at[group, number - 1])
                pltpu.sync_copy(place_scratch, more_place_ref.at[group, number - 1])
                return carry

            lax.fori_loop(1, passes, one_pass, 0)


def index(parcels, numbers, earlier, groups, lists_at, r_dev, cap, tile, block_rows):
    slots = 2 * r_dev * tile
    lines = 2 * r_dev * (tile + SPARE)
    more = -(-(min(block_rows, cap) - (tile - SPARE)) // tile)
    vmem, smem = pl.BlockSpec(memory_space=pltpu.VMEM), pl.BlockSpec(memory_space=pltpu.SMEM)
    any_spec = pl.BlockSpec(memory_space=pl.ANY)
    specs = [vmem, vmem, smem, smem, any_spec, any_spec]
    args = list(parcels)
    done, aliases = 0, {}
    if earlier is not None:
        done = groups - len(parcels)
        aliases = {1 + len(parcels) + place: place for place in (0, 1, 4, 5)}
        args += list(earlier[:4]) + [in_hbm(array) for array in earlier[4:]]
    return pl.pallas_call(
        functools.partial(index_kernel, r_dev, lists_at, cap, tile, block_rows, done),
        in_specs=[smem] + [vmem] * len(parcels) + (specs if done else []),
        out_specs=specs,
        out_shape=[
            jax.ShapeDtypeStruct((groups, lines, block_rows), BF16),
            jax.ShapeDtypeStruct((groups, cap, slots), BF16),
            jax.ShapeDtypeStruct((groups,), jnp.int32),
            jax.ShapeDtypeStruct((groups * r_dev,), jnp.int32),
            pltpu.HBM((groups, more, lines, block_rows), BF16),
            pltpu.HBM((groups, more, cap, slots), BF16),
        ],
        scratch_shapes=[pltpu.VMEM((lines, block_rows), BF16), pltpu.VMEM((cap, slots), BF16)],
        input_output_aliases=aliases,
        compiler_params=params(VMEM_BYTES),
        name="index",
    )(numbers, *args)


def lay_out(heard, number_ref, signal_ref):
    n_win = len(heard)
    r_dev, samples = heard[0].shape
    for distance, span in enumerate(heard):
        begin = lax.rem(number_ref[6] + n_win - distance, n_win) * samples
        signal_ref[:r_dev, pl.ds(pl.multiple_of(begin, LANES), samples)] = span.astype(F32)
    tail = signal_ref.shape[1] - n_win * samples
    signal_ref[:r_dev, n_win * samples :] = jnp.zeros((r_dev, tail), F32)


def first_sample(number_ref, v, n_win, samples):
    return lax.rem(number_ref[6] + n_win - v, n_win) * samples + number_ref[5]


def hankel_rows(signal_ref, r, begin, width, out_ref, place):
    length = width + LANES
    signal = signal_ref[r : r + 1, pl.ds(pl.multiple_of(begin, LANES), length)]
    base = jnp.broadcast_to(signal, (SHIFT_ROWS, length))
    sublane = lax.broadcasted_iota(jnp.int32, base.shape, 0)
    for bit in (1, 2, 4):
        base = jnp.where(sublane & bit != 0, pltpu.roll(base, length - bit, 1), base)
    for first in range(0, LANES, 2 * SHIFT_ROWS):
        both = []
        for shift in (first, first + SHIFT_ROWS):
            rolled = pltpu.roll(base, length - shift, 1) if shift else base
            both.append(rolled[:, :width])
        out_ref[place, first : first + 2 * SHIFT_ROWS, :] = jnp.concatenate(both, axis=0).astype(BF16)


def hankel_kernel(v, n_win, samples, done, number_ref, *refs):
    out_ref, signal_refs = refs[-2:]
    parcel_refs = refs[: -3 if done else -2]
    r_dev = parcel_refs[0].shape[0]
    begin = first_sample(number_ref, v, n_win, samples)
    for group, parcel_ref in enumerate(parcel_refs, done):
        signal_ref = signal_refs.at[group % 2]
        heard = [parcel_ref[:, w * samples : (w + 1) * samples] for w in range(n_win)]
        lay_out(heard, number_ref, signal_ref)
        for r in range(r_dev):
            hankel_rows(signal_ref, r, begin, out_ref.shape[2], out_ref, group * r_dev + r)


def build_hankel(parcels, numbers, earlier, groups, v, n_win, samples, width):
    r_dev = parcels[0].shape[0]
    shape = (groups * r_dev, LANES, width)
    vmem = pl.BlockSpec(memory_space=pltpu.VMEM)
    done = 0 if earlier is None else groups - len(parcels)
    copies = len(parcels) * r_dev * LANES * width
    return pl.pallas_call(
        functools.partial(hankel_kernel, v, n_win, samples, done),
        in_specs=[pl.BlockSpec(memory_space=pltpu.SMEM)] + [vmem] * (len(parcels) + (1 if done else 0)),
        out_specs=vmem,
        scratch_shapes=[pltpu.VMEM((2, SHIFT_ROWS, n_win * samples + LAGS), F32)],
        out_shape=jax.ShapeDtypeStruct(shape, BF16),
        input_output_aliases={1 + len(parcels): 0} if done else {},
        cost_estimate=pl.CostEstimate(flops=copies, bytes_accessed=2 * copies, transcendentals=0),
        compiler_params=params(VMEM_BYTES // 2),
        name="hankel",
    )(numbers, *parcels, *([earlier] if done else []))


def window_of(block, tile):
    return (tile - SPARE if block else 0), tile + SPARE


def pick_rows(block, pieces, pick, gathered, margin):
    count, samples = gathered.shape[0], pieces[0].shape[1]

    def step(t):
        ones = pick[block * count : (block + 1) * count, :]
        rows = jnp.concatenate([piece[:, t : t + STEP] for piece in pieces], axis=0)
        chosen = jnp.dot(ones, rows, preferred_element_type=F32)
        gathered[:, margin + t : margin + t + STEP] = chosen.astype(BF16)

    return [functools.partial(step, t) for t in range(0, samples, STEP)]


def margin_of(lag_dev):
    return lag_dev - STEP


def multiply(gathered, hankel_ref, place, r, rows, lag_dev):
    margin = margin_of(lag_dev)
    length = gathered.shape[1] - margin
    of_channel = slice(r * rows, (r + 1) * rows)
    shifted = [gathered[of_channel, margin - lag : margin - lag + length] for lag in range(0, lag_dev, STEP)]
    tiles = [hankel_ref[place, :, t : t + STEP] for t in range(0, length, LANES)]
    both = jnp.dot(jnp.concatenate(shifted, axis=0), jnp.concatenate(tiles, axis=0), preferred_element_type=F32)
    return [(slice(lag, lag + STEP), both[lag // STEP * rows :][:rows]) for lag in range(0, lag_dev, STEP)]


def split(total, terms, slots, lags):
    count = terms.shape[0] // 2
    upper = total.astype(BF16)
    terms[slots, lags] = upper
    terms[slice(count + slots.start, count + slots.stop), lags] = (total - upper.astype(F32)).astype(BF16)


def placed(place, terms):
    return jnp.dot(jnp.concatenate([place, place], axis=1), terms[...], preferred_element_type=F32)


def correlate_kernel(
    block, parts, v, tile, norming, prebuilt, first, last, steps, pass_ref, count_ref, number_ref, *refs
):
    refs = list(refs)
    pieces = [refs.pop(0) for _ in range(parts)]
    signal_ref, pick_ref, place_ref, more_pick_ref, more_place_ref = [refs.pop(0) for _ in range(5)]
    if not first:
        sums_ref, extra_ref = refs.pop(0), refs.pop(0)
    if last:
        out_hbm = refs.pop(0)
    else:
        handed_ref, left_ref = refs.pop(0), refs.pop(0)
    gathered, terms, extra, pick_scratch, place_scratch, out_ref, sems = refs[:7]
    begin, rows = window_of(block, tile)
    r_dev = gathered.shape[1] // rows
    samples = pieces[0].shape[1]
    at_once, lag_dev = out_ref.shape[0], out_ref.shape[2]
    base = pl.program_id(0) * at_once if steps > 1 else 0
    groups = steps * at_once
    margin = margin_of(lag_dev)

    def hankel_place(group):
        return group * r_dev if prebuilt else 0

    def target(group):
        return out_hbm.at[lax.rem(number_ref[4] + groups - group, groups)]

    if prebuilt:
        hankel_ref = signal_ref
    else:
        hankel_ref, row_ref = refs[7:]
        n_win = signal_ref.shape[2] // samples
        lay_out([signal_ref[0, :, w * samples : (w + 1) * samples] for w in range(n_win)], number_ref, row_ref)
        start = first_sample(number_ref, v, n_win, samples)
        for r in range(r_dev):
            hankel_rows(row_ref, r, start, hankel_ref.shape[2], hankel_ref, r)
    for start in (0, margin + samples) if margin else ():
        gathered[:, :, start : start + margin] = jnp.zeros(gathered.shape[:2] + (margin,), BF16)

    def channel(group, r, rows_of_pass, terms_of_pass):
        slots = slice(r * 2 * tile + begin, r * 2 * tile + begin + rows)
        others = [slice(r * 2 * tile, slots.start), slice(slots.stop, (r + 1) * 2 * tile)]
        others = [other for other in others if other.start < other.stop]
        for lags, total in multiply(rows_of_pass, hankel_ref, hankel_place(group) + r, r, rows, lag_dev):
            if not first:
                total += sums_ref[group, slots, lags]
            if last:
                split(total * norming, terms_of_pass, slots, lags)
                for other in others:
                    split(sums_ref[group, other, lags] * norming, terms_of_pass, other, lags)
            else:
                handed_ref[group, slots, lags] = total
                for other in others if first else []:
                    handed_ref[group, other, lags] = jnp.zeros((other.stop - other.start, STEP), F32)

    for step in pick_rows(block, pieces, pick_ref.at[0], gathered.at[0], margin):
        step()
    copies = []
    for place in range(at_once):
        ahead = []
        if place + 1 < at_once:
            ahead = pick_rows(block, pieces, pick_ref.at[place + 1], gathered.at[(place + 1) % 2], margin)
        share = -(-len(ahead) // r_dev)
        for r in range(r_dev):
            channel(base + place, r, gathered.at[place % 2], terms.at[place % 2])
            for step in ahead[r * share : (r + 1) * share]:
                step()
        if last:
            out_ref[place] = placed(place_ref[place], terms.at[place % 2])
            copies.append(pltpu.make_async_copy(out_ref.at[place], target(base + place), sems.at[place]))
            copies[-1].start()
    for copy in copies:
        copy.wait()

    def later_passes(place, carry):
        group = base + place

        @pl.when(pass_ref[group] > 1)
        def _():
            if first:
                extra[...] = jnp.zeros(extra.shape, F32)
            else:
                pltpu.sync_copy(extra_ref.at[group], extra)

            def one_pass(number, carry):
                pltpu.sync_copy(more_pick_ref.at[group, number - 1], pick_scratch)
                pltpu.sync_copy(more_place_ref.at[group, number - 1], place_scratch)
                for step in pick_rows(block, pieces, pick_scratch, gathered.at[0], margin):
                    step()
                terms[0] = jnp.zeros(terms.shape[1:], BF16)
                for r in range(r_dev):
                    needed = count_ref[group * r_dev + r] > (number - 1) * tile
                    slots = slice(r * 2 * tile + begin, r * 2 * tile + begin + rows)

                    @pl.when(needed)
                    def _():
                        hankel = hankel_place(group) + r
                        for lags, total in multiply(gathered.at[0], hankel_ref, hankel, r, rows, lag_dev):
                            split(total * norming, terms.at[0], slots, lags)

                extra[...] += placed(place_scratch[...], terms.at[0])
                return carry

            lax.fori_loop(1, pass_ref[group], one_pass, 0)
            if last:
                out_ref[place] += extra[...]
                pltpu.sync_copy(out_ref.at[place], target(group))
            else:
                pltpu.sync_copy(extra, left_ref.at[group])

        return carry

    lax.fori_loop(0, at_once, later_passes, 0)


def correlate(block, pieces, signal, prebuilt, numbers, v, matrices, before, last, tile, norming, lag_dev, n_win, r_dev):
    pick, place, passes, counts, more_pick, more_place = matrices
    groups, cap, slots = place.shape
    samples = pieces[0].shape[1]
    width = samples - LANES + lag_dev
    rows = window_of(block, tile)[1]
    at_once = math.gcd(groups, 4 if last else 2) if prebuilt else 1
    by_group = lambda shape: pl.BlockSpec(shape, lambda i, *_: (i, 0, 0))
    any_spec = pl.BlockSpec(memory_space=pl.ANY)
    whole_spec = pl.BlockSpec(memory_space=pltpu.VMEM)
    sums_shape = jax.ShapeDtypeStruct((groups, slots, lag_dev), F32)
    out_shape = jax.ShapeDtypeStruct((groups, cap, lag_dev), F32)
    in_specs = [whole_spec] * len(pieces)
    in_specs.append(whole_spec if prebuilt else by_group((1,) + signal.shape[1:]))
    in_specs += [by_group((at_once,) + pick.shape[1:]), by_group((at_once,) + place.shape[1:]), any_spec, any_spec]
    args = pieces + [signal, pick, place, in_hbm(more_pick), in_hbm(more_place)]
    aliases = {}
    if before is not None:
        in_specs += [whole_spec, any_spec]
        args += [before[0], in_hbm(before[1])]
        if not last:
            aliases = {3 + len(args) - 2: 0}
    scratch = [
        pltpu.VMEM((2, r_dev * rows, samples + 2 * margin_of(lag_dev)), BF16),
        pltpu.VMEM((2, 2 * slots, lag_dev), BF16),
        pltpu.VMEM((cap, lag_dev), F32),
        pltpu.VMEM(pick.shape[1:], BF16),
        pltpu.VMEM(place.shape[1:], BF16),
        pltpu.VMEM((at_once, cap, lag_dev), F32),
        pltpu.SemaphoreType.DMA((at_once,)),
    ]
    if not prebuilt:
        scratch.append(pltpu.VMEM((r_dev, LANES, width), BF16))
        scratch.append(pltpu.VMEM((SHIFT_ROWS, n_win * samples + LAGS), F32))
    body = functools.partial(
        correlate_kernel, block, len(pieces), v, tile, norming, prebuilt, before is None, last, groups // at_once
    )
    return pl.pallas_call(
        body,
        grid_spec=pltpu.PrefetchScalarGridSpec(
            num_scalar_prefetch=3,
            grid=(groups // at_once,),
            in_specs=in_specs,
            out_specs=any_spec if last else [whole_spec, any_spec],
            scratch_shapes=scratch,
        ),
        out_shape=out_shape if last else [sums_shape, pltpu.HBM(out_shape.shape, F32)],
        input_output_aliases=aliases,
        cost_estimate=pl.CostEstimate(
            flops=2 * groups * r_dev * rows * samples * (lag_dev + pick.shape[2]),
            bytes_accessed=2 * groups * slots * lag_dev * 4,
            transcendentals=0,
        ),
        compiler_params=params(VMEM_BYTES if prebuilt else 2 * VMEM_BYTES),
        name="correlate",
    )(passes, counts, numbers, *args)


def shards(sources, receivers, plan, pair_index, keep):
    _, block_rows, samples = sources.shape
    r_dev = receivers.shape[0]
    n_chan = lax.axis_size("chan")
    n_win = lax.axis_size("win")
    n_rep = lax.axis_size("rep")
    cap = pair_index.shape[3]
    lag_dev = LAGS // (n_win * n_rep)
    tile = max(16, cap // 8)
    norming = 1.0 / math.sqrt(samples * n_win)
    width = samples - LANES + lag_dev
    prebuilt = n_chan * r_dev * n_win * LANES * width * 2 <= HANKEL_BYTES

    heard = [receivers] + [turned(receivers, "win", v) for v in range(1, n_win)]
    owns = own_rows(sources[0], n_rep)
    parcels, numbers = pack(plan, heard, pair_index[0, 0], keep[0, 0], n_rep, lag_dev, block_rows, n_chan)
    own_parcel = parcels[0]
    parcels = [turned(parcels[k], "chan", k) for k in range(1, n_chan)]
    matrices = index([own_parcel], numbers, None, n_chan, n_win * samples, r_dev, cap, tile, block_rows)
    if prebuilt:
        signals = [build_hankel([own_parcel], numbers, None, n_chan, v, n_win, samples, width) for v in range(n_win)]

    arrived = [{0: own} for own in owns]

    def relay(step):
        for there in arrived:
            there[step] = swapped(there[1 - step], "chan", 0)
            if step < n_chan - 1:
                there[-step] = swapped(there[step - 1], "chan", 1)

    def after_arrival(step, value):
        for there in arrived:
            for key in (step, -step):
                if key in there:
                    value = lax.optimization_barrier((value, there[key]))[0]
        return value

    def before_start(step, value):
        for there in arrived:
            for key in (1 - step, step - 1):
                there[key] = lax.optimization_barrier((value, there[key]))[1]

    def halves(piece):
        return [piece] + [turned(piece, "rep", -u) for u in range(1, n_rep)]

    def spans(piece):
        return [piece] + [turned(piece, "win", v) for v in range(1, n_win)]

    relay(1)
    before_start(2, (matrices, parcels, signals) if prebuilt else (matrices, parcels))
    parcels = after_arrival(1, parcels)
    relay(2)
    matrices = index(parcels, numbers, matrices, n_chan, n_win * samples, r_dev, cap, tile, block_rows)
    if prebuilt:
        signals[0] = build_hankel(parcels, numbers, signals[0], n_chan, 0, n_win, samples, width)
        before_start(3, (matrices, signals[0]))
    else:
        signals = [jnp.stack([own_parcel] + parcels)[:, :, : n_win * samples]] * n_win
    reach = range(-(n_chan - 2), n_chan - 1)
    near = choose(numbers, 2, arrived, [offset for offset in reach if offset in arrived[0]])
    if prebuilt:
        parcels = after_arrival(2, parcels)
        parcels, near = lax.optimization_barrier((parcels, near))
        for v in range(1, n_win):
            signals[v] = build_hankel(parcels, numbers, signals[v], n_chan, v, n_win, samples, width)
    for step in range(3, n_chan):
        relay(step)
    near_spans = spans(near)
    calls = [(v, q) for v in range(n_win) for q in range(2)]
    calls = calls[:2] + [(v, q) for q in range(2) for v in range(1, n_win)]

    def add(call, span, result):
        v, q = call
        return correlate(
            q, halves(span), signals[v], prebuilt, numbers, v, matrices, result, call == calls[-1], tile, norming, lag_dev,
            n_win, r_dev,
        )

    result = add(calls[0], near, None)
    near_spans = after_arrival(n_chan - 1, near_spans)
    for there in arrived:
        there[n_chan - 1] = lax.optimization_barrier((result, signals, there[n_chan - 1]))[2]
    far_spans = spans(choose(numbers, 3, arrived, sorted(arrived[0])))
    result = add(calls[1], far_spans[0], result)
    for call in calls[2:]:
        if call == (1, 1):
            far_spans, result = lax.optimization_barrier((far_spans, result))
        result = add(call, (near_spans, far_spans)[call[1]][call[0]], result)
    return result[None, None]


def solution(mesh):
    placed_at = (
        P(("grp", "chan"), None, "win"),
        P(("grp", "chan"), "win"),
        P("grp", None),
        P("grp", "chan", None, None),
        P("grp", "chan", None, None),
    )
    return jax.shard_map(
        shards,
        mesh=mesh,
        in_specs=placed_at,
        out_specs=P(("grp", "chan"), None, None, None, ("win", "rep")),
        check_vma=False,
    )
```
